32 devices in a mesh: section: 8 (over z, y), dp: 4 (over x, core).
Axes of the slice: x: 2, y: 2, z: 4, core: 2. Of those that a mesh axis runs over, the one named last changes fastest.
Arguments:
- checkpoints: bfloat16 [8, 3, 64, 1024], P('section', None, None, 'dp'), may hold values from -6 to 6
- gain: float32 [8, 1024], P('section'), may hold values from 0.25 to 1.75
- w_in: bfloat16 [8, 1024, 8192], P('section', None, 'dp'), may hold values from -0.09375 to 0.09375
- w_out: bfloat16 [8, 8192, 1024], P('section', 'dp'), may hold values from -0.0625 to 0.0625
- cotangent: bfloat16 [3, 64, 4096], P(None, None, 'dp'), may hold values from -6 to 6
Outputs:
- grad_in: bfloat16 [8, 1024, 8192], P('section', None, 'dp')
- grad_out: bfloat16 [8, 8192, 1024], P('section', 'dp')
- grad_gain: float32 [8, 1024], P('section', 'dp')
- section_grads: bfloat16 [8, 3, 64, 1024], P('section', None, None, 'dp')
The draws below stay inside these ranges and needn't reach their ends.
All inputs are finite; a program needn't handle non-finite values.
Results may differ from the reference program's by a relative error of at most 0.04.
Values may be sent and summed in bfloat16 or wider, within the bound.
No kernel may reach another device: no remote copies, remote signals or barrier semaphores. Data moves between devices by JAX's collectives and lax.ppermute only.
A program may use at most 64 MiB of HBM per device.

```python
import jax
import jax.numpy as jnp
from jax import lax

D = 4096
FF = 8192
TOK = 64
MICRO = 3
QD = 1024
LAYERS = 2
N_SECTION = 8
N_DP = 4


def steps_of(own_key, extent, cuts, smallest, top_value):
    level, own = 1.0, jax.random.fold_in(own_key, 6)
    for axis_at, shards_of in cuts:
        heights = jnp.exp(jax.random.uniform(jax.random.fold_in(own, axis_at), (shards_of,), jnp.float32, smallest / len(cuts), top_value / len(cuts)))
        level = level * jnp.repeat(heights, extent[axis_at] // shards_of).reshape([-1 if axis == axis_at else 1 for axis in range(len(extent))])
    return level


def centred(stream_key, shape, deviation, most, split=(), kind=jnp.bfloat16):
    drawn = jax.random.normal(stream_key, shape, jnp.float32) * deviation
    if len(split) > 0:
        drawn = steps_of(stream_key, shape, split, -0.22, 0.18) * drawn
    return jnp.clip(drawn, min=-most, max=most).astype(kind)


def setup_inputs(seed: int = 0) -> dict:
    seeds = jax.random.split(jax.random.key(seed), 6)
    checkpoints = centred(seeds[0], (N_SECTION, MICRO, TOK, QD), 1.0, 6.0, ((0, 8), (3, 4)))
    gain = jnp.clip(1.0 + 0.15 * jax.random.normal(seeds[1], (N_SECTION, QD), jnp.float32), 0.25, 1.75)
    w_in = centred(seeds[2], (N_SECTION, QD, FF), D ** -0.5, 0.09375, ((0, 8), (2, 4)))
    w_out = centred(seeds[3], (N_SECTION, FF, QD), FF ** -0.5, 0.0625, ((0, 8), (1, 4)))
    cotangent = centred(seeds[4], (MICRO, TOK, D), 1.0, 6.0, ((2, 4),))
    return dict(checkpoints=checkpoints, gain=gain, w_in=w_in, w_out=w_out, cotangent=cotangent)


def gelu_tanh(value):
    return jax.nn.gelu(value, approximate=True)

def layer_back(x_saved, gain_row, weight_in, weight_out, grad_b):
    x_full = x_saved.astype(jnp.float32)
    scale = lax.rsqrt(lax.optimization_barrier(jnp.mean(x_full * x_full, axis=-1, keepdims=True)) + 1e-06)
    normed = x_full * scale
    scaled = (normed * gain_row).astype(jnp.bfloat16)
    act = jnp.dot(scaled, weight_in, preferred_element_type=jnp.float32)
    hidden, pull = jax.vjp(gelu_tanh, act)
    hidden_b = hidden.astype(jnp.bfloat16)
    dhid = jnp.dot(grad_b, weight_out.T, preferred_element_type=jnp.float32)
    dact = pull(dhid)[0].astype(jnp.bfloat16)
    gout = jnp.dot(hidden_b.T, grad_b, preferred_element_type=jnp.float32)
    gin = jnp.dot(scaled.T, dact, preferred_element_type=jnp.float32)
    share = FF // N_DP
    pieces = jnp.einsum('tnf,enf->nte', dact.astype(jnp.float32).reshape(TOK, N_DP, share), weight_in.astype(jnp.float32).reshape(D, N_DP, share))
    rounded = lax.optimization_barrier(pieces.astype(jnp.bfloat16))
    dnorm_in = lax.optimization_barrier(jnp.sum(rounded.astype(jnp.float32), axis=0))
    dnorm = dnorm_in * gain_row
    inner = lax.optimization_barrier(jnp.mean(dnorm * normed, axis=-1, keepdims=True))
    grad_x = (grad_b.astype(jnp.float32) + scale * (dnorm - normed * inner)).astype(jnp.bfloat16)
    dgain = lax.optimization_barrier(jnp.sum(dnorm_in * normed, axis=0))
    return (grad_x, gin, gout, dgain)

def reference(checkpoints, gain, w_in, w_out, cotangent):
    saved_all = checkpoints.reshape(LAYERS, 4, MICRO, TOK, QD).transpose(0, 2, 3, 1, 4).reshape(LAYERS, MICRO, TOK, D)
    gain_all = gain.reshape(LAYERS, D)
    win_all = w_in.reshape(LAYERS, D, FF)
    wout_all = w_out.reshape(LAYERS, 4, FF, QD).transpose(0, 2, 1, 3).reshape(LAYERS, FF, D)

    def one_section(grads, items):
        saved, gain_row, weight_in, weight_out = items

        def one_micro(pair):
            return layer_back(pair[0], gain_row, weight_in, weight_out, pair[1])
        grad_x, gin, gout, dgain = lax.map(one_micro, (saved, grads))
        result = (grad_x, lax.optimization_barrier(jnp.sum(gin, axis=0)).astype(jnp.bfloat16), lax.optimization_barrier(jnp.sum(gout, axis=0)).astype(jnp.bfloat16), lax.optimization_barrier(jnp.sum(dgain, axis=0)))
        return (grad_x, result)
    items = (saved_all[::-1], gain_all[::-1], win_all[::-1], wout_all[::-1])
    final, stacked = lax.scan(one_section, cotangent, items)
    grad_x, gin, gout, dgain = stacked
    gin = gin[::-1].reshape(N_SECTION, QD, FF)
    gout = gout[::-1].reshape(LAYERS, FF, 4, QD).transpose(0, 2, 1, 3).reshape(N_SECTION, FF, QD)
    dgain = dgain[::-1].reshape(N_SECTION, QD)
    grad_x = grad_x[::-1].reshape(LAYERS, MICRO, TOK, 4, QD).transpose(0, 3, 1, 2, 4).reshape(N_SECTION, MICRO, TOK, QD)
    return (gin, gout, dgain, grad_x)
```

```python
import jax
import jax.numpy as jnp
from jax import lax
from jax.sharding import PartitionSpec as P

F32 = jnp.float32
BF16 = jnp.bfloat16


def flip(block, axis, bits):
    count = lax.axis_size(axis)
    return lax.ppermute(block, axis, [(i, i ^ bits) for i in range(count)])


def side_rows(values, width):
    lead = values.astype(BF16)
    trail = (values - lead.astype(F32)).astype(BF16)
    flat = jnp.concatenate([lead, trail])
    return jnp.pad(flat, (0, 16 * width - flat.shape[0])).reshape(16, width)


def side_values(rows, count):
    flat = rows.reshape(-1)
    return flat[:count].astype(F32) + flat[count:2 * count].astype(F32)


def gelu_tanh(value):
    return jax.nn.gelu(value, approximate=True)


def shards(checkpoints, gain, w_in, w_out, cotangent):
    sections = lax.axis_size("section")
    n_dp = lax.axis_size("dp")
    here = lax.axis_index("section")
    lane = lax.axis_index("dp")
    layers = sections // 4
    mine = here % 4
    last = here // 4 == layers - 1
    _, micro, tok, share = checkpoints.shape
    rows = micro * tok
    quarter = share * n_dp
    width = 4 * quarter
    gain_row = gain[0]
    weight_in = w_in[0]
    weight_out = w_out[0]
    hidden = weight_in.shape[1]
    piece = hidden // 4
    core = lane % 2

    def gather_dp(block):
        bit = n_dp // 2
        parts = {0: block}
        while bit >= 1:
            other = flip(jnp.concatenate([parts[j] for j in parts], axis=1), "dp", bit)
            for at, j in enumerate(list(parts)):
                parts[j ^ bit] = other[:, at * block.shape[1]:(at + 1) * block.shape[1]]
            bit //= 2
        full = jnp.zeros((rows, quarter), block.dtype)
        for j, part in parts.items():
            full = lax.dynamic_update_slice(full, part, (0, (lane ^ j) * block.shape[1]))
        return full

    def cot_quarter(block):
        if n_dp < 4:
            whole = lax.all_gather(block, "dp", axis=1, tiled=True)
            return lax.dynamic_slice_in_dim(whole, mine * quarter, quarter, 1)
        per = n_dp // 4
        top = [s * n_dp + d for s in range(sections) for d in range(n_dp) if s // 4 == layers - 1]
        held = block
        far = lambda i, b: (i % n_dp // per ^ i // n_dp % 4) & b
        got = lax.ppermute(held, ("section", "dp"), [(i, i ^ 2 * per) for i in top if far(i, 3) == 0])
        held = jnp.where((lane // per ^ mine) & 2 == 0, held, got)
        got = lax.ppermute(held, ("section", "dp"), [(i, i ^ per) for i in top if far(i, 1) == 0])
        held = jnp.where((lane // per ^ mine) & 1 == 0, held, got)
        if per == 1:
            return held
        parts = {0: held}
        bit = per // 2
        while bit >= 1:
            for j in list(parts):
                parts[j ^ bit] = flip(parts[j], "dp", bit)
            bit //= 2
        full = jnp.zeros((rows, quarter), block.dtype)
        for j, part in parts.items():
            full = lax.dynamic_update_slice(full, part, (0, (lane % per ^ j) * block.shape[1]))
        return full

    def cut(values, j):
        return lax.dynamic_slice_in_dim(values, (mine ^ j) * piece, piece, 1)

    def fill(parts):
        full = jnp.zeros((rows, hidden), parts[0].dtype)
        for j, part in enumerate(parts):
            full = lax.dynamic_update_slice(full, part, (0, (mine ^ j) * piece))
        return full

    x_full = gather_dp(checkpoints[0].reshape(rows, share))
    cot = cot_quarter(cotangent.reshape(rows, cotangent.shape[2]))
    x_wide = x_full.astype(F32)
    scaled_raw = (x_wide * gain_row).astype(BF16)
    squares = jnp.sum(x_wide * x_wide, axis=1)

    act_raw = jnp.dot(scaled_raw, weight_in, preferred_element_type=F32)
    extra = side_rows(squares, piece)
    act = cut(act_raw, 0)
    for j in (3, 1, 2):
        got = flip(jnp.concatenate([cut(act_raw, j).astype(BF16), extra], axis=0), "section", j)
        act = act + got[:rows].astype(F32)
        squares = squares + side_values(got[rows:], rows)
    scale = lax.rsqrt(squares / width + 1e-06)[:, None]
    act = act * scale
    hid, pull = jax.vjp(gelu_tanh, act)
    hid = hid.astype(BF16)
    hid_full = fill([hid] + [flip(hid, "section", j) for j in (1, 2, 3)])
    normed = x_wide * scale
    scaled = (normed * gain_row).astype(BF16)

    def halves(values, side):
        pairs = values.reshape(rows, n_dp // 2, 2, share)
        return jnp.where(side == 0, pairs[:, :, 0], pairs[:, :, 1]).reshape(rows, quarter // 2)

    def own(values):
        return lax.dynamic_slice_in_dim(values, lane // 2 * share, share, 1)

    incoming = jnp.zeros((rows, quarter), BF16)
    normed_half = halves(normed, core)
    gain_half = halves(jnp.broadcast_to(gain_row, (rows, quarter)), core)
    for phase in range(layers):
        final = phase == layers - 1
        dy = jnp.where(last, cot, incoming) if phase > 0 else cot
        dhid_raw = jnp.dot(dy, weight_out.T, preferred_element_type=F32)
        dhid = cut(dhid_raw, 0)
        for j in (3, 1, 2):
            dhid = dhid + flip(cut(dhid_raw, j).astype(BF16), "section", j).astype(F32)
        dact = pull(dhid)[0].astype(BF16)
        inner = jnp.sum(dact.astype(F32) * act, axis=1)
        payload = jnp.concatenate([dact, side_rows(inner, piece)], axis=0)
        others = [flip(payload, "section", j) for j in (1, 2, 3)]
        for got in others:
            inner = inner + side_values(got[rows:], rows)
        dact_full = fill([dact] + [got[:rows] for got in others])
        part = jnp.dot(dact_full, weight_in.T, preferred_element_type=F32).astype(BF16)

        send = jnp.concatenate([halves(part, 1 - core), side_rows(inner, quarter // 2)], axis=0)
        got = flip(send, "dp", 1)
        dscaled = halves(part, core).astype(F32) + got[:rows].astype(F32)
        inner = inner + side_values(got[rows:], rows)
        bit = 2
        while bit < n_dp:
            send = jnp.concatenate([dscaled.astype(BF16), side_rows(inner, quarter // 2)], axis=0)
            got = flip(send, "dp", bit)
            dscaled = dscaled + got[:rows].astype(F32)
            inner = inner + side_values(got[rows:], rows)
            bit *= 2
        dnorm = dscaled * gain_half
        dy_half = halves(dy, core).astype(F32)
        grad_x = (dy_half + scale * (dnorm - normed_half * (inner / width)[:, None])).astype(BF16)
        if not final:
            down = lax.ppermute(grad_x, "section", [(i, i - 4) for i in range(4, sections)])
            other = flip(down, "dp", 1)
            pairs = jnp.where(
                core == 0,
                jnp.stack([down.reshape(rows, n_dp // 2, share), other.reshape(rows, n_dp // 2, share)], axis=2),
                jnp.stack([other.reshape(rows, n_dp // 2, share), down.reshape(rows, n_dp // 2, share)], axis=2),
            )
            incoming = pairs.reshape(rows, quarter)

    grad_out = jnp.dot(hid_full.T, dy, preferred_element_type=F32).astype(BF16)
    grad_in = jnp.dot(scaled.T, dact_full, preferred_element_type=F32).astype(BF16)
    grad_gain = jnp.sum(own(dscaled) * own(normed_half), axis=0)
    return (
        grad_in[None],
        grad_out[None],
        grad_gain[None],
        own(grad_x).reshape(1, micro, tok, share),
    )


def solution(mesh):
    in_specs = (
        P("section", None, None, "dp"),
        P("section", None),
        P("section", None, "dp"),
        P("section", "dp", None),
        P(None, None, "dp"),
    )
    out_specs = (
        P("section", None, "dp"),
        P("section", "dp", None),
        P("section", "dp"),
        P("section", None, None, "dp"),
    )
    return jax.shard_map(shards, mesh=mesh, in_specs=in_specs, out_specs=out_specs, check_vma=False)
```

```python
import jax
import jax.numpy as jnp
from jax import lax
from jax.sharding import PartitionSpec as P

F32 = jnp.float32
BF16 = jnp.bfloat16


def flip(block, axis, bits):
    count = lax.axis_size(axis)
    return lax.ppermute(block, axis, [(i, i ^ bits) for i in range(count)])


def side_rows(values, width):
    lead = values.astype(BF16)
    trail = (values - lead.astype(F32)).astype(BF16)
    flat = jnp.concatenate([lead, trail])
    return jnp.pad(flat, (0, 16 * width - flat.shape[0])).reshape(16, width)


def side_values(rows, count):
    flat = rows.reshape(-1)
    return flat[:count].astype(F32) + flat[count:2 * count].astype(F32)


def gelu_tanh(value):
    return jax.nn.gelu(value, approximate=True)


def shards(checkpoints, gain, w_in, w_out, cotangent):
    sections = lax.axis_size("section")
    n_dp = lax.axis_size("dp")
    here = lax.axis_index("section")
    lane = lax.axis_index("dp")
    layers = sections // 4
    mine = here % 4
    last = here // 4 == layers - 1
    _, micro, tok, share = checkpoints.shape
    rows = micro * tok
    quarter = share * n_dp
    width = 4 * quarter
    gain_row = gain[0]
    weight_in = w_in[0]
    weight_out = w_out[0]
    hidden = weight_in.shape[1]
    piece = hidden // 4
    core = lane % 2

    def gather_dp(block):
        bit = n_dp // 2
        parts = {0: block}
        while bit >= 1:
            other = flip(jnp.concatenate([parts[j] for j in parts], axis=1), "dp", bit)
            for at, j in enumerate(list(parts)):
                parts[j ^ bit] = other[:, at * block.shape[1]:(at + 1) * block.shape[1]]
            bit //= 2
        full = jnp.zeros((rows, quarter), block.dtype)
        for j, part in parts.items():
            full = lax.dynamic_update_slice(full, part, (0, (lane ^ j) * block.shape[1]))
        return full

    def cot_quarter(block):
        if n_dp < 4:
            whole = lax.all_gather(block, "dp", axis=1, tiled=True)
            return lax.dynamic_slice_in_dim(whole, mine * quarter, quarter, 1)
        per = n_dp // 4
        top = [s * n_dp + d for s in range(sections) for d in range(n_dp) if s // 4 == layers - 1]
        held = block
        far = lambda i, b: (i % n_dp // per ^ i // n_dp % 4) & b
        got = lax.ppermute(held, ("section", "dp"), [(i, i ^ 2 * per) for i in top if far(i, 3) == 0])
        held = jnp.where((lane // per ^ mine) & 2 == 0, held, got)
        got = lax.ppermute(held, ("section", "dp"), [(i, i ^ per) for i in top if far(i, 1) == 0])
        held = jnp.where((lane // per ^ mine) & 1 == 0, held, got)
        if per == 1:
            return held
        parts = {0: held}
        bit = per // 2
        while bit >= 1:
            for j in list(parts):
                parts[j ^ bit] = flip(parts[j], "dp", bit)
            bit //= 2
        full = jnp.zeros((rows, quarter), block.dtype)
        for j, part in parts.items():
            full = lax.dynamic_update_slice(full, part, (0, (lane % per ^ j) * block.shape[1]))
        return full

    def cut(values, j):
        return lax.dynamic_slice_in_dim(values, (mine ^ j) * piece, piece, 1)

    def fill(parts):
        full = jnp.zeros((rows, hidden), parts[0].dtype)
        for j, part in enumerate(parts):
            full = lax.dynamic_update_slice(full, part, (0, (mine ^ j) * piece))
        return full

    groups = [list(range(g, g + 4)) for g in range(0, sections, 4)]

    def swap(values):
        return lax.all_to_all(values, "section", 0, 0, axis_index_groups=groups)

    def to_all(values):
        return swap(jnp.broadcast_to(values, (4,) + values.shape))

    def pieces(values):
        return jnp.stack([values[:, i * piece:(i + 1) * piece] for i in range(4)])

    x_full = gather_dp(checkpoints[0].reshape(rows, share))
    cot = cot_quarter(cotangent.reshape(rows, cotangent.shape[2]))
    x_wide = x_full.astype(F32)
    scaled_raw = (x_wide * gain_row).astype(BF16)
    squares = jnp.sum(x_wide * x_wide, axis=1)

    act_raw = jnp.dot(scaled_raw, weight_in, preferred_element_type=F32)
    extra = side_rows(squares, piece)
    got = swap(jnp.stack([jnp.concatenate([act_raw[:, i * piece:(i + 1) * piece].astype(BF16), extra]) for i in range(4)]))
    act = jnp.sum(got[:, :rows].astype(F32), axis=0)
    squares = sum(side_values(got[i, rows:], rows) for i in range(4))
    scale = lax.rsqrt(squares / width + 1e-06)[:, None]
    act = act * scale
    hid, pull = jax.vjp(gelu_tanh, act)
    hid = hid.astype(BF16)
    hid_full = to_all(hid).transpose(1, 0, 2).reshape(rows, hidden)
    normed = x_wide * scale
    scaled = (normed * gain_row).astype(BF16)

    def halves(values, side):
        pairs = values.reshape(rows, n_dp // 2, 2, share)
        return jnp.where(side == 0, pairs[:, :, 0], pairs[:, :, 1]).reshape(rows, quarter // 2)

    def own(values):
        return lax.dynamic_slice_in_dim(values, lane // 2 * share, share, 1)

    incoming = jnp.zeros((rows, quarter), BF16)
    normed_half = halves(normed, core)
    gain_half = halves(jnp.broadcast_to(gain_row, (rows, quarter)), core)
    for phase in range(layers):
        final = phase == layers - 1
        dy = jnp.where(last, cot, incoming) if phase > 0 else cot
        dhid_raw = jnp.dot(dy, weight_out.T, preferred_element_type=F32)
        dhid = jnp.sum(swap(pieces(dhid_raw.astype(BF16))).astype(F32), axis=0)
        dact = pull(dhid)[0].astype(BF16)
        inner = jnp.sum(dact.astype(F32) * act, axis=1)
        payload = jnp.concatenate([dact, side_rows(inner, piece)], axis=0)
        got = to_all(payload)
        inner = sum(side_values(got[i, rows:], rows) for i in range(4))
        dact_full = got[:, :rows].transpose(1, 0, 2).reshape(rows, hidden)
        part = jnp.dot(dact_full, weight_in.T, preferred_element_type=F32).astype(BF16)

        send = jnp.concatenate([halves(part, 1 - core), side_rows(inner, quarter // 2)], axis=0)
        got = flip(send, "dp", 1)
        dscaled = halves(part, core).astype(F32) + got[:rows].astype(F32)
        inner = inner + side_values(got[rows:], rows)
        bit = 2
        while bit < n_dp:
            send = jnp.concatenate([dscaled.astype(BF16), side_rows(inner, quarter // 2)], axis=0)
            got = flip(send, "dp", bit)
            dscaled = dscaled + got[:rows].astype(F32)
            inner = inner + side_values(got[rows:], rows)
            bit *= 2
        dnorm = dscaled * gain_half
        dy_half = halves(dy, core).astype(F32)
        grad_x = (dy_half + scale * (dnorm - normed_half * (inner / width)[:, None])).astype(BF16)
        if not final:
            down = lax.ppermute(grad_x, "section", [(i, i - 4) for i in range(4, sections)])
            other = flip(down, "dp", 1)
            pairs = jnp.where(
                core == 0,
                jnp.stack([down.reshape(rows, n_dp // 2, share), other.reshape(rows, n_dp // 2, share)], axis=2),
                jnp.stack([other.reshape(rows, n_dp // 2, share), down.reshape(rows, n_dp // 2, share)], axis=2),
            )
            incoming = pairs.reshape(rows, quarter)

    grad_out = jnp.dot(hid_full.T, dy, preferred_element_type=F32).astype(BF16)
    grad_in = jnp.dot(scaled.T, dact_full, preferred_element_type=F32).astype(BF16)
    grad_gain = jnp.sum(own(dscaled) * own(normed_half), axis=0)
    return (
        grad_in[None],
        grad_out[None],
        grad_gain[None],
        own(grad_x).reshape(1, micro, tok, share),
    )


def solution(mesh):
    in_specs = (
        P("section", None, None, "dp"),
        P("section", None),
        P("section", None, "dp"),
        P("section", "dp", None),
        P(None, None, "dp"),
    )
    out_specs = (
        P("section", None, "dp"),
        P("section", "dp", None),
        P("section", "dp"),
        P("section", None, None, "dp"),
    )
    return jax.shard_map(shards, mesh=mesh, in_specs=in_specs, out_specs=out_specs, check_vma=False)
```

```python
import functools

import jax
import jax.numpy as jnp
from jax import lax
from jax.experimental import pallas as pl
from jax.experimental.pallas import tpu as pltpu
from jax.sharding import PartitionSpec as P

F32 = jnp.float32
BF16 = jnp.bfloat16


def flip(block, axis, bits):
    count = lax.axis_size(axis)
    return lax.ppermute(block, axis, [(i, i ^ bits) for i in range(count)])


def side_rows(values, width):
    lead = values.astype(BF16)
    trail = (values - lead.astype(F32)).astype(BF16)
    flat = jnp.concatenate([lead, trail])
    return jnp.pad(flat, (0, 16 * width - flat.shape[0])).reshape(16, width)


def side_values(rows, count):
    flat = rows.reshape(-1)
    return flat[:count].astype(F32) + flat[count:2 * count].astype(F32)


def gelu_tanh(value):
    return jax.nn.gelu(value, approximate=True)


def shards_of_any(checkpoints, gain, w_in, w_out, cotangent):
    sections = lax.axis_size("section")
    n_dp = lax.axis_size("dp")
    here = lax.axis_index("section")
    lane = lax.axis_index("dp")
    layers = sections // 4
    mine = here % 4
    last = here // 4 == layers - 1
    _, micro, tok, share = checkpoints.shape
    rows = micro * tok
    quarter = share * n_dp
    width = 4 * quarter
    gain_row = gain[0]
    weight_in = w_in[0]
    weight_out = w_out[0]
    hidden = weight_in.shape[1]
    piece = hidden // 4
    core = lane % 2

    def gather_dp(block):
        bit = n_dp // 2
        parts = {0: block}
        while bit >= 1:
            other = flip(jnp.concatenate([parts[j] for j in parts], axis=1), "dp", bit)
            for at, j in enumerate(list(parts)):
                parts[j ^ bit] = other[:, at * block.shape[1]:(at + 1) * block.shape[1]]
            bit //= 2
        full = jnp.zeros((rows, quarter), block.dtype)
        for j, part in parts.items():
            full = lax.dynamic_update_slice(full, part, (0, (lane ^ j) * block.shape[1]))
        return full

    def cot_quarter(block):
        if n_dp < 4:
            whole = lax.all_gather(block, "dp", axis=1, tiled=True)
            return lax.dynamic_slice_in_dim(whole, mine * quarter, quarter, 1)
        per = n_dp // 4
        top = [s * n_dp + d for s in range(sections) for d in range(n_dp) if s // 4 == layers - 1]
        held = block
        far = lambda i, b: (i % n_dp // per ^ i // n_dp % 4) & b
        got = lax.ppermute(held, ("section", "dp"), [(i, i ^ 2 * per) for i in top if far(i, 3) == 0])
        held = jnp.where((lane // per ^ mine) & 2 == 0, held, got)
        got = lax.ppermute(held, ("section", "dp"), [(i, i ^ per) for i in top if far(i, 1) == 0])
        held = jnp.where((lane // per ^ mine) & 1 == 0, held, got)
        if per == 1:
            return held
        parts = {0: held}
        bit = per // 2
        while bit >= 1:
            for j in list(parts):
                parts[j ^ bit] = flip(parts[j], "dp", bit)
            bit //= 2
        full = jnp.zeros((rows, quarter), block.dtype)
        for j, part in parts.items():
            full = lax.dynamic_update_slice(full, part, (0, (lane % per ^ j) * block.shape[1]))
        return full

    def cut(values, j):
        return lax.dynamic_slice_in_dim(values, (mine ^ j) * piece, piece, 1)

    def fill(parts):
        full = jnp.zeros((rows, hidden), parts[0].dtype)
        for j, part in enumerate(parts):
            full = lax.dynamic_update_slice(full, part, (0, (mine ^ j) * piece))
        return full

    x_full = gather_dp(checkpoints[0].reshape(rows, share))
    cot = cot_quarter(cotangent.reshape(rows, cotangent.shape[2]))
    x_wide = x_full.astype(F32)
    scaled_raw = (x_wide * gain_row).astype(BF16)
    squares = jnp.sum(x_wide * x_wide, axis=1)

    act_raw = jnp.dot(scaled_raw, weight_in, preferred_element_type=F32)
    extra = side_rows(squares, piece)
    act = cut(act_raw, 0)
    for j in (3, 1, 2):
        got = flip(jnp.concatenate([cut(act_raw, j).astype(BF16), extra], axis=0), "section", j)
        act = act + got[:rows].astype(F32)
        squares = squares + side_values(got[rows:], rows)
    scale = lax.rsqrt(squares / width + 1e-06)[:, None]
    act = act * scale
    hid, pull = jax.vjp(gelu_tanh, act)
    hid = hid.astype(BF16)
    hid_full = fill([hid] + [flip(hid, "section", j) for j in (1, 2, 3)])
    normed = x_wide * scale
    scaled = (normed * gain_row).astype(BF16)

    def halves(values, side):
        pairs = values.reshape(rows, n_dp // 2, 2, share)
        return jnp.where(side == 0, pairs[:, :, 0], pairs[:, :, 1]).reshape(rows, quarter // 2)

    def own(values):
        return lax.dynamic_slice_in_dim(values, lane // 2 * share, share, 1)

    incoming = jnp.zeros((rows, quarter), BF16)
    normed_half = halves(normed, core)
    gain_half = halves(jnp.broadcast_to(gain_row, (rows, quarter)), core)
    for phase in range(layers):
        final = phase == layers - 1
        dy = jnp.where(last, cot, incoming) if phase > 0 else cot
        dhid_raw = jnp.dot(dy, weight_out.T, preferred_element_type=F32)
        dhid = cut(dhid_raw, 0)
        for j in (3, 1, 2):
            dhid = dhid + flip(cut(dhid_raw, j).astype(BF16), "section", j).astype(F32)
        dact = pull(dhid)[0].astype(BF16)
        inner = jnp.sum(dact.astype(F32) * act, axis=1)
        payload = jnp.concatenate([dact, side_rows(inner, piece)], axis=0)
        others = [flip(payload, "section", j) for j in (1, 2, 3)]
        for got in others:
            inner = inner + side_values(got[rows:], rows)
        dact_full = fill([dact] + [got[:rows] for got in others])
        part = jnp.dot(dact_full, weight_in.T, preferred_element_type=F32).astype(BF16)

        send = jnp.concatenate([halves(part, 1 - core), side_rows(inner, quarter // 2)], axis=0)
        got = flip(send, "dp", 1)
        dscaled = halves(part, core).astype(F32) + got[:rows].astype(F32)
        inner = inner + side_values(got[rows:], rows)
        bit = 2
        while bit < n_dp:
            send = jnp.concatenate([dscaled.astype(BF16), side_rows(inner, quarter // 2)], axis=0)
            got = flip(send, "dp", bit)
            dscaled = dscaled + got[:rows].astype(F32)
            inner = inner + side_values(got[rows:], rows)
            bit *= 2
        dnorm = dscaled * gain_half
        dy_half = halves(dy, core).astype(F32)
        grad_x = (dy_half + scale * (dnorm - normed_half * (inner / width)[:, None])).astype(BF16)
        if not final:
            down = lax.ppermute(grad_x, "section", [(i, i - 4) for i in range(4, sections)])
            other = flip(down, "dp", 1)
            pairs = jnp.where(
                core == 0,
                jnp.stack([down.reshape(rows, n_dp // 2, share), other.reshape(rows, n_dp // 2, share)], axis=2),
                jnp.stack([other.reshape(rows, n_dp // 2, share), down.reshape(rows, n_dp // 2, share)], axis=2),
            )
            incoming = pairs.reshape(rows, quarter)

    grad_out = jnp.dot(hid_full.T, dy, preferred_element_type=F32).astype(BF16)
    grad_in = jnp.dot(scaled.T, dact_full, preferred_element_type=F32).astype(BF16)
    grad_gain = jnp.sum(own(dscaled) * own(normed_half), axis=0)
    return (
        grad_in[None],
        grad_out[None],
        grad_gain[None],
        own(grad_x).reshape(1, micro, tok, share),
    )


SIDE = 16
GELU_IN = 0.7978845608028654
GELU_CUBE = 0.044715


def resident(shape, dtype):
    return pltpu.VMEM(shape, dtype)


def local(body, outs, *args, scratch=(), flops=0):
    spec = pl.BlockSpec(memory_space=pltpu.VMEM)
    moved = sum(a.size * a.dtype.itemsize for a in args)
    return pl.pallas_call(
        body,
        out_shape=tuple(outs),
        in_specs=[spec] * len(args),
        out_specs=tuple(spec for _ in outs),
        scratch_shapes=list(scratch),
        compiler_params=pltpu.CompilerParams(vmem_limit_bytes=24 * 1024 * 1024),
        cost_estimate=pl.CostEstimate(flops=flops, bytes_accessed=moved, transcendentals=0),
    )(*args)


def diagonal(rows, width):
    return lax.broadcasted_iota(jnp.int32, (rows, width), 0) == lax.broadcasted_iota(jnp.int32, (rows, width), 1)


def as_row(column, width):
    rows = column.shape[0]
    return jnp.sum(jnp.where(diagonal(rows, width), column, 0.0), axis=0, keepdims=True)


def as_column(row, rows):
    return jnp.sum(jnp.where(diagonal(rows, row.shape[1]), row, 0.0), axis=1, keepdims=True)


def side_block(row):
    lead = row.astype(BF16).astype(F32)
    at = lax.broadcasted_iota(jnp.int32, (SIDE, row.shape[1]), 0)
    return jnp.where(at == 0, lead, jnp.where(at == 1, row - lead, 0.0)).astype(BF16)


def side_row(block):
    wide = block.astype(F32)
    return wide[0:1] + wide[1:2]


def load_kernel(in_ref, out_ref, in_held, out_held, sems):
    first = pltpu.make_async_copy(in_ref, in_held, sems.at[0])
    second = pltpu.make_async_copy(out_ref, out_held, sems.at[1])
    first.start()
    second.start()
    first.wait()
    second.wait()


def load(weight_in, weight_out):
    keep = pl.BlockSpec(memory_space=pltpu.VMEM)
    return pl.pallas_call(
        load_kernel,
        out_shape=(resident(weight_in.shape, BF16), resident(weight_out.shape, BF16)),
        in_specs=[pl.BlockSpec(memory_space=pl.ANY)] * 2,
        out_specs=(keep, keep),
        scratch_shapes=[pltpu.SemaphoreType.DMA((2,))],
        cost_estimate=pl.CostEstimate(flops=0, bytes_accessed=4 * weight_in.size * 2, transcendentals=0),
    )(weight_in, weight_out)


def place():
    return lax.axis_index("section") % 4, lax.axis_index("dp")


def dot_nt(left, right):
    return lax.dot_general(left, right, (((1,), (1,)), ((), ())), preferred_element_type=F32)


def dot_tn(left, right):
    return lax.dot_general(left, right, (((0,), (0,)), ((), ())), preferred_element_type=F32)


def slot(index, size):
    return pl.ds(pl.multiple_of(index * size, size), size)


def spread_in_kernel(x0, x1, x2, x3, gain, weight, own, s1, s2, s3, x_full, scaled):
    mine, lane = place()
    rows, share = x0.shape
    piece = own.shape[1]
    for d, part in enumerate((x0, x1, x2, x3)):
        x_full[:, slot(lane ^ d, share)] = part[...]
    wide = x_full[...].astype(F32)
    row = as_row(jnp.sum(wide * wide, axis=1, keepdims=True), piece)
    scaled[...] = (wide * gain[...]).astype(BF16)
    block = side_block(row)
    for d, out in ((3, s3), (2, s2), (1, s1)):
        out[:rows] = jnp.dot(scaled[...], weight[:, slot(mine ^ d, piece)], preferred_element_type=F32).astype(BF16)
        out[rows:] = block
    own[:rows] = jnp.dot(scaled[...], weight[:, slot(mine, piece)], preferred_element_type=F32)
    own[rows:] = jnp.broadcast_to(row, (SIDE, piece))


def spread_dy(dy, weight, mine, own, s1, s2, s3):
    piece = own.shape[1]
    for d, out in ((3, s3), (2, s2), (1, s1)):
        out[...] = dot_nt(dy[...], weight[slot(mine ^ d, piece), :]).astype(BF16)
    own[...] = dot_nt(dy[...], weight[slot(mine, piece), :])


def spread_first_kernel(held, got, weight, own, s1, s2, s3, dy):
    mine, lane = place()
    dy[...] = jnp.where((lane ^ mine) % 2 == 0, held[...], got[...])
    spread_dy(dy, weight, mine, own, s1, s2, s3)


def spread_next_kernel(layers, d0, d1, d2, d3, before, weight, own, s1, s2, s3, dy):
    mine, lane = place()
    share = d0.shape[1]
    last = lax.axis_index("section") // 4 == layers - 1

    @pl.when(last)
    def _():
        dy[...] = before[...]

    @pl.when(jnp.logical_not(last))
    def _():
        for d, part in enumerate((d0, d1, d2, d3)):
            dy[:, slot(lane ^ d, share)] = part[...]

    spread_dy(dy, weight, mine, own, s1, s2, s3)


def act_kernel(width, own, g1, g2, g3, act, slope, hid, scale):
    rows = act.shape[0]
    row = own[rows:rows + 1] + side_row(g1[rows:]) + side_row(g2[rows:]) + side_row(g3[rows:])
    r = lax.rsqrt(as_column(row, rows) / width + 1e-06)
    scale[...] = r
    a = (own[:rows] + g1[:rows].astype(F32) + g2[:rows].astype(F32) + g3[:rows].astype(F32)) * r
    act[...] = a
    square = a * a
    t = jnp.tanh(GELU_IN * (a + GELU_CUBE * (square * a)))
    half = 0.5 * (1.0 + t)
    hid[...] = (a * half).astype(BF16)
    slope[...] = half + 0.5 * a * (1.0 - t * t) * (GELU_IN * (1.0 + 3.0 * GELU_CUBE * square))


def dact_kernel(own, g1, g2, g3, act, slope, pay):
    rows, piece = own.shape
    dhid = own[...] + g1[...].astype(F32) + g2[...].astype(F32) + g3[...].astype(F32)
    da = (dhid * slope[...]).astype(BF16)
    pay[:rows] = da
    pay[rows:] = side_block(as_row(jnp.sum(da.astype(F32) * act[...], axis=1, keepdims=True), piece))


def back_kernel(p0, p1, p2, p3, weight, keep, send, full):
    mine, lane = place()
    rows = full.shape[0]
    piece = p0.shape[1]
    share = weight.shape[0] // 4
    row = side_row(p0[rows:]) + side_row(p1[rows:]) + side_row(p2[rows:]) + side_row(p3[rows:])
    for d, part in enumerate((p0, p1, p2, p3)):
        full[:, slot(mine ^ d, piece)] = part[:rows]
    for at, d in ((0, 1), (1, 3)):
        send[:rows, at * share:(at + 1) * share] = dot_nt(full[...], weight[slot(lane ^ d, share), :]).astype(BF16)
    send[rows:] = side_block(row)
    for at, d in ((0, 0), (1, 2)):
        keep[:rows, at * share:(at + 1) * share] = dot_nt(full[...], weight[slot(lane ^ d, share), :])
    keep[rows:] = jnp.broadcast_to(row, (SIDE, keep.shape[1]))


def middle_kernel(keep, got, rest, send):
    rows = keep.shape[0] - SIDE
    share = rest.shape[1]
    row = (keep[rows:rows + 1] + side_row(got[rows:]))[:, :share]
    send[:rows] = (keep[:rows, share:] + got[:rows, share:].astype(F32)).astype(BF16)
    send[rows:] = side_block(row)
    rest[:rows] = keep[:rows, :share] + got[:rows, :share].astype(F32)
    rest[rows:] = jnp.broadcast_to(row, (SIDE, share))


def finish_kernel(width, rest, got, x_own, dy, gain, scale, grad_x, *grad_gain):
    _, lane = place()
    rows, share = x_own.shape
    at = slot(lane, share)
    r = scale[...]
    du = rest[:rows] + got[:rows].astype(F32)
    normed = x_own[...].astype(F32) * r
    inner = as_column(rest[rows:rows + 1] + side_row(got[rows:]), rows) / width
    dnorm = du * gain[:, at]
    grad_x[...] = (dy[:, at].astype(F32) + r * (dnorm - normed * inner)).astype(BF16)
    if grad_gain:
        grad_gain[0][...] = jnp.sum(du * normed, axis=0, keepdims=True)


def grad_out_kernel(h0, h1, h2, h3, dy, out, held, sems):
    mine, _ = place()
    piece = h0.shape[1]
    copies = []
    for d, part in enumerate((h0, h1, h2, h3)):
        held[d] = dot_tn(part[...], dy[...]).astype(BF16)
        copies.append(pltpu.make_async_copy(held.at[d], out.at[slot(mine ^ d, piece), :], sems.at[d]))
        copies[-1].start()
    for copy in copies:
        copy.wait()


def grad_in_kernel(p0, p1, p2, p3, x_full, gain, scale, out, scaled, held, sems):
    mine, _ = place()
    rows = x_full.shape[0]
    piece = p0.shape[1]
    scaled[...] = (x_full[...].astype(F32) * scale[...] * gain[...]).astype(BF16)
    copies = []
    for d, part in enumerate((p0, p1, p2, p3)):
        held[d] = dot_tn(scaled[...], part[:rows]).astype(BF16)
        copies.append(pltpu.make_async_copy(held.at[d], out.at[:, slot(mine ^ d, piece)], sems.at[d]))
        copies[-1].start()
    for copy in copies:
        copy.wait()


def gradient(body, shape, block, *args, scratch=(), flops=0):
    return pl.pallas_call(
        body,
        out_shape=jax.ShapeDtypeStruct(shape, BF16),
        in_specs=[pl.BlockSpec(memory_space=pltpu.VMEM)] * len(args),
        out_specs=pl.BlockSpec(memory_space=pl.ANY),
        scratch_shapes=[*scratch, pltpu.VMEM((4,) + block, BF16), pltpu.SemaphoreType.DMA((4,))],
        compiler_params=pltpu.CompilerParams(vmem_limit_bytes=24 * 1024 * 1024),
        cost_estimate=pl.CostEstimate(flops=flops, bytes_accessed=2 * shape[0] * shape[1], transcendentals=0),
    )(*args)


def shards_of_four(checkpoints, gain, w_in, w_out, cotangent):
    sections = lax.axis_size("section")
    here = lax.axis_index("section")
    lane = lax.axis_index("dp")
    layers = sections // 4
    mine = here % 4
    _, micro, tok, share = checkpoints.shape
    rows = micro * tok
    quarter = share * 4
    width = 4 * quarter
    hidden = w_in.shape[2]
    piece = hidden // 4
    work = 2 * rows * quarter * hidden

    x0 = checkpoints[0].reshape(rows, share)
    cot = cotangent.reshape(rows, quarter)
    top = [s * 4 + d for s in range(sections) for d in range(4) if s // 4 == layers - 1]
    x2 = flip(x0, "dp", 2)
    x1 = flip(x0, "dp", 1)
    got = lax.ppermute(cot, ("section", "dp"), [(i, i ^ 2) for i in top if i % 4 == i // 4 % 4])
    weight_in, weight_out = w_in[0], w_out[0]
    x3 = flip(x2, "dp", 1)
    held = jnp.where((lane ^ mine) & 2 == 0, cot, got)
    got = lax.ppermute(held, ("section", "dp"), [(i, i ^ 1) for i in top if (i ^ i // 4) % 2 == 0])

    wide = (rows + SIDE, piece)
    own, s1, s2, s3, x_full = local(
        spread_in_kernel,
        [resident(wide, F32)] + [resident(wide, BF16)] * 3 + [resident((rows, quarter), BF16)],
        x0, x1, x2, x3, gain, weight_in,
        scratch=[pltpu.VMEM((rows, quarter), BF16)], flops=work,
    )
    g3 = flip(s3, "section", 3)
    g2 = flip(s2, "section", 2)
    g1 = flip(s1, "section", 1)
    act, slope, hid, scale = local(
        functools.partial(act_kernel, width),
        [resident((rows, piece), F32), resident((rows, piece), F32), resident((rows, piece), BF16), resident((rows, 1), F32)],
        own, g1, g2, g3,
    )

    spread_outs = [resident((rows, piece), F32)] + [resident((rows, piece), BF16)] * 3 + [resident((rows, quarter), BF16)]
    hids = None
    for phase in range(layers):
        final = phase == layers - 1
        if phase == 0:
            own, s1, s2, s3, dy = local(spread_first_kernel, spread_outs, held, got, weight_out, flops=work)
        else:
            own, s1, s2, s3, dy = local(
                functools.partial(spread_next_kernel, layers), spread_outs, *down, dy, weight_out, flops=work
            )
        g3 = flip(s3, "section", 3)
        g2 = flip(s2, "section", 2)
        g1 = flip(s1, "section", 1)
        (pay,) = local(dact_kernel, [resident(wide, BF16)], own, g1, g2, g3, act, slope)
        p3 = flip(pay, "section", 3)
        p2 = flip(pay, "section", 2)
        p1 = flip(pay, "section", 1)
        keep, send = local(
            back_kernel,
            [resident((rows + SIDE, 2 * share), F32), resident((rows + SIDE, 2 * share), BF16)],
            pay, p1, p2, p3, weight_in,
            scratch=[pltpu.VMEM((rows, hidden), BF16)], flops=work,
        )
        if phase == 0:
            send, hid = lax.optimization_barrier((send, hid))
            hids = [hid] + [flip(hid, "section", j) for j in (1, 2, 3)]
        got = flip(send, "dp", 1)
        rest, send = local(
            middle_kernel,
            [resident((rows + SIDE, share), F32), resident((rows + SIDE, share), BF16)],
            keep, got,
        )
        got = flip(send, "dp", 2)
        outs = [resident((rows, share), BF16)]
        if final:
            outs = [jax.ShapeDtypeStruct((rows, share), BF16), jax.ShapeDtypeStruct((1, share), F32)]
        finished = local(functools.partial(finish_kernel, width), outs, rest, got, x0, dy, gain, scale)
        if not final:
            d0 = lax.ppermute(finished[0], "section", [(i, i - 4) for i in range(4, sections)])
            d2 = flip(d0, "dp", 2)
            d1 = flip(d0, "dp", 1)
            d3 = flip(d2, "dp", 1)
            down = (d0, d1, d2, d3)

    grad_out = gradient(grad_out_kernel, (hidden, quarter), (piece, quarter), *hids, dy, flops=work)
    grad_in = gradient(
        grad_in_kernel, (quarter, hidden), (quarter, piece), pay, p1, p2, p3, x_full, gain, scale,
        scratch=[pltpu.VMEM((rows, quarter), BF16)], flops=work,
    )
    grad_x, grad_gain = finished
    return grad_in[None], grad_out[None], grad_gain, grad_x.reshape(1, micro, tok, share)


def shards(checkpoints, gain, w_in, w_out, cotangent):
    rows = checkpoints.shape[1] * checkpoints.shape[2]
    share = checkpoints.shape[3]
    piece = w_in.shape[2] // 4
    if lax.axis_size("dp") == 4 and rows % 16 == 0 and share % 128 == 0 and piece % 128 == 0 and rows <= min(share, piece):
        return shards_of_four(checkpoints, gain, w_in, w_out, cotangent)
    return shards_of_any(checkpoints, gain, w_in, w_out, cotangent)


def solution(mesh):
    in_specs = (
        P("section", None, None, "dp"),
        P("section", None),
        P("section", None, "dp"),
        P("section", "dp", None),
        P(None, None, "dp"),
    )
    out_specs = (
        P("section", None, "dp"),
        P("section", "dp", None),
        P("section", "dp"),
        P("section", None, None, "dp"),
    )
    return jax.shard_map(shards, mesh=mesh, in_specs=in_specs, out_specs=out_specs, check_vma=False)
```

```python
import functools

import jax
import jax.numpy as jnp
from jax import lax
from jax.experimental import pallas as pl
from jax.experimental.pallas import tpu as pltpu
from jax.sharding import PartitionSpec as P

F32 = jnp.float32
BF16 = jnp.bfloat16


def flip(block, axis, bits):
    count = lax.axis_size(axis)
    return lax.ppermute(block, axis, [(i, i ^ bits) for i in range(count)])


def side_rows(values, width):
    lead = values.astype(BF16)
    trail = (values - lead.astype(F32)).astype(BF16)
    flat = jnp.concatenate([lead, trail])
    return jnp.pad(flat, (0, 16 * width - flat.shape[0])).reshape(16, width)


def side_values(rows, count):
    flat = rows.reshape(-1)
    return flat[:count].astype(F32) + flat[count:2 * count].astype(F32)


def gelu_tanh(value):
    return jax.nn.gelu(value, approximate=True)


def shards_of_any(checkpoints, gain, w_in, w_out, cotangent):
    sections = lax.axis_size("section")
    n_dp = lax.axis_size("dp")
    here = lax.axis_index("section")
    lane = lax.axis_index("dp")
    layers = sections // 4
    mine = here % 4
    last = here // 4 == layers - 1
    _, micro, tok, share = checkpoints.shape
    rows = micro * tok
    quarter = share * n_dp
    width = 4 * quarter
    gain_row = gain[0]
    weight_in = w_in[0]
    weight_out = w_out[0]
    hidden = weight_in.shape[1]
    piece = hidden // 4
    core = lane % 2

    def gather_dp(block):
        bit = n_dp // 2
        parts = {0: block}
        while bit >= 1:
            other = flip(jnp.concatenate([parts[j] for j in parts], axis=1), "dp", bit)
            for at, j in enumerate(list(parts)):
                parts[j ^ bit] = other[:, at * block.shape[1]:(at + 1) * block.shape[1]]
            bit //= 2
        full = jnp.zeros((rows, quarter), block.dtype)
        for j, part in parts.items():
            full = lax.dynamic_update_slice(full, part, (0, (lane ^ j) * block.shape[1]))
        return full

    def cot_quarter(block):
        if n_dp < 4:
            whole = lax.all_gather(block, "dp", axis=1, tiled=True)
            return lax.dynamic_slice_in_dim(whole, mine * quarter, quarter, 1)
        per = n_dp // 4
        top = [s * n_dp + d for s in range(sections) for d in range(n_dp) if s // 4 == layers - 1]
        held = block
        far = lambda i, b: (i % n_dp // per ^ i // n_dp % 4) & b
        got = lax.ppermute(held, ("section", "dp"), [(i, i ^ 2 * per) for i in top if far(i, 3) == 0])
        held = jnp.where((lane // per ^ mine) & 2 == 0, held, got)
        got = lax.ppermute(held, ("section", "dp"), [(i, i ^ per) for i in top if far(i, 1) == 0])
        held = jnp.where((lane // per ^ mine) & 1 == 0, held, got)
        if per == 1:
            return held
        parts = {0: held}
        bit = per // 2
        while bit >= 1:
            for j in list(parts):
                parts[j ^ bit] = flip(parts[j], "dp", bit)
            bit //= 2
        full = jnp.zeros((rows, quarter), block.dtype)
        for j, part in parts.items():
            full = lax.dynamic_update_slice(full, part, (0, (lane % per ^ j) * block.shape[1]))
        return full

    def cut(values, j):
        return lax.dynamic_slice_in_dim(values, (mine ^ j) * piece, piece, 1)

    def fill(parts):
        full = jnp.zeros((rows, hidden), parts[0].dtype)
        for j, part in enumerate(parts):
            full = lax.dynamic_update_slice(full, part, (0, (mine ^ j) * piece))
        return full

    x_full = gather_dp(checkpoints[0].reshape(rows, share))
    cot = cot_quarter(cotangent.reshape(rows, cotangent.shape[2]))
    x_wide = x_full.astype(F32)
    scaled_raw = (x_wide * gain_row).astype(BF16)
    squares = jnp.sum(x_wide * x_wide, axis=1)

    act_raw = jnp.dot(scaled_raw, weight_in, preferred_element_type=F32)
    extra = side_rows(squares, piece)
    act = cut(act_raw, 0)
    for j in (3, 1, 2):
        got = flip(jnp.concatenate([cut(act_raw, j).astype(BF16), extra], axis=0), "section", j)
        act = act + got[:rows].astype(F32)
        squares = squares + side_values(got[rows:], rows)
    scale = lax.rsqrt(squares / width + 1e-06)[:, None]
    act = act * scale
    hid, pull = jax.vjp(gelu_tanh, act)
    hid = hid.astype(BF16)
    hid_full = fill([hid] + [flip(hid, "section", j) for j in (1, 2, 3)])
    normed = x_wide * scale
    scaled = (normed * gain_row).astype(BF16)

    def halves(values, side):
        pairs = values.reshape(rows, n_dp // 2, 2, share)
        return jnp.where(side == 0, pairs[:, :, 0], pairs[:, :, 1]).reshape(rows, quarter // 2)

    def own(values):
        return lax.dynamic_slice_in_dim(values, lane // 2 * share, share, 1)

    incoming = jnp.zeros((rows, quarter), BF16)
    normed_half = halves(normed, core)
    gain_half = halves(jnp.broadcast_to(gain_row, (rows, quarter)), core)
    for phase in range(layers):
        final = phase == layers - 1
        dy = jnp.where(last, cot, incoming) if phase > 0 else cot
        dhid_raw = jnp.dot(dy, weight_out.T, preferred_element_type=F32)
        dhid = cut(dhid_raw, 0)
        for j in (3, 1, 2):
            dhid = dhid + flip(cut(dhid_raw, j).astype(BF16), "section", j).astype(F32)
        dact = pull(dhid)[0].astype(BF16)
        inner = jnp.sum(dact.astype(F32) * act, axis=1)
        payload = jnp.concatenate([dact, side_rows(inner, piece)], axis=0)
        others = [flip(payload, "section", j) for j in (1, 2, 3)]
        for got in others:
            inner = inner + side_values(got[rows:], rows)
        dact_full = fill([dact] + [got[:rows] for got in others])
        part = jnp.dot(dact_full, weight_in.T, preferred_element_type=F32).astype(BF16)

        send = jnp.concatenate([halves(part, 1 - core), side_rows(inner, quarter // 2)], axis=0)
        got = flip(send, "dp", 1)
        dscaled = halves(part, core).astype(F32) + got[:rows].astype(F32)
        inner = inner + side_values(got[rows:], rows)
        bit = 2
        while bit < n_dp:
            send = jnp.concatenate([dscaled.astype(BF16), side_rows(inner, quarter // 2)], axis=0)
            got = flip(send, "dp", bit)
            dscaled = dscaled + got[:rows].astype(F32)
            inner = inner + side_values(got[rows:], rows)
            bit *= 2
        dnorm = dscaled * gain_half
        dy_half = halves(dy, core).astype(F32)
        grad_x = (dy_half + scale * (dnorm - normed_half * (inner / width)[:, None])).astype(BF16)
        if not final:
            down = lax.ppermute(grad_x, "section", [(i, i - 4) for i in range(4, sections)])
            other = flip(down, "dp", 1)
            pairs = jnp.where(
                core == 0,
                jnp.stack([down.reshape(rows, n_dp // 2, share), other.reshape(rows, n_dp // 2, share)], axis=2),
                jnp.stack([other.reshape(rows, n_dp // 2, share), down.reshape(rows, n_dp // 2, share)], axis=2),
            )
            incoming = pairs.reshape(rows, quarter)

    grad_out = jnp.dot(hid_full.T, dy, preferred_element_type=F32).astype(BF16)
    grad_in = jnp.dot(scaled.T, dact_full, preferred_element_type=F32).astype(BF16)
    grad_gain = jnp.sum(own(dscaled) * own(normed_half), axis=0)
    return (
        grad_in[None],
        grad_out[None],
        grad_gain[None],
        own(grad_x).reshape(1, micro, tok, share),
    )


SIDE = 16
GELU_IN = 0.7978845608028654
GELU_CUBE = 0.044715


def resident(shape, dtype):
    return pltpu.VMEM(shape, dtype)


def local(body, outs, *args, scratch=(), flops=0):
    spec = pl.BlockSpec(memory_space=pltpu.VMEM)
    moved = sum(a.size * a.dtype.itemsize for a in args)
    return pl.pallas_call(
        body,
        out_shape=tuple(outs),
        in_specs=[spec] * len(args),
        out_specs=tuple(spec for _ in outs),
        scratch_shapes=list(scratch),
        compiler_params=pltpu.CompilerParams(vmem_limit_bytes=16 * 1024 * 1024),
        cost_estimate=pl.CostEstimate(flops=flops, bytes_accessed=moved, transcendentals=0),
    )(*args)


def diagonal(rows, width):
    return lax.broadcasted_iota(jnp.int32, (rows, width), 0) == lax.broadcasted_iota(jnp.int32, (rows, width), 1)


def as_row(column, width):
    rows = column.shape[0]
    return jnp.sum(jnp.where(diagonal(rows, width), column, 0.0), axis=0, keepdims=True)


def as_column(row, rows):
    return jnp.sum(jnp.where(diagonal(rows, row.shape[1]), row, 0.0), axis=1, keepdims=True)


def side_block(row):
    lead = row.astype(BF16).astype(F32)
    at = lax.broadcasted_iota(jnp.int32, (SIDE, row.shape[1]), 0)
    return jnp.where(at == 0, lead, jnp.where(at == 1, row - lead, 0.0)).astype(BF16)


def side_row(block):
    wide = block.astype(F32)
    return wide[0:1] + wide[1:2]


def load_kernel(*refs):
    count = len(refs) // 2
    copies = [pltpu.make_async_copy(refs[i], refs[count + i], refs[-1].at[i]) for i in range(count)]
    for copy in copies:
        copy.start()
    for copy in copies:
        copy.wait()


def load(*arrays):
    return pl.pallas_call(
        load_kernel,
        out_shape=tuple(resident(a.shape, a.dtype) for a in arrays),
        in_specs=[pl.BlockSpec(memory_space=pl.ANY)] * len(arrays),
        out_specs=tuple(pl.BlockSpec(memory_space=pltpu.VMEM) for _ in arrays),
        scratch_shapes=[pltpu.SemaphoreType.DMA((len(arrays),))],
        compiler_params=pltpu.CompilerParams(vmem_limit_bytes=1024 * 1024),
        cost_estimate=pl.CostEstimate(flops=0, bytes_accessed=sum(2 * a.size * a.dtype.itemsize for a in arrays), transcendentals=0),
    )(*(pltpu.with_memory_space_constraint(a, pltpu.HBM) for a in arrays))


def place():
    return lax.axis_index("section") % 4, lax.axis_index("dp")


def dot_nt(left, right):
    return lax.dot_general(left, right, (((1,), (1,)), ((), ())), preferred_element_type=F32)


def dot_tn(left, right):
    return lax.dot_general(left, right, (((0,), (0,)), ((), ())), preferred_element_type=F32)


def slot(index, size):
    return pl.ds(pl.multiple_of(index * size, size), size)


def spread_in_kernel(x0, x1, x2, x3, gain, weight, own, s1, s2, s3, x_full, scaled):
    mine, lane = place()
    rows, share = x0.shape
    piece = own.shape[1]
    for d, part in enumerate((x0, x1, x2, x3)):
        x_full[:, slot(lane ^ d, share)] = part[...]
    wide = x_full[...].astype(F32)
    row = as_row(jnp.sum(wide * wide, axis=1, keepdims=True), piece)
    scaled[...] = (wide * gain[...]).astype(BF16)
    block = side_block(row)
    for d, out in ((3, s3), (2, s2), (1, s1)):
        out[:rows] = jnp.dot(scaled[...], weight[:, slot(mine ^ d, piece)], preferred_element_type=F32).astype(BF16)
        out[rows:] = block
    own[:rows] = jnp.dot(scaled[...], weight[:, slot(mine, piece)], preferred_element_type=F32)
    own[rows:] = jnp.broadcast_to(row, (SIDE, piece))


def spread_dy(dy, weight, mine, own, s1, s2, s3):
    piece = own.shape[1]
    for d, out in ((3, s3), (2, s2), (1, s1)):
        out[...] = dot_nt(dy[...], weight[slot(mine ^ d, piece), :]).astype(BF16)
    own[...] = dot_nt(dy[...], weight[slot(mine, piece), :])


def spread_first_kernel(c0, c1, c2, c3, weight, own, s1, s2, s3, dy):
    mine, lane = place()
    for d, part in enumerate((c0, c1, c2, c3)):
        @pl.when(lane ^ mine == d)
        def _(part=part):
            dy[...] = part[...]

    spread_dy(dy, weight, mine, own, s1, s2, s3)


def spread_next_kernel(layers, d0, d1, d2, d3, before, weight, own, s1, s2, s3, dy):
    mine, lane = place()
    share = d0.shape[1]
    last = lax.axis_index("section") // 4 == layers - 1

    @pl.when(last)
    def _():
        dy[...] = before[...]

    @pl.when(jnp.logical_not(last))
    def _():
        for d, part in enumerate((d0, d1, d2, d3)):
            dy[:, slot(lane ^ d, share)] = part[...]

    spread_dy(dy, weight, mine, own, s1, s2, s3)


def act_kernel(width, own, g1, g2, g3, act, slope, hid, scale):
    rows = act.shape[0]
    row = own[rows:rows + 1] + side_row(g1[rows:]) + side_row(g2[rows:]) + side_row(g3[rows:])
    r = lax.rsqrt(as_column(row, rows) / width + 1e-06)
    scale[...] = r
    a = (own[:rows] + g1[:rows].astype(F32) + g2[:rows].astype(F32) + g3[:rows].astype(F32)) * r
    act[...] = a
    square = a * a
    t = jnp.tanh(GELU_IN * (a + GELU_CUBE * (square * a)))
    half = 0.5 * (1.0 + t)
    hid[...] = (a * half).astype(BF16)
    slope[...] = half + 0.5 * a * (1.0 - t * t) * (GELU_IN * (1.0 + 3.0 * GELU_CUBE * square))


def dact_kernel(own, g1, g2, g3, act, slope, pay):
    rows, piece = own.shape
    dhid = own[...] + g1[...].astype(F32) + g2[...].astype(F32) + g3[...].astype(F32)
    da = (dhid * slope[...]).astype(BF16)
    pay[:rows] = da
    pay[rows:] = side_block(as_row(jnp.sum(da.astype(F32) * act[...], axis=1, keepdims=True), piece))


def back_kernel(p0, p1, p2, p3, weight, keep, send, full):
    mine, lane = place()
    rows = full.shape[0]
    piece = p0.shape[1]
    share = weight.shape[0] // 4
    row = side_row(p0[rows:]) + side_row(p1[rows:]) + side_row(p2[rows:]) + side_row(p3[rows:])
    for d, part in enumerate((p0, p1, p2, p3)):
        full[:, slot(mine ^ d, piece)] = part[:rows]
    for at, d in ((0, 1), (1, 3)):
        send[:rows, at * share:(at + 1) * share] = dot_nt(full[...], weight[slot(lane ^ d, share), :]).astype(BF16)
    send[rows:] = side_block(row)
    for at, d in ((0, 0), (1, 2)):
        keep[:rows, at * share:(at + 1) * share] = dot_nt(full[...], weight[slot(lane ^ d, share), :])
    keep[rows:] = jnp.broadcast_to(row, (SIDE, keep.shape[1]))


def middle_kernel(keep, got, rest, send):
    rows = keep.shape[0] - SIDE
    share = rest.shape[1]
    row = (keep[rows:rows + 1] + side_row(got[rows:]))[:, :share]
    send[:rows] = (keep[:rows, share:] + got[:rows, share:].astype(F32)).astype(BF16)
    send[rows:] = side_block(row)
    rest[:rows] = keep[:rows, :share] + got[:rows, :share].astype(F32)
    rest[rows:] = jnp.broadcast_to(row, (SIDE, share))


def finish_kernel(width, rest, got, x_own, dy, gain, scale, grad_x, *grad_gain):
    _, lane = place()
    rows, share = x_own.shape
    at = slot(lane, share)
    r = scale[...]
    du = rest[:rows] + got[:rows].astype(F32)
    normed = x_own[...].astype(F32) * r
    inner = as_column(rest[rows:rows + 1] + side_row(got[rows:]), rows) / width
    dnorm = du * gain[:, at]
    grad_x[...] = (dy[:, at].astype(F32) + r * (dnorm - normed * inner)).astype(BF16)
    if grad_gain:
        grad_gain[0][...] = jnp.sum(du * normed, axis=0, keepdims=True)


def grad_out_kernel(h0, h1, h2, h3, dy, out, held, sems):
    mine, _ = place()
    piece = h0.shape[1]
    copies = []
    for d, part in enumerate((h0, h1, h2, h3)):
        held[d] = dot_tn(part[...], dy[...]).astype(BF16)
        copies.append(pltpu.make_async_copy(held.at[d], out.at[slot(mine ^ d, piece), :], sems.at[d]))
        copies[-1].start()
    for copy in copies:
        copy.wait()


def grad_in_kernel(p0, p1, p2, p3, x_full, gain, scale, out, scaled, held, sems):
    mine, _ = place()
    rows = x_full.shape[0]
    piece = p0.shape[1]
    scaled[...] = (x_full[...].astype(F32) * scale[...] * gain[...]).astype(BF16)
    copies = []
    for d, part in enumerate((p0, p1, p2, p3)):
        held[d] = dot_tn(scaled[...], part[:rows]).astype(BF16)
        copies.append(pltpu.make_async_copy(held.at[d], out.at[:, slot(mine ^ d, piece)], sems.at[d]))
        copies[-1].start()
    for copy in copies:
        copy.wait()


def gradient(body, shape, block, *args, scratch=(), flops=0):
    return pl.pallas_call(
        body,
        out_shape=jax.ShapeDtypeStruct(shape, BF16),
        in_specs=[pl.BlockSpec(memory_space=pltpu.VMEM)] * len(args),
        out_specs=pl.BlockSpec(memory_space=pl.ANY),
        scratch_shapes=[*scratch, pltpu.VMEM((4,) + block, BF16), pltpu.SemaphoreType.DMA((4,))],
        compiler_params=pltpu.CompilerParams(vmem_limit_bytes=16 * 1024 * 1024),
        cost_estimate=pl.CostEstimate(flops=flops, bytes_accessed=2 * shape[0] * shape[1], transcendentals=0),
    )(*args)


def shards_of_four(checkpoints, gain, w_in, w_out, cotangent):
    sections = lax.axis_size("section")
    here = lax.axis_index("section")
    lane = lax.axis_index("dp")
    layers = sections // 4
    mine = here % 4
    _, micro, tok, share = checkpoints.shape
    rows = micro * tok
    quarter = share * 4
    width = 4 * quarter
    hidden = w_in.shape[2]
    piece = hidden // 4
    work = 2 * rows * quarter * hidden

    x0 = checkpoints[0].reshape(rows, share)
    cot = cotangent.reshape(rows, quarter)
    top = [s * 4 + d for s in range(sections) for d in range(4) if s // 4 == layers - 1]
    x2 = flip(x0, "dp", 2)
    x1 = flip(x0, "dp", 1)
    weight_in, weight_out, x0, gain, c0 = load(w_in[0], w_out[0], x0, gain, cot)
    x2, x1, cot, weight_in = lax.optimization_barrier((x2, x1, cot, weight_in))
    c2 = lax.ppermute(cot, ("section", "dp"), [(i, i ^ 2) for i in top if i % 4 == i // 4 % 4])
    c1 = lax.ppermute(cot, ("section", "dp"), [(i, i ^ 1) for i in top if i % 4 == i // 4 % 4])
    x3 = flip(x2, "dp", 1)
    wide = (rows + SIDE, piece)
    own, s1, s2, s3, x_full = local(
        spread_in_kernel,
        [resident(wide, F32)] + [resident(wide, BF16)] * 3 + [resident((rows, quarter), BF16)],
        x0, x1, x2, x3, gain, weight_in,
        scratch=[pltpu.VMEM((rows, quarter), BF16)], flops=work,
    )
    s3, c2 = lax.optimization_barrier((s3, c2))
    g3 = flip(s3, "section", 3)
    g2 = flip(s2, "section", 2)
    g1 = flip(s1, "section", 1)
    c3 = lax.ppermute(c2, ("section", "dp"), [(i, i ^ 1) for i in top if i % 4 == i // 4 % 4 ^ 2])
    act, slope, hid, scale = local(
        functools.partial(act_kernel, width),
        [resident((rows, piece), F32), resident((rows, piece), F32), resident((rows, piece), BF16), resident((rows, 1), F32)],
        own, g1, g2, g3,
    )

    spread_outs = [resident((rows, piece), F32)] + [resident((rows, piece), BF16)] * 3 + [resident((rows, quarter), BF16)]

    def gather_hidden(block):
        return [block] + [flip(block, "section", j) for j in (1, 2, 3)]

    if layers == 1:
        hids = gather_hidden(hid)
    for phase in range(layers):
        final = phase == layers - 1
        if phase == 0:
            own, s1, s2, s3, dy = local(spread_first_kernel, spread_outs, c0, c1, c2, c3, weight_out, flops=work)
        else:
            down, hids = lax.optimization_barrier((down, hids))
            own, s1, s2, s3, dy = local(
                functools.partial(spread_next_kernel, layers), spread_outs, *down, dy, weight_out, flops=work
            )
        g3 = flip(s3, "section", 3)
        g2 = flip(s2, "section", 2)
        g1 = flip(s1, "section", 1)
        if final:
            grad_out = gradient(grad_out_kernel, (hidden, quarter), (piece, quarter), *hids, dy, flops=work)
            own, grad_out = lax.optimization_barrier((own, grad_out))
        (pay,) = local(dact_kernel, [resident(wide, BF16)], own, g1, g2, g3, act, slope)
        p3 = flip(pay, "section", 3)
        p2 = flip(pay, "section", 2)
        p1 = flip(pay, "section", 1)
        keep, send = local(
            back_kernel,
            [resident((rows + SIDE, 2 * share), F32), resident((rows + SIDE, 2 * share), BF16)],
            pay, p1, p2, p3, weight_in,
            scratch=[pltpu.VMEM((rows, hidden), BF16)], flops=work,
        )
        got = flip(send, "dp", 1)
        rest, send = local(
            middle_kernel,
            [resident((rows + SIDE, share), F32), resident((rows + SIDE, share), BF16)],
            keep, got,
        )
        if phase == 0 and not final:
            send, hid = lax.optimization_barrier((send, hid))
            hids = gather_hidden(hid)
        got = flip(send, "dp", 2)
        if final:
            grad_in = gradient(
                grad_in_kernel, (quarter, hidden), (quarter, piece), pay, p1, p2, p3, x_full, gain, scale,
                scratch=[pltpu.VMEM((rows, quarter), BF16)], flops=work,
            )
            got, grad_in = lax.optimization_barrier((got, grad_in))
        outs = [resident((rows, share), BF16)]
        if final:
            outs = [jax.ShapeDtypeStruct((rows, share), BF16), jax.ShapeDtypeStruct((1, share), F32)]
        finished = local(functools.partial(finish_kernel, width), outs, rest, got, x0, dy, gain, scale)
        if not final:
            d0 = lax.ppermute(finished[0], "section", [(i, i - 4) for i in range(4, sections)])
            d2 = flip(d0, "dp", 2)
            d1 = flip(d0, "dp", 1)
            d3 = flip(d2, "dp", 1)
            down = (d0, d1, d2, d3)

    grad_x, grad_gain = finished
    return grad_in[None], grad_out[None], grad_gain, grad_x.reshape(1, micro, tok, share)


def shards(checkpoints, gain, w_in, w_out, cotangent):
    rows = checkpoints.shape[1] * checkpoints.shape[2]
    share = checkpoints.shape[3]
    piece = w_in.shape[2] // 4
    if lax.axis_size("dp") == 4 and rows % 16 == 0 and share % 128 == 0 and piece % 128 == 0 and rows <= min(share, piece):
        return shards_of_four(checkpoints, gain, w_in, w_out, cotangent)
    return shards_of_any(checkpoints, gain, w_in, w_out, cotangent)


def solution(mesh):
    in_specs = (
        P("section", None, None, "dp"),
        P("section", None),
        P("section", None, "dp"),
        P("section", "dp", None),
        P(None, None, "dp"),
    )
    out_specs = (
        P("section", None, "dp"),
        P("section", "dp", None),
        P("section", "dp"),
        P("section", None, None, "dp"),
    )
    return jax.shard_map(shards, mesh=mesh, in_specs=in_specs, out_specs=out_specs, check_vma=False)
```

```python
import functools

import jax
import jax.numpy as jnp
from jax import lax
from jax.experimental import pallas as pl
from jax.experimental.pallas import tpu as pltpu
from jax.sharding import PartitionSpec as P

F32 = jnp.float32
BF16 = jnp.bfloat16


def flip(block, axis, bits):
    count = lax.axis_size(axis)
    return lax.ppermute(block, axis, [(i, i ^ bits) for i in range(count)])


def side_rows(values, width):
    lead = values.astype(BF16)
    trail = (values - lead.astype(F32)).astype(BF16)
    flat = jnp.concatenate([lead, trail])
    return jnp.pad(flat, (0, 16 * width - flat.shape[0])).reshape(16, width)


def side_values(rows, count):
    flat = rows.reshape(-1)
    return flat[:count].astype(F32) + flat[count:2 * count].astype(F32)


def gelu_tanh(value):
    return jax.nn.gelu(value, approximate=True)


def shards_of_any(checkpoints, gain, w_in, w_out, cotangent):
    sections = lax.axis_size("section")
    n_dp = lax.axis_size("dp")
    here = lax.axis_index("section")
    lane = lax.axis_index("dp")
    layers = sections // 4
    mine = here % 4
    last = here // 4 == layers - 1
    _, micro, tok, share = checkpoints.shape
    rows = micro * tok
    quarter = share * n_dp
    width = 4 * quarter
    gain_row = gain[0]
    weight_in = w_in[0]
    weight_out = w_out[0]
    hidden = weight_in.shape[1]
    piece = hidden // 4
    core = lane % 2

    def gather_dp(block):
        bit = n_dp // 2
        parts = {0: block}
        while bit >= 1:
            other = flip(jnp.concatenate([parts[j] for j in parts], axis=1), "dp", bit)
            for at, j in enumerate(list(parts)):
                parts[j ^ bit] = other[:, at * block.shape[1]:(at + 1) * block.shape[1]]
            bit //= 2
        full = jnp.zeros((rows, quarter), block.dtype)
        for j, part in parts.items():
            full = lax.dynamic_update_slice(full, part, (0, (lane ^ j) * block.shape[1]))
        return full

    def cot_quarter(block):
        if n_dp < 4:
            whole = lax.all_gather(block, "dp", axis=1, tiled=True)
            return lax.dynamic_slice_in_dim(whole, mine * quarter, quarter, 1)
        per = n_dp // 4
        top = [s * n_dp + d for s in range(sections) for d in range(n_dp) if s // 4 == layers - 1]
        held = block
        far = lambda i, b: (i % n_dp // per ^ i // n_dp % 4) & b
        got = lax.ppermute(held, ("section", "dp"), [(i, i ^ 2 * per) for i in top if far(i, 3) == 0])
        held = jnp.where((lane // per ^ mine) & 2 == 0, held, got)
        got = lax.ppermute(held, ("section", "dp"), [(i, i ^ per) for i in top if far(i, 1) == 0])
        held = jnp.where((lane // per ^ mine) & 1 == 0, held, got)
        if per == 1:
            return held
        parts = {0: held}
        bit = per // 2
        while bit >= 1:
            for j in list(parts):
                parts[j ^ bit] = flip(parts[j], "dp", bit)
            bit //= 2
        full = jnp.zeros((rows, quarter), block.dtype)
        for j, part in parts.items():
            full = lax.dynamic_update_slice(full, part, (0, (lane % per ^ j) * block.shape[1]))
        return full

    def cut(values, j):
        return lax.dynamic_slice_in_dim(values, (mine ^ j) * piece, piece, 1)

    def fill(parts):
        full = jnp.zeros((rows, hidden), parts[0].dtype)
        for j, part in enumerate(parts):
            full = lax.dynamic_update_slice(full, part, (0, (mine ^ j) * piece))
        return full

    x_full = gather_dp(checkpoints[0].reshape(rows, share))
    cot = cot_quarter(cotangent.reshape(rows, cotangent.shape[2]))
    x_wide = x_full.astype(F32)
    scaled_raw = (x_wide * gain_row).astype(BF16)
    squares = jnp.sum(x_wide * x_wide, axis=1)

    act_raw = jnp.dot(scaled_raw, weight_in, preferred_element_type=F32)
    extra = side_rows(squares, piece)
    act = cut(act_raw, 0)
    for j in (3, 1, 2):
        got = flip(jnp.concatenate([cut(act_raw, j).astype(BF16), extra], axis=0), "section", j)
        act = act + got[:rows].astype(F32)
        squares = squares + side_values(got[rows:], rows)
    scale = lax.rsqrt(squares / width + 1e-06)[:, None]
    act = act * scale
    hid, pull = jax.vjp(gelu_tanh, act)
    hid = hid.astype(BF16)
    hid_full = fill([hid] + [flip(hid, "section", j) for j in (1, 2, 3)])
    normed = x_wide * scale
    scaled = (normed * gain_row).astype(BF16)

    def halves(values, side):
        pairs = values.reshape(rows, n_dp // 2, 2, share)
        return jnp.where(side == 0, pairs[:, :, 0], pairs[:, :, 1]).reshape(rows, quarter // 2)

    def own(values):
        return lax.dynamic_slice_in_dim(values, lane // 2 * share, share, 1)

    incoming = jnp.zeros((rows, quarter), BF16)
    normed_half = halves(normed, core)
    gain_half = halves(jnp.broadcast_to(gain_row, (rows, quarter)), core)
    for phase in range(layers):
        final = phase == layers - 1
        dy = jnp.where(last, cot, incoming) if phase > 0 else cot
        dhid_raw = jnp.dot(dy, weight_out.T, preferred_element_type=F32)
        dhid = cut(dhid_raw, 0)
        for j in (3, 1, 2):
            dhid = dhid + flip(cut(dhid_raw, j).astype(BF16), "section", j).astype(F32)
        dact = pull(dhid)[0].astype(BF16)
        inner = jnp.sum(dact.astype(F32) * act, axis=1)
        payload = jnp.concatenate([dact, side_rows(inner, piece)], axis=0)
        others = [flip(payload, "section", j) for j in (1, 2, 3)]
        for got in others:
            inner = inner + side_values(got[rows:], rows)
        dact_full = fill([dact] + [got[:rows] for got in others])
        part = jnp.dot(dact_full, weight_in.T, preferred_element_type=F32).astype(BF16)

        send = jnp.concatenate([halves(part, 1 - core), side_rows(inner, quarter // 2)], axis=0)
        got = flip(send, "dp", 1)
        dscaled = halves(part, core).astype(F32) + got[:rows].astype(F32)
        inner = inner + side_values(got[rows:], rows)
        bit = 2
        while bit < n_dp:
            send = jnp.concatenate([dscaled.astype(BF16), side_rows(inner, quarter // 2)], axis=0)
            got = flip(send, "dp", bit)
            dscaled = dscaled + got[:rows].astype(F32)
            inner = inner + side_values(got[rows:], rows)
            bit *= 2
        dnorm = dscaled * gain_half
        dy_half = halves(dy, core).astype(F32)
        grad_x = (dy_half + scale * (dnorm - normed_half * (inner / width)[:, None])).astype(BF16)
        if not final:
            down = lax.ppermute(grad_x, "section", [(i, i - 4) for i in range(4, sections)])
            other = flip(down, "dp", 1)
            pairs = jnp.where(
                core == 0,
                jnp.stack([down.reshape(rows, n_dp // 2, share), other.reshape(rows, n_dp // 2, share)], axis=2),
                jnp.stack([other.reshape(rows, n_dp // 2, share), down.reshape(rows, n_dp // 2, share)], axis=2),
            )
            incoming = pairs.reshape(rows, quarter)

    grad_out = jnp.dot(hid_full.T, dy, preferred_element_type=F32).astype(BF16)
    grad_in = jnp.dot(scaled.T, dact_full, preferred_element_type=F32).astype(BF16)
    grad_gain = jnp.sum(own(dscaled) * own(normed_half), axis=0)
    return (
        grad_in[None],
        grad_out[None],
        grad_gain[None],
        own(grad_x).reshape(1, micro, tok, share),
    )


SIDE = 16
GELU_IN = 0.7978845608028654
GELU_CUBE = 0.044715


def resident(shape, dtype):
    return pltpu.VMEM(shape, dtype)


def local(body, outs, *args, scratch=(), flops=0):
    spec = pl.BlockSpec(memory_space=pltpu.VMEM)
    moved = sum(a.size * a.dtype.itemsize for a in args)
    return pl.pallas_call(
        body,
        out_shape=tuple(outs),
        in_specs=[spec] * len(args),
        out_specs=tuple(spec for _ in outs),
        scratch_shapes=list(scratch),
        compiler_params=pltpu.CompilerParams(vmem_limit_bytes=16 * 1024 * 1024),
        cost_estimate=pl.CostEstimate(flops=flops, bytes_accessed=moved, transcendentals=0),
    )(*args)


def diagonal(rows, width):
    return lax.broadcasted_iota(jnp.int32, (rows, width), 0) == lax.broadcasted_iota(jnp.int32, (rows, width), 1)


def as_row(column, width):
    rows = column.shape[0]
    return jnp.sum(jnp.where(diagonal(rows, width), column, 0.0), axis=0, keepdims=True)


def as_column(row, rows):
    return jnp.sum(jnp.where(diagonal(rows, row.shape[1]), row, 0.0), axis=1, keepdims=True)


def side_block(row):
    lead = row.astype(BF16).astype(F32)
    at = lax.broadcasted_iota(jnp.int32, (SIDE, row.shape[1]), 0)
    return jnp.where(at == 0, lead, jnp.where(at == 1, row - lead, 0.0)).astype(BF16)


def side_row(block):
    wide = block.astype(F32)
    return wide[0:1] + wide[1:2]


def load_kernel(*refs):
    count = len(refs) // 2
    copies = [pltpu.make_async_copy(refs[i], refs[count + i], refs[-1].at[i]) for i in range(count)]
    for copy in copies:
        copy.start()
    for copy in copies:
        copy.wait()


def load(*arrays):
    return pl.pallas_call(
        load_kernel,
        out_shape=tuple(resident(a.shape, a.dtype) for a in arrays),
        in_specs=[pl.BlockSpec(memory_space=pl.ANY)] * len(arrays),
        out_specs=tuple(pl.BlockSpec(memory_space=pltpu.VMEM) for _ in arrays),
        scratch_shapes=[pltpu.SemaphoreType.DMA((len(arrays),))],
        compiler_params=pltpu.CompilerParams(vmem_limit_bytes=1024 * 1024),
        cost_estimate=pl.CostEstimate(flops=0, bytes_accessed=sum(2 * a.size * a.dtype.itemsize for a in arrays), transcendentals=0),
    )(*(pltpu.with_memory_space_constraint(a, pltpu.HBM) for a in arrays))


def place():
    return lax.axis_index("section") % 4, lax.axis_index("dp")


def dot_nt(left, right):
    return lax.dot_general(left, right, (((1,), (1,)), ((), ())), preferred_element_type=F32)


def dot_tn(left, right):
    return lax.dot_general(left, right, (((0,), (0,)), ((), ())), preferred_element_type=F32)


def slot(index, size):
    return pl.ds(pl.multiple_of(index * size, size), size)


def spread_in_kernel(x0, x1, x2, x3, gain, weight, own, s1, s2, s3, x_full, scaled):
    mine, lane = place()
    rows, share = x0.shape
    piece = own.shape[1]
    for d, part in enumerate((x0, x1, x2, x3)):
        x_full[:, slot(lane ^ d, share)] = part[...]
    wide = x_full[...].astype(F32)
    row = as_row(jnp.sum(wide * wide, axis=1, keepdims=True), piece)
    scaled[...] = (wide * gain[...]).astype(BF16)
    block = side_block(row)
    for d, out in ((3, s3), (2, s2), (1, s1)):
        out[:rows] = jnp.dot(scaled[...], weight[:, slot(mine ^ d, piece)], preferred_element_type=F32).astype(BF16)
        out[rows:] = block
    own[:rows] = jnp.dot(scaled[...], weight[:, slot(mine, piece)], preferred_element_type=F32)
    own[rows:] = jnp.broadcast_to(row, (SIDE, piece))


def spread_dy(dy, weight, mine, own, s1, s2, s3):
    piece = own.shape[1]
    for d, out in ((3, s3), (2, s2), (1, s1)):
        out[...] = dot_nt(dy[...], weight[slot(mine ^ d, piece), :]).astype(BF16)
    own[...] = dot_nt(dy[...], weight[slot(mine, piece), :])


def spread_first_kernel(c0, c1, c2, c3, weight, own, s1, s2, s3, dy):
    mine, lane = place()
    for d, part in enumerate((c0, c1, c2, c3)):
        @pl.when(lane ^ mine == d)
        def _(part=part):
            dy[...] = part[...]

    spread_dy(dy, weight, mine, own, s1, s2, s3)


def spread_next_kernel(layers, d0, d1, d2, d3, before, weight, own, s1, s2, s3, dy):
    mine, lane = place()
    share = d0.shape[1]
    last = lax.axis_index("section") // 4 == layers - 1

    @pl.when(last)
    def _():
        dy[...] = before[...]

    @pl.when(jnp.logical_not(last))
    def _():
        for d, part in enumerate((d0, d1, d2, d3)):
            dy[:, slot(lane ^ d, share)] = part[...]

    spread_dy(dy, weight, mine, own, s1, s2, s3)


def act_kernel(width, own, g1, g2, g3, act, slope, hid, scale):
    rows = act.shape[0]
    row = own[rows:rows + 1] + side_row(g1[rows:]) + side_row(g2[rows:]) + side_row(g3[rows:])
    r = lax.rsqrt(as_column(row, rows) / width + 1e-06)
    scale[...] = r
    a = (own[:rows] + g1[:rows].astype(F32) + g2[:rows].astype(F32) + g3[:rows].astype(F32)) * r
    act[...] = a
    square = a * a
    t = jnp.tanh(GELU_IN * (a + GELU_CUBE * (square * a)))
    half = 0.5 * (1.0 + t)
    hid[...] = (a * half).astype(BF16)
    slope[...] = half + 0.5 * a * (1.0 - t * t) * (GELU_IN * (1.0 + 3.0 * GELU_CUBE * square))


def dact_kernel(own, g1, g2, g3, act, slope, pay):
    rows, piece = own.shape
    dhid = own[...] + g1[...].astype(F32) + g2[...].astype(F32) + g3[...].astype(F32)
    da = (dhid * slope[...]).astype(BF16)
    pay[:rows] = da
    pay[rows:] = side_block(as_row(jnp.sum(da.astype(F32) * act[...], axis=1, keepdims=True), piece))


def back_kernel(p0, p1, p2, p3, weight, keep, send, full):
    mine, lane = place()
    rows = full.shape[0]
    piece = p0.shape[1]
    share = weight.shape[0] // 4
    row = side_row(p0[rows:]) + side_row(p1[rows:]) + side_row(p2[rows:]) + side_row(p3[rows:])
    for d, part in enumerate((p0, p1, p2, p3)):
        full[:, slot(mine ^ d, piece)] = part[:rows]
    for at, d in ((0, 1), (1, 3)):
        send[:rows, at * share:(at + 1) * share] = dot_nt(full[...], weight[slot(lane ^ d, share), :]).astype(BF16)
    send[rows:] = side_block(row)
    for at, d in ((0, 0), (1, 2)):
        keep[:rows, at * share:(at + 1) * share] = dot_nt(full[...], weight[slot(lane ^ d, share), :])
    keep[rows:] = jnp.broadcast_to(row, (SIDE, keep.shape[1]))


def middle_kernel(keep, got, rest, send):
    rows = keep.shape[0] - SIDE
    share = rest.shape[1]
    row = (keep[rows:rows + 1] + side_row(got[rows:]))[:, :share]
    send[:rows] = (keep[:rows, share:] + got[:rows, share:].astype(F32)).astype(BF16)
    send[rows:] = side_block(row)
    rest[:rows] = keep[:rows, :share] + got[:rows, :share].astype(F32)
    rest[rows:] = jnp.broadcast_to(row, (SIDE, share))


def finish_kernel(width, rest, got, x_own, dy, gain, scale, grad_x, *grad_gain):
    _, lane = place()
    rows, share = x_own.shape
    at = slot(lane, share)
    r = scale[...]
    du = rest[:rows] + got[:rows].astype(F32)
    normed = x_own[...].astype(F32) * r
    inner = as_column(rest[rows:rows + 1] + side_row(got[rows:]), rows) / width
    dnorm = du * gain[:, at]
    grad_x[...] = (dy[:, at].astype(F32) + r * (dnorm - normed * inner)).astype(BF16)
    if grad_gain:
        grad_gain[0][...] = jnp.sum(du * normed, axis=0, keepdims=True)


def grad_out_kernel(h0, h1, h2, h3, dy, out, held, sems):
    mine, _ = place()
    piece = h0.shape[1]
    copies = []
    for d, part in enumerate((h0, h1, h2, h3)):
        held[d] = dot_tn(part[...], dy[...]).astype(BF16)
        copies.append(pltpu.make_async_copy(held.at[d], out.at[slot(mine ^ d, piece), :], sems.at[d]))
        copies[-1].start()
    for copy in copies:
        copy.wait()


def grad_in_kernel(p0, p1, p2, p3, x_full, gain, scale, out, scaled, held, sems):
    mine, _ = place()
    rows = x_full.shape[0]
    piece = p0.shape[1]
    scaled[...] = (x_full[...].astype(F32) * scale[...] * gain[...]).astype(BF16)
    copies = []
    for d, part in enumerate((p0, p1, p2, p3)):
        held[d] = dot_tn(scaled[...], part[:rows]).astype(BF16)
        copies.append(pltpu.make_async_copy(held.at[d], out.at[:, slot(mine ^ d, piece)], sems.at[d]))
        copies[-1].start()
    for copy in copies:
        copy.wait()


def gradient(body, shape, block, *args, scratch=(), flops=0):
    return pl.pallas_call(
        body,
        out_shape=jax.ShapeDtypeStruct(shape, BF16),
        in_specs=[pl.BlockSpec(memory_space=pltpu.VMEM)] * len(args),
        out_specs=pl.BlockSpec(memory_space=pl.ANY),
        scratch_shapes=[*scratch, pltpu.VMEM((4,) + block, BF16), pltpu.SemaphoreType.DMA((4,))],
        compiler_params=pltpu.CompilerParams(vmem_limit_bytes=16 * 1024 * 1024),
        cost_estimate=pl.CostEstimate(flops=flops, bytes_accessed=2 * shape[0] * shape[1], transcendentals=0),
    )(*args)


def shards_of_four(checkpoints, gain, w_in, w_out, cotangent):
    sections = lax.axis_size("section")
    here = lax.axis_index("section")
    lane = lax.axis_index("dp")
    layers = sections // 4
    mine = here % 4
    _, micro, tok, share = checkpoints.shape
    rows = micro * tok
    quarter = share * 4
    width = 4 * quarter
    hidden = w_in.shape[2]
    piece = hidden // 4
    work = 2 * rows * quarter * hidden

    x0 = checkpoints[0].reshape(rows, share)
    cot = cotangent.reshape(rows, quarter)
    top = [s * 4 + d for s in range(sections) for d in range(4) if s // 4 == layers - 1]
    x2 = flip(x0, "dp", 2)
    x1 = flip(x0, "dp", 1)
    weight_in, x0, gain = load(w_in[0], x0, gain)
    x2, x1, cot, weight_in = lax.optimization_barrier((x2, x1, cot, weight_in))
    c2, c3 = [lax.ppermute(cot, ("section", "dp"), [(i, i ^ d) for i in top if i % 4 == i // 4 % 4]) for d in (2, 3)]
    x3 = flip(x2, "dp", 1)

    wide = (rows + SIDE, piece)
    own, s1, s2, s3, x_full = local(
        spread_in_kernel,
        [resident(wide, F32)] + [resident(wide, BF16)] * 3 + [resident((rows, quarter), BF16)],
        x0, x1, x2, x3, gain, weight_in,
        scratch=[pltpu.VMEM((rows, quarter), BF16)], flops=work,
    )
    s1, s2, s3, cot, w_out = lax.optimization_barrier((s1, s2, s3, cot, w_out))
    g3 = flip(s3, "section", 3)
    g2 = flip(s2, "section", 2)
    g1 = flip(s1, "section", 1)
    c1 = lax.ppermute(cot, ("section", "dp"), [(i, i ^ 1) for i in top if i % 4 == i // 4 % 4])
    weight_out, c0 = load(w_out[0], cot)
    act, slope, hid, scale = local(
        functools.partial(act_kernel, width),
        [resident((rows, piece), F32), resident((rows, piece), F32), resident((rows, piece), BF16), resident((rows, 1), F32)],
        own, g1, g2, g3,
    )

    spread_outs = [resident((rows, piece), F32)] + [resident((rows, piece), BF16)] * 3 + [resident((rows, quarter), BF16)]

    def gather_hidden(block):
        return [block] + [flip(block, "section", j) for j in (1, 2, 3)]

    if layers == 1:
        hids = gather_hidden(hid)
    for phase in range(layers):
        final = phase == layers - 1
        if phase == 0:
            own, s1, s2, s3, dy = local(spread_first_kernel, spread_outs, c0, c1, c2, c3, weight_out, flops=work)
        else:
            down, hids = lax.optimization_barrier((down, hids))
            own, s1, s2, s3, dy = local(
                functools.partial(spread_next_kernel, layers), spread_outs, *down, dy, weight_out, flops=work
            )
        g3 = flip(s3, "section", 3)
        g2 = flip(s2, "section", 2)
        g1 = flip(s1, "section", 1)
        if final:
            grad_out = gradient(grad_out_kernel, (hidden, quarter), (piece, quarter), *hids, dy, flops=work)
            own, grad_out = lax.optimization_barrier((own, grad_out))
        (pay,) = local(dact_kernel, [resident(wide, BF16)], own, g1, g2, g3, act, slope)
        p3 = flip(pay, "section", 3)
        p2 = flip(pay, "section", 2)
        p1 = flip(pay, "section", 1)
        keep, send = local(
            back_kernel,
            [resident((rows + SIDE, 2 * share), F32), resident((rows + SIDE, 2 * share), BF16)],
            pay, p1, p2, p3, weight_in,
            scratch=[pltpu.VMEM((rows, hidden), BF16)], flops=work,
        )
        got = flip(send, "dp", 1)
        rest, send = local(
            middle_kernel,
            [resident((rows + SIDE, share), F32), resident((rows + SIDE, share), BF16)],
            keep, got,
        )
        if phase == 0 and not final:
            send, hid = lax.optimization_barrier((send, hid))
            hids = gather_hidden(hid)
        got = flip(send, "dp", 2)
        if final:
            grad_in = gradient(
                grad_in_kernel, (quarter, hidden), (quarter, piece), pay, p1, p2, p3, x_full, gain, scale,
                scratch=[pltpu.VMEM((rows, quarter), BF16)], flops=work,
            )
            got, grad_in = lax.optimization_barrier((got, grad_in))
        outs = [resident((rows, share), BF16)]
        if final:
            outs = [jax.ShapeDtypeStruct((rows, share), BF16), jax.ShapeDtypeStruct((1, share), F32)]
        finished = local(functools.partial(finish_kernel, width), outs, rest, got, x0, dy, gain, scale)
        if not final:
            d0 = lax.ppermute(finished[0], "section", [(i, i - 4) for i in range(4, sections)])
            d2 = flip(d0, "dp", 2)
            d1 = flip(d0, "dp", 1)
            d3 = flip(d2, "dp", 1)
            down = (d0, d1, d2, d3)

    grad_x, grad_gain = finished
    return grad_in[None], grad_out[None], grad_gain, grad_x.reshape(1, micro, tok, share)


def shards(checkpoints, gain, w_in, w_out, cotangent):
    rows = checkpoints.shape[1] * checkpoints.shape[2]
    share = checkpoints.shape[3]
    piece = w_in.shape[2] // 4
    if lax.axis_size("dp") == 4 and rows % 16 == 0 and share % 128 == 0 and piece % 128 == 0 and rows <= min(share, piece):
        return shards_of_four(checkpoints, gain, w_in, w_out, cotangent)
    return shards_of_any(checkpoints, gain, w_in, w_out, cotangent)


def solution(mesh):
    in_specs = (
        P("section", None, None, "dp"),
        P("section", None),
        P("section", None, "dp"),
        P("section", "dp", None),
        P(None, None, "dp"),
    )
    out_specs = (
        P("section", None, "dp"),
        P("section", "dp", None),
        P("section", "dp"),
        P("section", None, None, "dp"),
    )
    return jax.shard_map(shards, mesh=mesh, in_specs=in_specs, out_specs=out_specs, check_vma=False)
```

```python
import functools

import jax
import jax.numpy as jnp
from jax import lax
from jax.experimental import pallas as pl
from jax.experimental.pallas import tpu as pltpu
from jax.sharding import PartitionSpec as P

F32 = jnp.float32
BF16 = jnp.bfloat16


def flip(block, axis, bits):
    count = lax.axis_size(axis)
    return lax.ppermute(block, axis, [(i, i ^ bits) for i in range(count)])


def side_rows(values, width):
    lead = values.astype(BF16)
    trail = (values - lead.astype(F32)).astype(BF16)
    flat = jnp.concatenate([lead, trail])
    return jnp.pad(flat, (0, 16 * width - flat.shape[0])).reshape(16, width)


def side_values(rows, count):
    flat = rows.reshape(-1)
    return flat[:count].astype(F32) + flat[count:2 * count].astype(F32)


def gelu_tanh(value):
    return jax.nn.gelu(value, approximate=True)


def shards_of_any(checkpoints, gain, w_in, w_out, cotangent):
    sections = lax.axis_size("section")
    n_dp = lax.axis_size("dp")
    here = lax.axis_index("section")
    lane = lax.axis_index("dp")
    layers = sections // 4
    mine = here % 4
    last = here // 4 == layers - 1
    _, micro, tok, share = checkpoints.shape
    rows = micro * tok
    quarter = share * n_dp
    width = 4 * quarter
    gain_row = gain[0]
    weight_in = w_in[0]
    weight_out = w_out[0]
    hidden = weight_in.shape[1]
    piece = hidden // 4
    core = lane % 2

    def gather_dp(block):
        bit = n_dp // 2
        parts = {0: block}
        while bit >= 1:
            other = flip(jnp.concatenate([parts[j] for j in parts], axis=1), "dp", bit)
            for at, j in enumerate(list(parts)):
                parts[j ^ bit] = other[:, at * block.shape[1]:(at + 1) * block.shape[1]]
            bit //= 2
        full = jnp.zeros((rows, quarter), block.dtype)
        for j, part in parts.items():
            full = lax.dynamic_update_slice(full, part, (0, (lane ^ j) * block.shape[1]))
        return full

    def cot_quarter(block):
        if n_dp < 4:
            whole = lax.all_gather(block, "dp", axis=1, tiled=True)
            return lax.dynamic_slice_in_dim(whole, mine * quarter, quarter, 1)
        per = n_dp // 4
        top = [s * n_dp + d for s in range(sections) for d in range(n_dp) if s // 4 == layers - 1]
        held = block
        far = lambda i, b: (i % n_dp // per ^ i // n_dp % 4) & b
        got = lax.ppermute(held, ("section", "dp"), [(i, i ^ 2 * per) for i in top if far(i, 3) == 0])
        held = jnp.where((lane // per ^ mine) & 2 == 0, held, got)
        got = lax.ppermute(held, ("section", "dp"), [(i, i ^ per) for i in top if far(i, 1) == 0])
        held = jnp.where((lane // per ^ mine) & 1 == 0, held, got)
        if per == 1:
            return held
        parts = {0: held}
        bit = per // 2
        while bit >= 1:
            for j in list(parts):
                parts[j ^ bit] = flip(parts[j], "dp", bit)
            bit //= 2
        full = jnp.zeros((rows, quarter), block.dtype)
        for j, part in parts.items():
            full = lax.dynamic_update_slice(full, part, (0, (lane % per ^ j) * block.shape[1]))
        return full

    def cut(values, j):
        return lax.dynamic_slice_in_dim(values, (mine ^ j) * piece, piece, 1)

    def fill(parts):
        full = jnp.zeros((rows, hidden), parts[0].dtype)
        for j, part in enumerate(parts):
            full = lax.dynamic_update_slice(full, part, (0, (mine ^ j) * piece))
        return full

    x_full = gather_dp(checkpoints[0].reshape(rows, share))
    cot = cot_quarter(cotangent.reshape(rows, cotangent.shape[2]))
    x_wide = x_full.astype(F32)
    scaled_raw = (x_wide * gain_row).astype(BF16)
    squares = jnp.sum(x_wide * x_wide, axis=1)

    act_raw = jnp.dot(scaled_raw, weight_in, preferred_element_type=F32)
    extra = side_rows(squares, piece)
    act = cut(act_raw, 0)
    for j in (3, 1, 2):
        got = flip(jnp.concatenate([cut(act_raw, j).astype(BF16), extra], axis=0), "section", j)
        act = act + got[:rows].astype(F32)
        squares = squares + side_values(got[rows:], rows)
    scale = lax.rsqrt(squares / width + 1e-06)[:, None]
    act = act * scale
    hid, pull = jax.vjp(gelu_tanh, act)
    hid = hid.astype(BF16)
    hid_full = fill([hid] + [flip(hid, "section", j) for j in (1, 2, 3)])
    normed = x_wide * scale
    scaled = (normed * gain_row).astype(BF16)

    def halves(values, side):
        pairs = values.reshape(rows, n_dp // 2, 2, share)
        return jnp.where(side == 0, pairs[:, :, 0], pairs[:, :, 1]).reshape(rows, quarter // 2)

    def own(values):
        return lax.dynamic_slice_in_dim(values, lane // 2 * share, share, 1)

    incoming = jnp.zeros((rows, quarter), BF16)
    normed_half = halves(normed, core)
    gain_half = halves(jnp.broadcast_to(gain_row, (rows, quarter)), core)
    for phase in range(layers):
        final = phase == layers - 1
        dy = jnp.where(last, cot, incoming) if phase > 0 else cot
        dhid_raw = jnp.dot(dy, weight_out.T, preferred_element_type=F32)
        dhid = cut(dhid_raw, 0)
        for j in (3, 1, 2):
            dhid = dhid + flip(cut(dhid_raw, j).astype(BF16), "section", j).astype(F32)
        dact = pull(dhid)[0].astype(BF16)
        inner = jnp.sum(dact.astype(F32) * act, axis=1)
        payload = jnp.concatenate([dact, side_rows(inner, piece)], axis=0)
        others = [flip(payload, "section", j) for j in (1, 2, 3)]
        for got in others:
            inner = inner + side_values(got[rows:], rows)
        dact_full = fill([dact] + [got[:rows] for got in others])
        part = jnp.dot(dact_full, weight_in.T, preferred_element_type=F32).astype(BF16)

        send = jnp.concatenate([halves(part, 1 - core), side_rows(inner, quarter // 2)], axis=0)
        got = flip(send, "dp", 1)
        dscaled = halves(part, core).astype(F32) + got[:rows].astype(F32)
        inner = inner + side_values(got[rows:], rows)
        bit = 2
        while bit < n_dp:
            send = jnp.concatenate([dscaled.astype(BF16), side_rows(inner, quarter // 2)], axis=0)
            got = flip(send, "dp", bit)
            dscaled = dscaled + got[:rows].astype(F32)
            inner = inner + side_values(got[rows:], rows)
            bit *= 2
        dnorm = dscaled * gain_half
        dy_half = halves(dy, core).astype(F32)
        grad_x = (dy_half + scale * (dnorm - normed_half * (inner / width)[:, None])).astype(BF16)
        if not final:
            down = lax.ppermute(grad_x, "section", [(i, i - 4) for i in range(4, sections)])
            other = flip(down, "dp", 1)
            pairs = jnp.where(
                core == 0,
                jnp.stack([down.reshape(rows, n_dp // 2, share), other.reshape(rows, n_dp // 2, share)], axis=2),
                jnp.stack([other.reshape(rows, n_dp // 2, share), down.reshape(rows, n_dp // 2, share)], axis=2),
            )
            incoming = pairs.reshape(rows, quarter)

    grad_out = jnp.dot(hid_full.T, dy, preferred_element_type=F32).astype(BF16)
    grad_in = jnp.dot(scaled.T, dact_full, preferred_element_type=F32).astype(BF16)
    grad_gain = jnp.sum(own(dscaled) * own(normed_half), axis=0)
    return (
        grad_in[None],
        grad_out[None],
        grad_gain[None],
        own(grad_x).reshape(1, micro, tok, share),
    )


SIDE = 16
GELU_IN = 0.7978845608028654
GELU_CUBE = 0.044715


def resident(shape, dtype):
    return pltpu.VMEM(shape, dtype)


def local(body, outs, *args, scratch=(), flops=0):
    spec = pl.BlockSpec(memory_space=pltpu.VMEM)
    moved = sum(a.size * a.dtype.itemsize for a in args)
    return pl.pallas_call(
        body,
        out_shape=tuple(outs),
        in_specs=[spec] * len(args),
        out_specs=tuple(spec for _ in outs),
        scratch_shapes=list(scratch),
        compiler_params=pltpu.CompilerParams(vmem_limit_bytes=16 * 1024 * 1024),
        cost_estimate=pl.CostEstimate(flops=flops, bytes_accessed=moved, transcendentals=0),
    )(*args)


def diagonal(rows, width):
    return lax.broadcasted_iota(jnp.int32, (rows, width), 0) == lax.broadcasted_iota(jnp.int32, (rows, width), 1)


def as_row(column, width):
    rows = column.shape[0]
    return jnp.sum(jnp.where(diagonal(rows, width), column, 0.0), axis=0, keepdims=True)


def as_column(row, rows):
    return jnp.sum(jnp.where(diagonal(rows, row.shape[1]), row, 0.0), axis=1, keepdims=True)


def side_block(row):
    lead = row.astype(BF16).astype(F32)
    at = lax.broadcasted_iota(jnp.int32, (SIDE, row.shape[1]), 0)
    return jnp.where(at == 0, lead, jnp.where(at == 1, row - lead, 0.0)).astype(BF16)


def side_row(block):
    wide = block.astype(F32)
    return wide[0:1] + wide[1:2]


def load_kernel(*refs):
    count = len(refs) // 2
    copies = [pltpu.make_async_copy(refs[i], refs[count + i], refs[-1].at[i]) for i in range(count)]
    for copy in copies:
        copy.start()
    for copy in copies:
        copy.wait()


def load(*arrays):
    return pl.pallas_call(
        load_kernel,
        out_shape=tuple(resident(a.shape, a.dtype) for a in arrays),
        in_specs=[pl.BlockSpec(memory_space=pl.ANY)] * len(arrays),
        out_specs=tuple(pl.BlockSpec(memory_space=pltpu.VMEM) for _ in arrays),
        scratch_shapes=[pltpu.SemaphoreType.DMA((len(arrays),))],
        compiler_params=pltpu.CompilerParams(vmem_limit_bytes=1024 * 1024),
        cost_estimate=pl.CostEstimate(flops=0, bytes_accessed=sum(2 * a.size * a.dtype.itemsize for a in arrays), transcendentals=0),
    )(*(pltpu.with_memory_space_constraint(a, pltpu.HBM) for a in arrays))


def place():
    return lax.axis_index("section") % 4, lax.axis_index("dp")


def dot_nt(left, right):
    return lax.dot_general(left, right, (((1,), (1,)), ((), ())), preferred_element_type=F32)


def dot_tn(left, right):
    return lax.dot_general(left, right, (((0,), (0,)), ((), ())), preferred_element_type=F32)


def slot(index, size):
    return pl.ds(pl.multiple_of(index * size, size), size)


def spread_in_kernel(x0, x1, x2, x3, gain, weight, own, s1, s2, s3, x_full, scaled):
    mine, lane = place()
    rows, share = x0.shape
    piece = own.shape[1]
    for d, part in enumerate((x0, x1, x2, x3)):
        x_full[:, slot(lane ^ d, share)] = part[...]
    wide = x_full[...].astype(F32)
    row = as_row(jnp.sum(wide * wide, axis=1, keepdims=True), piece)
    scaled[...] = (wide * gain[...]).astype(BF16)
    block = side_block(row)
    for d, out in ((3, s3), (2, s2), (1, s1)):
        out[:rows] = jnp.dot(scaled[...], weight[:, slot(mine ^ d, piece)], preferred_element_type=F32).astype(BF16)
        out[rows:] = block
    own[:rows] = jnp.dot(scaled[...], weight[:, slot(mine, piece)], preferred_element_type=F32)
    own[rows:] = jnp.broadcast_to(row, (SIDE, piece))


def spread_dy(dy, weight, mine, own, s1, s2, s3):
    piece = own.shape[1]
    for d, out in ((3, s3), (2, s2), (1, s1)):
        out[...] = dot_nt(dy[...], weight[slot(mine ^ d, piece), :]).astype(BF16)
    own[...] = dot_nt(dy[...], weight[slot(mine, piece), :])


def spread_first_kernel(start, c0, c1, c2, c3, weight, own, s1, s2, s3, dy):
    mine, lane = place()
    count = dy.shape[0]
    for d, part in enumerate((c0, c1, c2, c3)):
        @pl.when(lane ^ mine == d)
        def _(part=part):
            dy[...] = part[start:start + count]

    spread_dy(dy, weight, mine, own, s1, s2, s3)


def spread_next_kernel(layers, d0, d1, d2, d3, before, weight, own, s1, s2, s3, dy):
    mine, lane = place()
    share = d0.shape[1]
    last = lax.axis_index("section") // 4 == layers - 1

    @pl.when(last)
    def _():
        dy[...] = before[...]

    @pl.when(jnp.logical_not(last))
    def _():
        for d, part in enumerate((d0, d1, d2, d3)):
            dy[:, slot(lane ^ d, share)] = part[...]

    spread_dy(dy, weight, mine, own, s1, s2, s3)


def act_kernel(width, own, g1, g2, g3, act, slope, hid, scale):
    rows = act.shape[0]
    row = own[rows:rows + 1] + side_row(g1[rows:]) + side_row(g2[rows:]) + side_row(g3[rows:])
    r = lax.rsqrt(as_column(row, rows) / width + 1e-06)
    scale[...] = r
    a = (own[:rows] + g1[:rows].astype(F32) + g2[:rows].astype(F32) + g3[:rows].astype(F32)) * r
    act[...] = a
    square = a * a
    t = jnp.tanh(GELU_IN * (a + GELU_CUBE * (square * a)))
    half = 0.5 * (1.0 + t)
    hid[...] = (a * half).astype(BF16)
    slope[...] = half + 0.5 * a * (1.0 - t * t) * (GELU_IN * (1.0 + 3.0 * GELU_CUBE * square))


def dact_kernel(start, own, g1, g2, g3, act, slope, pay):
    rows, piece = own.shape
    at = slice(start, start + rows)
    dhid = own[...] + g1[...].astype(F32) + g2[...].astype(F32) + g3[...].astype(F32)
    da = (dhid * slope[at]).astype(BF16)
    pay[:rows] = da
    pay[rows:] = side_block(as_row(jnp.sum(da.astype(F32) * act[at], axis=1, keepdims=True), piece))


def back_kernel(p0, p1, p2, p3, weight, keep, send, full):
    mine, lane = place()
    rows = full.shape[0]
    piece = p0.shape[1]
    share = weight.shape[0] // 4
    row = side_row(p0[rows:]) + side_row(p1[rows:]) + side_row(p2[rows:]) + side_row(p3[rows:])
    for d, part in enumerate((p0, p1, p2, p3)):
        full[:, slot(mine ^ d, piece)] = part[:rows]
    for at, d in ((0, 1), (1, 3)):
        send[:rows, at * share:(at + 1) * share] = dot_nt(full[...], weight[slot(lane ^ d, share), :]).astype(BF16)
    send[rows:] = side_block(row)
    for at, d in ((0, 0), (1, 2)):
        keep[:rows, at * share:(at + 1) * share] = dot_nt(full[...], weight[slot(lane ^ d, share), :])
    keep[rows:] = jnp.broadcast_to(row, (SIDE, keep.shape[1]))


def middle_kernel(keep, got, rest, send):
    rows = keep.shape[0] - SIDE
    share = rest.shape[1]
    row = (keep[rows:rows + 1] + side_row(got[rows:]))[:, :share]
    send[:rows] = (keep[:rows, share:] + got[:rows, share:].astype(F32)).astype(BF16)
    send[rows:] = side_block(row)
    rest[:rows] = keep[:rows, :share] + got[:rows, :share].astype(F32)
    rest[rows:] = jnp.broadcast_to(row, (SIDE, share))


def input_gradient(width, start, rest, got, x_own, dy, gain, scale):
    _, lane = place()
    rows, share = dy.shape[0], x_own.shape[1]
    mine = slice(start, start + rows)
    at = slot(lane, share)
    r = scale[mine]
    du = rest[:rows] + got[:rows].astype(F32)
    normed = x_own[mine].astype(F32) * r
    inner = as_column(rest[rows:rows + 1] + side_row(got[rows:]), rows) / width
    dnorm = du * gain[:, at]
    grad_x = (dy[:, at].astype(F32) + r * (dnorm - normed * inner)).astype(BF16)
    return grad_x, jnp.sum(du * normed, axis=0, keepdims=True)


def finish_kernel(width, start, rest, got, x_own, dy, gain, scale, grad_x):
    grad_x[...] = input_gradient(width, start, rest, got, x_own, dy, gain, scale)[0]


def finish_all_kernel(width, starts, x_own, gain, scale, *refs):
    *groups, grad_x, grad_gain = refs
    total = 0.0
    for i, start in enumerate(starts):
        rest, got, dy = groups[3 * i:3 * i + 3]
        part, gain_part = input_gradient(width, start, rest, got, x_own, dy, gain, scale)
        grad_x[start:start + part.shape[0]] = part
        total = total + gain_part
    grad_gain[...] = total


def grad_out_kernel(starts, h0, h1, h2, h3, *refs):
    *dys, out, dy, held, sems = refs
    mine, _ = place()
    piece = h0.shape[1]
    for start, part in zip(starts, dys):
        dy[start:start + part.shape[0]] = part[...]
    copies = []
    for d, part in enumerate((h0, h1, h2, h3)):
        held[d] = dot_tn(part[...], dy[...]).astype(BF16)
        copies.append(pltpu.make_async_copy(held.at[d], out.at[slot(mine ^ d, piece), :], sems.at[d]))
        copies[-1].start()
    for copy in copies:
        copy.wait()


def grad_in_kernel(starts, x_full, gain, scale, *refs):
    *pays, out, scaled, da, held, sems = refs
    mine, _ = place()
    piece = da.shape[1]
    scaled[...] = (x_full[...].astype(F32) * scale[...] * gain[...]).astype(BF16)
    copies = []
    for d in range(4):
        for i, start in enumerate(starts):
            part = pays[4 * i + d]
            count = part.shape[0] - SIDE
            da[start:start + count] = part[:count]
        held[d] = dot_tn(scaled[...], da[...]).astype(BF16)
        copies.append(pltpu.make_async_copy(held.at[d], out.at[:, slot(mine ^ d, piece)], sems.at[d]))
        copies[-1].start()
    for copy in copies:
        copy.wait()


def gradient(body, shape, block, *args, scratch=(), flops=0):
    return pl.pallas_call(
        body,
        out_shape=jax.ShapeDtypeStruct(shape, BF16),
        in_specs=[pl.BlockSpec(memory_space=pltpu.VMEM)] * len(args),
        out_specs=pl.BlockSpec(memory_space=pl.ANY),
        scratch_shapes=[*scratch, pltpu.VMEM((4,) + block, BF16), pltpu.SemaphoreType.DMA((4,))],
        compiler_params=pltpu.CompilerParams(vmem_limit_bytes=16 * 1024 * 1024),
        cost_estimate=pl.CostEstimate(flops=flops, bytes_accessed=2 * shape[0] * shape[1], transcendentals=0),
    )(*args)


def shards_of_four(checkpoints, gain, w_in, w_out, cotangent):
    sections = lax.axis_size("section")
    here = lax.axis_index("section")
    lane = lax.axis_index("dp")
    layers = sections // 4
    mine = here % 4
    _, micro, tok, share = checkpoints.shape
    rows = micro * tok
    quarter = share * 4
    width = 4 * quarter
    hidden = w_in.shape[2]
    piece = hidden // 4
    work = 2 * rows * quarter * hidden

    x0 = checkpoints[0].reshape(rows, share)
    cot = cotangent.reshape(rows, quarter)
    top = [s * 4 + d for s in range(sections) for d in range(4) if s // 4 == layers - 1]
    x2 = flip(x0, "dp", 2)
    x1 = flip(x0, "dp", 1)
    weight_in, x0, gain = load(w_in[0], x0, gain)
    x2, x1, cot, weight_in = lax.optimization_barrier((x2, x1, cot, weight_in))
    c2, c3 = [lax.ppermute(cot, ("section", "dp"), [(i, i ^ d) for i in top if i % 4 == i // 4 % 4]) for d in (2, 3)]
    x3 = flip(x2, "dp", 1)

    wide = (rows + SIDE, piece)
    own, s1, s2, s3, x_full = local(
        spread_in_kernel,
        [resident(wide, F32)] + [resident(wide, BF16)] * 3 + [resident((rows, quarter), BF16)],
        x0, x1, x2, x3, gain, weight_in,
        scratch=[pltpu.VMEM((rows, quarter), BF16)], flops=work,
    )
    s1, s2, s3, cot, w_out = lax.optimization_barrier((s1, s2, s3, cot, w_out))
    g3 = flip(s3, "section", 3)
    g2 = flip(s2, "section", 2)
    g1 = flip(s1, "section", 1)
    c1 = lax.ppermute(cot, ("section", "dp"), [(i, i ^ 1) for i in top if i % 4 == i // 4 % 4])
    weight_out, c0 = load(w_out[0], cot)
    act, slope, hid, scale = local(
        functools.partial(act_kernel, width),
        [resident((rows, piece), F32), resident((rows, piece), F32), resident((rows, piece), BF16), resident((rows, 1), F32)],
        own, g1, g2, g3,
    )

    def gather_hidden(block):
        return [block] + [flip(block, "section", j) for j in (1, 2, 3)]

    groups = 2 if rows % (2 * SIDE) == 0 else 1
    count = rows // groups
    starts = [i * count for i in range(groups)]
    wide = (count + SIDE, piece)
    half = (count + SIDE, 2 * share)
    narrow = (count + SIDE, share)
    spread_outs = [resident((count, piece), F32)] + [resident((count, piece), BF16)] * 3 + [resident((count, quarter), BF16)]
    hids = gather_hidden(hid) if layers == 1 else None
    dys = [None] * groups
    down = [None] * groups
    for phase in range(layers):
        final = phase == layers - 1
        spread = [None] * groups
        for i, start in enumerate(starts):
            if phase == 0:
                *sent, dys[i] = local(
                    functools.partial(spread_first_kernel, start), spread_outs, c0, c1, c2, c3, weight_out, flops=work // groups
                )
            else:
                d0 = down[i]
                d2 = flip(d0, "dp", 2)
                parts = (d0, flip(d0, "dp", 1), d2, flip(d2, "dp", 1))
                if i > 0:
                    parts, spread[i - 1] = lax.optimization_barrier((parts, spread[i - 1]))
                if i == groups - 1:
                    parts, hids = lax.optimization_barrier((parts, hids))
                *sent, dys[i] = local(
                    functools.partial(spread_next_kernel, layers), spread_outs, *parts, dys[i], weight_out, flops=work // groups
                )
            spread[i] = sent
        spread = [[sent[0]] + [flip(sent[d], "section", d) for d in (1, 2, 3)] for sent in spread]
        if final:
            grad_out = gradient(
                functools.partial(grad_out_kernel, starts), (hidden, quarter), (piece, quarter), *hids, *dys,
                scratch=[pltpu.VMEM((rows, quarter), BF16)], flops=work,
            )
            spread[-1], grad_out = lax.optimization_barrier((spread[-1], grad_out))
        pays = [None] * groups
        for i, start in enumerate(starts):
            (pay,) = local(functools.partial(dact_kernel, start), [resident(wide, BF16)], *spread[i], act, slope)
            pays[i] = [pay] + [flip(pay, "section", d) for d in (1, 2, 3)]
        ends = [None] * groups
        for i in range(groups):
            keep, send = local(
                back_kernel, [resident(half, F32), resident(half, BF16)], *pays[i], weight_in,
                scratch=[pltpu.VMEM((count, hidden), BF16)], flops=work // groups,
            )
            rest, send = local(middle_kernel, [resident(narrow, F32), resident(narrow, BF16)], keep, flip(send, "dp", 1))
            ends[i] = (rest, send)
        ends = [(rest, flip(send, "dp", 2)) for rest, send in ends]
        if final:
            grad_in = gradient(
                functools.partial(grad_in_kernel, starts), (quarter, hidden), (quarter, piece), x_full, gain, scale,
                *[part for pay in pays for part in pay],
                scratch=[pltpu.VMEM((rows, quarter), BF16), pltpu.VMEM((rows, piece), BF16)], flops=work,
            )
            ends[-1], grad_in = lax.optimization_barrier((ends[-1], grad_in))
            grad_x, grad_gain = local(
                functools.partial(finish_all_kernel, width, starts),
                [jax.ShapeDtypeStruct((rows, share), BF16), jax.ShapeDtypeStruct((1, share), F32)],
                x0, gain, scale, *[ref for i in range(groups) for ref in (*ends[i], dys[i])],
            )
            break
        for i, start in enumerate(starts):
            (lower,) = local(
                functools.partial(finish_kernel, width, start), [resident((count, share), BF16)],
                *ends[i], x0, dys[i], gain, scale,
            )
            if i == groups - 1 and phase == 0:
                lower, hid = lax.optimization_barrier((lower, hid))
                hids = gather_hidden(hid)
            down[i] = lax.ppermute(lower, "section", [(j, j - 4) for j in range(4, sections)])

    return grad_in[None], grad_out[None], grad_gain, grad_x.reshape(1, micro, tok, share)


def shards(checkpoints, gain, w_in, w_out, cotangent):
    rows = checkpoints.shape[1] * checkpoints.shape[2]
    share = checkpoints.shape[3]
    piece = w_in.shape[2] // 4
    if lax.axis_size("dp") == 4 and rows % 16 == 0 and share % 128 == 0 and piece % 128 == 0 and rows <= min(share, piece):
        return shards_of_four(checkpoints, gain, w_in, w_out, cotangent)
    return shards_of_any(checkpoints, gain, w_in, w_out, cotangent)


def solution(mesh):
    in_specs = (
        P("section", None, None, "dp"),
        P("section", None),
        P("section", None, "dp"),
        P("section", "dp", None),
        P(None, None, "dp"),
    )
    out_specs = (
        P("section", None, "dp"),
        P("section", "dp", None),
        P("section", "dp"),
        P("section", None, None, "dp"),
    )
    return jax.shard_map(shards, mesh=mesh, in_specs=in_specs, out_specs=out_specs, check_vma=False)
```

```python
import functools

import jax
import jax.numpy as jnp
from jax import lax
from jax.experimental import pallas as pl
from jax.experimental.pallas import tpu as pltpu
from jax.sharding import PartitionSpec as P

F32 = jnp.float32
BF16 = jnp.bfloat16


def flip(block, axis, bits):
    count = lax.axis_size(axis)
    return lax.ppermute(block, axis, [(i, i ^ bits) for i in range(count)])


def side_rows(values, width):
    lead = values.astype(BF16)
    trail = (values - lead.astype(F32)).astype(BF16)
    flat = jnp.concatenate([lead, trail])
    return jnp.pad(flat, (0, 16 * width - flat.shape[0])).reshape(16, width)


def side_values(rows, count):
    flat = rows.reshape(-1)
    return flat[:count].astype(F32) + flat[count:2 * count].astype(F32)


def gelu_tanh(value):
    return jax.nn.gelu(value, approximate=True)


def shards_of_any(checkpoints, gain, w_in, w_out, cotangent):
    sections = lax.axis_size("section")
    n_dp = lax.axis_size("dp")
    here = lax.axis_index("section")
    lane = lax.axis_index("dp")
    layers = sections // 4
    mine = here % 4
    last = here // 4 == layers - 1
    _, micro, tok, share = checkpoints.shape
    rows = micro * tok
    quarter = share * n_dp
    width = 4 * quarter
    gain_row = gain[0]
    weight_in = w_in[0]
    weight_out = w_out[0]
    hidden = weight_in.shape[1]
    piece = hidden // 4
    core = lane % 2

    def gather_dp(block):
        bit = n_dp // 2
        parts = {0: block}
        while bit >= 1:
            other = flip(jnp.concatenate([parts[j] for j in parts], axis=1), "dp", bit)
            for at, j in enumerate(list(parts)):
                parts[j ^ bit] = other[:, at * block.shape[1]:(at + 1) * block.shape[1]]
            bit //= 2
        full = jnp.zeros((rows, quarter), block.dtype)
        for j, part in parts.items():
            full = lax.dynamic_update_slice(full, part, (0, (lane ^ j) * block.shape[1]))
        return full

    def cot_quarter(block):
        if n_dp < 4:
            whole = lax.all_gather(block, "dp", axis=1, tiled=True)
            return lax.dynamic_slice_in_dim(whole, mine * quarter, quarter, 1)
        per = n_dp // 4
        top = [s * n_dp + d for s in range(sections) for d in range(n_dp) if s // 4 == layers - 1]
        held = block
        far = lambda i, b: (i % n_dp // per ^ i // n_dp % 4) & b
        got = lax.ppermute(held, ("section", "dp"), [(i, i ^ 2 * per) for i in top if far(i, 3) == 0])
        held = jnp.where((lane // per ^ mine) & 2 == 0, held, got)
        got = lax.ppermute(held, ("section", "dp"), [(i, i ^ per) for i in top if far(i, 1) == 0])
        held = jnp.where((lane // per ^ mine) & 1 == 0, held, got)
        if per == 1:
            return held
        parts = {0: held}
        bit = per // 2
        while bit >= 1:
            for j in list(parts):
                parts[j ^ bit] = flip(parts[j], "dp", bit)
            bit //= 2
        full = jnp.zeros((rows, quarter), block.dtype)
        for j, part in parts.items():
            full = lax.dynamic_update_slice(full, part, (0, (lane % per ^ j) * block.shape[1]))
        return full

    def cut(values, j):
        return lax.dynamic_slice_in_dim(values, (mine ^ j) * piece, piece, 1)

    def fill(parts):
        full = jnp.zeros((rows, hidden), parts[0].dtype)
        for j, part in enumerate(parts):
            full = lax.dynamic_update_slice(full, part, (0, (mine ^ j) * piece))
        return full

    x_full = gather_dp(checkpoints[0].reshape(rows, share))
    cot = cot_quarter(cotangent.reshape(rows, cotangent.shape[2]))
    x_wide = x_full.astype(F32)
    scaled_raw = (x_wide * gain_row).astype(BF16)
    squares = jnp.sum(x_wide * x_wide, axis=1)

    act_raw = jnp.dot(scaled_raw, weight_in, preferred_element_type=F32)
    extra = side_rows(squares, piece)
    act = cut(act_raw, 0)
    for j in (3, 1, 2):
        got = flip(jnp.concatenate([cut(act_raw, j).astype(BF16), extra], axis=0), "section", j)
        act = act + got[:rows].astype(F32)
        squares = squares + side_values(got[rows:], rows)
    scale = lax.rsqrt(squares / width + 1e-06)[:, None]
    act = act * scale
    hid, pull = jax.vjp(gelu_tanh, act)
    hid = hid.astype(BF16)
    hid_full = fill([hid] + [flip(hid, "section", j) for j in (1, 2, 3)])
    normed = x_wide * scale
    scaled = (normed * gain_row).astype(BF16)

    def halves(values, side):
        pairs = values.reshape(rows, n_dp // 2, 2, share)
        return jnp.where(side == 0, pairs[:, :, 0], pairs[:, :, 1]).reshape(rows, quarter // 2)

    def own(values):
        return lax.dynamic_slice_in_dim(values, lane // 2 * share, share, 1)

    incoming = jnp.zeros((rows, quarter), BF16)
    normed_half = halves(normed, core)
    gain_half = halves(jnp.broadcast_to(gain_row, (rows, quarter)), core)
    for phase in range(layers):
        final = phase == layers - 1
        dy = jnp.where(last, cot, incoming) if phase > 0 else cot
        dhid_raw = jnp.dot(dy, weight_out.T, preferred_element_type=F32)
        dhid = cut(dhid_raw, 0)
        for j in (3, 1, 2):
            dhid = dhid + flip(cut(dhid_raw, j).astype(BF16), "section", j).astype(F32)
        dact = pull(dhid)[0].astype(BF16)
        inner = jnp.sum(dact.astype(F32) * act, axis=1)
        payload = jnp.concatenate([dact, side_rows(inner, piece)], axis=0)
        others = [flip(payload, "section", j) for j in (1, 2, 3)]
        for got in others:
            inner = inner + side_values(got[rows:], rows)
        dact_full = fill([dact] + [got[:rows] for got in others])
        part = jnp.dot(dact_full, weight_in.T, preferred_element_type=F32).astype(BF16)

        send = jnp.concatenate([halves(part, 1 - core), side_rows(inner, quarter // 2)], axis=0)
        got = flip(send, "dp", 1)
        dscaled = halves(part, core).astype(F32) + got[:rows].astype(F32)
        inner = inner + side_values(got[rows:], rows)
        bit = 2
        while bit < n_dp:
            send = jnp.concatenate([dscaled.astype(BF16), side_rows(inner, quarter // 2)], axis=0)
            got = flip(send, "dp", bit)
            dscaled = dscaled + got[:rows].astype(F32)
            inner = inner + side_values(got[rows:], rows)
            bit *= 2
        dnorm = dscaled * gain_half
        dy_half = halves(dy, core).astype(F32)
        grad_x = (dy_half + scale * (dnorm - normed_half * (inner / width)[:, None])).astype(BF16)
        if not final:
            down = lax.ppermute(grad_x, "section", [(i, i - 4) for i in range(4, sections)])
            other = flip(down, "dp", 1)
            pairs = jnp.where(
                core == 0,
                jnp.stack([down.reshape(rows, n_dp // 2, share), other.reshape(rows, n_dp // 2, share)], axis=2),
                jnp.stack([other.reshape(rows, n_dp // 2, share), down.reshape(rows, n_dp // 2, share)], axis=2),
            )
            incoming = pairs.reshape(rows, quarter)

    grad_out = jnp.dot(hid_full.T, dy, preferred_element_type=F32).astype(BF16)
    grad_in = jnp.dot(scaled.T, dact_full, preferred_element_type=F32).astype(BF16)
    grad_gain = jnp.sum(own(dscaled) * own(normed_half), axis=0)
    return (
        grad_in[None],
        grad_out[None],
        grad_gain[None],
        own(grad_x).reshape(1, micro, tok, share),
    )


SIDE = 16
GELU_IN = 0.7978845608028654
GELU_CUBE = 0.044715


def resident(shape, dtype):
    return pltpu.VMEM(shape, dtype)


def local(body, outs, *args, scratch=(), flops=0):
    spec = pl.BlockSpec(memory_space=pltpu.VMEM)
    moved = sum(a.size * a.dtype.itemsize for a in args)
    return pl.pallas_call(
        body,
        out_shape=tuple(outs),
        in_specs=[spec] * len(args),
        out_specs=tuple(spec for _ in outs),
        scratch_shapes=list(scratch),
        compiler_params=pltpu.CompilerParams(vmem_limit_bytes=16 * 1024 * 1024),
        cost_estimate=pl.CostEstimate(flops=flops, bytes_accessed=moved, transcendentals=0),
    )(*args)


def diagonal(rows, width):
    return lax.broadcasted_iota(jnp.int32, (rows, width), 0) == lax.broadcasted_iota(jnp.int32, (rows, width), 1)


def as_row(column, width):
    rows = column.shape[0]
    return jnp.sum(jnp.where(diagonal(rows, width), column, 0.0), axis=0, keepdims=True)


def as_column(row, rows):
    return jnp.sum(jnp.where(diagonal(rows, row.shape[1]), row, 0.0), axis=1, keepdims=True)


def side_block(row):
    lead = row.astype(BF16).astype(F32)
    at = lax.broadcasted_iota(jnp.int32, (SIDE, row.shape[1]), 0)
    return jnp.where(at == 0, lead, jnp.where(at == 1, row - lead, 0.0)).astype(BF16)


def side_row(block):
    wide = block.astype(F32)
    return wide[0:1] + wide[1:2]


def load_kernel(*refs):
    count = len(refs) // 2
    copies = [pltpu.make_async_copy(refs[i], refs[count + i], refs[-1].at[i]) for i in range(count)]
    for copy in copies:
        copy.start()
    for copy in copies:
        copy.wait()


def load(*arrays):
    return pl.pallas_call(
        load_kernel,
        out_shape=tuple(resident(a.shape, a.dtype) for a in arrays),
        in_specs=[pl.BlockSpec(memory_space=pl.ANY)] * len(arrays),
        out_specs=tuple(pl.BlockSpec(memory_space=pltpu.VMEM) for _ in arrays),
        scratch_shapes=[pltpu.SemaphoreType.DMA((len(arrays),))],
        compiler_params=pltpu.CompilerParams(vmem_limit_bytes=1024 * 1024),
        cost_estimate=pl.CostEstimate(flops=0, bytes_accessed=sum(2 * a.size * a.dtype.itemsize for a in arrays), transcendentals=0),
    )(*(pltpu.with_memory_space_constraint(a, pltpu.HBM) for a in arrays))


def place():
    return lax.axis_index("section") % 4, lax.axis_index("dp")


def dot_nt(left, right):
    return lax.dot_general(left, right, (((1,), (1,)), ((), ())), preferred_element_type=F32)


def dot_tn(left, right):
    return lax.dot_general(left, right, (((0,), (0,)), ((), ())), preferred_element_type=F32)


def slot(index, size):
    return pl.ds(pl.multiple_of(index * size, size), size)


def spread_in_kernel(x0, x1, x2, x3, gain, weight, own, s1, s2, s3, x_full, scaled):
    mine, lane = place()
    rows, share = x0.shape
    piece = own.shape[1]
    for d, part in enumerate((x0, x1, x2, x3)):
        x_full[:, slot(lane ^ d, share)] = part[...]
    wide = x_full[...].astype(F32)
    row = as_row(jnp.sum(wide * wide, axis=1, keepdims=True), piece)
    scaled[...] = (wide * gain[...]).astype(BF16)
    block = side_block(row)
    for d, out in ((3, s3), (2, s2), (1, s1)):
        out[:rows] = jnp.dot(scaled[...], weight[:, slot(mine ^ d, piece)], preferred_element_type=F32).astype(BF16)
        out[rows:] = block
    own[:rows] = jnp.dot(scaled[...], weight[:, slot(mine, piece)], preferred_element_type=F32)
    own[rows:] = jnp.broadcast_to(row, (SIDE, piece))


def spread_dy(dy, weight, mine, own, s1, s2, s3):
    piece = own.shape[1]
    for d, out in ((3, s3), (2, s2), (1, s1)):
        out[...] = dot_nt(dy[...], weight[slot(mine ^ d, piece), :]).astype(BF16)
    own[...] = dot_nt(dy[...], weight[slot(mine, piece), :])


def pick_kernel(c0, c2, held):
    mine, lane = place()

    @pl.when(((lane ^ mine) & 2) == 0)
    def _():
        held[...] = c0[...]

    @pl.when(((lane ^ mine) & 2) != 0)
    def _():
        held[...] = c2[...]


def spread_first_kernel(held, got, weight, own, s1, s2, s3, dy):
    mine, lane = place()

    @pl.when(((lane ^ mine) & 1) == 0)
    def _():
        dy[...] = held[...]

    @pl.when(((lane ^ mine) & 1) != 0)
    def _():
        dy[...] = got[...]

    spread_dy(dy, weight, mine, own, s1, s2, s3)


def spread_next_kernel(layers, d0, d1, d2, d3, before, weight, own, s1, s2, s3, dy):
    mine, lane = place()
    share = d0.shape[1]
    last = lax.axis_index("section") // 4 == layers - 1

    @pl.when(last)
    def _():
        dy[...] = before[...]

    @pl.when(jnp.logical_not(last))
    def _():
        for d, part in enumerate((d0, d1, d2, d3)):
            dy[:, slot(lane ^ d, share)] = part[...]

    spread_dy(dy, weight, mine, own, s1, s2, s3)


def act_kernel(width, own, g1, g2, g3, act, slope, hid, scale):
    rows = act.shape[0]
    row = own[rows:rows + 1] + side_row(g1[rows:]) + side_row(g2[rows:]) + side_row(g3[rows:])
    r = lax.rsqrt(as_column(row, rows) / width + 1e-06)
    scale[...] = r
    a = (own[:rows] + g1[:rows].astype(F32) + g2[:rows].astype(F32) + g3[:rows].astype(F32)) * r
    act[...] = a
    square = a * a
    t = jnp.tanh(GELU_IN * (a + GELU_CUBE * (square * a)))
    half = 0.5 * (1.0 + t)
    hid[...] = (a * half).astype(BF16)
    slope[...] = half + 0.5 * a * (1.0 - t * t) * (GELU_IN * (1.0 + 3.0 * GELU_CUBE * square))


def dact_kernel(own, g1, g2, g3, act, slope, pay):
    rows, piece = own.shape
    dhid = own[...] + g1[...].astype(F32) + g2[...].astype(F32) + g3[...].astype(F32)
    da = (dhid * slope[...]).astype(BF16)
    pay[:rows] = da
    pay[rows:] = side_block(as_row(jnp.sum(da.astype(F32) * act[...], axis=1, keepdims=True), piece))


def back_kernel(p0, p1, p2, p3, weight, keep, send, full):
    mine, lane = place()
    rows = full.shape[0]
    piece = p0.shape[1]
    share = weight.shape[0] // 4
    row = side_row(p0[rows:]) + side_row(p1[rows:]) + side_row(p2[rows:]) + side_row(p3[rows:])
    for d, part in enumerate((p0, p1, p2, p3)):
        full[:, slot(mine ^ d, piece)] = part[:rows]
    for at, d in ((0, 1), (1, 3)):
        send[:rows, at * share:(at + 1) * share] = dot_nt(full[...], weight[slot(lane ^ d, share), :]).astype(BF16)
    send[rows:] = side_block(row)
    for at, d in ((0, 0), (1, 2)):
        keep[:rows, at * share:(at + 1) * share] = dot_nt(full[...], weight[slot(lane ^ d, share), :])
    keep[rows:] = jnp.broadcast_to(row, (SIDE, keep.shape[1]))


def middle_kernel(keep, got, rest, send):
    rows = keep.shape[0] - SIDE
    share = rest.shape[1]
    row = (keep[rows:rows + 1] + side_row(got[rows:]))[:, :share]
    send[:rows] = (keep[:rows, share:] + got[:rows, share:].astype(F32)).astype(BF16)
    send[rows:] = side_block(row)
    rest[:rows] = keep[:rows, :share] + got[:rows, :share].astype(F32)
    rest[rows:] = jnp.broadcast_to(row, (SIDE, share))


def finish_kernel(width, rest, got, x_own, dy, gain, scale, grad_x, *grad_gain):
    _, lane = place()
    rows, share = x_own.shape
    at = slot(lane, share)
    r = scale[...]
    du = rest[:rows] + got[:rows].astype(F32)
    normed = x_own[...].astype(F32) * r
    inner = as_column(rest[rows:rows + 1] + side_row(got[rows:]), rows) / width
    dnorm = du * gain[:, at]
    grad_x[...] = (dy[:, at].astype(F32) + r * (dnorm - normed * inner)).astype(BF16)
    if grad_gain:
        grad_gain[0][...] = jnp.sum(du * normed, axis=0, keepdims=True)


def grad_out_kernel(h0, h1, h2, h3, dy, out, held, sems):
    mine, _ = place()
    piece = h0.shape[1]
    copies = []
    for d, part in enumerate((h0, h1, h2, h3)):
        held[d] = dot_tn(part[...], dy[...]).astype(BF16)
        copies.append(pltpu.make_async_copy(held.at[d], out.at[slot(mine ^ d, piece), :], sems.at[d]))
        copies[-1].start()
    for copy in copies:
        copy.wait()


def grad_in_kernel(p0, p1, p2, p3, x_full, gain, scale, out, scaled, held, sems):
    mine, _ = place()
    rows = x_full.shape[0]
    piece = p0.shape[1]
    scaled[...] = (x_full[...].astype(F32) * scale[...] * gain[...]).astype(BF16)
    copies = []
    for d, part in enumerate((p0, p1, p2, p3)):
        held[d] = dot_tn(scaled[...], part[:rows]).astype(BF16)
        copies.append(pltpu.make_async_copy(held.at[d], out.at[:, slot(mine ^ d, piece)], sems.at[d]))
        copies[-1].start()
    for copy in copies:
        copy.wait()


def gradient(body, shape, block, *args, scratch=(), flops=0):
    return pl.pallas_call(
        body,
        out_shape=jax.ShapeDtypeStruct(shape, BF16),
        in_specs=[pl.BlockSpec(memory_space=pltpu.VMEM)] * len(args),
        out_specs=pl.BlockSpec(memory_space=pl.ANY),
        scratch_shapes=[*scratch, pltpu.VMEM((4,) + block, BF16), pltpu.SemaphoreType.DMA((4,))],
        compiler_params=pltpu.CompilerParams(vmem_limit_bytes=16 * 1024 * 1024),
        cost_estimate=pl.CostEstimate(flops=flops, bytes_accessed=2 * shape[0] * shape[1], transcendentals=0),
    )(*args)


def shards_of_four(checkpoints, gain, w_in, w_out, cotangent):
    sections = lax.axis_size("section")
    here = lax.axis_index("section")
    lane = lax.axis_index("dp")
    layers = sections // 4
    mine = here % 4
    _, micro, tok, share = checkpoints.shape
    rows = micro * tok
    quarter = share * 4
    width = 4 * quarter
    hidden = w_in.shape[2]
    piece = hidden // 4
    work = 2 * rows * quarter * hidden

    x0 = checkpoints[0].reshape(rows, share)
    cot = cotangent.reshape(rows, quarter)
    top = [s * 4 + d for s in range(sections) for d in range(4) if s // 4 == layers - 1]
    x2 = flip(x0, "dp", 2)
    x1 = flip(x0, "dp", 1)
    c2 = lax.ppermute(cot, ("section", "dp"), [(i, i ^ 2) for i in top if i % 4 == i // 4 % 4])
    weight_in, x0, gain = load(w_in[0], x0, gain)
    weight_out, c0 = load(w_out[0], cot)
    x2, x1, weight_in = lax.optimization_barrier((x2, x1, weight_in))
    x3 = flip(x2, "dp", 1)
    x3, c2, weight_out, c0 = lax.optimization_barrier((x3, c2, weight_out, c0))

    wide = (rows + SIDE, piece)
    own, s1, s2, s3, x_full = local(
        spread_in_kernel,
        [resident(wide, F32)] + [resident(wide, BF16)] * 3 + [resident((rows, quarter), BF16)],
        x0, x1, x2, x3, gain, weight_in,
        scratch=[pltpu.VMEM((rows, quarter), BF16)], flops=work,
    )
    s3, c2 = lax.optimization_barrier((s3, c2))
    (held,) = local(pick_kernel, [resident((rows, quarter), BF16)], c0, c2)
    got = lax.ppermute(held, ("section", "dp"), [(i, i ^ 1) for i in top if (i ^ i // 4) % 2 == 0])
    g3 = flip(s3, "section", 3)
    g2 = flip(s2, "section", 2)
    g1 = flip(s1, "section", 1)
    act, slope, hid, scale = local(
        functools.partial(act_kernel, width),
        [resident((rows, piece), F32), resident((rows, piece), F32), resident((rows, piece), BF16), resident((rows, 1), F32)],
        own, g1, g2, g3,
    )

    spread_outs = [resident((rows, piece), F32)] + [resident((rows, piece), BF16)] * 3 + [resident((rows, quarter), BF16)]

    def gather_hidden(block):
        return [block] + [flip(block, "section", j) for j in (1, 2, 3)]

    if layers == 1:
        hids = gather_hidden(hid)
    for phase in range(layers):
        final = phase == layers - 1
        if phase == 0:
            own, s1, s2, s3, dy = local(spread_first_kernel, spread_outs, held, got, weight_out, flops=work)
        else:
            down, hids = lax.optimization_barrier((down, hids))
            own, s1, s2, s3, dy = local(
                functools.partial(spread_next_kernel, layers), spread_outs, *down, dy, weight_out, flops=work
            )
        g3 = flip(s3, "section", 3)
        g2 = flip(s2, "section", 2)
        g1 = flip(s1, "section", 1)
        if final:
            grad_out = gradient(grad_out_kernel, (hidden, quarter), (piece, quarter), *hids, dy, flops=work)
            own, grad_out = lax.optimization_barrier((own, grad_out))
        (pay,) = local(dact_kernel, [resident(wide, BF16)], own, g1, g2, g3, act, slope)
        p3 = flip(pay, "section", 3)
        p2 = flip(pay, "section", 2)
        p1 = flip(pay, "section", 1)
        keep, send = local(
            back_kernel,
            [resident((rows + SIDE, 2 * share), F32), resident((rows + SIDE, 2 * share), BF16)],
            pay, p1, p2, p3, weight_in,
            scratch=[pltpu.VMEM((rows, hidden), BF16)], flops=work,
        )
        got = flip(send, "dp", 1)
        rest, send = local(
            middle_kernel,
            [resident((rows + SIDE, share), F32), resident((rows + SIDE, share), BF16)],
            keep, got,
        )
        if phase == 0 and not final:
            send, hid = lax.optimization_barrier((send, hid))
            hids = gather_hidden(hid)
        got = flip(send, "dp", 2)
        if final:
            grad_in = gradient(
                grad_in_kernel, (quarter, hidden), (quarter, piece), pay, p1, p2, p3, x_full, gain, scale,
                scratch=[pltpu.VMEM((rows, quarter), BF16)], flops=work,
            )
            got, grad_in = lax.optimization_barrier((got, grad_in))
        outs = [resident((rows, share), BF16)]
        if final:
            outs = [jax.ShapeDtypeStruct((rows, share), BF16), jax.ShapeDtypeStruct((1, share), F32)]
        finished = local(functools.partial(finish_kernel, width), outs, rest, got, x0, dy, gain, scale)
        if not final:
            d0 = lax.ppermute(finished[0], "section", [(i, i - 4) for i in range(4, sections)])
            d2 = flip(d0, "dp", 2)
            d1 = flip(d0, "dp", 1)
            d3 = flip(d2, "dp", 1)
            down = (d0, d1, d2, d3)

    grad_x, grad_gain = finished
    return grad_in[None], grad_out[None], grad_gain, grad_x.reshape(1, micro, tok, share)


def shards(checkpoints, gain, w_in, w_out, cotangent):
    rows = checkpoints.shape[1] * checkpoints.shape[2]
    share = checkpoints.shape[3]
    piece = w_in.shape[2] // 4
    if lax.axis_size("dp") == 4 and rows % 16 == 0 and share % 128 == 0 and piece % 128 == 0 and rows <= min(share, piece):
        return shards_of_four(checkpoints, gain, w_in, w_out, cotangent)
    return shards_of_any(checkpoints, gain, w_in, w_out, cotangent)


def solution(mesh):
    in_specs = (
        P("section", None, None, "dp"),
        P("section", None),
        P("section", None, "dp"),
        P("section", "dp", None),
        P(None, None, "dp"),
    )
    out_specs = (
        P("section", None, "dp"),
        P("section", "dp", None),
        P("section", "dp"),
        P("section", None, None, "dp"),
    )
    return jax.shard_map(shards, mesh=mesh, in_specs=in_specs, out_specs=out_specs, check_vma=False)
```

```python
import functools

import jax
import jax.numpy as jnp
from jax import lax
from jax.experimental import pallas as pl
from jax.experimental.pallas import tpu as pltpu
from jax.sharding import PartitionSpec as P

F32 = jnp.float32
BF16 = jnp.bfloat16


def flip(block, axis, bits):
    count = lax.axis_size(axis)
    return lax.ppermute(block, axis, [(i, i ^ bits) for i in range(count)])


def side_rows(values, width):
    lead = values.astype(BF16)
    trail = (values - lead.astype(F32)).astype(BF16)
    flat = jnp.concatenate([lead, trail])
    return jnp.pad(flat, (0, 16 * width - flat.shape[0])).reshape(16, width)


def side_values(rows, count):
    flat = rows.reshape(-1)
    return flat[:count].astype(F32) + flat[count:2 * count].astype(F32)


def gelu_tanh(value):
    return jax.nn.gelu(value, approximate=True)


def shards_of_any(checkpoints, gain, w_in, w_out, cotangent):
    sections = lax.axis_size("section")
    n_dp = lax.axis_size("dp")
    here = lax.axis_index("section")
    lane = lax.axis_index("dp")
    layers = sections // 4
    mine = here % 4
    last = here // 4 == layers - 1
    _, micro, tok, share = checkpoints.shape
    rows = micro * tok
    quarter = share * n_dp
    width = 4 * quarter
    gain_row = gain[0]
    weight_in = w_in[0]
    weight_out = w_out[0]
    hidden = weight_in.shape[1]
    piece = hidden // 4
    core = lane % 2

    def gather_dp(block):
        bit = n_dp // 2
        parts = {0: block}
        while bit >= 1:
            other = flip(jnp.concatenate([parts[j] for j in parts], axis=1), "dp", bit)
            for at, j in enumerate(list(parts)):
                parts[j ^ bit] = other[:, at * block.shape[1]:(at + 1) * block.shape[1]]
            bit //= 2
        full = jnp.zeros((rows, quarter), block.dtype)
        for j, part in parts.items():
            full = lax.dynamic_update_slice(full, part, (0, (lane ^ j) * block.shape[1]))
        return full

    def cot_quarter(block):
        if n_dp < 4:
            whole = lax.all_gather(block, "dp", axis=1, tiled=True)
            return lax.dynamic_slice_in_dim(whole, mine * quarter, quarter, 1)
        per = n_dp // 4
        top = [s * n_dp + d for s in range(sections) for d in range(n_dp) if s // 4 == layers - 1]
        held = block
        far = lambda i, b: (i % n_dp // per ^ i // n_dp % 4) & b
        got = lax.ppermute(held, ("section", "dp"), [(i, i ^ 2 * per) for i in top if far(i, 3) == 0])
        held = jnp.where((lane // per ^ mine) & 2 == 0, held, got)
        got = lax.ppermute(held, ("section", "dp"), [(i, i ^ per) for i in top if far(i, 1) == 0])
        held = jnp.where((lane // per ^ mine) & 1 == 0, held, got)
        if per == 1:
            return held
        parts = {0: held}
        bit = per // 2
        while bit >= 1:
            for j in list(parts):
                parts[j ^ bit] = flip(parts[j], "dp", bit)
            bit //= 2
        full = jnp.zeros((rows, quarter), block.dtype)
        for j, part in parts.items():
            full = lax.dynamic_update_slice(full, part, (0, (lane % per ^ j) * block.shape[1]))
        return full

    def cut(values, j):
        return lax.dynamic_slice_in_dim(values, (mine ^ j) * piece, piece, 1)

    def fill(parts):
        full = jnp.zeros((rows, hidden), parts[0].dtype)
        for j, part in enumerate(parts):
            full = lax.dynamic_update_slice(full, part, (0, (mine ^ j) * piece))
        return full

    x_full = gather_dp(checkpoints[0].reshape(rows, share))
    cot = cot_quarter(cotangent.reshape(rows, cotangent.shape[2]))
    x_wide = x_full.astype(F32)
    scaled_raw = (x_wide * gain_row).astype(BF16)
    squares = jnp.sum(x_wide * x_wide, axis=1)

    act_raw = jnp.dot(scaled_raw, weight_in, preferred_element_type=F32)
    extra = side_rows(squares, piece)
    act = cut(act_raw, 0)
    for j in (3, 1, 2):
        got = flip(jnp.concatenate([cut(act_raw, j).astype(BF16), extra], axis=0), "section", j)
        act = act + got[:rows].astype(F32)
        squares = squares + side_values(got[rows:], rows)
    scale = lax.rsqrt(squares / width + 1e-06)[:, None]
    act = act * scale
    hid, pull = jax.vjp(gelu_tanh, act)
    hid = hid.astype(BF16)
    hid_full = fill([hid] + [flip(hid, "section", j) for j in (1, 2, 3)])
    normed = x_wide * scale
    scaled = (normed * gain_row).astype(BF16)

    def halves(values, side):
        pairs = values.reshape(rows, n_dp // 2, 2, share)
        return jnp.where(side == 0, pairs[:, :, 0], pairs[:, :, 1]).reshape(rows, quarter // 2)

    def own(values):
        return lax.dynamic_slice_in_dim(values, lane // 2 * share, share, 1)

    incoming = jnp.zeros((rows, quarter), BF16)
    normed_half = halves(normed, core)
    gain_half = halves(jnp.broadcast_to(gain_row, (rows, quarter)), core)
    for phase in range(layers):
        final = phase == layers - 1
        dy = jnp.where(last, cot, incoming) if phase > 0 else cot
        dhid_raw = jnp.dot(dy, weight_out.T, preferred_element_type=F32)
        dhid = cut(dhid_raw, 0)
        for j in (3, 1, 2):
            dhid = dhid + flip(cut(dhid_raw, j).astype(BF16), "section", j).astype(F32)
        dact = pull(dhid)[0].astype(BF16)
        inner = jnp.sum(dact.astype(F32) * act, axis=1)
        payload = jnp.concatenate([dact, side_rows(inner, piece)], axis=0)
        others = [flip(payload, "section", j) for j in (1, 2, 3)]
        for got in others:
            inner = inner + side_values(got[rows:], rows)
        dact_full = fill([dact] + [got[:rows] for got in others])
        part = jnp.dot(dact_full, weight_in.T, preferred_element_type=F32).astype(BF16)

        send = jnp.concatenate([halves(part, 1 - core), side_rows(inner, quarter // 2)], axis=0)
        got = flip(send, "dp", 1)
        dscaled = halves(part, core).astype(F32) + got[:rows].astype(F32)
        inner = inner + side_values(got[rows:], rows)
        bit = 2
        while bit < n_dp:
            send = jnp.concatenate([dscaled.astype(BF16), side_rows(inner, quarter // 2)], axis=0)
            got = flip(send, "dp", bit)
            dscaled = dscaled + got[:rows].astype(F32)
            inner = inner + side_values(got[rows:], rows)
            bit *= 2
        dnorm = dscaled * gain_half
        dy_half = halves(dy, core).astype(F32)
        grad_x = (dy_half + scale * (dnorm - normed_half * (inner / width)[:, None])).astype(BF16)
        if not final:
            down = lax.ppermute(grad_x, "section", [(i, i - 4) for i in range(4, sections)])
            other = flip(down, "dp", 1)
            pairs = jnp.where(
                core == 0,
                jnp.stack([down.reshape(rows, n_dp // 2, share), other.reshape(rows, n_dp // 2, share)], axis=2),
                jnp.stack([other.reshape(rows, n_dp // 2, share), down.reshape(rows, n_dp // 2, share)], axis=2),
            )
            incoming = pairs.reshape(rows, quarter)

    grad_out = jnp.dot(hid_full.T, dy, preferred_element_type=F32).astype(BF16)
    grad_in = jnp.dot(scaled.T, dact_full, preferred_element_type=F32).astype(BF16)
    grad_gain = jnp.sum(own(dscaled) * own(normed_half), axis=0)
    return (
        grad_in[None],
        grad_out[None],
        grad_gain[None],
        own(grad_x).reshape(1, micro, tok, share),
    )


SIDE = 16
GELU_IN = 0.7978845608028654
GELU_CUBE = 0.044715


def resident(shape, dtype):
    return pltpu.VMEM(shape, dtype)


def local(body, outs, *args, scratch=(), flops=0):
    spec = pl.BlockSpec(memory_space=pltpu.VMEM)
    moved = sum(a.size * a.dtype.itemsize for a in args)
    return pl.pallas_call(
        body,
        out_shape=tuple(outs),
        in_specs=[spec] * len(args),
        out_specs=tuple(spec for _ in outs),
        scratch_shapes=list(scratch),
        compiler_params=pltpu.CompilerParams(vmem_limit_bytes=16 * 1024 * 1024),
        cost_estimate=pl.CostEstimate(flops=flops, bytes_accessed=moved, transcendentals=0),
    )(*args)


def diagonal(rows, width):
    return lax.broadcasted_iota(jnp.int32, (rows, width), 0) == lax.broadcasted_iota(jnp.int32, (rows, width), 1)


def as_row(column, width):
    rows = column.shape[0]
    return jnp.sum(jnp.where(diagonal(rows, width), column, 0.0), axis=0, keepdims=True)


def as_column(row, rows):
    return jnp.sum(jnp.where(diagonal(rows, row.shape[1]), row, 0.0), axis=1, keepdims=True)


def side_block(row):
    lead = row.astype(BF16).astype(F32)
    at = lax.broadcasted_iota(jnp.int32, (SIDE, row.shape[1]), 0)
    return jnp.where(at == 0, lead, jnp.where(at == 1, row - lead, 0.0)).astype(BF16)


def side_row(block):
    wide = block.astype(F32)
    return wide[0:1] + wide[1:2]


def load_kernel(*refs):
    count = len(refs) // 2
    copies = [pltpu.make_async_copy(refs[i], refs[count + i], refs[-1].at[i]) for i in range(count)]
    for copy in copies:
        copy.start()
    for copy in copies:
        copy.wait()


def load(*arrays):
    return pl.pallas_call(
        load_kernel,
        out_shape=tuple(resident(a.shape, a.dtype) for a in arrays),
        in_specs=[pl.BlockSpec(memory_space=pl.ANY)] * len(arrays),
        out_specs=tuple(pl.BlockSpec(memory_space=pltpu.VMEM) for _ in arrays),
        scratch_shapes=[pltpu.SemaphoreType.DMA((len(arrays),))],
        compiler_params=pltpu.CompilerParams(vmem_limit_bytes=1024 * 1024),
        cost_estimate=pl.CostEstimate(flops=0, bytes_accessed=sum(2 * a.size * a.dtype.itemsize for a in arrays), transcendentals=0),
    )(*(pltpu.with_memory_space_constraint(a, pltpu.HBM) for a in arrays))


def place():
    return lax.axis_index("section") % 4, lax.axis_index("dp")


def dot_nt(left, right):
    return lax.dot_general(left, right, (((1,), (1,)), ((), ())), preferred_element_type=F32)


def dot_tn(left, right):
    return lax.dot_general(left, right, (((0,), (0,)), ((), ())), preferred_element_type=F32)


def slot(index, size):
    return pl.ds(pl.multiple_of(index * size, size), size)


def spread_in_kernel(x0, x1, x2, x3, gain, weight, own, s1, s2, s3, x_full, scaled):
    mine, lane = place()
    rows, share = x0.shape
    piece = own.shape[1]
    for d, part in enumerate((x0, x1, x2, x3)):
        x_full[:, slot(lane ^ d, share)] = part[...]
    wide = x_full[...].astype(F32)
    row = as_row(jnp.sum(wide * wide, axis=1, keepdims=True), piece)
    scaled[...] = (wide * gain[...]).astype(BF16)
    block = side_block(row)
    for d, out in ((3, s3), (2, s2), (1, s1)):
        out[:rows] = jnp.dot(scaled[...], weight[:, slot(mine ^ d, piece)], preferred_element_type=F32).astype(BF16)
        out[rows:] = block
    own[:rows] = jnp.dot(scaled[...], weight[:, slot(mine, piece)], preferred_element_type=F32)
    own[rows:] = jnp.broadcast_to(row, (SIDE, piece))


def spread_dy(dy, weight, mine, own, s1, s2, s3):
    piece = own.shape[1]
    for d, out in ((3, s3), (2, s2), (1, s1)):
        out[...] = dot_nt(dy[...], weight[slot(mine ^ d, piece), :]).astype(BF16)
    own[...] = dot_nt(dy[...], weight[slot(mine, piece), :])


def spread_first_kernel(c0, c1, c2, c3, weight, own, s1, s2, s3, dy):
    mine, lane = place()
    for d, part in enumerate((c0, c1, c2, c3)):
        @pl.when(lane ^ mine == d)
        def _(part=part):
            dy[...] = part[...]

    spread_dy(dy, weight, mine, own, s1, s2, s3)


def spread_next_kernel(layers, d0, d1, d2, d3, before, weight, own, s1, s2, s3, dy):
    mine, lane = place()
    share = d0.shape[1]
    last = lax.axis_index("section") // 4 == layers - 1

    @pl.when(last)
    def _():
        dy[...] = before[...]

    @pl.when(jnp.logical_not(last))
    def _():
        for d, part in enumerate((d0, d1, d2, d3)):
            dy[:, slot(lane ^ d, share)] = part[...]

    spread_dy(dy, weight, mine, own, s1, s2, s3)


def act_kernel(width, own, g1, g2, g3, act, slope, hid, scale):
    rows = act.shape[0]
    row = own[rows:rows + 1] + side_row(g1[rows:]) + side_row(g2[rows:]) + side_row(g3[rows:])
    r = lax.rsqrt(as_column(row, rows) / width + 1e-06)
    scale[...] = r
    a = (own[:rows] + g1[:rows].astype(F32) + g2[:rows].astype(F32) + g3[:rows].astype(F32)) * r
    act[...] = a
    square = a * a
    t = jnp.tanh(GELU_IN * (a + GELU_CUBE * (square * a)))
    half = 0.5 * (1.0 + t)
    hid[...] = (a * half).astype(BF16)
    slope[...] = half + 0.5 * a * (1.0 - t * t) * (GELU_IN * (1.0 + 3.0 * GELU_CUBE * square))


def dact_kernel(own, g1, g2, g3, act, slope, pay):
    rows, piece = own.shape
    dhid = own[...] + g1[...].astype(F32) + g2[...].astype(F32) + g3[...].astype(F32)
    da = (dhid * slope[...]).astype(BF16)
    pay[:rows] = da
    pay[rows:] = side_block(as_row(jnp.sum(da.astype(F32) * act[...], axis=1, keepdims=True), piece))


def back_kernel(p0, p1, p2, p3, weight, keep, send, full):
    mine, lane = place()
    rows = full.shape[0]
    piece = p0.shape[1]
    share = weight.shape[0] // 4
    row = side_row(p0[rows:]) + side_row(p1[rows:]) + side_row(p2[rows:]) + side_row(p3[rows:])
    for d, part in enumerate((p0, p1, p2, p3)):
        full[:, slot(mine ^ d, piece)] = part[:rows]
    for at, d in ((0, 1), (1, 3)):
        send[:rows, at * share:(at + 1) * share] = dot_nt(full[...], weight[slot(lane ^ d, share), :]).astype(BF16)
    send[rows:] = side_block(row)
    for at, d in ((0, 0), (1, 2)):
        keep[:rows, at * share:(at + 1) * share] = dot_nt(full[...], weight[slot(lane ^ d, share), :])
    keep[rows:] = jnp.broadcast_to(row, (SIDE, keep.shape[1]))


def middle_kernel(keep, got, rest, send):
    rows = keep.shape[0] - SIDE
    share = rest.shape[1]
    row = (keep[rows:rows + 1] + side_row(got[rows:]))[:, :share]
    send[:rows] = (keep[:rows, share:] + got[:rows, share:].astype(F32)).astype(BF16)
    send[rows:] = side_block(row)
    rest[:rows] = keep[:rows, :share] + got[:rows, :share].astype(F32)
    rest[rows:] = jnp.broadcast_to(row, (SIDE, share))


def finish_kernel(width, rest, got, x_own, dy, gain, scale, grad_x, *grad_gain):
    _, lane = place()
    rows, share = x_own.shape
    at = slot(lane, share)
    r = scale[...]
    du = rest[:rows] + got[:rows].astype(F32)
    normed = x_own[...].astype(F32) * r
    inner = as_column(rest[rows:rows + 1] + side_row(got[rows:]), rows) / width
    dnorm = du * gain[:, at]
    grad_x[...] = (dy[:, at].astype(F32) + r * (dnorm - normed * inner)).astype(BF16)
    if grad_gain:
        grad_gain[0][...] = jnp.sum(du * normed, axis=0, keepdims=True)


def grad_out_kernel(h0, h1, h2, h3, dy, out, held, sems):
    mine, _ = place()
    piece = h0.shape[1]
    copies = []
    for d, part in enumerate((h0, h1, h2, h3)):
        held[d] = dot_tn(part[...], dy[...]).astype(BF16)
        copies.append(pltpu.make_async_copy(held.at[d], out.at[slot(mine ^ d, piece), :], sems.at[d]))
        copies[-1].start()
    for copy in copies:
        copy.wait()


def grad_in_kernel(p0, p1, p2, p3, x_full, gain, scale, out, scaled, held, sems):
    mine, _ = place()
    rows = x_full.shape[0]
    piece = p0.shape[1]
    scaled[...] = (x_full[...].astype(F32) * scale[...] * gain[...]).astype(BF16)
    copies = []
    for d, part in enumerate((p0, p1, p2, p3)):
        held[d] = dot_tn(scaled[...], part[:rows]).astype(BF16)
        copies.append(pltpu.make_async_copy(held.at[d], out.at[:, slot(mine ^ d, piece)], sems.at[d]))
        copies[-1].start()
    for copy in copies:
        copy.wait()


def gradient(body, shape, block, *args, scratch=(), flops=0):
    return pl.pallas_call(
        body,
        out_shape=jax.ShapeDtypeStruct(shape, BF16),
        in_specs=[pl.BlockSpec(memory_space=pltpu.VMEM)] * len(args),
        out_specs=pl.BlockSpec(memory_space=pl.ANY),
        scratch_shapes=[*scratch, pltpu.VMEM((4,) + block, BF16), pltpu.SemaphoreType.DMA((4,))],
        compiler_params=pltpu.CompilerParams(vmem_limit_bytes=16 * 1024 * 1024),
        cost_estimate=pl.CostEstimate(flops=flops, bytes_accessed=2 * shape[0] * shape[1], transcendentals=0),
    )(*args)


def shards_of_four(checkpoints, gain, w_in, w_out, cotangent):
    sections = lax.axis_size("section")
    here = lax.axis_index("section")
    lane = lax.axis_index("dp")
    layers = sections // 4
    mine = here % 4
    _, micro, tok, share = checkpoints.shape
    rows = micro * tok
    quarter = share * 4
    width = 4 * quarter
    hidden = w_in.shape[2]
    piece = hidden // 4
    work = 2 * rows * quarter * hidden

    x0 = checkpoints[0].reshape(rows, share)
    cot = cotangent.reshape(rows, quarter)
    top = [s * 4 + d for s in range(sections) for d in range(4) if s // 4 == layers - 1]
    x2 = flip(x0, "dp", 2)
    x1 = flip(x0, "dp", 1)
    weight_in, x0, gain = load(w_in[0], x0, gain)
    x2, x1, cot, weight_in = lax.optimization_barrier((x2, x1, cot, weight_in))
    c2 = lax.ppermute(cot, ("section", "dp"), [(i, i ^ 2) for i in top if i % 4 == i // 4 % 4])
    c3 = lax.ppermute(cot, ("section", "dp"), [(i ^ 8, i ^ 3) for i in top if i % 4 == i // 4 % 4])
    x3 = flip(x2, "dp", 1)

    wide = (rows + SIDE, piece)
    own, s1, s2, s3, x_full = local(
        spread_in_kernel,
        [resident(wide, F32)] + [resident(wide, BF16)] * 3 + [resident((rows, quarter), BF16)],
        x0, x1, x2, x3, gain, weight_in,
        scratch=[pltpu.VMEM((rows, quarter), BF16)], flops=work,
    )
    s1, s2, s3, cot, w_out = lax.optimization_barrier((s1, s2, s3, cot, w_out))
    g3 = flip(s3, "section", 3)
    g2 = flip(s2, "section", 2)
    g1 = flip(s1, "section", 1)
    c1 = lax.ppermute(cot, ("section", "dp"), [(i, i ^ 1) for i in top if i % 4 == i // 4 % 4])
    weight_out, c0 = load(w_out[0], cot)
    act, slope, hid, scale = local(
        functools.partial(act_kernel, width),
        [resident((rows, piece), F32), resident((rows, piece), F32), resident((rows, piece), BF16), resident((rows, 1), F32)],
        own, g1, g2, g3,
    )

    spread_outs = [resident((rows, piece), F32)] + [resident((rows, piece), BF16)] * 3 + [resident((rows, quarter), BF16)]

    def gather_hidden(block):
        return [block] + [flip(block, "section", j) for j in (1, 2, 3)]

    if layers == 1:
        hids = gather_hidden(hid)
    for phase in range(layers):
        final = phase == layers - 1
        if phase == 0:
            own, s1, s2, s3, dy = local(spread_first_kernel, spread_outs, c0, c1, c2, c3, weight_out, flops=work)
        else:
            down, hids = lax.optimization_barrier((down, hids))
            own, s1, s2, s3, dy = local(
                functools.partial(spread_next_kernel, layers), spread_outs, *down, dy, weight_out, flops=work
            )
        g3 = flip(s3, "section", 3)
        g2 = flip(s2, "section", 2)
        g1 = flip(s1, "section", 1)
        if final:
            grad_out = gradient(grad_out_kernel, (hidden, quarter), (piece, quarter), *hids, dy, flops=work)
            own, grad_out = lax.optimization_barrier((own, grad_out))
        (pay,) = local(dact_kernel, [resident(wide, BF16)], own, g1, g2, g3, act, slope)
        p3 = flip(pay, "section", 3)
        p2 = flip(pay, "section", 2)
        p1 = flip(pay, "section", 1)
        keep, send = local(
            back_kernel,
            [resident((rows + SIDE, 2 * share), F32), resident((rows + SIDE, 2 * share), BF16)],
            pay, p1, p2, p3, weight_in,
            scratch=[pltpu.VMEM((rows, hidden), BF16)], flops=work,
        )
        got = flip(send, "dp", 1)
        rest, send = local(
            middle_kernel,
            [resident((rows + SIDE, share), F32), resident((rows + SIDE, share), BF16)],
            keep, got,
        )
        if phase == 0 and not final:
            send, hid = lax.optimization_barrier((send, hid))
            hids = gather_hidden(hid)
        got = flip(send, "dp", 2)
        if final:
            grad_in = gradient(
                grad_in_kernel, (quarter, hidden), (quarter, piece), pay, p1, p2, p3, x_full, gain, scale,
                scratch=[pltpu.VMEM((rows, quarter), BF16)], flops=work,
            )
            got, grad_in = lax.optimization_barrier((got, grad_in))
        outs = [resident((rows, share), BF16)]
        if final:
            outs = [jax.ShapeDtypeStruct((rows, share), BF16), jax.ShapeDtypeStruct((1, share), F32)]
        finished = local(functools.partial(finish_kernel, width), outs, rest, got, x0, dy, gain, scale)
        if not final:
            d0 = lax.ppermute(finished[0], "section", [(i, i - 4) for i in range(4, sections)])
            d2 = flip(d0, "dp", 2)
            d1 = flip(d0, "dp", 1)
            d3 = flip(d2, "dp", 1)
            down = (d0, d1, d2, d3)

    grad_x, grad_gain = finished
    return grad_in[None], grad_out[None], grad_gain, grad_x.reshape(1, micro, tok, share)


def shards(checkpoints, gain, w_in, w_out, cotangent):
    rows = checkpoints.shape[1] * checkpoints.shape[2]
    share = checkpoints.shape[3]
    piece = w_in.shape[2] // 4
    if lax.axis_size("dp") == 4 and rows % 16 == 0 and share % 128 == 0 and piece % 128 == 0 and rows <= min(share, piece):
        return shards_of_four(checkpoints, gain, w_in, w_out, cotangent)
    return shards_of_any(checkpoints, gain, w_in, w_out, cotangent)


def solution(mesh):
    in_specs = (
        P("section", None, None, "dp"),
        P("section", None),
        P("section", None, "dp"),
        P("section", "dp", None),
        P(None, None, "dp"),
    )
    out_specs = (
        P("section", None, "dp"),
        P("section", "dp", None),
        P("section", "dp"),
        P("section", None, None, "dp"),
    )
    return jax.shard_map(shards, mesh=mesh, in_specs=in_specs, out_specs=out_specs, check_vma=False)
```

```python
import functools

import jax
import jax.numpy as jnp
from jax import lax
from jax.experimental import pallas as pl
from jax.experimental.pallas import tpu as pltpu
from jax.sharding import PartitionSpec as P

F32 = jnp.float32
BF16 = jnp.bfloat16


def flip(block, axis, bits):
    count = lax.axis_size(axis)
    return lax.ppermute(block, axis, [(i, i ^ bits) for i in range(count)])


def side_rows(values, width):
    lead = values.astype(BF16)
    trail = (values - lead.astype(F32)).astype(BF16)
    flat = jnp.concatenate([lead, trail])
    return jnp.pad(flat, (0, 16 * width - flat.shape[0])).reshape(16, width)


def side_values(rows, count):
    flat = rows.reshape(-1)
    return flat[:count].astype(F32) + flat[count:2 * count].astype(F32)


def gelu_tanh(value):
    return jax.nn.gelu(value, approximate=True)


def shards_of_any(checkpoints, gain, w_in, w_out, cotangent):
    sections = lax.axis_size("section")
    n_dp = lax.axis_size("dp")
    here = lax.axis_index("section")
    lane = lax.axis_index("dp")
    layers = sections // 4
    mine = here % 4
    last = here // 4 == layers - 1
    _, micro, tok, share = checkpoints.shape
    rows = micro * tok
    quarter = share * n_dp
    width = 4 * quarter
    gain_row = gain[0]
    weight_in = w_in[0]
    weight_out = w_out[0]
    hidden = weight_in.shape[1]
    piece = hidden // 4
    core = lane % 2

    def gather_dp(block):
        bit = n_dp // 2
        parts = {0: block}
        while bit >= 1:
            other = flip(jnp.concatenate([parts[j] for j in parts], axis=1), "dp", bit)
            for at, j in enumerate(list(parts)):
                parts[j ^ bit] = other[:, at * block.shape[1]:(at + 1) * block.shape[1]]
            bit //= 2
        full = jnp.zeros((rows, quarter), block.dtype)
        for j, part in parts.items():
            full = lax.dynamic_update_slice(full, part, (0, (lane ^ j) * block.shape[1]))
        return full

    def cot_quarter(block):
        if n_dp < 4:
            whole = lax.all_gather(block, "dp", axis=1, tiled=True)
            return lax.dynamic_slice_in_dim(whole, mine * quarter, quarter, 1)
        per = n_dp // 4
        top = [s * n_dp + d for s in range(sections) for d in range(n_dp) if s // 4 == layers - 1]
        held = block
        far = lambda i, b: (i % n_dp // per ^ i // n_dp % 4) & b
        got = lax.ppermute(held, ("section", "dp"), [(i, i ^ 2 * per) for i in top if far(i, 3) == 0])
        held = jnp.where((lane // per ^ mine) & 2 == 0, held, got)
        got = lax.ppermute(held, ("section", "dp"), [(i, i ^ per) for i in top if far(i, 1) == 0])
        held = jnp.where((lane // per ^ mine) & 1 == 0, held, got)
        if per == 1:
            return held
        parts = {0: held}
        bit = per // 2
        while bit >= 1:
            for j in list(parts):
                parts[j ^ bit] = flip(parts[j], "dp", bit)
            bit //= 2
        full = jnp.zeros((rows, quarter), block.dtype)
        for j, part in parts.items():
            full = lax.dynamic_update_slice(full, part, (0, (lane % per ^ j) * block.shape[1]))
        return full

    def cut(values, j):
        return lax.dynamic_slice_in_dim(values, (mine ^ j) * piece, piece, 1)

    def fill(parts):
        full = jnp.zeros((rows, hidden), parts[0].dtype)
        for j, part in enumerate(parts):
            full = lax.dynamic_update_slice(full, part, (0, (mine ^ j) * piece))
        return full

    x_full = gather_dp(checkpoints[0].reshape(rows, share))
    cot = cot_quarter(cotangent.reshape(rows, cotangent.shape[2]))
    x_wide = x_full.astype(F32)
    scaled_raw = (x_wide * gain_row).astype(BF16)
    squares = jnp.sum(x_wide * x_wide, axis=1)

    act_raw = jnp.dot(scaled_raw, weight_in, preferred_element_type=F32)
    extra = side_rows(squares, piece)
    act = cut(act_raw, 0)
    for j in (3, 1, 2):
        got = flip(jnp.concatenate([cut(act_raw, j).astype(BF16), extra], axis=0), "section", j)
        act = act + got[:rows].astype(F32)
        squares = squares + side_values(got[rows:], rows)
    scale = lax.rsqrt(squares / width + 1e-06)[:, None]
    act = act * scale
    hid, pull = jax.vjp(gelu_tanh, act)
    hid = hid.astype(BF16)
    hid_full = fill([hid] + [flip(hid, "section", j) for j in (1, 2, 3)])
    normed = x_wide * scale
    scaled = (normed * gain_row).astype(BF16)

    def halves(values, side):
        pairs = values.reshape(rows, n_dp // 2, 2, share)
        return jnp.where(side == 0, pairs[:, :, 0], pairs[:, :, 1]).reshape(rows, quarter // 2)

    def own(values):
        return lax.dynamic_slice_in_dim(values, lane // 2 * share, share, 1)

    incoming = jnp.zeros((rows, quarter), BF16)
    normed_half = halves(normed, core)
    gain_half = halves(jnp.broadcast_to(gain_row, (rows, quarter)), core)
    for phase in range(layers):
        final = phase == layers - 1
        dy = jnp.where(last, cot, incoming) if phase > 0 else cot
        dhid_raw = jnp.dot(dy, weight_out.T, preferred_element_type=F32)
        dhid = cut(dhid_raw, 0)
        for j in (3, 1, 2):
            dhid = dhid + flip(cut(dhid_raw, j).astype(BF16), "section", j).astype(F32)
        dact = pull(dhid)[0].astype(BF16)
        inner = jnp.sum(dact.astype(F32) * act, axis=1)
        payload = jnp.concatenate([dact, side_rows(inner, piece)], axis=0)
        others = [flip(payload, "section", j) for j in (1, 2, 3)]
        for got in others:
            inner = inner + side_values(got[rows:], rows)
        dact_full = fill([dact] + [got[:rows] for got in others])
        part = jnp.dot(dact_full, weight_in.T, preferred_element_type=F32).astype(BF16)

        send = jnp.concatenate([halves(part, 1 - core), side_rows(inner, quarter // 2)], axis=0)
        got = flip(send, "dp", 1)
        dscaled = halves(part, core).astype(F32) + got[:rows].astype(F32)
        inner = inner + side_values(got[rows:], rows)
        bit = 2
        while bit < n_dp:
            send = jnp.concatenate([dscaled.astype(BF16), side_rows(inner, quarter // 2)], axis=0)
            got = flip(send, "dp", bit)
            dscaled = dscaled + got[:rows].astype(F32)
            inner = inner + side_values(got[rows:], rows)
            bit *= 2
        dnorm = dscaled * gain_half
        dy_half = halves(dy, core).astype(F32)
        grad_x = (dy_half + scale * (dnorm - normed_half * (inner / width)[:, None])).astype(BF16)
        if not final:
            down = lax.ppermute(grad_x, "section", [(i, i - 4) for i in range(4, sections)])
            other = flip(down, "dp", 1)
            pairs = jnp.where(
                core == 0,
                jnp.stack([down.reshape(rows, n_dp // 2, share), other.reshape(rows, n_dp // 2, share)], axis=2),
                jnp.stack([other.reshape(rows, n_dp // 2, share), down.reshape(rows, n_dp // 2, share)], axis=2),
            )
            incoming = pairs.reshape(rows, quarter)

    grad_out = jnp.dot(hid_full.T, dy, preferred_element_type=F32).astype(BF16)
    grad_in = jnp.dot(scaled.T, dact_full, preferred_element_type=F32).astype(BF16)
    grad_gain = jnp.sum(own(dscaled) * own(normed_half), axis=0)
    return (
        grad_in[None],
        grad_out[None],
        grad_gain[None],
        own(grad_x).reshape(1, micro, tok, share),
    )


SIDE = 16
GELU_IN = 0.7978845608028654
GELU_CUBE = 0.044715


def resident(shape, dtype):
    return pltpu.VMEM(shape, dtype)


def local(body, outs, *args, scratch=(), flops=0):
    spec = pl.BlockSpec(memory_space=pltpu.VMEM)
    moved = sum(a.size * a.dtype.itemsize for a in args)
    return pl.pallas_call(
        body,
        out_shape=tuple(outs),
        in_specs=[spec] * len(args),
        out_specs=tuple(spec for _ in outs),
        scratch_shapes=list(scratch),
        compiler_params=pltpu.CompilerParams(vmem_limit_bytes=16 * 1024 * 1024),
        cost_estimate=pl.CostEstimate(flops=flops, bytes_accessed=moved, transcendentals=0),
    )(*args)


def diagonal(rows, width):
    return lax.broadcasted_iota(jnp.int32, (rows, width), 0) == lax.broadcasted_iota(jnp.int32, (rows, width), 1)


def as_row(column, width):
    rows = column.shape[0]
    return jnp.sum(jnp.where(diagonal(rows, width), column, 0.0), axis=0, keepdims=True)


def as_column(row, rows):
    return jnp.sum(jnp.where(diagonal(rows, row.shape[1]), row, 0.0), axis=1, keepdims=True)


def side_block(row):
    lead = row.astype(BF16).astype(F32)
    at = lax.broadcasted_iota(jnp.int32, (SIDE, row.shape[1]), 0)
    return jnp.where(at == 0, lead, jnp.where(at == 1, row - lead, 0.0)).astype(BF16)


def side_row(block):
    wide = block.astype(F32)
    return wide[0:1] + wide[1:2]


def load_kernel(*refs):
    count = len(refs) // 2
    copies = [pltpu.make_async_copy(refs[i], refs[count + i], refs[-1].at[i]) for i in range(count)]
    for copy in copies:
        copy.start()
    for copy in copies:
        copy.wait()


def load(*arrays):
    return pl.pallas_call(
        load_kernel,
        out_shape=tuple(resident(a.shape, a.dtype) for a in arrays),
        in_specs=[pl.BlockSpec(memory_space=pl.ANY)] * len(arrays),
        out_specs=tuple(pl.BlockSpec(memory_space=pltpu.VMEM) for _ in arrays),
        scratch_shapes=[pltpu.SemaphoreType.DMA((len(arrays),))],
        compiler_params=pltpu.CompilerParams(vmem_limit_bytes=1024 * 1024),
        cost_estimate=pl.CostEstimate(flops=0, bytes_accessed=sum(2 * a.size * a.dtype.itemsize for a in arrays), transcendentals=0),
    )(*(pltpu.with_memory_space_constraint(a, pltpu.HBM) for a in arrays))


def place():
    return lax.axis_index("section") % 4, lax.axis_index("dp")


def dot_nt(left, right):
    return lax.dot_general(left, right, (((1,), (1,)), ((), ())), preferred_element_type=F32)


def dot_tn(left, right):
    return lax.dot_general(left, right, (((0,), (0,)), ((), ())), preferred_element_type=F32)


def slot(index, size):
    return pl.ds(pl.multiple_of(index * size, size), size)


def spread_in_kernel(x0, x1, x2, x3, gain, weight, own, s1, s2, s3, x_full, scaled):
    mine, lane = place()
    rows, share = x0.shape
    piece = own.shape[1]
    for d, part in enumerate((x0, x1, x2, x3)):
        x_full[:, slot(lane ^ d, share)] = part[...]
    wide = x_full[...].astype(F32)
    row = as_row(jnp.sum(wide * wide, axis=1, keepdims=True), piece)
    scaled[...] = (wide * gain[...]).astype(BF16)
    block = side_block(row)
    for d, out in ((3, s3), (2, s2), (1, s1)):
        out[:rows] = jnp.dot(scaled[...], weight[:, slot(mine ^ d, piece)], preferred_element_type=F32).astype(BF16)
        out[rows:] = block
    own[:rows] = jnp.dot(scaled[...], weight[:, slot(mine, piece)], preferred_element_type=F32)
    own[rows:] = jnp.broadcast_to(row, (SIDE, piece))


def spread_dy(dy, weight, mine, own, s1, s2, s3):
    piece = own.shape[1]
    for d, out in ((3, s3), (2, s2), (1, s1)):
        out[...] = dot_nt(dy[...], weight[slot(mine ^ d, piece), :]).astype(BF16)
    own[...] = dot_nt(dy[...], weight[slot(mine, piece), :])


def spread_first_kernel(cot, sent, weight, own, s1, s2, s3, dy):
    mine, lane = place()

    @pl.when(lane == mine)
    def _():
        dy[...] = cot[...]

    @pl.when(lane != mine)
    def _():
        dy[...] = sent[...]

    spread_dy(dy, weight, mine, own, s1, s2, s3)


def spread_next_kernel(layers, d0, d1, d2, d3, before, weight, own, s1, s2, s3, dy):
    mine, lane = place()
    share = d0.shape[1]
    last = lax.axis_index("section") // 4 == layers - 1

    @pl.when(last)
    def _():
        dy[...] = before[...]

    @pl.when(jnp.logical_not(last))
    def _():
        for d, part in enumerate((d0, d1, d2, d3)):
            dy[:, slot(lane ^ d, share)] = part[...]

    spread_dy(dy, weight, mine, own, s1, s2, s3)


def act_kernel(width, own, g1, g2, g3, act, slope, hid, scale):
    rows = act.shape[0]
    row = own[rows:rows + 1] + side_row(g1[rows:]) + side_row(g2[rows:]) + side_row(g3[rows:])
    r = lax.rsqrt(as_column(row, rows) / width + 1e-06)
    scale[...] = r
    a = (own[:rows] + g1[:rows].astype(F32) + g2[:rows].astype(F32) + g3[:rows].astype(F32)) * r
    act[...] = a
    square = a * a
    t = jnp.tanh(GELU_IN * (a + GELU_CUBE * (square * a)))
    half = 0.5 * (1.0 + t)
    hid[...] = (a * half).astype(BF16)
    slope[...] = half + 0.5 * a * (1.0 - t * t) * (GELU_IN * (1.0 + 3.0 * GELU_CUBE * square))


def dact_kernel(own, g1, g2, g3, act, slope, pay):
    rows, piece = own.shape
    dhid = own[...] + g1[...].astype(F32) + g2[...].astype(F32) + g3[...].astype(F32)
    da = (dhid * slope[...]).astype(BF16)
    pay[:rows] = da
    pay[rows:] = side_block(as_row(jnp.sum(da.astype(F32) * act[...], axis=1, keepdims=True), piece))


def back_kernel(p0, p1, p2, p3, weight, keep, send, full):
    mine, lane = place()
    rows = full.shape[0]
    piece = p0.shape[1]
    share = weight.shape[0] // 4
    row = side_row(p0[rows:]) + side_row(p1[rows:]) + side_row(p2[rows:]) + side_row(p3[rows:])
    for d, part in enumerate((p0, p1, p2, p3)):
        full[:, slot(mine ^ d, piece)] = part[:rows]
    for at, d in ((0, 1), (1, 3)):
        send[:rows, at * share:(at + 1) * share] = dot_nt(full[...], weight[slot(lane ^ d, share), :]).astype(BF16)
    send[rows:] = side_block(row)
    for at, d in ((0, 0), (1, 2)):
        keep[:rows, at * share:(at + 1) * share] = dot_nt(full[...], weight[slot(lane ^ d, share), :])
    keep[rows:] = jnp.broadcast_to(row, (SIDE, keep.shape[1]))


def middle_kernel(keep, got, rest, send):
    rows = keep.shape[0] - SIDE
    share = rest.shape[1]
    row = (keep[rows:rows + 1] + side_row(got[rows:]))[:, :share]
    send[:rows] = (keep[:rows, share:] + got[:rows, share:].astype(F32)).astype(BF16)
    send[rows:] = side_block(row)
    rest[:rows] = keep[:rows, :share] + got[:rows, :share].astype(F32)
    rest[rows:] = jnp.broadcast_to(row, (SIDE, share))


def finish_kernel(width, rest, got, x_own, dy, gain, scale, grad_x, *grad_gain):
    _, lane = place()
    rows, share = x_own.shape
    at = slot(lane, share)
    r = scale[...]
    du = rest[:rows] + got[:rows].astype(F32)
    normed = x_own[...].astype(F32) * r
    inner = as_column(rest[rows:rows + 1] + side_row(got[rows:]), rows) / width
    dnorm = du * gain[:, at]
    grad_x[...] = (dy[:, at].astype(F32) + r * (dnorm - normed * inner)).astype(BF16)
    if grad_gain:
        grad_gain[0][...] = jnp.sum(du * normed, axis=0, keepdims=True)


def grad_out_kernel(h0, h1, h2, h3, dy, out, held, sems):
    mine, _ = place()
    piece = h0.shape[1]
    copies = []
    for d, part in enumerate((h0, h1, h2, h3)):
        held[d] = dot_tn(part[...], dy[...]).astype(BF16)
        copies.append(pltpu.make_async_copy(held.at[d], out.at[slot(mine ^ d, piece), :], sems.at[d]))
        copies[-1].start()
    for copy in copies:
        copy.wait()


def grad_in_kernel(p0, p1, p2, p3, x_full, gain, scale, out, scaled, held, sems):
    mine, _ = place()
    rows = x_full.shape[0]
    piece = p0.shape[1]
    scaled[...] = (x_full[...].astype(F32) * scale[...] * gain[...]).astype(BF16)
    copies = []
    for d, part in enumerate((p0, p1, p2, p3)):
        held[d] = dot_tn(scaled[...], part[:rows]).astype(BF16)
        copies.append(pltpu.make_async_copy(held.at[d], out.at[:, slot(mine ^ d, piece)], sems.at[d]))
        copies[-1].start()
    for copy in copies:
        copy.wait()


def gradient(body, shape, block, *args, scratch=(), flops=0):
    return pl.pallas_call(
        body,
        out_shape=jax.ShapeDtypeStruct(shape, BF16),
        in_specs=[pl.BlockSpec(memory_space=pltpu.VMEM)] * len(args),
        out_specs=pl.BlockSpec(memory_space=pl.ANY),
        scratch_shapes=[*scratch, pltpu.VMEM((4,) + block, BF16), pltpu.SemaphoreType.DMA((4,))],
        compiler_params=pltpu.CompilerParams(vmem_limit_bytes=16 * 1024 * 1024),
        cost_estimate=pl.CostEstimate(flops=flops, bytes_accessed=2 * shape[0] * shape[1], transcendentals=0),
    )(*args)


def shards_of_four(checkpoints, gain, w_in, w_out, cotangent):
    sections = lax.axis_size("section")
    here = lax.axis_index("section")
    lane = lax.axis_index("dp")
    layers = sections // 4
    mine = here % 4
    _, micro, tok, share = checkpoints.shape
    rows = micro * tok
    quarter = share * 4
    width = 4 * quarter
    hidden = w_in.shape[2]
    piece = hidden // 4
    work = 2 * rows * quarter * hidden

    x0 = checkpoints[0].reshape(rows, share)
    cot = cotangent.reshape(rows, quarter)
    top = [s * 4 + d for s in range(sections) for d in range(4) if s // 4 == layers - 1]
    x2 = flip(x0, "dp", 2)
    x1 = flip(x0, "dp", 1)
    weight_in, x0, gain = load(w_in[0], x0, gain)
    x2, x1, cot, weight_in = lax.optimization_barrier((x2, x1, cot, weight_in))
    sent = lax.ppermute(cot, ("section", "dp"), [((i // 4 ^ near) * 4 + i // 4 % 4, i) for i in top for near in (1, 0, 2) if i // 4 % 4 ^ i % 4 == (2, 1, 3)[near]])
    x3 = flip(x2, "dp", 1)

    wide = (rows + SIDE, piece)
    own, s1, s2, s3, x_full = local(
        spread_in_kernel,
        [resident(wide, F32)] + [resident(wide, BF16)] * 3 + [resident((rows, quarter), BF16)],
        x0, x1, x2, x3, gain, weight_in,
        scratch=[pltpu.VMEM((rows, quarter), BF16)], flops=work,
    )
    s1, s2, s3, cot, w_out = lax.optimization_barrier((s1, s2, s3, cot, w_out))
    g3 = flip(s3, "section", 3)
    g2 = flip(s2, "section", 2)
    g1 = flip(s1, "section", 1)
    weight_out, cot = load(w_out[0], cot)
    act, slope, hid, scale = local(
        functools.partial(act_kernel, width),
        [resident((rows, piece), F32), resident((rows, piece), F32), resident((rows, piece), BF16), resident((rows, 1), F32)],
        own, g1, g2, g3,
    )

    spread_outs = [resident((rows, piece), F32)] + [resident((rows, piece), BF16)] * 3 + [resident((rows, quarter), BF16)]

    def gather_hidden(block):
        return [block] + [flip(block, "section", j) for j in (1, 2, 3)]

    if layers == 1:
        hids = gather_hidden(hid)
    for phase in range(layers):
        final = phase == layers - 1
        if phase == 0:
            own, s1, s2, s3, dy = local(spread_first_kernel, spread_outs, cot, sent, weight_out, flops=work)
        else:
            down, hids = lax.optimization_barrier((down, hids))
            own, s1, s2, s3, dy = local(
                functools.partial(spread_next_kernel, layers), spread_outs, *down, dy, weight_out, flops=work
            )
        g3 = flip(s3, "section", 3)
        g2 = flip(s2, "section", 2)
        g1 = flip(s1, "section", 1)
        if final:
            grad_out = gradient(grad_out_kernel, (hidden, quarter), (piece, quarter), *hids, dy, flops=work)
            own, grad_out = lax.optimization_barrier((own, grad_out))
        (pay,) = local(dact_kernel, [resident(wide, BF16)], own, g1, g2, g3, act, slope)
        p3 = flip(pay, "section", 3)
        p2 = flip(pay, "section", 2)
        p1 = flip(pay, "section", 1)
        keep, send = local(
            back_kernel,
            [resident((rows + SIDE, 2 * share), F32), resident((rows + SIDE, 2 * share), BF16)],
            pay, p1, p2, p3, weight_in,
            scratch=[pltpu.VMEM((rows, hidden), BF16)], flops=work,
        )
        got = flip(send, "dp", 1)
        rest, send = local(
            middle_kernel,
            [resident((rows + SIDE, share), F32), resident((rows + SIDE, share), BF16)],
            keep, got,
        )
        if phase == 0 and not final:
            send, hid = lax.optimization_barrier((send, hid))
            hids = gather_hidden(hid)
        got = flip(send, "dp", 2)
        if final:
            grad_in = gradient(
                grad_in_kernel, (quarter, hidden), (quarter, piece), pay, p1, p2, p3, x_full, gain, scale,
                scratch=[pltpu.VMEM((rows, quarter), BF16)], flops=work,
            )
            got, grad_in = lax.optimization_barrier((got, grad_in))
        outs = [resident((rows, share), BF16)]
        if final:
            outs = [jax.ShapeDtypeStruct((rows, share), BF16), jax.ShapeDtypeStruct((1, share), F32)]
        finished = local(functools.partial(finish_kernel, width), outs, rest, got, x0, dy, gain, scale)
        if not final:
            d0 = lax.ppermute(finished[0], "section", [(i, i - 4) for i in range(4, sections)])
            d2 = flip(d0, "dp", 2)
            d1 = flip(d0, "dp", 1)
            d3 = flip(d2, "dp", 1)
            down = (d0, d1, d2, d3)

    grad_x, grad_gain = finished
    return grad_in[None], grad_out[None], grad_gain, grad_x.reshape(1, micro, tok, share)


def shards(checkpoints, gain, w_in, w_out, cotangent):
    rows = checkpoints.shape[1] * checkpoints.shape[2]
    share = checkpoints.shape[3]
    piece = w_in.shape[2] // 4
    if lax.axis_size("dp") == 4 and rows % 16 == 0 and share % 128 == 0 and piece % 128 == 0 and rows <= min(share, piece):
        return shards_of_four(checkpoints, gain, w_in, w_out, cotangent)
    return shards_of_any(checkpoints, gain, w_in, w_out, cotangent)


def solution(mesh):
    in_specs = (
        P("section", None, None, "dp"),
        P("section", None),
        P("section", None, "dp"),
        P("section", "dp", None),
        P(None, None, "dp"),
    )
    out_specs = (
        P("section", None, "dp"),
        P("section", "dp", None),
        P("section", "dp"),
        P("section", None, None, "dp"),
    )
    return jax.shard_map(shards, mesh=mesh, in_specs=in_specs, out_specs=out_specs, check_vma=False)
```

```python
import functools

import jax
import jax.numpy as jnp
from jax import lax
from jax.experimental import pallas as pl
from jax.experimental.pallas import tpu as pltpu
from jax.sharding import PartitionSpec as P

F32 = jnp.float32
BF16 = jnp.bfloat16


def flip(block, axis, bits):
    count = lax.axis_size(axis)
    return lax.ppermute(block, axis, [(i, i ^ bits) for i in range(count)])


def side_rows(values, width):
    lead = values.astype(BF16)
    trail = (values - lead.astype(F32)).astype(BF16)
    flat = jnp.concatenate([lead, trail])
    return jnp.pad(flat, (0, 16 * width - flat.shape[0])).reshape(16, width)


def side_values(rows, count):
    flat = rows.reshape(-1)
    return flat[:count].astype(F32) + flat[count:2 * count].astype(F32)


def gelu_tanh(value):
    return jax.nn.gelu(value, approximate=True)


def shards_of_any(checkpoints, gain, w_in, w_out, cotangent):
    sections = lax.axis_size("section")
    n_dp = lax.axis_size("dp")
    here = lax.axis_index("section")
    lane = lax.axis_index("dp")
    layers = sections // 4
    mine = here % 4
    last = here // 4 == layers - 1
    _, micro, tok, share = checkpoints.shape
    rows = micro * tok
    quarter = share * n_dp
    width = 4 * quarter
    gain_row = gain[0]
    weight_in = w_in[0]
    weight_out = w_out[0]
    hidden = weight_in.shape[1]
    piece = hidden // 4
    core = lane % 2

    def gather_dp(block):
        bit = n_dp // 2
        parts = {0: block}
        while bit >= 1:
            other = flip(jnp.concatenate([parts[j] for j in parts], axis=1), "dp", bit)
            for at, j in enumerate(list(parts)):
                parts[j ^ bit] = other[:, at * block.shape[1]:(at + 1) * block.shape[1]]
            bit //= 2
        full = jnp.zeros((rows, quarter), block.dtype)
        for j, part in parts.items():
            full = lax.dynamic_update_slice(full, part, (0, (lane ^ j) * block.shape[1]))
        return full

    def cot_quarter(block):
        if n_dp < 4:
            whole = lax.all_gather(block, "dp", axis=1, tiled=True)
            return lax.dynamic_slice_in_dim(whole, mine * quarter, quarter, 1)
        per = n_dp // 4
        top = [s * n_dp + d for s in range(sections) for d in range(n_dp) if s // 4 == layers - 1]
        held = block
        far = lambda i, b: (i % n_dp // per ^ i // n_dp % 4) & b
        got = lax.ppermute(held, ("section", "dp"), [(i, i ^ 2 * per) for i in top if far(i, 3) == 0])
        held = jnp.where((lane // per ^ mine) & 2 == 0, held, got)
        got = lax.ppermute(held, ("section", "dp"), [(i, i ^ per) for i in top if far(i, 1) == 0])
        held = jnp.where((lane // per ^ mine) & 1 == 0, held, got)
        if per == 1:
            return held
        parts = {0: held}
        bit = per // 2
        while bit >= 1:
            for j in list(parts):
                parts[j ^ bit] = flip(parts[j], "dp", bit)
            bit //= 2
        full = jnp.zeros((rows, quarter), block.dtype)
        for j, part in parts.items():
            full = lax.dynamic_update_slice(full, part, (0, (lane % per ^ j) * block.shape[1]))
        return full

    def cut(values, j):
        return lax.dynamic_slice_in_dim(values, (mine ^ j) * piece, piece, 1)

    def fill(parts):
        full = jnp.zeros((rows, hidden), parts[0].dtype)
        for j, part in enumerate(parts):
            full = lax.dynamic_update_slice(full, part, (0, (mine ^ j) * piece))
        return full

    x_full = gather_dp(checkpoints[0].reshape(rows, share))
    cot = cot_quarter(cotangent.reshape(rows, cotangent.shape[2]))
    x_wide = x_full.astype(F32)
    scaled_raw = (x_wide * gain_row).astype(BF16)
    squares = jnp.sum(x_wide * x_wide, axis=1)

    act_raw = jnp.dot(scaled_raw, weight_in, preferred_element_type=F32)
    extra = side_rows(squares, piece)
    act = cut(act_raw, 0)
    for j in (3, 1, 2):
        got = flip(jnp.concatenate([cut(act_raw, j).astype(BF16), extra], axis=0), "section", j)
        act = act + got[:rows].astype(F32)
        squares = squares + side_values(got[rows:], rows)
    scale = lax.rsqrt(squares / width + 1e-06)[:, None]
    act = act * scale
    hid, pull = jax.vjp(gelu_tanh, act)
    hid = hid.astype(BF16)
    hid_full = fill([hid] + [flip(hid, "section", j) for j in (1, 2, 3)])
    normed = x_wide * scale
    scaled = (normed * gain_row).astype(BF16)

    def halves(values, side):
        pairs = values.reshape(rows, n_dp // 2, 2, share)
        return jnp.where(side == 0, pairs[:, :, 0], pairs[:, :, 1]).reshape(rows, quarter // 2)

    def own(values):
        return lax.dynamic_slice_in_dim(values, lane // 2 * share, share, 1)

    incoming = jnp.zeros((rows, quarter), BF16)
    normed_half = halves(normed, core)
    gain_half = halves(jnp.broadcast_to(gain_row, (rows, quarter)), core)
    for phase in range(layers):
        final = phase == layers - 1
        dy = jnp.where(last, cot, incoming) if phase > 0 else cot
        dhid_raw = jnp.dot(dy, weight_out.T, preferred_element_type=F32)
        dhid = cut(dhid_raw, 0)
        for j in (3, 1, 2):
            dhid = dhid + flip(cut(dhid_raw, j).astype(BF16), "section", j).astype(F32)
        dact = pull(dhid)[0].astype(BF16)
        inner = jnp.sum(dact.astype(F32) * act, axis=1)
        payload = jnp.concatenate([dact, side_rows(inner, piece)], axis=0)
        others = [flip(payload, "section", j) for j in (1, 2, 3)]
        for got in others:
            inner = inner + side_values(got[rows:], rows)
        dact_full = fill([dact] + [got[:rows] for got in others])
        part = jnp.dot(dact_full, weight_in.T, preferred_element_type=F32).astype(BF16)

        send = jnp.concatenate([halves(part, 1 - core), side_rows(inner, quarter // 2)], axis=0)
        got = flip(send, "dp", 1)
        dscaled = halves(part, core).astype(F32) + got[:rows].astype(F32)
        inner = inner + side_values(got[rows:], rows)
        bit = 2
        while bit < n_dp:
            send = jnp.concatenate([dscaled.astype(BF16), side_rows(inner, quarter // 2)], axis=0)
            got = flip(send, "dp", bit)
            dscaled = dscaled + got[:rows].astype(F32)
            inner = inner + side_values(got[rows:], rows)
            bit *= 2
        dnorm = dscaled * gain_half
        dy_half = halves(dy, core).astype(F32)
        grad_x = (dy_half + scale * (dnorm - normed_half * (inner / width)[:, None])).astype(BF16)
        if not final:
            down = lax.ppermute(grad_x, "section", [(i, i - 4) for i in range(4, sections)])
            other = flip(down, "dp", 1)
            pairs = jnp.where(
                core == 0,
                jnp.stack([down.reshape(rows, n_dp // 2, share), other.reshape(rows, n_dp // 2, share)], axis=2),
                jnp.stack([other.reshape(rows, n_dp // 2, share), down.reshape(rows, n_dp // 2, share)], axis=2),
            )
            incoming = pairs.reshape(rows, quarter)

    grad_out = jnp.dot(hid_full.T, dy, preferred_element_type=F32).astype(BF16)
    grad_in = jnp.dot(scaled.T, dact_full, preferred_element_type=F32).astype(BF16)
    grad_gain = jnp.sum(own(dscaled) * own(normed_half), axis=0)
    return (
        grad_in[None],
        grad_out[None],
        grad_gain[None],
        own(grad_x).reshape(1, micro, tok, share),
    )


SIDE = 16
GELU_IN = 0.7978845608028654
GELU_CUBE = 0.044715


def resident(shape, dtype):
    return pltpu.VMEM(shape, dtype)


def local(body, outs, *args, scratch=(), flops=0):
    spec = pl.BlockSpec(memory_space=pltpu.VMEM)
    moved = sum(a.size * a.dtype.itemsize for a in args)
    return pl.pallas_call(
        body,
        out_shape=tuple(outs),
        in_specs=[spec] * len(args),
        out_specs=tuple(spec for _ in outs),
        scratch_shapes=list(scratch),
        compiler_params=pltpu.CompilerParams(vmem_limit_bytes=16 * 1024 * 1024),
        cost_estimate=pl.CostEstimate(flops=flops, bytes_accessed=moved, transcendentals=0),
    )(*args)


def diagonal(rows, width):
    return lax.broadcasted_iota(jnp.int32, (rows, width), 0) == lax.broadcasted_iota(jnp.int32, (rows, width), 1)


def as_row(column, width):
    rows = column.shape[0]
    return jnp.sum(jnp.where(diagonal(rows, width), column, 0.0), axis=0, keepdims=True)


def as_column(row, rows):
    return jnp.sum(jnp.where(diagonal(rows, row.shape[1]), row, 0.0), axis=1, keepdims=True)


def side_block(row):
    lead = row.astype(BF16).astype(F32)
    at = lax.broadcasted_iota(jnp.int32, (SIDE, row.shape[1]), 0)
    return jnp.where(at == 0, lead, jnp.where(at == 1, row - lead, 0.0)).astype(BF16)


def side_row(block):
    wide = block.astype(F32)
    return wide[0:1] + wide[1:2]


def load_kernel(*refs):
    count = len(refs) // 2
    copies = [pltpu.make_async_copy(refs[i], refs[count + i], refs[-1].at[i]) for i in range(count)]
    for copy in copies:
        copy.start()
    for copy in copies:
        copy.wait()


def load(*arrays):
    return pl.pallas_call(
        load_kernel,
        out_shape=tuple(resident(a.shape, a.dtype) for a in arrays),
        in_specs=[pl.BlockSpec(memory_space=pl.ANY)] * len(arrays),
        out_specs=tuple(pl.BlockSpec(memory_space=pltpu.VMEM) for _ in arrays),
        scratch_shapes=[pltpu.SemaphoreType.DMA((len(arrays),))],
        compiler_params=pltpu.CompilerParams(vmem_limit_bytes=1024 * 1024),
        cost_estimate=pl.CostEstimate(flops=0, bytes_accessed=sum(2 * a.size * a.dtype.itemsize for a in arrays), transcendentals=0),
    )(*(pltpu.with_memory_space_constraint(a, pltpu.HBM) for a in arrays))


def place():
    return lax.axis_index("section") % 4, lax.axis_index("dp")


def dot_nt(left, right):
    return lax.dot_general(left, right, (((1,), (1,)), ((), ())), preferred_element_type=F32)


def dot_tn(left, right):
    return lax.dot_general(left, right, (((0,), (0,)), ((), ())), preferred_element_type=F32)


def slot(index, size):
    return pl.ds(pl.multiple_of(index * size, size), size)


def spread_in_kernel(x0, x1, x2, x3, gain, weight, own, s1, s2, s3, x_full, scaled):
    mine, lane = place()
    rows, share = x0.shape
    piece = own.shape[1]
    for d, part in enumerate((x0, x1, x2, x3)):
        x_full[:, slot(lane ^ d, share)] = part[...]
    wide = x_full[...].astype(F32)
    row = as_row(jnp.sum(wide * wide, axis=1, keepdims=True), piece)
    scaled[...] = (wide * gain[...]).astype(BF16)
    block = side_block(row)
    for d, out in ((3, s3), (2, s2), (1, s1)):
        out[:rows] = jnp.dot(scaled[...], weight[:, slot(mine ^ d, piece)], preferred_element_type=F32).astype(BF16)
        out[rows:] = block
    own[:rows] = jnp.dot(scaled[...], weight[:, slot(mine, piece)], preferred_element_type=F32)
    own[rows:] = jnp.broadcast_to(row, (SIDE, piece))


def spread_dy(dy, weight, mine, own, s1, s2, s3):
    piece = own.shape[1]
    for d, out in ((3, s3), (2, s2), (1, s1)):
        out[...] = dot_nt(dy[...], weight[slot(mine ^ d, piece), :]).astype(BF16)
    own[...] = dot_nt(dy[...], weight[slot(mine, piece), :])


def spread_first_kernel(cot, sent, weight, own, s1, s2, s3, dy):
    mine, lane = place()

    @pl.when(lane == mine)
    def _():
        dy[...] = cot[...]

    @pl.when(lane != mine)
    def _():
        dy[...] = sent[...]

    spread_dy(dy, weight, mine, own, s1, s2, s3)


def spread_next_kernel(layers, d0, d1, d2, d3, before, weight, own, s1, s2, s3, dy):
    mine, lane = place()
    share = d0.shape[1]
    last = lax.axis_index("section") // 4 == layers - 1

    @pl.when(last)
    def _():
        dy[...] = before[...]

    @pl.when(jnp.logical_not(last))
    def _():
        for d, part in enumerate((d0, d1, d2, d3)):
            dy[:, slot(lane ^ d, share)] = part[...]

    spread_dy(dy, weight, mine, own, s1, s2, s3)


def act_kernel(width, own, g1, g2, g3, act, slope, hid, scale):
    rows = act.shape[0]
    row = own[rows:rows + 1] + side_row(g1[rows:]) + side_row(g2[rows:]) + side_row(g3[rows:])
    r = lax.rsqrt(as_column(row, rows) / width + 1e-06)
    scale[...] = r
    a = (own[:rows] + g1[:rows].astype(F32) + g2[:rows].astype(F32) + g3[:rows].astype(F32)) * r
    act[...] = a
    square = a * a
    t = jnp.tanh(GELU_IN * (a + GELU_CUBE * (square * a)))
    half = 0.5 * (1.0 + t)
    hid[...] = (a * half).astype(BF16)
    slope[...] = half + 0.5 * a * (1.0 - t * t) * (GELU_IN * (1.0 + 3.0 * GELU_CUBE * square))


def dact_kernel(own, g1, g2, g3, act, slope, pay):
    rows, piece = own.shape
    dhid = own[...] + g1[...].astype(F32) + g2[...].astype(F32) + g3[...].astype(F32)
    da = (dhid * slope[...]).astype(BF16)
    pay[:rows] = da
    pay[rows:] = side_block(as_row(jnp.sum(da.astype(F32) * act[...], axis=1, keepdims=True), piece))


def back_kernel(p0, p1, p2, p3, weight, keep, send, full):
    mine, lane = place()
    rows = full.shape[0]
    piece = p0.shape[1]
    share = weight.shape[0] // 4
    row = side_row(p0[rows:]) + side_row(p1[rows:]) + side_row(p2[rows:]) + side_row(p3[rows:])
    for d, part in enumerate((p0, p1, p2, p3)):
        full[:, slot(mine ^ d, piece)] = part[:rows]
    for at, d in ((0, 1), (1, 3)):
        send[:rows, at * share:(at + 1) * share] = dot_nt(full[...], weight[slot(lane ^ d, share), :]).astype(BF16)
    send[rows:] = side_block(row)
    for at, d in ((0, 0), (1, 2)):
        keep[:rows, at * share:(at + 1) * share] = dot_nt(full[...], weight[slot(lane ^ d, share), :])
    keep[rows:] = jnp.broadcast_to(row, (SIDE, keep.shape[1]))


def middle_kernel(keep, got, rest, send):
    rows = keep.shape[0] - SIDE
    share = rest.shape[1]
    row = (keep[rows:rows + 1] + side_row(got[rows:]))[:, :share]
    send[:rows] = (keep[:rows, share:] + got[:rows, share:].astype(F32)).astype(BF16)
    send[rows:] = side_block(row)
    rest[:rows] = keep[:rows, :share] + got[:rows, :share].astype(F32)
    rest[rows:] = jnp.broadcast_to(row, (SIDE, share))


def finish_kernel(width, rest, got, x_own, dy, gain, scale, grad_x, *grad_gain):
    _, lane = place()
    rows, share = x_own.shape
    at = slot(lane, share)
    r = scale[...]
    du = rest[:rows] + got[:rows].astype(F32)
    normed = x_own[...].astype(F32) * r
    inner = as_column(rest[rows:rows + 1] + side_row(got[rows:]), rows) / width
    dnorm = du * gain[:, at]
    grad_x[...] = (dy[:, at].astype(F32) + r * (dnorm - normed * inner)).astype(BF16)
    if grad_gain:
        grad_gain[0][...] = jnp.sum(du * normed, axis=0, keepdims=True)


def grad_out_kernel(h0, h1, h2, h3, dy, out, held, sems):
    mine, _ = place()
    piece = h0.shape[1]
    copies = []
    for d, part in enumerate((h0, h1, h2, h3)):
        held[d] = dot_tn(part[...], dy[...]).astype(BF16)
        copies.append(pltpu.make_async_copy(held.at[d], out.at[slot(mine ^ d, piece), :], sems.at[d]))
        copies[-1].start()
    for copy in copies:
        copy.wait()


def grad_in_kernel(p0, p1, p2, p3, x_full, gain, scale, out, scaled, held, sems):
    mine, _ = place()
    rows = x_full.shape[0]
    piece = p0.shape[1]
    scaled[...] = (x_full[...].astype(F32) * scale[...] * gain[...]).astype(BF16)
    copies = []
    for d, part in enumerate((p0, p1, p2, p3)):
        held[d] = dot_tn(scaled[...], part[:rows]).astype(BF16)
        copies.append(pltpu.make_async_copy(held.at[d], out.at[:, slot(mine ^ d, piece)], sems.at[d]))
        copies[-1].start()
    for copy in copies:
        copy.wait()


def gradient(body, shape, block, *args, scratch=(), flops=0):
    return pl.pallas_call(
        body,
        out_shape=jax.ShapeDtypeStruct(shape, BF16),
        in_specs=[pl.BlockSpec(memory_space=pltpu.VMEM)] * len(args),
        out_specs=pl.BlockSpec(memory_space=pl.ANY),
        scratch_shapes=[*scratch, pltpu.VMEM((4,) + block, BF16), pltpu.SemaphoreType.DMA((4,))],
        compiler_params=pltpu.CompilerParams(vmem_limit_bytes=16 * 1024 * 1024),
        cost_estimate=pl.CostEstimate(flops=flops, bytes_accessed=2 * shape[0] * shape[1], transcendentals=0),
    )(*args)


def shards_of_four(checkpoints, gain, w_in, w_out, cotangent):
    sections = lax.axis_size("section")
    here = lax.axis_index("section")
    lane = lax.axis_index("dp")
    layers = sections // 4
    mine = here % 4
    _, micro, tok, share = checkpoints.shape
    rows = micro * tok
    quarter = share * 4
    width = 4 * quarter
    hidden = w_in.shape[2]
    piece = hidden // 4
    work = 2 * rows * quarter * hidden

    x0 = checkpoints[0].reshape(rows, share)
    cot = cotangent.reshape(rows, quarter)
    top = [s * 4 + d for s in range(sections) for d in range(4) if s // 4 == layers - 1]
    x2 = flip(x0, "dp", 2)
    x1 = flip(x0, "dp", 1)
    weight_in, x0, gain = load(w_in[0], x0, gain)
    x2, x1, weight_in = lax.optimization_barrier((x2, x1, weight_in))
    sent = lax.ppermute(cot, ("section", "dp"), [((i // 4 ^ near) * 4 + i // 4 % 4, i) for i in top for near in (1, 0, 2) if i // 4 % 4 ^ i % 4 == (2, 1, 3)[near]])
    x3 = flip(x2, "dp", 1)

    wide = (rows + SIDE, piece)
    own, s1, s2, s3, x_full = local(
        spread_in_kernel,
        [resident(wide, F32)] + [resident(wide, BF16)] * 3 + [resident((rows, quarter), BF16)],
        x0, x1, x2, x3, gain, weight_in,
        scratch=[pltpu.VMEM((rows, quarter), BF16)], flops=work,
    )
    s1, s2, s3, cot, w_out = lax.optimization_barrier((s1, s2, s3, cot, w_out))
    s2, sent = lax.optimization_barrier((s2, sent))
    g3 = flip(s3, "section", 3)
    g2 = flip(s2, "section", 2)
    g1 = flip(s1, "section", 1)
    weight_out, cot = load(w_out[0], cot)
    act, slope, hid, scale = local(
        functools.partial(act_kernel, width),
        [resident((rows, piece), F32), resident((rows, piece), F32), resident((rows, piece), BF16), resident((rows, 1), F32)],
        own, g1, g2, g3,
    )

    spread_outs = [resident((rows, piece), F32)] + [resident((rows, piece), BF16)] * 3 + [resident((rows, quarter), BF16)]

    def gather_hidden(block):
        return [block] + [flip(block, "section", j) for j in (1, 2, 3)]

    if layers == 1:
        hids = gather_hidden(hid)
    for phase in range(layers):
        final = phase == layers - 1
        if phase == 0:
            own, s1, s2, s3, dy = local(spread_first_kernel, spread_outs, cot, sent, weight_out, flops=work)
        else:
            down, hids = lax.optimization_barrier((down, hids))
            own, s1, s2, s3, dy = local(
                functools.partial(spread_next_kernel, layers), spread_outs, *down, dy, weight_out, flops=work
            )
        g3 = flip(s3, "section", 3)
        g2 = flip(s2, "section", 2)
        g1 = flip(s1, "section", 1)
        if final:
            grad_out = gradient(grad_out_kernel, (hidden, quarter), (piece, quarter), *hids, dy, flops=work)
            own, grad_out = lax.optimization_barrier((own, grad_out))
        (pay,) = local(dact_kernel, [resident(wide, BF16)], own, g1, g2, g3, act, slope)
        p3 = flip(pay, "section", 3)
        p2 = flip(pay, "section", 2)
        p1 = flip(pay, "section", 1)
        keep, send = local(
            back_kernel,
            [resident((rows + SIDE, 2 * share), F32), resident((rows + SIDE, 2 * share), BF16)],
            pay, p1, p2, p3, weight_in,
            scratch=[pltpu.VMEM((rows, hidden), BF16)], flops=work,
        )
        got = flip(send, "dp", 1)
        rest, send = local(
            middle_kernel,
            [resident((rows + SIDE, share), F32), resident((rows + SIDE, share), BF16)],
            keep, got,
        )
        if phase == 0 and not final:
            send, hid = lax.optimization_barrier((send, hid))
            hids = gather_hidden(hid)
        got = flip(send, "dp", 2)
        if final:
            grad_in = gradient(
                grad_in_kernel, (quarter, hidden), (quarter, piece), pay, p1, p2, p3, x_full, gain, scale,
                scratch=[pltpu.VMEM((rows, quarter), BF16)], flops=work,
            )
            got, grad_in = lax.optimization_barrier((got, grad_in))
        outs = [resident((rows, share), BF16)]
        if final:
            outs = [jax.ShapeDtypeStruct((rows, share), BF16), jax.ShapeDtypeStruct((1, share), F32)]
        finished = local(functools.partial(finish_kernel, width), outs, rest, got, x0, dy, gain, scale)
        if not final:
            d0 = lax.ppermute(finished[0], "section", [(i, i - 4) for i in range(4, sections)])
            d2 = flip(d0, "dp", 2)
            d1 = flip(d0, "dp", 1)
            d3 = flip(d2, "dp", 1)
            down = (d0, d1, d2, d3)

    grad_x, grad_gain = finished
    return grad_in[None], grad_out[None], grad_gain, grad_x.reshape(1, micro, tok, share)


def shards(checkpoints, gain, w_in, w_out, cotangent):
    rows = checkpoints.shape[1] * checkpoints.shape[2]
    share = checkpoints.shape[3]
    piece = w_in.shape[2] // 4
    if lax.axis_size("dp") == 4 and rows % 16 == 0 and share % 128 == 0 and piece % 128 == 0 and rows <= min(share, piece):
        return shards_of_four(checkpoints, gain, w_in, w_out, cotangent)
    return shards_of_any(checkpoints, gain, w_in, w_out, cotangent)


def solution(mesh):
    in_specs = (
        P("section", None, None, "dp"),
        P("section", None),
        P("section", None, "dp"),
        P("section", "dp", None),
        P(None, None, "dp"),
    )
    out_specs = (
        P("section", None, "dp"),
        P("section", "dp", None),
        P("section", "dp"),
        P("section", None, None, "dp"),
    )
    return jax.shard_map(shards, mesh=mesh, in_specs=in_specs, out_specs=out_specs, check_vma=False)
```

```python
import functools

import jax
import jax.numpy as jnp
from jax import lax
from jax.experimental import pallas as pl
from jax.experimental.pallas import tpu as pltpu
from jax.sharding import PartitionSpec as P

F32 = jnp.float32
BF16 = jnp.bfloat16


def flip(block, axis, bits):
    count = lax.axis_size(axis)
    return lax.ppermute(block, axis, [(i, i ^ bits) for i in range(count)])


def side_rows(values, width):
    lead = values.astype(BF16)
    trail = (values - lead.astype(F32)).astype(BF16)
    flat = jnp.concatenate([lead, trail])
    return jnp.pad(flat, (0, 16 * width - flat.shape[0])).reshape(16, width)


def side_values(rows, count):
    flat = rows.reshape(-1)
    return flat[:count].astype(F32) + flat[count:2 * count].astype(F32)


def gelu_tanh(value):
    return jax.nn.gelu(value, approximate=True)


def shards_of_any(checkpoints, gain, w_in, w_out, cotangent):
    sections = lax.axis_size("section")
    n_dp = lax.axis_size("dp")
    here = lax.axis_index("section")
    lane = lax.axis_index("dp")
    layers = sections // 4
    mine = here % 4
    last = here // 4 == layers - 1
    _, micro, tok, share = checkpoints.shape
    rows = micro * tok
    quarter = share * n_dp
    width = 4 * quarter
    gain_row = gain[0]
    weight_in = w_in[0]
    weight_out = w_out[0]
    hidden = weight_in.shape[1]
    piece = hidden // 4
    core = lane % 2

    def gather_dp(block):
        bit = n_dp // 2
        parts = {0: block}
        while bit >= 1:
            other = flip(jnp.concatenate([parts[j] for j in parts], axis=1), "dp", bit)
            for at, j in enumerate(list(parts)):
                parts[j ^ bit] = other[:, at * block.shape[1]:(at + 1) * block.shape[1]]
            bit //= 2
        full = jnp.zeros((rows, quarter), block.dtype)
        for j, part in parts.items():
            full = lax.dynamic_update_slice(full, part, (0, (lane ^ j) * block.shape[1]))
        return full

    def cot_quarter(block):
        if n_dp < 4:
            whole = lax.all_gather(block, "dp", axis=1, tiled=True)
            return lax.dynamic_slice_in_dim(whole, mine * quarter, quarter, 1)
        per = n_dp // 4
        top = [s * n_dp + d for s in range(sections) for d in range(n_dp) if s // 4 == layers - 1]
        held = block
        far = lambda i, b: (i % n_dp // per ^ i // n_dp % 4) & b
        got = lax.ppermute(held, ("section", "dp"), [(i, i ^ 2 * per) for i in top if far(i, 3) == 0])
        held = jnp.where((lane // per ^ mine) & 2 == 0, held, got)
        got = lax.ppermute(held, ("section", "dp"), [(i, i ^ per) for i in top if far(i, 1) == 0])
        held = jnp.where((lane // per ^ mine) & 1 == 0, held, got)
        if per == 1:
            return held
        parts = {0: held}
        bit = per // 2
        while bit >= 1:
            for j in list(parts):
                parts[j ^ bit] = flip(parts[j], "dp", bit)
            bit //= 2
        full = jnp.zeros((rows, quarter), block.dtype)
        for j, part in parts.items():
            full = lax.dynamic_update_slice(full, part, (0, (lane % per ^ j) * block.shape[1]))
        return full

    def cut(values, j):
        return lax.dynamic_slice_in_dim(values, (mine ^ j) * piece, piece, 1)

    def fill(parts):
        full = jnp.zeros((rows, hidden), parts[0].dtype)
        for j, part in enumerate(parts):
            full = lax.dynamic_update_slice(full, part, (0, (mine ^ j) * piece))
        return full

    x_full = gather_dp(checkpoints[0].reshape(rows, share))
    cot = cot_quarter(cotangent.reshape(rows, cotangent.shape[2]))
    x_wide = x_full.astype(F32)
    scaled_raw = (x_wide * gain_row).astype(BF16)
    squares = jnp.sum(x_wide * x_wide, axis=1)

    act_raw = jnp.dot(scaled_raw, weight_in, preferred_element_type=F32)
    extra = side_rows(squares, piece)
    act = cut(act_raw, 0)
    for j in (3, 1, 2):
        got = flip(jnp.concatenate([cut(act_raw, j).astype(BF16), extra], axis=0), "section", j)
        act = act + got[:rows].astype(F32)
        squares = squares + side_values(got[rows:], rows)
    scale = lax.rsqrt(squares / width + 1e-06)[:, None]
    act = act * scale
    hid, pull = jax.vjp(gelu_tanh, act)
    hid = hid.astype(BF16)
    hid_full = fill([hid] + [flip(hid, "section", j) for j in (1, 2, 3)])
    normed = x_wide * scale
    scaled = (normed * gain_row).astype(BF16)

    def halves(values, side):
        pairs = values.reshape(rows, n_dp // 2, 2, share)
        return jnp.where(side == 0, pairs[:, :, 0], pairs[:, :, 1]).reshape(rows, quarter // 2)

    def own(values):
        return lax.dynamic_slice_in_dim(values, lane // 2 * share, share, 1)

    incoming = jnp.zeros((rows, quarter), BF16)
    normed_half = halves(normed, core)
    gain_half = halves(jnp.broadcast_to(gain_row, (rows, quarter)), core)
    for phase in range(layers):
        final = phase == layers - 1
        dy = jnp.where(last, cot, incoming) if phase > 0 else cot
        dhid_raw = jnp.dot(dy, weight_out.T, preferred_element_type=F32)
        dhid = cut(dhid_raw, 0)
        for j in (3, 1, 2):
            dhid = dhid + flip(cut(dhid_raw, j).astype(BF16), "section", j).astype(F32)
        dact = pull(dhid)[0].astype(BF16)
        inner = jnp.sum(dact.astype(F32) * act, axis=1)
        payload = jnp.concatenate([dact, side_rows(inner, piece)], axis=0)
        others = [flip(payload, "section", j) for j in (1, 2, 3)]
        for got in others:
            inner = inner + side_values(got[rows:], rows)
        dact_full = fill([dact] + [got[:rows] for got in others])
        part = jnp.dot(dact_full, weight_in.T, preferred_element_type=F32).astype(BF16)

        send = jnp.concatenate([halves(part, 1 - core), side_rows(inner, quarter // 2)], axis=0)
        got = flip(send, "dp", 1)
        dscaled = halves(part, core).astype(F32) + got[:rows].astype(F32)
        inner = inner + side_values(got[rows:], rows)
        bit = 2
        while bit < n_dp:
            send = jnp.concatenate([dscaled.astype(BF16), side_rows(inner, quarter // 2)], axis=0)
            got = flip(send, "dp", bit)
            dscaled = dscaled + got[:rows].astype(F32)
            inner = inner + side_values(got[rows:], rows)
            bit *= 2
        dnorm = dscaled * gain_half
        dy_half = halves(dy, core).astype(F32)
        grad_x = (dy_half + scale * (dnorm - normed_half * (inner / width)[:, None])).astype(BF16)
        if not final:
            down = lax.ppermute(grad_x, "section", [(i, i - 4) for i in range(4, sections)])
            other = flip(down, "dp", 1)
            pairs = jnp.where(
                core == 0,
                jnp.stack([down.reshape(rows, n_dp // 2, share), other.reshape(rows, n_dp // 2, share)], axis=2),
                jnp.stack([other.reshape(rows, n_dp // 2, share), down.reshape(rows, n_dp // 2, share)], axis=2),
            )
            incoming = pairs.reshape(rows, quarter)

    grad_out = jnp.dot(hid_full.T, dy, preferred_element_type=F32).astype(BF16)
    grad_in = jnp.dot(scaled.T, dact_full, preferred_element_type=F32).astype(BF16)
    grad_gain = jnp.sum(own(dscaled) * own(normed_half), axis=0)
    return (
        grad_in[None],
        grad_out[None],
        grad_gain[None],
        own(grad_x).reshape(1, micro, tok, share),
    )


SIDE = 16
GELU_IN = 0.7978845608028654
GELU_CUBE = 0.044715


def resident(shape, dtype):
    return pltpu.VMEM(shape, dtype)


def local(body, outs, *args, scratch=(), flops=0):
    spec = pl.BlockSpec(memory_space=pltpu.VMEM)
    moved = sum(a.size * a.dtype.itemsize for a in args)
    return pl.pallas_call(
        body,
        out_shape=tuple(outs),
        in_specs=[spec] * len(args),
        out_specs=tuple(spec for _ in outs),
        scratch_shapes=list(scratch),
        compiler_params=pltpu.CompilerParams(vmem_limit_bytes=16 * 1024 * 1024),
        cost_estimate=pl.CostEstimate(flops=flops, bytes_accessed=moved, transcendentals=0),
    )(*args)


def diagonal(rows, width):
    return lax.broadcasted_iota(jnp.int32, (rows, width), 0) == lax.broadcasted_iota(jnp.int32, (rows, width), 1)


def as_row(column, width):
    rows = column.shape[0]
    return jnp.sum(jnp.where(diagonal(rows, width), column, 0.0), axis=0, keepdims=True)


def as_column(row, rows):
    return jnp.sum(jnp.where(diagonal(rows, row.shape[1]), row, 0.0), axis=1, keepdims=True)


def side_block(row):
    lead = row.astype(BF16).astype(F32)
    at = lax.broadcasted_iota(jnp.int32, (SIDE, row.shape[1]), 0)
    return jnp.where(at == 0, lead, jnp.where(at == 1, row - lead, 0.0)).astype(BF16)


def side_row(block):
    wide = block.astype(F32)
    return wide[0:1] + wide[1:2]


def load_kernel(*refs):
    count = len(refs) // 2
    copies = [pltpu.make_async_copy(refs[i], refs[count + i], refs[-1].at[i]) for i in range(count)]
    for copy in copies:
        copy.start()
    for copy in copies:
        copy.wait()


def load(*arrays):
    return pl.pallas_call(
        load_kernel,
        out_shape=tuple(resident(a.shape, a.dtype) for a in arrays),
        in_specs=[pl.BlockSpec(memory_space=pl.ANY)] * len(arrays),
        out_specs=tuple(pl.BlockSpec(memory_space=pltpu.VMEM) for _ in arrays),
        scratch_shapes=[pltpu.SemaphoreType.DMA((len(arrays),))],
        compiler_params=pltpu.CompilerParams(vmem_limit_bytes=1024 * 1024),
        cost_estimate=pl.CostEstimate(flops=0, bytes_accessed=sum(2 * a.size * a.dtype.itemsize for a in arrays), transcendentals=0),
    )(*(pltpu.with_memory_space_constraint(a, pltpu.HBM) for a in arrays))


def place():
    return lax.axis_index("section") % 4, lax.axis_index("dp")


def dot_nt(left, right):
    return lax.dot_general(left, right, (((1,), (1,)), ((), ())), preferred_element_type=F32)


def dot_tn(left, right):
    return lax.dot_general(left, right, (((0,), (0,)), ((), ())), preferred_element_type=F32)


def slot(index, size):
    return pl.ds(pl.multiple_of(index * size, size), size)


def spread_in_part(part, at, gain, weight, mine, total, begin):
    share = part.shape[1]
    piece = weight.shape[1] // 4
    scaled = (part[...].astype(F32) * gain[:, slot(at, share)]).astype(BF16)
    for d in (3, 2, 1, 0):
        block = jnp.dot(scaled, weight[slot(at, share), slot(mine ^ d, piece)], preferred_element_type=F32)
        columns = slice(d * piece, (d + 1) * piece)
        total[:, columns] = block if begin else total[:, columns] + block


def square_sum(part):
    wide = part[...].astype(F32)
    return jnp.sum(wide * wide, axis=1, keepdims=True)


def spread_in_first_kernel(x0, x1, gain, weight, total):
    mine, lane = place()
    spread_in_part(x0, lane, gain, weight, mine, total, True)
    spread_in_part(x1, lane ^ 1, gain, weight, mine, total, False)


def spread_in_last_kernel(x0, x1, x2, x3, gain, weight, before, own, s1, s2, s3, x_full, total):
    mine, lane = place()
    rows, share = x0.shape
    piece = own.shape[1]
    total[...] = before[...]
    spread_in_part(x2, lane ^ 2, gain, weight, mine, total, False)
    spread_in_part(x3, lane ^ 3, gain, weight, mine, total, False)
    row = as_row(square_sum(x0) + square_sum(x1) + square_sum(x2) + square_sum(x3), piece)
    block = side_block(row)
    for d, out in ((3, s3), (2, s2), (1, s1)):
        out[:rows] = total[:, d * piece:(d + 1) * piece].astype(BF16)
        out[rows:] = block
    own[:rows] = total[:, :piece]
    own[rows:] = jnp.broadcast_to(row, (SIDE, piece))
    for d, part in enumerate((x0, x1, x2, x3)):
        x_full[:, slot(lane ^ d, share)] = part[...]


def spread_dy(dy, weight, mine, own, s1, s2, s3):
    piece = own.shape[1]
    for d, out in ((3, s3), (2, s2), (1, s1)):
        out[...] = dot_nt(dy[...], weight[slot(mine ^ d, piece), :]).astype(BF16)
    own[...] = dot_nt(dy[...], weight[slot(mine, piece), :])


def spread_first_kernel(cot, sent, weight, own, s1, s2, s3, dy):
    mine, lane = place()

    @pl.when(lane == mine)
    def _():
        dy[...] = cot[...]

    @pl.when(lane != mine)
    def _():
        dy[...] = sent[...]

    spread_dy(dy, weight, mine, own, s1, s2, s3)


def spread_next_kernel(layers, ds, begin, end, *refs):
    parts, refs = refs[:len(ds)], refs[len(ds):]
    before, weight = refs[:2]
    refs = refs[2:]
    mine, lane = place()
    rows, share = parts[0].shape
    piece = weight.shape[0] // 4
    last = lax.axis_index("section") // 4 == layers - 1
    if begin:
        (total,) = refs
    elif end:
        earlier, *others, own, s1, s2, s3, dy, total = refs
        total[...] = earlier[...]
    else:
        earlier, total = refs
        total[...] = earlier[...]
    for i, (d, part) in enumerate(zip(ds, parts)):
        at = slot(lane ^ d, share)
        value = jnp.where(last, before[:, at], part[...])
        for j in (3, 2, 1, 0):
            block = dot_nt(value, weight[slot(mine ^ j, piece), at])
            columns = slice(j * piece, (j + 1) * piece)
            total[:, columns] = block if begin and i == 0 else total[:, columns] + block
    if end:
        for j, out in ((3, s3), (2, s2), (1, s1)):
            out[...] = total[:, j * piece:(j + 1) * piece].astype(BF16)
        own[...] = total[:, :piece]
        done = [d for d in range(4) if d not in ds]

        @pl.when(last)
        def _():
            dy[...] = before[...]

        @pl.when(jnp.logical_not(last))
        def _():
            for d, part in zip((*done, *ds), (*others, *parts)):
                dy[:, slot(lane ^ d, share)] = part[...]


def act_kernel(width, own, g1, g2, g3, act, slope, hid, scale):
    rows = act.shape[0]
    row = own[rows:rows + 1] + side_row(g1[rows:]) + side_row(g2[rows:]) + side_row(g3[rows:])
    r = lax.rsqrt(as_column(row, rows) / width + 1e-06)
    scale[...] = r
    a = (own[:rows] + g1[:rows].astype(F32) + g2[:rows].astype(F32) + g3[:rows].astype(F32)) * r
    act[...] = a
    square = a * a
    t = jnp.tanh(GELU_IN * (a + GELU_CUBE * (square * a)))
    half = 0.5 * (1.0 + t)
    hid[...] = (a * half).astype(BF16)
    slope[...] = half + 0.5 * a * (1.0 - t * t) * (GELU_IN * (1.0 + 3.0 * GELU_CUBE * square))


def dact_kernel(own, g1, g2, g3, act, slope, pay):
    rows, piece = own.shape
    dhid = own[...] + g1[...].astype(F32) + g2[...].astype(F32) + g3[...].astype(F32)
    da = (dhid * slope[...]).astype(BF16)
    pay[:rows] = da
    pay[rows:] = side_block(as_row(jnp.sum(da.astype(F32) * act[...], axis=1, keepdims=True), piece))


def back_part(part, j, weight, mine, lane, total, begin):
    rows = total.shape[0]
    piece = part.shape[1]
    share = weight.shape[0] // 4
    for d in (1, 3, 0, 2):
        block = dot_nt(part[:rows], weight[slot(lane ^ d, share), slot(mine ^ j, piece)])
        columns = slice(d * share, (d + 1) * share)
        total[:, columns] = block if begin else total[:, columns] + block


def back_kernel(js, begin, *refs):
    *parts, weight = refs[:len(js) + 1]
    *earlier, total = refs[len(js) + 1:]
    mine, lane = place()
    if not begin:
        total[...] = earlier[0][...]
    for i, (j, part) in enumerate(zip(js, parts)):
        back_part(part, j, weight, mine, lane, total, begin and i == 0)


def back_last_kernel(p0, p1, p2, p3, weight, earlier, keep, send, total):
    mine, lane = place()
    rows = total.shape[0]
    share = weight.shape[0] // 4
    total[...] = earlier[...]
    back_part(p1, 1, weight, mine, lane, total, False)
    row = side_row(p0[rows:]) + side_row(p1[rows:]) + side_row(p2[rows:]) + side_row(p3[rows:])
    for at, d in ((0, 1), (1, 3)):
        send[:rows, at * share:(at + 1) * share] = total[:, d * share:(d + 1) * share].astype(BF16)
    send[rows:] = side_block(row)
    for at, d in ((0, 0), (1, 2)):
        keep[:rows, at * share:(at + 1) * share] = total[:, d * share:(d + 1) * share]
    keep[rows:] = jnp.broadcast_to(row, (SIDE, keep.shape[1]))


def middle_kernel(keep, got, rest, send):
    rows = keep.shape[0] - SIDE
    share = rest.shape[1]
    row = (keep[rows:rows + 1] + side_row(got[rows:]))[:, :share]
    send[:rows] = (keep[:rows, share:] + got[:rows, share:].astype(F32)).astype(BF16)
    send[rows:] = side_block(row)
    rest[:rows] = keep[:rows, :share] + got[:rows, :share].astype(F32)
    rest[rows:] = jnp.broadcast_to(row, (SIDE, share))


def finish_kernel(width, rest, got, x_own, dy, gain, scale, grad_x, *grad_gain):
    _, lane = place()
    rows, share = x_own.shape
    at = slot(lane, share)
    r = scale[...]
    du = rest[:rows] + got[:rows].astype(F32)
    normed = x_own[...].astype(F32) * r
    inner = as_column(rest[rows:rows + 1] + side_row(got[rows:]), rows) / width
    dnorm = du * gain[:, at]
    grad_x[...] = (dy[:, at].astype(F32) + r * (dnorm - normed * inner)).astype(BF16)
    if grad_gain:
        grad_gain[0][...] = jnp.sum(du * normed, axis=0, keepdims=True)


def grad_out_kernel(h0, h1, h2, h3, dy, out, held, sems):
    mine, _ = place()
    piece = h0.shape[1]
    copies = []
    for d, part in enumerate((h0, h1, h2, h3)):
        held[d] = dot_tn(part[...], dy[...]).astype(BF16)
        copies.append(pltpu.make_async_copy(held.at[d], out.at[slot(mine ^ d, piece), :], sems.at[d]))
        copies[-1].start()
    for copy in copies:
        copy.wait()


def grad_in_kernel(p0, p1, p2, p3, x_full, gain, scale, out, scaled, held, sems):
    mine, _ = place()
    rows = x_full.shape[0]
    piece = p0.shape[1]
    scaled[...] = (x_full[...].astype(F32) * scale[...] * gain[...]).astype(BF16)
    copies = []
    for d, part in enumerate((p0, p1, p2, p3)):
        held[d] = dot_tn(scaled[...], part[:rows]).astype(BF16)
        copies.append(pltpu.make_async_copy(held.at[d], out.at[:, slot(mine ^ d, piece)], sems.at[d]))
        copies[-1].start()
    for copy in copies:
        copy.wait()


def gradient(body, shape, block, *args, scratch=(), flops=0):
    return pl.pallas_call(
        body,
        out_shape=jax.ShapeDtypeStruct(shape, BF16),
        in_specs=[pl.BlockSpec(memory_space=pltpu.VMEM)] * len(args),
        out_specs=pl.BlockSpec(memory_space=pl.ANY),
        scratch_shapes=[*scratch, pltpu.VMEM((4,) + block, BF16), pltpu.SemaphoreType.DMA((4,))],
        compiler_params=pltpu.CompilerParams(vmem_limit_bytes=16 * 1024 * 1024),
        cost_estimate=pl.CostEstimate(flops=flops, bytes_accessed=2 * shape[0] * shape[1], transcendentals=0),
    )(*args)


def shards_of_four(checkpoints, gain, w_in, w_out, cotangent):
    sections = lax.axis_size("section")
    here = lax.axis_index("section")
    lane = lax.axis_index("dp")
    layers = sections // 4
    mine = here % 4
    _, micro, tok, share = checkpoints.shape
    rows = micro * tok
    quarter = share * 4
    width = 4 * quarter
    hidden = w_in.shape[2]
    piece = hidden // 4
    work = 2 * rows * quarter * hidden

    x0 = checkpoints[0].reshape(rows, share)
    cot = cotangent.reshape(rows, quarter)
    top = [s * 4 + d for s in range(sections) for d in range(4) if s // 4 == layers - 1]
    x2 = flip(x0, "dp", 2)
    x1 = flip(x0, "dp", 1)
    weight_in, x0, gain = load(w_in[0], x0, gain)
    x2, x1, weight_in = lax.optimization_barrier((x2, x1, weight_in))
    sent = lax.ppermute(cot, ("section", "dp"), [((i // 4 ^ near) * 4 + i // 4 % 4, i) for i in top for near in (1, 0, 2) if i // 4 % 4 ^ i % 4 == (2, 1, 3)[near]])
    x3 = flip(x2, "dp", 1)

    wide = (rows + SIDE, piece)
    (begun,) = local(spread_in_first_kernel, [resident((rows, hidden), F32)], x0, x1, gain, weight_in, flops=work)
    own, s1, s2, s3, x_full = local(
        spread_in_last_kernel,
        [resident(wide, F32)] + [resident(wide, BF16)] * 3 + [resident((rows, quarter), BF16)],
        x0, x1, x2, x3, gain, weight_in, begun,
        scratch=[pltpu.VMEM((rows, hidden), F32)], flops=work,
    )
    s1, s2, s3, cot, w_out = lax.optimization_barrier((s1, s2, s3, cot, w_out))
    s2, sent = lax.optimization_barrier((s2, sent))
    g3 = flip(s3, "section", 3)
    g2 = flip(s2, "section", 2)
    g1 = flip(s1, "section", 1)
    weight_out, cot = load(w_out[0], cot)
    act, slope, hid, scale = local(
        functools.partial(act_kernel, width),
        [resident((rows, piece), F32), resident((rows, piece), F32), resident((rows, piece), BF16), resident((rows, 1), F32)],
        own, g1, g2, g3,
    )

    spread_outs = [resident((rows, piece), F32)] + [resident((rows, piece), BF16)] * 3 + [resident((rows, quarter), BF16)]

    def gather_hidden(block):
        return [block] + [flip(block, "section", j) for j in (1, 2, 3)]

    if layers == 1:
        hids = gather_hidden(hid)
    for phase in range(layers):
        final = phase == layers - 1
        if phase == 0:
            own, s1, s2, s3, dy = local(spread_first_kernel, spread_outs, cot, sent, weight_out, flops=work)
        else:
            d0, d1, d2, d3 = down
            d3, hids = lax.optimization_barrier((d3, hids))
            total = [resident((rows, hidden), F32)]
            step = functools.partial(spread_next_kernel, layers)
            begun = local(functools.partial(step, (0,), True, False), total, d0, dy, weight_out, flops=work // 4)
            begun = local(functools.partial(step, (1, 2), False, False), total, d1, d2, dy, weight_out, *begun, flops=work // 2)
            own, s1, s2, s3, dy = local(
                functools.partial(step, (3,), False, True), spread_outs, d3, dy, weight_out, *begun, d0, d1, d2,
                scratch=[pltpu.VMEM((rows, hidden), F32)], flops=work // 4,
            )
        g3 = flip(s3, "section", 3)
        g2 = flip(s2, "section", 2)
        g1 = flip(s1, "section", 1)
        if final:
            grad_out = gradient(grad_out_kernel, (hidden, quarter), (piece, quarter), *hids, dy, flops=work)
            own, grad_out = lax.optimization_barrier((own, grad_out))
        (pay,) = local(dact_kernel, [resident(wide, BF16)], own, g1, g2, g3, act, slope)
        p3 = flip(pay, "section", 3)
        p2 = flip(pay, "section", 2)
        p1 = flip(pay, "section", 1)
        total = [resident((rows, quarter), F32)]
        begun = local(functools.partial(back_kernel, (0,), True), total, pay, weight_in, flops=work // 4)
        begun = local(functools.partial(back_kernel, (3, 2), False), total, p3, p2, weight_in, *begun, flops=work // 2)
        keep, send = local(
            back_last_kernel,
            [resident((rows + SIDE, 2 * share), F32), resident((rows + SIDE, 2 * share), BF16)],
            pay, p1, p2, p3, weight_in, *begun,
            scratch=[pltpu.VMEM((rows, quarter), F32)], flops=work // 4,
        )
        got = flip(send, "dp", 1)
        rest, send = local(
            middle_kernel,
            [resident((rows + SIDE, share), F32), resident((rows + SIDE, share), BF16)],
            keep, got,
        )
        if phase == 0 and not final:
            send, hid = lax.optimization_barrier((send, hid))
            hids = gather_hidden(hid)
        got = flip(send, "dp", 2)
        if final:
            grad_in = gradient(
                grad_in_kernel, (quarter, hidden), (quarter, piece), pay, p1, p2, p3, x_full, gain, scale,
                scratch=[pltpu.VMEM((rows, quarter), BF16)], flops=work,
            )
            got, grad_in = lax.optimization_barrier((got, grad_in))
        outs = [resident((rows, share), BF16)]
        if final:
            outs = [jax.ShapeDtypeStruct((rows, share), BF16), jax.ShapeDtypeStruct((1, share), F32)]
        finished = local(functools.partial(finish_kernel, width), outs, rest, got, x0, dy, gain, scale)
        if not final:
            d0 = lax.ppermute(finished[0], "section", [(i, i - 4) for i in range(4, sections)])
            d2 = flip(d0, "dp", 2)
            d1 = flip(d0, "dp", 1)
            d3 = flip(d2, "dp", 1)
            down = (d0, d1, d2, d3)

    grad_x, grad_gain = finished
    return grad_in[None], grad_out[None], grad_gain, grad_x.reshape(1, micro, tok, share)


def shards(checkpoints, gain, w_in, w_out, cotangent):
    rows = checkpoints.shape[1] * checkpoints.shape[2]
    share = checkpoints.shape[3]
    piece = w_in.shape[2] // 4
    if lax.axis_size("dp") == 4 and rows % 16 == 0 and share % 128 == 0 and piece % 128 == 0 and rows <= min(share, piece):
        return shards_of_four(checkpoints, gain, w_in, w_out, cotangent)
    return shards_of_any(checkpoints, gain, w_in, w_out, cotangent)


def solution(mesh):
    in_specs = (
        P("section", None, None, "dp"),
        P("section", None),
        P("section", None, "dp"),
        P("section", "dp", None),
        P(None, None, "dp"),
    )
    out_specs = (
        P("section", None, "dp"),
        P("section", "dp", None),
        P("section", "dp"),
        P("section", None, None, "dp"),
    )
    return jax.shard_map(shards, mesh=mesh, in_specs=in_specs, out_specs=out_specs, check_vma=False)
```

```python
import functools

import jax
import jax.numpy as jnp
from jax import lax
from jax.experimental import pallas as pl
from jax.experimental.pallas import tpu as pltpu
from jax.sharding import PartitionSpec as P

F32 = jnp.float32
BF16 = jnp.bfloat16


def flip(block, axis, bits):
    count = lax.axis_size(axis)
    return lax.ppermute(block, axis, [(i, i ^ bits) for i in range(count)])


def side_rows(values, width):
    lead = values.astype(BF16)
    trail = (values - lead.astype(F32)).astype(BF16)
    flat = jnp.concatenate([lead, trail])
    return jnp.pad(flat, (0, 16 * width - flat.shape[0])).reshape(16, width)


def side_values(rows, count):
    flat = rows.reshape(-1)
    return flat[:count].astype(F32) + flat[count:2 * count].astype(F32)


def gelu_tanh(value):
    return jax.nn.gelu(value, approximate=True)


def shards_of_any(checkpoints, gain, w_in, w_out, cotangent):
    sections = lax.axis_size("section")
    n_dp = lax.axis_size("dp")
    here = lax.axis_index("section")
    lane = lax.axis_index("dp")
    layers = sections // 4
    mine = here % 4
    last = here // 4 == layers - 1
    _, micro, tok, share = checkpoints.shape
    rows = micro * tok
    quarter = share * n_dp
    width = 4 * quarter
    gain_row = gain[0]
    weight_in = w_in[0]
    weight_out = w_out[0]
    hidden = weight_in.shape[1]
    piece = hidden // 4
    core = lane % 2

    def gather_dp(block):
        bit = n_dp // 2
        parts = {0: block}
        while bit >= 1:
            other = flip(jnp.concatenate([parts[j] for j in parts], axis=1), "dp", bit)
            for at, j in enumerate(list(parts)):
                parts[j ^ bit] = other[:, at * block.shape[1]:(at + 1) * block.shape[1]]
            bit //= 2
        full = jnp.zeros((rows, quarter), block.dtype)
        for j, part in parts.items():
            full = lax.dynamic_update_slice(full, part, (0, (lane ^ j) * block.shape[1]))
        return full

    def cot_quarter(block):
        if n_dp < 4:
            whole = lax.all_gather(block, "dp", axis=1, tiled=True)
            return lax.dynamic_slice_in_dim(whole, mine * quarter, quarter, 1)
        per = n_dp // 4
        top = [s * n_dp + d for s in range(sections) for d in range(n_dp) if s // 4 == layers - 1]
        held = block
        far = lambda i, b: (i % n_dp // per ^ i // n_dp % 4) & b
        got = lax.ppermute(held, ("section", "dp"), [(i, i ^ 2 * per) for i in top if far(i, 3) == 0])
        held = jnp.where((lane // per ^ mine) & 2 == 0, held, got)
        got = lax.ppermute(held, ("section", "dp"), [(i, i ^ per) for i in top if far(i, 1) == 0])
        held = jnp.where((lane // per ^ mine) & 1 == 0, held, got)
        if per == 1:
            return held
        parts = {0: held}
        bit = per // 2
        while bit >= 1:
            for j in list(parts):
                parts[j ^ bit] = flip(parts[j], "dp", bit)
            bit //= 2
        full = jnp.zeros((rows, quarter), block.dtype)
        for j, part in parts.items():
            full = lax.dynamic_update_slice(full, part, (0, (lane % per ^ j) * block.shape[1]))
        return full

    def cut(values, j):
        return lax.dynamic_slice_in_dim(values, (mine ^ j) * piece, piece, 1)

    def fill(parts):
        full = jnp.zeros((rows, hidden), parts[0].dtype)
        for j, part in enumerate(parts):
            full = lax.dynamic_update_slice(full, part, (0, (mine ^ j) * piece))
        return full

    x_full = gather_dp(checkpoints[0].reshape(rows, share))
    cot = cot_quarter(cotangent.reshape(rows, cotangent.shape[2]))
    x_wide = x_full.astype(F32)
    scaled_raw = (x_wide * gain_row).astype(BF16)
    squares = jnp.sum(x_wide * x_wide, axis=1)

    act_raw = jnp.dot(scaled_raw, weight_in, preferred_element_type=F32)
    extra = side_rows(squares, piece)
    act = cut(act_raw, 0)
    for j in (3, 1, 2):
        got = flip(jnp.concatenate([cut(act_raw, j).astype(BF16), extra], axis=0), "section", j)
        act = act + got[:rows].astype(F32)
        squares = squares + side_values(got[rows:], rows)
    scale = lax.rsqrt(squares / width + 1e-06)[:, None]
    act = act * scale
    hid, pull = jax.vjp(gelu_tanh, act)
    hid = hid.astype(BF16)
    hid_full = fill([hid] + [flip(hid, "section", j) for j in (1, 2, 3)])
    normed = x_wide * scale
    scaled = (normed * gain_row).astype(BF16)

    def halves(values, side):
        pairs = values.reshape(rows, n_dp // 2, 2, share)
        return jnp.where(side == 0, pairs[:, :, 0], pairs[:, :, 1]).reshape(rows, quarter // 2)

    def own(values):
        return lax.dynamic_slice_in_dim(values, lane // 2 * share, share, 1)

    incoming = jnp.zeros((rows, quarter), BF16)
    normed_half = halves(normed, core)
    gain_half = halves(jnp.broadcast_to(gain_row, (rows, quarter)), core)
    for phase in range(layers):
        final = phase == layers - 1
        dy = jnp.where(last, cot, incoming) if phase > 0 else cot
        dhid_raw = jnp.dot(dy, weight_out.T, preferred_element_type=F32)
        dhid = cut(dhid_raw, 0)
        for j in (3, 1, 2):
            dhid = dhid + flip(cut(dhid_raw, j).astype(BF16), "section", j).astype(F32)
        dact = pull(dhid)[0].astype(BF16)
        inner = jnp.sum(dact.astype(F32) * act, axis=1)
        payload = jnp.concatenate([dact, side_rows(inner, piece)], axis=0)
        others = [flip(payload, "section", j) for j in (1, 2, 3)]
        for got in others:
            inner = inner + side_values(got[rows:], rows)
        dact_full = fill([dact] + [got[:rows] for got in others])
        part = jnp.dot(dact_full, weight_in.T, preferred_element_type=F32).astype(BF16)

        send = jnp.concatenate([halves(part, 1 - core), side_rows(inner, quarter // 2)], axis=0)
        got = flip(send, "dp", 1)
        dscaled = halves(part, core).astype(F32) + got[:rows].astype(F32)
        inner = inner + side_values(got[rows:], rows)
        bit = 2
        while bit < n_dp:
            send = jnp.concatenate([dscaled.astype(BF16), side_rows(inner, quarter // 2)], axis=0)
            got = flip(send, "dp", bit)
            dscaled = dscaled + got[:rows].astype(F32)
            inner = inner + side_values(got[rows:], rows)
            bit *= 2
        dnorm = dscaled * gain_half
        dy_half = halves(dy, core).astype(F32)
        grad_x = (dy_half + scale * (dnorm - normed_half * (inner / width)[:, None])).astype(BF16)
        if not final:
            down = lax.ppermute(grad_x, "section", [(i, i - 4) for i in range(4, sections)])
            other = flip(down, "dp", 1)
            pairs = jnp.where(
                core == 0,
                jnp.stack([down.reshape(rows, n_dp // 2, share), other.reshape(rows, n_dp // 2, share)], axis=2),
                jnp.stack([other.reshape(rows, n_dp // 2, share), down.reshape(rows, n_dp // 2, share)], axis=2),
            )
            incoming = pairs.reshape(rows, quarter)

    grad_out = jnp.dot(hid_full.T, dy, preferred_element_type=F32).astype(BF16)
    grad_in = jnp.dot(scaled.T, dact_full, preferred_element_type=F32).astype(BF16)
    grad_gain = jnp.sum(own(dscaled) * own(normed_half), axis=0)
    return (
        grad_in[None],
        grad_out[None],
        grad_gain[None],
        own(grad_x).reshape(1, micro, tok, share),
    )


SIDE = 16
GELU_IN = 0.7978845608028654
GELU_CUBE = 0.044715


def resident(shape, dtype):
    return pltpu.VMEM(shape, dtype)


def local(body, outs, *args, scratch=(), flops=0):
    spec = pl.BlockSpec(memory_space=pltpu.VMEM)
    moved = sum(a.size * a.dtype.itemsize for a in args)
    return pl.pallas_call(
        body,
        out_shape=tuple(outs),
        in_specs=[spec] * len(args),
        out_specs=tuple(spec for _ in outs),
        scratch_shapes=list(scratch),
        compiler_params=pltpu.CompilerParams(vmem_limit_bytes=16 * 1024 * 1024),
        cost_estimate=pl.CostEstimate(flops=flops, bytes_accessed=moved, transcendentals=0),
    )(*args)


def diagonal(rows, width):
    return lax.broadcasted_iota(jnp.int32, (rows, width), 0) == lax.broadcasted_iota(jnp.int32, (rows, width), 1)


def as_row(column, width):
    rows = column.shape[0]
    return jnp.sum(jnp.where(diagonal(rows, width), column, 0.0), axis=0, keepdims=True)


def as_column(row, rows):
    return jnp.sum(jnp.where(diagonal(rows, row.shape[1]), row, 0.0), axis=1, keepdims=True)


def side_block(row):
    lead = row.astype(BF16).astype(F32)
    at = lax.broadcasted_iota(jnp.int32, (SIDE, row.shape[1]), 0)
    return jnp.where(at == 0, lead, jnp.where(at == 1, row - lead, 0.0)).astype(BF16)


def side_row(block):
    wide = block.astype(F32)
    return wide[0:1] + wide[1:2]


def load_kernel(*refs):
    count = len(refs) // 2
    copies = [pltpu.make_async_copy(refs[i], refs[count + i], refs[-1].at[i]) for i in range(count)]
    for copy in copies:
        copy.start()
    for copy in copies:
        copy.wait()


def load(*arrays):
    return pl.pallas_call(
        load_kernel,
        out_shape=tuple(resident(a.shape, a.dtype) for a in arrays),
        in_specs=[pl.BlockSpec(memory_space=pl.ANY)] * len(arrays),
        out_specs=tuple(pl.BlockSpec(memory_space=pltpu.VMEM) for _ in arrays),
        scratch_shapes=[pltpu.SemaphoreType.DMA((len(arrays),))],
        compiler_params=pltpu.CompilerParams(vmem_limit_bytes=1024 * 1024),
        cost_estimate=pl.CostEstimate(flops=0, bytes_accessed=sum(2 * a.size * a.dtype.itemsize for a in arrays), transcendentals=0),
    )(*(pltpu.with_memory_space_constraint(a, pltpu.HBM) for a in arrays))


def place():
    return lax.axis_index("section") % 4, lax.axis_index("dp")


def dot_nt(left, right):
    return lax.dot_general(left, right, (((1,), (1,)), ((), ())), preferred_element_type=F32)


def dot_tn(left, right):
    return lax.dot_general(left, right, (((0,), (0,)), ((), ())), preferred_element_type=F32)


def slot(index, size):
    return pl.ds(pl.multiple_of(index * size, size), size)


def spread_in_part(part, at, gain, weight, mine, total, begin):
    share = part.shape[1]
    piece = weight.shape[1] // 4
    scaled = (part[...].astype(F32) * gain[:, slot(at, share)]).astype(BF16)
    for d in (3, 2, 1, 0):
        block = jnp.dot(scaled, weight[slot(at, share), slot(mine ^ d, piece)], preferred_element_type=F32)
        columns = slice(d * piece, (d + 1) * piece)
        total[:, columns] = block if begin else total[:, columns] + block


def square_sum(part):
    wide = part[...].astype(F32)
    return jnp.sum(wide * wide, axis=1, keepdims=True)


def spread_in_first_kernel(x0, x1, gain, weight, total):
    mine, lane = place()
    spread_in_part(x0, lane, gain, weight, mine, total, True)
    spread_in_part(x1, lane ^ 1, gain, weight, mine, total, False)


def spread_in_last_kernel(x0, x1, x2, x3, gain, weight, before, own, s1, s2, s3, x_full, total):
    mine, lane = place()
    rows, share = x0.shape
    piece = own.shape[1]
    total[...] = before[...]
    spread_in_part(x2, lane ^ 2, gain, weight, mine, total, False)
    spread_in_part(x3, lane ^ 3, gain, weight, mine, total, False)
    row = as_row(square_sum(x0) + square_sum(x1) + square_sum(x2) + square_sum(x3), piece)
    block = side_block(row)
    for d, out in ((3, s3), (2, s2), (1, s1)):
        out[:rows] = total[:, d * piece:(d + 1) * piece].astype(BF16)
        out[rows:] = block
    own[:rows] = total[:, :piece]
    own[rows:] = jnp.broadcast_to(row, (SIDE, piece))
    for d, part in enumerate((x0, x1, x2, x3)):
        x_full[:, slot(lane ^ d, share)] = part[...]


def spread_dy(dy, weight, mine, own, s1, s2, s3):
    piece = own.shape[1]
    for d, out in ((3, s3), (2, s2), (1, s1)):
        out[...] = dot_nt(dy[...], weight[slot(mine ^ d, piece), :]).astype(BF16)
    own[...] = dot_nt(dy[...], weight[slot(mine, piece), :])


def spread_first_kernel(cot, sent, weight, own, s1, s2, s3, dy):
    mine, lane = place()

    @pl.when(lane == mine)
    def _():
        dy[...] = cot[...]

    @pl.when(lane != mine)
    def _():
        dy[...] = sent[...]

    spread_dy(dy, weight, mine, own, s1, s2, s3)


def spread_next_kernel(layers, ds, begin, end, *refs):
    parts, refs = refs[:len(ds)], refs[len(ds):]
    before, weight = refs[:2]
    refs = refs[2:]
    mine, lane = place()
    rows, share = parts[0].shape
    piece = weight.shape[0] // 4
    last = lax.axis_index("section") // 4 == layers - 1
    if begin:
        (total,) = refs
    elif end:
        earlier, *others, own, s1, s2, s3, dy, total = refs
        total[...] = earlier[...]
    else:
        earlier, total = refs
        total[...] = earlier[...]
    for i, (d, part) in enumerate(zip(ds, parts)):
        at = slot(lane ^ d, share)
        value = jnp.where(last, before[:, at], part[...])
        for j in (3, 2, 1, 0):
            block = dot_nt(value, weight[slot(mine ^ j, piece), at])
            columns = slice(j * piece, (j + 1) * piece)
            total[:, columns] = block if begin and i == 0 else total[:, columns] + block
    if end:
        for j, out in ((3, s3), (2, s2), (1, s1)):
            out[...] = total[:, j * piece:(j + 1) * piece].astype(BF16)
        own[...] = total[:, :piece]
        done = [d for d in range(4) if d not in ds]

        @pl.when(last)
        def _():
            dy[...] = before[...]

        @pl.when(jnp.logical_not(last))
        def _():
            for d, part in zip((*done, *ds), (*others, *parts)):
                dy[:, slot(lane ^ d, share)] = part[...]


def act_kernel(width, own, g1, g2, g3, act, slope, hid, scale):
    rows = act.shape[0]
    row = own[rows:rows + 1] + side_row(g1[rows:]) + side_row(g2[rows:]) + side_row(g3[rows:])
    r = lax.rsqrt(as_column(row, rows) / width + 1e-06)
    scale[...] = r
    a = (own[:rows] + g1[:rows].astype(F32) + g2[:rows].astype(F32) + g3[:rows].astype(F32)) * r
    act[...] = a
    square = a * a
    t = jnp.tanh(GELU_IN * (a + GELU_CUBE * (square * a)))
    half = 0.5 * (1.0 + t)
    hid[...] = (a * half).astype(BF16)
    slope[...] = half + 0.5 * a * (1.0 - t * t) * (GELU_IN * (1.0 + 3.0 * GELU_CUBE * square))


def dact_kernel(own, g1, g2, g3, act, slope, pay):
    rows, piece = own.shape
    dhid = own[...] + g1[...].astype(F32) + g2[...].astype(F32) + g3[...].astype(F32)
    da = (dhid * slope[...]).astype(BF16)
    pay[:rows] = da
    pay[rows:] = side_block(as_row(jnp.sum(da.astype(F32) * act[...], axis=1, keepdims=True), piece))


def back_part(part, j, weight, mine, lane, total, begin):
    rows = total.shape[0]
    piece = part.shape[1]
    share = weight.shape[0] // 4
    for d in (1, 3, 0, 2):
        block = dot_nt(part[:rows], weight[slot(lane ^ d, share), slot(mine ^ j, piece)])
        columns = slice(d * share, (d + 1) * share)
        total[:, columns] = block if begin else total[:, columns] + block


def back_kernel(js, begin, *refs):
    *parts, weight = refs[:len(js) + 1]
    *earlier, total = refs[len(js) + 1:]
    mine, lane = place()
    if not begin:
        total[...] = earlier[0][...]
    for i, (j, part) in enumerate(zip(js, parts)):
        back_part(part, j, weight, mine, lane, total, begin and i == 0)


def back_last_kernel(p0, p1, p2, p3, weight, earlier, keep, send, total):
    mine, lane = place()
    rows = total.shape[0]
    share = weight.shape[0] // 4
    total[...] = earlier[...]
    back_part(p1, 1, weight, mine, lane, total, False)
    row = side_row(p0[rows:]) + side_row(p1[rows:]) + side_row(p2[rows:]) + side_row(p3[rows:])
    for at, d in ((0, 1), (1, 3)):
        send[:rows, at * share:(at + 1) * share] = total[:, d * share:(d + 1) * share].astype(BF16)
    send[rows:] = side_block(row)
    for at, d in ((0, 0), (1, 2)):
        keep[:rows, at * share:(at + 1) * share] = total[:, d * share:(d + 1) * share]
    keep[rows:] = jnp.broadcast_to(row, (SIDE, keep.shape[1]))


def middle_kernel(keep, got, rest, send):
    rows = keep.shape[0] - SIDE
    share = rest.shape[1]
    row = (keep[rows:rows + 1] + side_row(got[rows:]))[:, :share]
    send[:rows] = (keep[:rows, share:] + got[:rows, share:].astype(F32)).astype(BF16)
    send[rows:] = side_block(row)
    rest[:rows] = keep[:rows, :share] + got[:rows, :share].astype(F32)
    rest[rows:] = jnp.broadcast_to(row, (SIDE, share))


def finish_kernel(width, rest, got, x_own, dy, gain, scale, grad_x, *grad_gain):
    _, lane = place()
    rows, share = x_own.shape
    at = slot(lane, share)
    r = scale[...]
    du = rest[:rows] + got[:rows].astype(F32)
    normed = x_own[...].astype(F32) * r
    inner = as_column(rest[rows:rows + 1] + side_row(got[rows:]), rows) / width
    dnorm = du * gain[:, at]
    grad_x[...] = (dy[:, at].astype(F32) + r * (dnorm - normed * inner)).astype(BF16)
    if grad_gain:
        grad_gain[0][...] = jnp.sum(du * normed, axis=0, keepdims=True)


def grad_out_kernel(h0, h1, h2, h3, dy, out, held, sems):
    mine, _ = place()
    piece = h0.shape[1]
    copies = []
    for d, part in enumerate((h0, h1, h2, h3)):
        held[d] = dot_tn(part[...], dy[...]).astype(BF16)
        copies.append(pltpu.make_async_copy(held.at[d], out.at[slot(mine ^ d, piece), :], sems.at[d]))
        copies[-1].start()
    for copy in copies:
        copy.wait()


def grad_in_kernel(p0, p1, p2, p3, x_full, gain, scale, out, scaled, held, sems):
    mine, _ = place()
    rows = x_full.shape[0]
    piece = p0.shape[1]
    scaled[...] = (x_full[...].astype(F32) * scale[...] * gain[...]).astype(BF16)
    copies = []
    for d, part in enumerate((p0, p1, p2, p3)):
        held[d] = dot_tn(scaled[...], part[:rows]).astype(BF16)
        copies.append(pltpu.make_async_copy(held.at[d], out.at[:, slot(mine ^ d, piece)], sems.at[d]))
        copies[-1].start()
    for copy in copies:
        copy.wait()


def gradient(body, shape, block, *args, scratch=(), flops=0):
    return pl.pallas_call(
        body,
        out_shape=jax.ShapeDtypeStruct(shape, BF16),
        in_specs=[pl.BlockSpec(memory_space=pltpu.VMEM)] * len(args),
        out_specs=pl.BlockSpec(memory_space=pl.ANY),
        scratch_shapes=[*scratch, pltpu.VMEM((4,) + block, BF16), pltpu.SemaphoreType.DMA((4,))],
        compiler_params=pltpu.CompilerParams(vmem_limit_bytes=16 * 1024 * 1024),
        cost_estimate=pl.CostEstimate(flops=flops, bytes_accessed=2 * shape[0] * shape[1], transcendentals=0),
    )(*args)


def shards_of_four(checkpoints, gain, w_in, w_out, cotangent):
    sections = lax.axis_size("section")
    here = lax.axis_index("section")
    lane = lax.axis_index("dp")
    layers = sections // 4
    mine = here % 4
    _, micro, tok, share = checkpoints.shape
    rows = micro * tok
    quarter = share * 4
    width = 4 * quarter
    hidden = w_in.shape[2]
    piece = hidden // 4
    work = 2 * rows * quarter * hidden

    x0 = checkpoints[0].reshape(rows, share)
    cot = cotangent.reshape(rows, quarter)
    top = [s * 4 + d for s in range(sections) for d in range(4) if s // 4 == layers - 1]
    x2 = flip(x0, "dp", 2)
    x1 = flip(x0, "dp", 1)
    weight_in, x0, gain = load(w_in[0], x0, gain)
    x2, x1, weight_in = lax.optimization_barrier((x2, x1, weight_in))
    sent = lax.ppermute(cot, ("section", "dp"), [((i // 4 ^ near) * 4 + i // 4 % 4, i) for i in top for near in (1, 0, 2) if i // 4 % 4 ^ i % 4 == (2, 1, 3)[near]])
    x3 = flip(x2, "dp", 1)

    wide = (rows + SIDE, piece)
    (begun,) = local(spread_in_first_kernel, [resident((rows, hidden), F32)], x0, x1, gain, weight_in, flops=work)
    own, s1, s2, s3, x_full = local(
        spread_in_last_kernel,
        [resident(wide, F32)] + [resident(wide, BF16)] * 3 + [resident((rows, quarter), BF16)],
        x0, x1, x2, x3, gain, weight_in, begun,
        scratch=[pltpu.VMEM((rows, hidden), F32)], flops=work,
    )
    s1, s2, s3, cot, w_out = lax.optimization_barrier((s1, s2, s3, cot, w_out))
    g3 = flip(s3, "section", 3)
    g2 = flip(s2, "section", 2)
    g1 = flip(s1, "section", 1)
    weight_out, cot = load(w_out[0], cot)
    act, slope, hid, scale = local(
        functools.partial(act_kernel, width),
        [resident((rows, piece), F32), resident((rows, piece), F32), resident((rows, piece), BF16), resident((rows, 1), F32)],
        own, g3, g2, g1,
    )

    spread_outs = [resident((rows, piece), F32)] + [resident((rows, piece), BF16)] * 3 + [resident((rows, quarter), BF16)]

    def gather_hidden(block):
        return [block] + [flip(block, "section", j) for j in (1, 2, 3)]

    if layers == 1:
        hids = gather_hidden(hid)
    for phase in range(layers):
        final = phase == layers - 1
        if phase == 0:
            own, s1, s2, s3, dy = local(spread_first_kernel, spread_outs, cot, sent, weight_out, flops=work)
        else:
            d0, d1, d2, d3 = down
            first, hids = lax.optimization_barrier((d0, hids))
            total = [resident((rows, hidden), F32)]
            step = functools.partial(spread_next_kernel, layers)
            begun = local(functools.partial(step, (0,), True, False), total, first, dy, weight_out, flops=work // 4)
            begun = local(functools.partial(step, (1, 2), False, False), total, d1, d2, dy, weight_out, *begun, flops=work // 2)
            own, s1, s2, s3, dy = local(
                functools.partial(step, (3,), False, True), spread_outs, d3, dy, weight_out, *begun, d0, d1, d2,
                scratch=[pltpu.VMEM((rows, hidden), F32)], flops=work // 4,
            )
        g3 = flip(s3, "section", 3)
        g2 = flip(s2, "section", 2)
        g1 = flip(s1, "section", 1)
        if final:
            grad_out = gradient(grad_out_kernel, (hidden, quarter), (piece, quarter), *hids, dy, flops=work)
            own, grad_out = lax.optimization_barrier((own, grad_out))
        (pay,) = local(dact_kernel, [resident(wide, BF16)], own, g3, g2, g1, act, slope)
        p3 = flip(pay, "section", 3)
        p2 = flip(pay, "section", 2)
        p1 = flip(pay, "section", 1)
        total = [resident((rows, quarter), F32)]
        begun = local(functools.partial(back_kernel, (0,), True), total, pay, weight_in, flops=work // 4)
        begun = local(functools.partial(back_kernel, (3, 2), False), total, p3, p2, weight_in, *begun, flops=work // 2)
        keep, send = local(
            back_last_kernel,
            [resident((rows + SIDE, 2 * share), F32), resident((rows + SIDE, 2 * share), BF16)],
            pay, p1, p2, p3, weight_in, *begun,
            scratch=[pltpu.VMEM((rows, quarter), F32)], flops=work // 4,
        )
        got = flip(send, "dp", 1)
        rest, send = local(
            middle_kernel,
            [resident((rows + SIDE, share), F32), resident((rows + SIDE, share), BF16)],
            keep, got,
        )
        if phase == 0 and not final:
            send, hid = lax.optimization_barrier((send, hid))
            hids = gather_hidden(hid)
        got = flip(send, "dp", 2)
        if final:
            grad_in = gradient(
                grad_in_kernel, (quarter, hidden), (quarter, piece), pay, p1, p2, p3, x_full, gain, scale,
                scratch=[pltpu.VMEM((rows, quarter), BF16)], flops=work,
            )
            got, grad_in = lax.optimization_barrier((got, grad_in))
        outs = [resident((rows, share), BF16)]
        if final:
            outs = [jax.ShapeDtypeStruct((rows, share), BF16), jax.ShapeDtypeStruct((1, share), F32)]
        finished = local(functools.partial(finish_kernel, width), outs, rest, got, x0, dy, gain, scale)
        if not final:
            d0 = lax.ppermute(finished[0], "section", [(i, i - 4) for i in range(4, sections)])
            d2 = flip(d0, "dp", 2)
            d1 = flip(d0, "dp", 1)
            d3 = flip(d2, "dp", 1)
            down = (d0, d1, d2, d3)

    grad_x, grad_gain = finished
    return grad_in[None], grad_out[None], grad_gain, grad_x.reshape(1, micro, tok, share)


def shards(checkpoints, gain, w_in, w_out, cotangent):
    rows = checkpoints.shape[1] * checkpoints.shape[2]
    share = checkpoints.shape[3]
    piece = w_in.shape[2] // 4
    if lax.axis_size("dp") == 4 and rows % 16 == 0 and share % 128 == 0 and piece % 128 == 0 and rows <= min(share, piece):
        return shards_of_four(checkpoints, gain, w_in, w_out, cotangent)
    return shards_of_any(checkpoints, gain, w_in, w_out, cotangent)


def solution(mesh):
    in_specs = (
        P("section", None, None, "dp"),
        P("section", None),
        P("section", None, "dp"),
        P("section", "dp", None),
        P(None, None, "dp"),
    )
    out_specs = (
        P("section", None, "dp"),
        P("section", "dp", None),
        P("section", "dp"),
        P("section", None, None, "dp"),
    )
    return jax.shard_map(shards, mesh=mesh, in_specs=in_specs, out_specs=out_specs, check_vma=False)
```

```python
import functools

import jax
import jax.numpy as jnp
from jax import lax
from jax.experimental import pallas as pl
from jax.experimental.pallas import tpu as pltpu
from jax.sharding import PartitionSpec as P

F32 = jnp.float32
BF16 = jnp.bfloat16


def flip(block, axis, bits):
    count = lax.axis_size(axis)
    return lax.ppermute(block, axis, [(i, i ^ bits) for i in range(count)])


def side_rows(values, width):
    lead = values.astype(BF16)
    trail = (values - lead.astype(F32)).astype(BF16)
    flat = jnp.concatenate([lead, trail])
    return jnp.pad(flat, (0, 16 * width - flat.shape[0])).reshape(16, width)


def side_values(rows, count):
    flat = rows.reshape(-1)
    return flat[:count].astype(F32) + flat[count:2 * count].astype(F32)


def gelu_tanh(value):
    return jax.nn.gelu(value, approximate=True)


def shards_of_any(checkpoints, gain, w_in, w_out, cotangent):
    sections = lax.axis_size("section")
    n_dp = lax.axis_size("dp")
    here = lax.axis_index("section")
    lane = lax.axis_index("dp")
    layers = sections // 4
    mine = here % 4
    last = here // 4 == layers - 1
    _, micro, tok, share = checkpoints.shape
    rows = micro * tok
    quarter = share * n_dp
    width = 4 * quarter
    gain_row = gain[0]
    weight_in = w_in[0]
    weight_out = w_out[0]
    hidden = weight_in.shape[1]
    piece = hidden // 4
    core = lane % 2

    def gather_dp(block):
        bit = n_dp // 2
        parts = {0: block}
        while bit >= 1:
            other = flip(jnp.concatenate([parts[j] for j in parts], axis=1), "dp", bit)
            for at, j in enumerate(list(parts)):
                parts[j ^ bit] = other[:, at * block.shape[1]:(at + 1) * block.shape[1]]
            bit //= 2
        full = jnp.zeros((rows, quarter), block.dtype)
        for j, part in parts.items():
            full = lax.dynamic_update_slice(full, part, (0, (lane ^ j) * block.shape[1]))
        return full

    def cot_quarter(block):
        if n_dp < 4:
            whole = lax.all_gather(block, "dp", axis=1, tiled=True)
            return lax.dynamic_slice_in_dim(whole, mine * quarter, quarter, 1)
        per = n_dp // 4
        top = [s * n_dp + d for s in range(sections) for d in range(n_dp) if s // 4 == layers - 1]
        held = block
        far = lambda i, b: (i % n_dp // per ^ i // n_dp % 4) & b
        got = lax.ppermute(held, ("section", "dp"), [(i, i ^ 2 * per) for i in top if far(i, 3) == 0])
        held = jnp.where((lane // per ^ mine) & 2 == 0, held, got)
        got = lax.ppermute(held, ("section", "dp"), [(i, i ^ per) for i in top if far(i, 1) == 0])
        held = jnp.where((lane // per ^ mine) & 1 == 0, held, got)
        if per == 1:
            return held
        parts = {0: held}
        bit = per // 2
        while bit >= 1:
            for j in list(parts):
                parts[j ^ bit] = flip(parts[j], "dp", bit)
            bit //= 2
        full = jnp.zeros((rows, quarter), block.dtype)
        for j, part in parts.items():
            full = lax.dynamic_update_slice(full, part, (0, (lane % per ^ j) * block.shape[1]))
        return full

    def cut(values, j):
        return lax.dynamic_slice_in_dim(values, (mine ^ j) * piece, piece, 1)

    def fill(parts):
        full = jnp.zeros((rows, hidden), parts[0].dtype)
        for j, part in enumerate(parts):
            full = lax.dynamic_update_slice(full, part, (0, (mine ^ j) * piece))
        return full

    x_full = gather_dp(checkpoints[0].reshape(rows, share))
    cot = cot_quarter(cotangent.reshape(rows, cotangent.shape[2]))
    x_wide = x_full.astype(F32)
    scaled_raw = (x_wide * gain_row).astype(BF16)
    squares = jnp.sum(x_wide * x_wide, axis=1)

    act_raw = jnp.dot(scaled_raw, weight_in, preferred_element_type=F32)
    extra = side_rows(squares, piece)
    act = cut(act_raw, 0)
    for j in (3, 1, 2):
        got = flip(jnp.concatenate([cut(act_raw, j).astype(BF16), extra], axis=0), "section", j)
        act = act + got[:rows].astype(F32)
        squares = squares + side_values(got[rows:], rows)
    scale = lax.rsqrt(squares / width + 1e-06)[:, None]
    act = act * scale
    hid, pull = jax.vjp(gelu_tanh, act)
    hid = hid.astype(BF16)
    hid_full = fill([hid] + [flip(hid, "section", j) for j in (1, 2, 3)])
    normed = x_wide * scale
    scaled = (normed * gain_row).astype(BF16)

    def halves(values, side):
        pairs = values.reshape(rows, n_dp // 2, 2, share)
        return jnp.where(side == 0, pairs[:, :, 0], pairs[:, :, 1]).reshape(rows, quarter // 2)

    def own(values):
        return lax.dynamic_slice_in_dim(values, lane // 2 * share, share, 1)

    incoming = jnp.zeros((rows, quarter), BF16)
    normed_half = halves(normed, core)
    gain_half = halves(jnp.broadcast_to(gain_row, (rows, quarter)), core)
    for phase in range(layers):
        final = phase == layers - 1
        dy = jnp.where(last, cot, incoming) if phase > 0 else cot
        dhid_raw = jnp.dot(dy, weight_out.T, preferred_element_type=F32)
        dhid = cut(dhid_raw, 0)
        for j in (3, 1, 2):
            dhid = dhid + flip(cut(dhid_raw, j).astype(BF16), "section", j).astype(F32)
        dact = pull(dhid)[0].astype(BF16)
        inner = jnp.sum(dact.astype(F32) * act, axis=1)
        payload = jnp.concatenate([dact, side_rows(inner, piece)], axis=0)
        others = [flip(payload, "section", j) for j in (1, 2, 3)]
        for got in others:
            inner = inner + side_values(got[rows:], rows)
        dact_full = fill([dact] + [got[:rows] for got in others])
        part = jnp.dot(dact_full, weight_in.T, preferred_element_type=F32).astype(BF16)

        send = jnp.concatenate([halves(part, 1 - core), side_rows(inner, quarter // 2)], axis=0)
        got = flip(send, "dp", 1)
        dscaled = halves(part, core).astype(F32) + got[:rows].astype(F32)
        inner = inner + side_values(got[rows:], rows)
        bit = 2
        while bit < n_dp:
            send = jnp.concatenate([dscaled.astype(BF16), side_rows(inner, quarter // 2)], axis=0)
            got = flip(send, "dp", bit)
            dscaled = dscaled + got[:rows].astype(F32)
            inner = inner + side_values(got[rows:], rows)
            bit *= 2
        dnorm = dscaled * gain_half
        dy_half = halves(dy, core).astype(F32)
        grad_x = (dy_half + scale * (dnorm - normed_half * (inner / width)[:, None])).astype(BF16)
        if not final:
            down = lax.ppermute(grad_x, "section", [(i, i - 4) for i in range(4, sections)])
            other = flip(down, "dp", 1)
            pairs = jnp.where(
                core == 0,
                jnp.stack([down.reshape(rows, n_dp // 2, share), other.reshape(rows, n_dp // 2, share)], axis=2),
                jnp.stack([other.reshape(rows, n_dp // 2, share), down.reshape(rows, n_dp // 2, share)], axis=2),
            )
            incoming = pairs.reshape(rows, quarter)

    grad_out = jnp.dot(hid_full.T, dy, preferred_element_type=F32).astype(BF16)
    grad_in = jnp.dot(scaled.T, dact_full, preferred_element_type=F32).astype(BF16)
    grad_gain = jnp.sum(own(dscaled) * own(normed_half), axis=0)
    return (
        grad_in[None],
        grad_out[None],
        grad_gain[None],
        own(grad_x).reshape(1, micro, tok, share),
    )


SIDE = 16
GELU_IN = 0.7978845608028654
GELU_CUBE = 0.044715


def resident(shape, dtype):
    return pltpu.VMEM(shape, dtype)


def local(body, outs, *args, scratch=(), flops=0):
    spec = pl.BlockSpec(memory_space=pltpu.VMEM)
    moved = sum(a.size * a.dtype.itemsize for a in args)
    return pl.pallas_call(
        body,
        out_shape=tuple(outs),
        in_specs=[spec] * len(args),
        out_specs=tuple(spec for _ in outs),
        scratch_shapes=list(scratch),
        compiler_params=pltpu.CompilerParams(vmem_limit_bytes=16 * 1024 * 1024),
        cost_estimate=pl.CostEstimate(flops=flops, bytes_accessed=moved, transcendentals=0),
    )(*args)


def diagonal(rows, width):
    return lax.broadcasted_iota(jnp.int32, (rows, width), 0) == lax.broadcasted_iota(jnp.int32, (rows, width), 1)


def as_row(column, width):
    rows = column.shape[0]
    return jnp.sum(jnp.where(diagonal(rows, width), column, 0.0), axis=0, keepdims=True)


def as_column(row, rows):
    return jnp.sum(jnp.where(diagonal(rows, row.shape[1]), row, 0.0), axis=1, keepdims=True)


def side_block(row):
    lead = row.astype(BF16).astype(F32)
    at = lax.broadcasted_iota(jnp.int32, (SIDE, row.shape[1]), 0)
    return jnp.where(at == 0, lead, jnp.where(at == 1, row - lead, 0.0)).astype(BF16)


def side_row(block):
    wide = block.astype(F32)
    return wide[0:1] + wide[1:2]


def load_parts(array):
    parts = 8 if array.shape[0] * array.shape[1] * array.dtype.itemsize >= 2 ** 20 and array.shape[0] % 128 == 0 else 1
    count = array.shape[0] // parts
    return [pl.ds(i * count, count) for i in range(parts)]


def load_kernel(*refs):
    count = len(refs) // 2
    pairs = [(refs[i].at[at], refs[count + i].at[at]) for i in range(count) for at in load_parts(refs[i])]
    copies = [pltpu.make_async_copy(source, held, refs[-1].at[i]) for i, (source, held) in enumerate(pairs)]
    for copy in copies:
        copy.start()
    for copy in copies:
        copy.wait()


def load(*arrays):
    return pl.pallas_call(
        load_kernel,
        out_shape=tuple(resident(a.shape, a.dtype) for a in arrays),
        in_specs=[pl.BlockSpec(memory_space=pl.ANY)] * len(arrays),
        out_specs=tuple(pl.BlockSpec(memory_space=pltpu.VMEM) for _ in arrays),
        scratch_shapes=[pltpu.SemaphoreType.DMA((sum(len(load_parts(a)) for a in arrays),))],
        compiler_params=pltpu.CompilerParams(vmem_limit_bytes=1024 * 1024),
        cost_estimate=pl.CostEstimate(flops=0, bytes_accessed=sum(2 * a.size * a.dtype.itemsize for a in arrays), transcendentals=0),
    )(*(pltpu.with_memory_space_constraint(a, pltpu.HBM) for a in arrays))


def place():
    return lax.axis_index("section") % 4, lax.axis_index("dp")


def dot_nt(left, right):
    return lax.dot_general(left, right, (((1,), (1,)), ((), ())), preferred_element_type=F32)


def dot_tn(left, right):
    return lax.dot_general(left, right, (((0,), (0,)), ((), ())), preferred_element_type=F32)


def slot(index, size):
    return pl.ds(pl.multiple_of(index * size, size), size)


def spread_in_part(part, at, gain, weight, mine, total, begin):
    share = part.shape[1]
    piece = weight.shape[1] // 4
    scaled = (part[...].astype(F32) * gain[:, slot(at, share)]).astype(BF16)
    for d in (3, 2, 1, 0):
        block = jnp.dot(scaled, weight[slot(at, share), slot(mine ^ d, piece)], preferred_element_type=F32)
        columns = slice(d * piece, (d + 1) * piece)
        total[:, columns] = block if begin else total[:, columns] + block


def square_sum(part):
    wide = part[...].astype(F32)
    return jnp.sum(wide * wide, axis=1, keepdims=True)


def spread_in_first_kernel(x0, x1, gain, weight, total):
    mine, lane = place()
    spread_in_part(x0, lane, gain, weight, mine, total, True)
    spread_in_part(x1, lane ^ 1, gain, weight, mine, total, False)


def spread_in_last_kernel(x0, x1, x2, x3, gain, weight, before, own, s1, s2, s3, x_full, total):
    mine, lane = place()
    rows, share = x0.shape
    piece = own.shape[1]
    total[...] = before[...]
    spread_in_part(x2, lane ^ 2, gain, weight, mine, total, False)
    spread_in_part(x3, lane ^ 3, gain, weight, mine, total, False)
    row = as_row(square_sum(x0) + square_sum(x1) + square_sum(x2) + square_sum(x3), piece)
    block = side_block(row)
    for d, out in ((3, s3), (2, s2), (1, s1)):
        out[:rows] = total[:, d * piece:(d + 1) * piece].astype(BF16)
        out[rows:] = block
    own[:rows] = total[:, :piece]
    own[rows:] = jnp.broadcast_to(row, (SIDE, piece))
    for d, part in enumerate((x0, x1, x2, x3)):
        x_full[:, slot(lane ^ d, share)] = part[...]


def spread_dy(dy, weight, mine, own, s1, s2, s3):
    piece = own.shape[1]
    for d, out in ((3, s3), (2, s2), (1, s1)):
        out[...] = dot_nt(dy[...], weight[slot(mine ^ d, piece), :]).astype(BF16)
    own[...] = dot_nt(dy[...], weight[slot(mine, piece), :])


def spread_first_kernel(cot, sent, weight, own, s1, s2, s3, dy):
    mine, lane = place()

    @pl.when(lane == mine)
    def _():
        dy[...] = cot[...]

    @pl.when(lane != mine)
    def _():
        dy[...] = sent[...]

    spread_dy(dy, weight, mine, own, s1, s2, s3)


def spread_next_kernel(layers, ds, begin, end, *refs):
    parts, refs = refs[:len(ds)], refs[len(ds):]
    before, weight = refs[:2]
    refs = refs[2:]
    mine, lane = place()
    rows, share = parts[0].shape
    piece = weight.shape[0] // 4
    last = lax.axis_index("section") // 4 == layers - 1
    if begin:
        (total,) = refs
    elif end:
        earlier, *others, own, s1, s2, s3, dy, total = refs
        total[...] = earlier[...]
    else:
        earlier, total = refs
        total[...] = earlier[...]
    for i, (d, part) in enumerate(zip(ds, parts)):
        at = slot(lane ^ d, share)
        value = jnp.where(last, before[:, at], part[...])
        for j in (3, 2, 1, 0):
            block = dot_nt(value, weight[slot(mine ^ j, piece), at])
            columns = slice(j * piece, (j + 1) * piece)
            total[:, columns] = block if begin and i == 0 else total[:, columns] + block
    if end:
        for j, out in ((3, s3), (2, s2), (1, s1)):
            out[...] = total[:, j * piece:(j + 1) * piece].astype(BF16)
        own[...] = total[:, :piece]
        done = [d for d in range(4) if d not in ds]

        @pl.when(last)
        def _():
            dy[...] = before[...]

        @pl.when(jnp.logical_not(last))
        def _():
            for d, part in zip((*done, *ds), (*others, *parts)):
                dy[:, slot(lane ^ d, share)] = part[...]


def act_kernel(width, own, g1, g2, g3, act, slope, hid, scale):
    rows = act.shape[0]
    row = own[rows:rows + 1] + side_row(g1[rows:]) + side_row(g2[rows:]) + side_row(g3[rows:])
    r = lax.rsqrt(as_column(row, rows) / width + 1e-06)
    scale[...] = r
    a = (own[:rows] + g1[:rows].astype(F32) + g2[:rows].astype(F32) + g3[:rows].astype(F32)) * r
    act[...] = a
    square = a * a
    t = jnp.tanh(GELU_IN * (a + GELU_CUBE * (square * a)))
    half = 0.5 * (1.0 + t)
    hid[...] = (a * half).astype(BF16)
    slope[...] = half + 0.5 * a * (1.0 - t * t) * (GELU_IN * (1.0 + 3.0 * GELU_CUBE * square))


def dact_kernel(own, g1, g2, g3, act, slope, pay):
    rows, piece = own.shape
    dhid = own[...] + g1[...].astype(F32) + g2[...].astype(F32) + g3[...].astype(F32)
    da = (dhid * slope[...]).astype(BF16)
    pay[:rows] = da
    pay[rows:] = side_block(as_row(jnp.sum(da.astype(F32) * act[...], axis=1, keepdims=True), piece))


def back_part(part, j, weight, mine, lane, total, begin):
    rows = total.shape[0]
    piece = part.shape[1]
    share = weight.shape[0] // 4
    for d in (1, 3, 0, 2):
        block = dot_nt(part[:rows], weight[slot(lane ^ d, share), slot(mine ^ j, piece)])
        columns = slice(d * share, (d + 1) * share)
        total[:, columns] = block if begin else total[:, columns] + block


def back_kernel(js, begin, *refs):
    *parts, weight = refs[:len(js) + 1]
    *earlier, total = refs[len(js) + 1:]
    mine, lane = place()
    if not begin:
        total[...] = earlier[0][...]
    for i, (j, part) in enumerate(zip(js, parts)):
        back_part(part, j, weight, mine, lane, total, begin and i == 0)


def back_last_kernel(p0, p1, p2, p3, weight, earlier, keep, send, total):
    mine, lane = place()
    rows = total.shape[0]
    share = weight.shape[0] // 4
    total[...] = earlier[...]
    back_part(p1, 1, weight, mine, lane, total, False)
    row = side_row(p0[rows:]) + side_row(p1[rows:]) + side_row(p2[rows:]) + side_row(p3[rows:])
    for at, d in ((0, 1), (1, 3)):
        send[:rows, at * share:(at + 1) * share] = total[:, d * share:(d + 1) * share].astype(BF16)
    send[rows:] = side_block(row)
    for at, d in ((0, 0), (1, 2)):
        keep[:rows, at * share:(at + 1) * share] = total[:, d * share:(d + 1) * share]
    keep[rows:] = jnp.broadcast_to(row, (SIDE, keep.shape[1]))


def middle_kernel(keep, got, rest, send):
    rows = keep.shape[0] - SIDE
    share = rest.shape[1]
    row = (keep[rows:rows + 1] + side_row(got[rows:]))[:, :share]
    send[:rows] = (keep[:rows, share:] + got[:rows, share:].astype(F32)).astype(BF16)
    send[rows:] = side_block(row)
    rest[:rows] = keep[:rows, :share] + got[:rows, :share].astype(F32)
    rest[rows:] = jnp.broadcast_to(row, (SIDE, share))


def finish_kernel(width, rest, got, x_own, dy, gain, scale, grad_x, *grad_gain):
    _, lane = place()
    rows, share = x_own.shape
    at = slot(lane, share)
    r = scale[...]
    du = rest[:rows] + got[:rows].astype(F32)
    normed = x_own[...].astype(F32) * r
    inner = as_column(rest[rows:rows + 1] + side_row(got[rows:]), rows) / width
    dnorm = du * gain[:, at]
    grad_x[...] = (dy[:, at].astype(F32) + r * (dnorm - normed * inner)).astype(BF16)
    if grad_gain:
        grad_gain[0][...] = jnp.sum(du * normed, axis=0, keepdims=True)


def grad_out_kernel(h0, h1, h2, h3, dy, out, held, sems):
    mine, _ = place()
    piece = h0.shape[1]
    copies = []
    for d, part in enumerate((h0, h1, h2, h3)):
        held[d] = dot_tn(part[...], dy[...]).astype(BF16)
        copies.append(pltpu.make_async_copy(held.at[d], out.at[slot(mine ^ d, piece), :], sems.at[d]))
        copies[-1].start()
    for copy in copies:
        copy.wait()


def grad_in_kernel(p0, p1, p2, p3, x_full, gain, scale, out, scaled, held, sems):
    mine, _ = place()
    rows = x_full.shape[0]
    piece = p0.shape[1]
    scaled[...] = (x_full[...].astype(F32) * scale[...] * gain[...]).astype(BF16)
    copies = []
    for d, part in enumerate((p0, p1, p2, p3)):
        held[d] = dot_tn(scaled[...], part[:rows]).astype(BF16)
        copies.append(pltpu.make_async_copy(held.at[d], out.at[:, slot(mine ^ d, piece)], sems.at[d]))
        copies[-1].start()
    for copy in copies:
        copy.wait()


def gradient(body, shape, block, *args, scratch=(), flops=0):
    return pl.pallas_call(
        body,
        out_shape=jax.ShapeDtypeStruct(shape, BF16),
        in_specs=[pl.BlockSpec(memory_space=pltpu.VMEM)] * len(args),
        out_specs=pl.BlockSpec(memory_space=pl.ANY),
        scratch_shapes=[*scratch, pltpu.VMEM((4,) + block, BF16), pltpu.SemaphoreType.DMA((4,))],
        compiler_params=pltpu.CompilerParams(vmem_limit_bytes=16 * 1024 * 1024),
        cost_estimate=pl.CostEstimate(flops=flops, bytes_accessed=2 * shape[0] * shape[1], transcendentals=0),
    )(*args)


def shards_of_four(checkpoints, gain, w_in, w_out, cotangent):
    sections = lax.axis_size("section")
    here = lax.axis_index("section")
    lane = lax.axis_index("dp")
    layers = sections // 4
    mine = here % 4
    _, micro, tok, share = checkpoints.shape
    rows = micro * tok
    quarter = share * 4
    width = 4 * quarter
    hidden = w_in.shape[2]
    piece = hidden // 4
    work = 2 * rows * quarter * hidden

    x0 = checkpoints[0].reshape(rows, share)
    cot = cotangent.reshape(rows, quarter)
    top = [s * 4 + d for s in range(sections) for d in range(4) if s // 4 == layers - 1]
    x2 = flip(x0, "dp", 2)
    x1 = flip(x0, "dp", 1)
    weight_in, x0, gain = load(w_in[0], x0, gain)
    x2, x1, weight_in = lax.optimization_barrier((x2, x1, weight_in))
    sent = lax.ppermute(cot, ("section", "dp"), [((i // 4 ^ near) * 4 + i // 4 % 4, i) for i in top for near in (1, 0, 2) if i // 4 % 4 ^ i % 4 == (2, 1, 3)[near]])
    x3 = flip(x2, "dp", 1)

    wide = (rows + SIDE, piece)
    (begun,) = local(spread_in_first_kernel, [resident((rows, hidden), F32)], x0, x1, gain, weight_in, flops=work)
    own, s1, s2, s3, x_full = local(
        spread_in_last_kernel,
        [resident(wide, F32)] + [resident(wide, BF16)] * 3 + [resident((rows, quarter), BF16)],
        x0, x1, x2, x3, gain, weight_in, begun,
        scratch=[pltpu.VMEM((rows, hidden), F32)], flops=4 * work,
    )
    s1, s2, s3, cot, w_out = lax.optimization_barrier((s1, s2, s3, cot, w_out))
    g3 = flip(s3, "section", 3)
    g2 = flip(s2, "section", 2)
    g1 = flip(s1, "section", 1)
    weight_out, cot = load(w_out[0], cot)
    act, slope, hid, scale = local(
        functools.partial(act_kernel, width),
        [resident((rows, piece), F32), resident((rows, piece), F32), resident((rows, piece), BF16), resident((rows, 1), F32)],
        own, g1, g2, g3,
    )

    spread_outs = [resident((rows, piece), F32)] + [resident((rows, piece), BF16)] * 3 + [resident((rows, quarter), BF16)]

    def gather_hidden(block):
        return [block] + [flip(block, "section", j) for j in (1, 2, 3)]

    if layers == 1:
        hids = gather_hidden(hid)
    for phase in range(layers):
        final = phase == layers - 1
        if phase == 0:
            own, s1, s2, s3, dy = local(spread_first_kernel, spread_outs, cot, sent, weight_out, flops=work)
        else:
            d0, d1, d2, d3 = down
            first, hids = lax.optimization_barrier((d0, hids))
            total = [resident((rows, hidden), F32)]
            step = functools.partial(spread_next_kernel, layers)
            begun = local(functools.partial(step, (0,), True, False), total, first, dy, weight_out, flops=work // 4)
            begun = local(functools.partial(step, (1, 2), False, False), total, d1, d2, dy, weight_out, *begun, flops=work // 2)
            own, s1, s2, s3, dy = local(
                functools.partial(step, (3,), False, True), spread_outs, d3, dy, weight_out, *begun, d0, d1, d2,
                scratch=[pltpu.VMEM((rows, hidden), F32)], flops=work // 4,
            )
        g3 = flip(s3, "section", 3)
        g2 = flip(s2, "section", 2)
        g1 = flip(s1, "section", 1)
        if final:
            grad_out = gradient(grad_out_kernel, (hidden, quarter), (piece, quarter), *hids, dy, flops=work)
            own, grad_out = lax.optimization_barrier((own, grad_out))
        (pay,) = local(dact_kernel, [resident(wide, BF16)], own, g1, g2, g3, act, slope)
        p3 = flip(pay, "section", 3)
        p2 = flip(pay, "section", 2)
        p1 = flip(pay, "section", 1)
        total = [resident((rows, quarter), F32)]
        begun = local(functools.partial(back_kernel, (0,), True), total, pay, weight_in, flops=work // 4)
        begun = local(functools.partial(back_kernel, (3, 2), False), total, p3, p2, weight_in, *begun, flops=work // 2)
        keep, send = local(
            back_last_kernel,
            [resident((rows + SIDE, 2 * share), F32), resident((rows + SIDE, 2 * share), BF16)],
            pay, p1, p2, p3, weight_in, *begun,
            scratch=[pltpu.VMEM((rows, quarter), F32)], flops=work // 4,
        )
        got = flip(send, "dp", 1)
        rest, send = local(
            middle_kernel,
            [resident((rows + SIDE, share), F32), resident((rows + SIDE, share), BF16)],
            keep, got,
        )
        if phase == 0 and not final:
            send, hid = lax.optimization_barrier((send, hid))
            hids = gather_hidden(hid)
        got = flip(send, "dp", 2)
        if final:
            grad_in = gradient(
                grad_in_kernel, (quarter, hidden), (quarter, piece), pay, p1, p2, p3, x_full, gain, scale,
                scratch=[pltpu.VMEM((rows, quarter), BF16)], flops=work,
            )
            got, grad_in = lax.optimization_barrier((got, grad_in))
        outs = [resident((rows, share), BF16)]
        if final:
            outs = [jax.ShapeDtypeStruct((rows, share), BF16), jax.ShapeDtypeStruct((1, share), F32)]
        finished = local(functools.partial(finish_kernel, width), outs, rest, got, x0, dy, gain, scale)
        if not final:
            d0 = lax.ppermute(finished[0], "section", [(i, i - 4) for i in range(4, sections)])
            d2 = flip(d0, "dp", 2)
            d1 = flip(d0, "dp", 1)
            d3 = flip(d2, "dp", 1)
            down = (d0, d1, d2, d3)

    grad_x, grad_gain = finished
    return grad_in[None], grad_out[None], grad_gain, grad_x.reshape(1, micro, tok, share)


def shards(checkpoints, gain, w_in, w_out, cotangent):
    rows = checkpoints.shape[1] * checkpoints.shape[2]
    share = checkpoints.shape[3]
    piece = w_in.shape[2] // 4
    if lax.axis_size("dp") == 4 and rows % 16 == 0 and share % 128 == 0 and piece % 128 == 0 and rows <= min(share, piece):
        return shards_of_four(checkpoints, gain, w_in, w_out, cotangent)
    return shards_of_any(checkpoints, gain, w_in, w_out, cotangent)


def solution(mesh):
    in_specs = (
        P("section", None, None, "dp"),
        P("section", None),
        P("section", None, "dp"),
        P("section", "dp", None),
        P(None, None, "dp"),
    )
    out_specs = (
        P("section", None, "dp"),
        P("section", "dp", None),
        P("section", "dp"),
        P("section", None, None, "dp"),
    )
    return jax.shard_map(shards, mesh=mesh, in_specs=in_specs, out_specs=out_specs, check_vma=False)
```

```python
import functools

import jax
import jax.numpy as jnp
from jax import lax
from jax.experimental import pallas as pl
from jax.experimental.pallas import tpu as pltpu
from jax.sharding import PartitionSpec as P

F32 = jnp.float32
BF16 = jnp.bfloat16


def flip(block, axis, bits):
    count = lax.axis_size(axis)
    return lax.ppermute(block, axis, [(i, i ^ bits) for i in range(count)])


def side_rows(values, width):
    lead = values.astype(BF16)
    trail = (values - lead.astype(F32)).astype(BF16)
    flat = jnp.concatenate([lead, trail])
    return jnp.pad(flat, (0, 16 * width - flat.shape[0])).reshape(16, width)


def side_values(rows, count):
    flat = rows.reshape(-1)
    return flat[:count].astype(F32) + flat[count:2 * count].astype(F32)


def gelu_tanh(value):
    return jax.nn.gelu(value, approximate=True)


def shards_of_any(checkpoints, gain, w_in, w_out, cotangent):
    sections = lax.axis_size("section")
    n_dp = lax.axis_size("dp")
    here = lax.axis_index("section")
    lane = lax.axis_index("dp")
    layers = sections // 4
    mine = here % 4
    last = here // 4 == layers - 1
    _, micro, tok, share = checkpoints.shape
    rows = micro * tok
    quarter = share * n_dp
    width = 4 * quarter
    gain_row = gain[0]
    weight_in = w_in[0]
    weight_out = w_out[0]
    hidden = weight_in.shape[1]
    piece = hidden // 4
    core = lane % 2

    def gather_dp(block):
        bit = n_dp // 2
        parts = {0: block}
        while bit >= 1:
            other = flip(jnp.concatenate([parts[j] for j in parts], axis=1), "dp", bit)
            for at, j in enumerate(list(parts)):
                parts[j ^ bit] = other[:, at * block.shape[1]:(at + 1) * block.shape[1]]
            bit //= 2
        full = jnp.zeros((rows, quarter), block.dtype)
        for j, part in parts.items():
            full = lax.dynamic_update_slice(full, part, (0, (lane ^ j) * block.shape[1]))
        return full

    def cot_quarter(block):
        if n_dp < 4:
            whole = lax.all_gather(block, "dp", axis=1, tiled=True)
            return lax.dynamic_slice_in_dim(whole, mine * quarter, quarter, 1)
        per = n_dp // 4
        top = [s * n_dp + d for s in range(sections) for d in range(n_dp) if s // 4 == layers - 1]
        held = block
        far = lambda i, b: (i % n_dp // per ^ i // n_dp % 4) & b
        got = lax.ppermute(held, ("section", "dp"), [(i, i ^ 2 * per) for i in top if far(i, 3) == 0])
        held = jnp.where((lane // per ^ mine) & 2 == 0, held, got)
        got = lax.ppermute(held, ("section", "dp"), [(i, i ^ per) for i in top if far(i, 1) == 0])
        held = jnp.where((lane // per ^ mine) & 1 == 0, held, got)
        if per == 1:
            return held
        parts = {0: held}
        bit = per // 2
        while bit >= 1:
            for j in list(parts):
                parts[j ^ bit] = flip(parts[j], "dp", bit)
            bit //= 2
        full = jnp.zeros((rows, quarter), block.dtype)
        for j, part in parts.items():
            full = lax.dynamic_update_slice(full, part, (0, (lane % per ^ j) * block.shape[1]))
        return full

    def cut(values, j):
        return lax.dynamic_slice_in_dim(values, (mine ^ j) * piece, piece, 1)

    def fill(parts):
        full = jnp.zeros((rows, hidden), parts[0].dtype)
        for j, part in enumerate(parts):
            full = lax.dynamic_update_slice(full, part, (0, (mine ^ j) * piece))
        return full

    x_full = gather_dp(checkpoints[0].reshape(rows, share))
    cot = cot_quarter(cotangent.reshape(rows, cotangent.shape[2]))
    x_wide = x_full.astype(F32)
    scaled_raw = (x_wide * gain_row).astype(BF16)
    squares = jnp.sum(x_wide * x_wide, axis=1)

    act_raw = jnp.dot(scaled_raw, weight_in, preferred_element_type=F32)
    extra = side_rows(squares, piece)
    act = cut(act_raw, 0)
    for j in (3, 1, 2):
        got = flip(jnp.concatenate([cut(act_raw, j).astype(BF16), extra], axis=0), "section", j)
        act = act + got[:rows].astype(F32)
        squares = squares + side_values(got[rows:], rows)
    scale = lax.rsqrt(squares / width + 1e-06)[:, None]
    act = act * scale
    hid, pull = jax.vjp(gelu_tanh, act)
    hid = hid.astype(BF16)
    hid_full = fill([hid] + [flip(hid, "section", j) for j in (1, 2, 3)])
    normed = x_wide * scale
    scaled = (normed * gain_row).astype(BF16)

    def halves(values, side):
        pairs = values.reshape(rows, n_dp // 2, 2, share)
        return jnp.where(side == 0, pairs[:, :, 0], pairs[:, :, 1]).reshape(rows, quarter // 2)

    def own(values):
        return lax.dynamic_slice_in_dim(values, lane // 2 * share, share, 1)

    incoming = jnp.zeros((rows, quarter), BF16)
    normed_half = halves(normed, core)
    gain_half = halves(jnp.broadcast_to(gain_row, (rows, quarter)), core)
    for phase in range(layers):
        final = phase == layers - 1
        dy = jnp.where(last, cot, incoming) if phase > 0 else cot
        dhid_raw = jnp.dot(dy, weight_out.T, preferred_element_type=F32)
        dhid = cut(dhid_raw, 0)
        for j in (3, 1, 2):
            dhid = dhid + flip(cut(dhid_raw, j).astype(BF16), "section", j).astype(F32)
        dact = pull(dhid)[0].astype(BF16)
        inner = jnp.sum(dact.astype(F32) * act, axis=1)
        payload = jnp.concatenate([dact, side_rows(inner, piece)], axis=0)
        others = [flip(payload, "section", j) for j in (1, 2, 3)]
        for got in others:
            inner = inner + side_values(got[rows:], rows)
        dact_full = fill([dact] + [got[:rows] for got in others])
        part = jnp.dot(dact_full, weight_in.T, preferred_element_type=F32).astype(BF16)

        send = jnp.concatenate([halves(part, 1 - core), side_rows(inner, quarter // 2)], axis=0)
        got = flip(send, "dp", 1)
        dscaled = halves(part, core).astype(F32) + got[:rows].astype(F32)
        inner = inner + side_values(got[rows:], rows)
        bit = 2
        while bit < n_dp:
            send = jnp.concatenate([dscaled.astype(BF16), side_rows(inner, quarter // 2)], axis=0)
            got = flip(send, "dp", bit)
            dscaled = dscaled + got[:rows].astype(F32)
            inner = inner + side_values(got[rows:], rows)
            bit *= 2
        dnorm = dscaled * gain_half
        dy_half = halves(dy, core).astype(F32)
        grad_x = (dy_half + scale * (dnorm - normed_half * (inner / width)[:, None])).astype(BF16)
        if not final:
            down = lax.ppermute(grad_x, "section", [(i, i - 4) for i in range(4, sections)])
            other = flip(down, "dp", 1)
            pairs = jnp.where(
                core == 0,
                jnp.stack([down.reshape(rows, n_dp // 2, share), other.reshape(rows, n_dp // 2, share)], axis=2),
                jnp.stack([other.reshape(rows, n_dp // 2, share), down.reshape(rows, n_dp // 2, share)], axis=2),
            )
            incoming = pairs.reshape(rows, quarter)

    grad_out = jnp.dot(hid_full.T, dy, preferred_element_type=F32).astype(BF16)
    grad_in = jnp.dot(scaled.T, dact_full, preferred_element_type=F32).astype(BF16)
    grad_gain = jnp.sum(own(dscaled) * own(normed_half), axis=0)
    return (
        grad_in[None],
        grad_out[None],
        grad_gain[None],
        own(grad_x).reshape(1, micro, tok, share),
    )


SIDE = 16
GELU_IN = 0.7978845608028654
GELU_CUBE = 0.044715


def resident(shape, dtype):
    return pltpu.VMEM(shape, dtype)


def local(body, outs, *args, scratch=(), flops=0):
    spec = pl.BlockSpec(memory_space=pltpu.VMEM)
    moved = sum(a.size * a.dtype.itemsize for a in args)
    return pl.pallas_call(
        body,
        out_shape=tuple(outs),
        in_specs=[spec] * len(args),
        out_specs=tuple(spec for _ in outs),
        scratch_shapes=list(scratch),
        compiler_params=pltpu.CompilerParams(vmem_limit_bytes=16 * 1024 * 1024),
        cost_estimate=pl.CostEstimate(flops=flops, bytes_accessed=moved, transcendentals=0),
    )(*args)


def diagonal(rows, width):
    return lax.broadcasted_iota(jnp.int32, (rows, width), 0) == lax.broadcasted_iota(jnp.int32, (rows, width), 1)


def as_row(column, width):
    rows = column.shape[0]
    return jnp.sum(jnp.where(diagonal(rows, width), column, 0.0), axis=0, keepdims=True)


def as_column(row, rows):
    return jnp.sum(jnp.where(diagonal(rows, row.shape[1]), row, 0.0), axis=1, keepdims=True)


def side_block(row):
    lead = row.astype(BF16).astype(F32)
    at = lax.broadcasted_iota(jnp.int32, (SIDE, row.shape[1]), 0)
    return jnp.where(at == 0, lead, jnp.where(at == 1, row - lead, 0.0)).astype(BF16)


def side_row(block):
    wide = block.astype(F32)
    return wide[0:1] + wide[1:2]


def load_kernel(*refs):
    count = len(refs) // 2
    copies = [pltpu.make_async_copy(refs[i], refs[count + i], refs[-1].at[i]) for i in range(count)]
    for copy in copies:
        copy.start()
    for copy in copies:
        copy.wait()


def load(*arrays):
    return pl.pallas_call(
        load_kernel,
        out_shape=tuple(resident(a.shape, a.dtype) for a in arrays),
        in_specs=[pl.BlockSpec(memory_space=pl.ANY)] * len(arrays),
        out_specs=tuple(pl.BlockSpec(memory_space=pltpu.VMEM) for _ in arrays),
        scratch_shapes=[pltpu.SemaphoreType.DMA((len(arrays),))],
        compiler_params=pltpu.CompilerParams(vmem_limit_bytes=1024 * 1024),
        cost_estimate=pl.CostEstimate(flops=0, bytes_accessed=sum(2 * a.size * a.dtype.itemsize for a in arrays), transcendentals=0),
    )(*(pltpu.with_memory_space_constraint(a, pltpu.HBM) for a in arrays))


def place():
    return lax.axis_index("section") % 4, lax.axis_index("dp")


def dot_nt(left, right):
    return lax.dot_general(left, right, (((1,), (1,)), ((), ())), preferred_element_type=F32)


def dot_tn(left, right):
    return lax.dot_general(left, right, (((0,), (0,)), ((), ())), preferred_element_type=F32)


def slot(index, size):
    return pl.ds(pl.multiple_of(index * size, size), size)


def spread_in_part(part, at, gain, weight, mine, total, begin):
    share = part.shape[1]
    piece = weight.shape[1] // 4
    scaled = (part[...].astype(F32) * gain[:, slot(at, share)]).astype(BF16)
    for d in (3, 2, 1, 0):
        block = jnp.dot(scaled, weight[slot(at, share), slot(mine ^ d, piece)], preferred_element_type=F32)
        columns = slice(d * piece, (d + 1) * piece)
        total[:, columns] = block if begin else total[:, columns] + block


def square_sum(part):
    wide = part[...].astype(F32)
    return jnp.sum(wide * wide, axis=1, keepdims=True)


def spread_in_first_kernel(x0, x1, gain, weight, total):
    mine, lane = place()
    spread_in_part(x0, lane, gain, weight, mine, total, True)
    spread_in_part(x1, lane ^ 1, gain, weight, mine, total, False)


def spread_in_last_kernel(x0, x1, x2, x3, gain, weight, before, own, s1, s2, s3, x_full, total):
    mine, lane = place()
    rows, share = x0.shape
    piece = own.shape[1]
    total[...] = before[...]
    spread_in_part(x2, lane ^ 2, gain, weight, mine, total, False)
    spread_in_part(x3, lane ^ 3, gain, weight, mine, total, False)
    row = as_row(square_sum(x0) + square_sum(x1) + square_sum(x2) + square_sum(x3), piece)
    block = side_block(row)
    for d, out in ((3, s3), (2, s2), (1, s1)):
        out[:rows] = total[:, d * piece:(d + 1) * piece].astype(BF16)
        out[rows:] = block
    own[:rows] = total[:, :piece]
    own[rows:] = jnp.broadcast_to(row, (SIDE, piece))
    for d, part in enumerate((x0, x1, x2, x3)):
        x_full[:, slot(lane ^ d, share)] = part[...]


def spread_dy(dy, weight, mine, own, s1, s2, s3):
    piece = own.shape[1]
    for d, out in ((3, s3), (2, s2), (1, s1)):
        out[...] = dot_nt(dy[...], weight[slot(mine ^ d, piece), :]).astype(BF16)
    own[...] = dot_nt(dy[...], weight[slot(mine, piece), :])


def spread_first_kernel(cot, sent, weight, own, s1, s2, s3, dy):
    mine, lane = place()

    @pl.when(lane == mine)
    def _():
        dy[...] = cot[...]

    @pl.when(lane != mine)
    def _():
        dy[...] = sent[...]

    spread_dy(dy, weight, mine, own, s1, s2, s3)


def spread_next_kernel(layers, ds, begin, end, *refs):
    parts, refs = refs[:len(ds)], refs[len(ds):]
    before, weight = refs[:2]
    refs = refs[2:]
    mine, lane = place()
    rows, share = parts[0].shape
    piece = weight.shape[0] // 4
    last = lax.axis_index("section") // 4 == layers - 1
    if begin:
        (total,) = refs
    elif end:
        earlier, *others, own, s1, s2, s3, dy, total = refs
        total[...] = earlier[...]
    else:
        earlier, total = refs
        total[...] = earlier[...]
    for i, (d, part) in enumerate(zip(ds, parts)):
        at = slot(lane ^ d, share)
        value = jnp.where(last, before[:, at], part[...])
        for j in (3, 2, 1, 0):
            block = dot_nt(value, weight[slot(mine ^ j, piece), at])
            columns = slice(j * piece, (j + 1) * piece)
            total[:, columns] = block if begin and i == 0 else total[:, columns] + block
    if end:
        for j, out in ((3, s3), (2, s2), (1, s1)):
            out[...] = total[:, j * piece:(j + 1) * piece].astype(BF16)
        own[...] = total[:, :piece]
        done = [d for d in range(4) if d not in ds]

        @pl.when(last)
        def _():
            dy[...] = before[...]

        @pl.when(jnp.logical_not(last))
        def _():
            for d, part in zip((*done, *ds), (*others, *parts)):
                dy[:, slot(lane ^ d, share)] = part[...]


def act_kernel(width, own, g1, g2, g3, act, slope, hid, scale):
    rows = act.shape[0]
    row = own[rows:rows + 1] + side_row(g1[rows:]) + side_row(g2[rows:]) + side_row(g3[rows:])
    r = lax.rsqrt(as_column(row, rows) / width + 1e-06)
    scale[...] = r
    a = (own[:rows] + g1[:rows].astype(F32) + g2[:rows].astype(F32) + g3[:rows].astype(F32)) * r
    act[...] = a
    square = a * a
    t = jnp.tanh(GELU_IN * (a + GELU_CUBE * (square * a)))
    half = 0.5 * (1.0 + t)
    hid[...] = (a * half).astype(BF16)
    slope[...] = half + 0.5 * a * (1.0 - t * t) * (GELU_IN * (1.0 + 3.0 * GELU_CUBE * square))


def dact_kernel(own, g1, g2, g3, act, slope, pay):
    rows, piece = own.shape
    dhid = own[...] + g1[...].astype(F32) + g2[...].astype(F32) + g3[...].astype(F32)
    da = (dhid * slope[...]).astype(BF16)
    pay[:rows] = da
    pay[rows:] = side_block(as_row(jnp.sum(da.astype(F32) * act[...], axis=1, keepdims=True), piece))


def back_part(part, j, weight, mine, lane, total, begin):
    rows = total.shape[0]
    piece = part.shape[1]
    share = weight.shape[0] // 4
    for d in (1, 3, 0, 2):
        block = dot_nt(part[:rows], weight[slot(lane ^ d, share), slot(mine ^ j, piece)])
        columns = slice(d * share, (d + 1) * share)
        total[:, columns] = block if begin else total[:, columns] + block


def back_kernel(js, begin, *refs):
    *parts, weight = refs[:len(js) + 1]
    *earlier, total = refs[len(js) + 1:]
    mine, lane = place()
    if not begin:
        total[...] = earlier[0][...]
    for i, (j, part) in enumerate(zip(js, parts)):
        back_part(part, j, weight, mine, lane, total, begin and i == 0)


def back_last_kernel(p0, p1, p2, p3, weight, earlier, keep, send, total):
    mine, lane = place()
    rows = total.shape[0]
    share = weight.shape[0] // 4
    total[...] = earlier[...]
    back_part(p1, 1, weight, mine, lane, total, False)
    row = side_row(p0[rows:]) + side_row(p1[rows:]) + side_row(p2[rows:]) + side_row(p3[rows:])
    for at, d in ((0, 1), (1, 3)):
        send[:rows, at * share:(at + 1) * share] = total[:, d * share:(d + 1) * share].astype(BF16)
    send[rows:] = side_block(row)
    for at, d in ((0, 0), (1, 2)):
        keep[:rows, at * share:(at + 1) * share] = total[:, d * share:(d + 1) * share]
    keep[rows:] = jnp.broadcast_to(row, (SIDE, keep.shape[1]))


def middle_kernel(keep, got, rest, send):
    rows = keep.shape[0] - SIDE
    share = rest.shape[1]
    row = (keep[rows:rows + 1] + side_row(got[rows:]))[:, :share]
    send[:rows] = (keep[:rows, share:] + got[:rows, share:].astype(F32)).astype(BF16)
    send[rows:] = side_block(row)
    rest[:rows] = keep[:rows, :share] + got[:rows, :share].astype(F32)
    rest[rows:] = jnp.broadcast_to(row, (SIDE, share))


def finish_kernel(width, rest, got, x_own, dy, gain, scale, grad_x, *grad_gain):
    _, lane = place()
    rows, share = x_own.shape
    at = slot(lane, share)
    r = scale[...]
    du = rest[:rows] + got[:rows].astype(F32)
    normed = x_own[...].astype(F32) * r
    inner = as_column(rest[rows:rows + 1] + side_row(got[rows:]), rows) / width
    dnorm = du * gain[:, at]
    grad_x[...] = (dy[:, at].astype(F32) + r * (dnorm - normed * inner)).astype(BF16)
    if grad_gain:
        grad_gain[0][...] = jnp.sum(du * normed, axis=0, keepdims=True)


def grad_out_kernel(h0, h1, h2, h3, dy, out, held, sems):
    mine, _ = place()
    piece = h0.shape[1]
    copies = []
    for d, part in enumerate((h0, h1, h2, h3)):
        held[d] = dot_tn(part[...], dy[...]).astype(BF16)
        copies.append(pltpu.make_async_copy(held.at[d], out.at[slot(mine ^ d, piece), :], sems.at[d]))
        copies[-1].start()
    for copy in copies:
        copy.wait()


def grad_in_kernel(p0, p1, p2, p3, x_full, gain, scale, out, scaled, held, sems):
    mine, _ = place()
    rows = x_full.shape[0]
    piece = p0.shape[1]
    scaled[...] = (x_full[...].astype(F32) * scale[...] * gain[...]).astype(BF16)
    copies = []
    for d, part in enumerate((p0, p1, p2, p3)):
        held[d] = dot_tn(scaled[...], part[:rows]).astype(BF16)
        copies.append(pltpu.make_async_copy(held.at[d], out.at[:, slot(mine ^ d, piece)], sems.at[d]))
        copies[-1].start()
    for copy in copies:
        copy.wait()


def gradient(body, shape, block, *args, scratch=(), flops=0):
    return pl.pallas_call(
        body,
        out_shape=jax.ShapeDtypeStruct(shape, BF16),
        in_specs=[pl.BlockSpec(memory_space=pltpu.VMEM)] * len(args),
        out_specs=pl.BlockSpec(memory_space=pl.ANY),
        scratch_shapes=[*scratch, pltpu.VMEM((4,) + block, BF16), pltpu.SemaphoreType.DMA((4,))],
        compiler_params=pltpu.CompilerParams(vmem_limit_bytes=16 * 1024 * 1024),
        cost_estimate=pl.CostEstimate(flops=flops, bytes_accessed=2 * shape[0] * shape[1], transcendentals=0),
    )(*args)


def shards_of_four(checkpoints, gain, w_in, w_out, cotangent):
    sections = lax.axis_size("section")
    here = lax.axis_index("section")
    lane = lax.axis_index("dp")
    layers = sections // 4
    mine = here % 4
    _, micro, tok, share = checkpoints.shape
    rows = micro * tok
    quarter = share * 4
    width = 4 * quarter
    hidden = w_in.shape[2]
    piece = hidden // 4
    work = 2 * rows * quarter * hidden

    x0 = checkpoints[0].reshape(rows, share)
    cot = cotangent.reshape(rows, quarter)
    top = [s * 4 + d for s in range(sections) for d in range(4) if s // 4 == layers - 1]
    x2 = flip(x0, "dp", 2)
    x1 = flip(x0, "dp", 1)
    weight_in, x0, gain = load(w_in[0], x0, gain)
    x2, x1, weight_in = lax.optimization_barrier((x2, x1, weight_in))
    sent = lax.ppermute(cot, ("section", "dp"), [((i // 4 ^ near) * 4 + i // 4 % 4, i) for i in top for near in (1, 0, 2) if i // 4 % 4 ^ i % 4 == (2, 1, 3)[near]])
    x3 = flip(x2, "dp", 1)

    wide = (rows + SIDE, piece)
    (begun,) = local(spread_in_first_kernel, [resident((rows, hidden), F32)], x0, x1, gain, weight_in, flops=work)
    own, s1, s2, s3, x_full = local(
        spread_in_last_kernel,
        [resident(wide, F32)] + [resident(wide, BF16)] * 3 + [resident((rows, quarter), BF16)],
        x0, x1, x2, x3, gain, weight_in, begun,
        scratch=[pltpu.VMEM((rows, hidden), F32)], flops=work,
    )
    s1, s2, s3, cot, w_out = lax.optimization_barrier((s1, s2, s3, cot, w_out))
    g3 = flip(s3, "section", 3)
    g2 = flip(s2, "section", 2)
    g1 = flip(s1, "section", 1)
    weight_out, cot = load(w_out[0], cot)
    act, slope, hid, scale = local(
        functools.partial(act_kernel, width),
        [resident((rows, piece), F32), resident((rows, piece), F32), resident((rows, piece), BF16), resident((rows, 1), F32)],
        own, g1, g2, g3,
    )

    spread_outs = [resident((rows, piece), F32)] + [resident((rows, piece), BF16)] * 3 + [resident((rows, quarter), BF16)]

    def gather_hidden(block):
        return [block] + [flip(block, "section", j) for j in (1, 2, 3)]

    if layers == 1:
        hids = gather_hidden(hid)
    for phase in range(layers):
        final = phase == layers - 1
        if phase == 0:
            own, s1, s2, s3, dy = local(spread_first_kernel, spread_outs, cot, sent, weight_out, flops=work)
        else:
            d0, d1, d2, d3 = down
            first, hids = lax.optimization_barrier((d0, hids))
            total = [resident((rows, hidden), F32)]
            step = functools.partial(spread_next_kernel, layers)
            begun = local(functools.partial(step, (0,), True, False), total, first, dy, weight_out, flops=work // 4)
            begun = local(functools.partial(step, (1, 2), False, False), total, d1, d2, dy, weight_out, *begun, flops=work // 2)
            own, s1, s2, s3, dy = local(
                functools.partial(step, (3,), False, True), spread_outs, d3, dy, weight_out, *begun, d0, d1, d2,
                scratch=[pltpu.VMEM((rows, hidden), F32)], flops=work // 4,
            )
        g3 = flip(s3, "section", 3)
        g2 = flip(s2, "section", 2)
        g1 = flip(s1, "section", 1)
        if final:
            grad_out = gradient(grad_out_kernel, (hidden, quarter), (piece, quarter), *hids, dy, flops=work)
            own, grad_out = lax.optimization_barrier((own, grad_out))
        (pay,) = local(dact_kernel, [resident(wide, BF16)], own, g1, g2, g3, act, slope)
        p3 = flip(pay, "section", 3)
        p2 = flip(pay, "section", 2)
        p1 = flip(pay, "section", 1)
        total = [resident((rows, quarter), F32)]
        begun = local(functools.partial(back_kernel, (0,), True), total, pay, weight_in, flops=work // 4)
        begun = local(functools.partial(back_kernel, (3, 2), False), total, p3, p2, weight_in, *begun, flops=work // 2)
        keep, send = local(
            back_last_kernel,
            [resident((rows + SIDE, 2 * share), F32), resident((rows + SIDE, 2 * share), BF16)],
            pay, p1, p2, p3, weight_in, *begun,
            scratch=[pltpu.VMEM((rows, quarter), F32)], flops=work // 4,
        )
        got = flip(send, "dp", 1)
        rest, send = local(
            middle_kernel,
            [resident((rows + SIDE, share), F32), resident((rows + SIDE, share), BF16)],
            keep, got,
        )
        if phase == 0 and not final:
            send, hid = lax.optimization_barrier((send, hid))
            hids = gather_hidden(hid)
        got = flip(send, "dp", 2)
        if final:
            grad_in = gradient(
                grad_in_kernel, (quarter, hidden), (quarter, piece), pay, p1, p2, p3, x_full, gain, scale,
                scratch=[pltpu.VMEM((rows, quarter), BF16)], flops=work,
            )
            got, grad_in = lax.optimization_barrier((got, grad_in))
        outs = [resident((rows, share), BF16)]
        if final:
            outs = [jax.ShapeDtypeStruct((rows, share), BF16), jax.ShapeDtypeStruct((1, share), F32)]
        finished = local(functools.partial(finish_kernel, width), outs, rest, got, x0, dy, gain, scale)
        if not final:
            d0 = lax.ppermute(finished[0], "section", [(i, i - 4) for i in range(4, sections)])
            d2 = flip(d0, "dp", 2)
            d1 = flip(d0, "dp", 1)
            d3 = flip(d2, "dp", 1)
            down = (d0, d1, d2, d3)

    grad_x, grad_gain = finished
    return grad_in[None], grad_out[None], grad_gain, grad_x.reshape(1, micro, tok, share)


def shards(checkpoints, gain, w_in, w_out, cotangent):
    rows = checkpoints.shape[1] * checkpoints.shape[2]
    share = checkpoints.shape[3]
    piece = w_in.shape[2] // 4
    if lax.axis_size("dp") == 4 and rows % 16 == 0 and share % 128 == 0 and piece % 128 == 0 and rows <= min(share, piece):
        return shards_of_four(checkpoints, gain, w_in, w_out, cotangent)
    return shards_of_any(checkpoints, gain, w_in, w_out, cotangent)


def solution(mesh):
    in_specs = (
        P("section", None, None, "dp"),
        P("section", None),
        P("section", None, "dp"),
        P("section", "dp", None),
        P(None, None, "dp"),
    )
    out_specs = (
        P("section", None, "dp"),
        P("section", "dp", None),
        P("section", "dp"),
        P("section", None, None, "dp"),
    )
    return jax.shard_map(shards, mesh=mesh, in_specs=in_specs, out_specs=out_specs, check_vma=False)
```

```python
import functools

import jax
import jax.numpy as jnp
from jax import lax
from jax.experimental import pallas as pl
from jax.experimental.pallas import tpu as pltpu
from jax.sharding import PartitionSpec as P

F32 = jnp.float32
BF16 = jnp.bfloat16


def flip(block, axis, bits):
    count = lax.axis_size(axis)
    return lax.ppermute(block, axis, [(i, i ^ bits) for i in range(count)])


def side_rows(values, width):
    lead = values.astype(BF16)
    trail = (values - lead.astype(F32)).astype(BF16)
    flat = jnp.concatenate([lead, trail])
    return jnp.pad(flat, (0, 16 * width - flat.shape[0])).reshape(16, width)


def side_values(rows, count):
    flat = rows.reshape(-1)
    return flat[:count].astype(F32) + flat[count:2 * count].astype(F32)


def gelu_tanh(value):
    return jax.nn.gelu(value, approximate=True)


def shards_of_any(checkpoints, gain, w_in, w_out, cotangent):
    sections = lax.axis_size("section")
    n_dp = lax.axis_size("dp")
    here = lax.axis_index("section")
    lane = lax.axis_index("dp")
    layers = sections // 4
    mine = here % 4
    last = here // 4 == layers - 1
    _, micro, tok, share = checkpoints.shape
    rows = micro * tok
    quarter = share * n_dp
    width = 4 * quarter
    gain_row = gain[0]
    weight_in = w_in[0]
    weight_out = w_out[0]
    hidden = weight_in.shape[1]
    piece = hidden // 4
    core = lane % 2

    def gather_dp(block):
        bit = n_dp // 2
        parts = {0: block}
        while bit >= 1:
            other = flip(jnp.concatenate([parts[j] for j in parts], axis=1), "dp", bit)
            for at, j in enumerate(list(parts)):
                parts[j ^ bit] = other[:, at * block.shape[1]:(at + 1) * block.shape[1]]
            bit //= 2
        full = jnp.zeros((rows, quarter), block.dtype)
        for j, part in parts.items():
            full = lax.dynamic_update_slice(full, part, (0, (lane ^ j) * block.shape[1]))
        return full

    def cot_quarter(block):
        if n_dp < 4:
            whole = lax.all_gather(block, "dp", axis=1, tiled=True)
            return lax.dynamic_slice_in_dim(whole, mine * quarter, quarter, 1)
        per = n_dp // 4
        top = [s * n_dp + d for s in range(sections) for d in range(n_dp) if s // 4 == layers - 1]
        held = block
        far = lambda i, b: (i % n_dp // per ^ i // n_dp % 4) & b
        got = lax.ppermute(held, ("section", "dp"), [(i, i ^ 2 * per) for i in top if far(i, 3) == 0])
        held = jnp.where((lane // per ^ mine) & 2 == 0, held, got)
        got = lax.ppermute(held, ("section", "dp"), [(i, i ^ per) for i in top if far(i, 1) == 0])
        held = jnp.where((lane // per ^ mine) & 1 == 0, held, got)
        if per == 1:
            return held
        parts = {0: held}
        bit = per // 2
        while bit >= 1:
            for j in list(parts):
                parts[j ^ bit] = flip(parts[j], "dp", bit)
            bit //= 2
        full = jnp.zeros((rows, quarter), block.dtype)
        for j, part in parts.items():
            full = lax.dynamic_update_slice(full, part, (0, (lane % per ^ j) * block.shape[1]))
        return full

    def cut(values, j):
        return lax.dynamic_slice_in_dim(values, (mine ^ j) * piece, piece, 1)

    def fill(parts):
        full = jnp.zeros((rows, hidden), parts[0].dtype)
        for j, part in enumerate(parts):
            full = lax.dynamic_update_slice(full, part, (0, (mine ^ j) * piece))
        return full

    x_full = gather_dp(checkpoints[0].reshape(rows, share))
    cot = cot_quarter(cotangent.reshape(rows, cotangent.shape[2]))
    x_wide = x_full.astype(F32)
    scaled_raw = (x_wide * gain_row).astype(BF16)
    squares = jnp.sum(x_wide * x_wide, axis=1)

    act_raw = jnp.dot(scaled_raw, weight_in, preferred_element_type=F32)
    extra = side_rows(squares, piece)
    act = cut(act_raw, 0)
    for j in (3, 1, 2):
        got = flip(jnp.concatenate([cut(act_raw, j).astype(BF16), extra], axis=0), "section", j)
        act = act + got[:rows].astype(F32)
        squares = squares + side_values(got[rows:], rows)
    scale = lax.rsqrt(squares / width + 1e-06)[:, None]
    act = act * scale
    hid, pull = jax.vjp(gelu_tanh, act)
    hid = hid.astype(BF16)
    hid_full = fill([hid] + [flip(hid, "section", j) for j in (1, 2, 3)])
    normed = x_wide * scale
    scaled = (normed * gain_row).astype(BF16)

    def halves(values, side):
        pairs = values.reshape(rows, n_dp // 2, 2, share)
        return jnp.where(side == 0, pairs[:, :, 0], pairs[:, :, 1]).reshape(rows, quarter // 2)

    def own(values):
        return lax.dynamic_slice_in_dim(values, lane // 2 * share, share, 1)

    incoming = jnp.zeros((rows, quarter), BF16)
    normed_half = halves(normed, core)
    gain_half = halves(jnp.broadcast_to(gain_row, (rows, quarter)), core)
    for phase in range(layers):
        final = phase == layers - 1
        dy = jnp.where(last, cot, incoming) if phase > 0 else cot
        dhid_raw = jnp.dot(dy, weight_out.T, preferred_element_type=F32)
        dhid = cut(dhid_raw, 0)
        for j in (3, 1, 2):
            dhid = dhid + flip(cut(dhid_raw, j).astype(BF16), "section", j).astype(F32)
        dact = pull(dhid)[0].astype(BF16)
        inner = jnp.sum(dact.astype(F32) * act, axis=1)
        payload = jnp.concatenate([dact, side_rows(inner, piece)], axis=0)
        others = [flip(payload, "section", j) for j in (1, 2, 3)]
        for got in others:
            inner = inner + side_values(got[rows:], rows)
        dact_full = fill([dact] + [got[:rows] for got in others])
        part = jnp.dot(dact_full, weight_in.T, preferred_element_type=F32).astype(BF16)

        send = jnp.concatenate([halves(part, 1 - core), side_rows(inner, quarter // 2)], axis=0)
        got = flip(send, "dp", 1)
        dscaled = halves(part, core).astype(F32) + got[:rows].astype(F32)
        inner = inner + side_values(got[rows:], rows)
        bit = 2
        while bit < n_dp:
            send = jnp.concatenate([dscaled.astype(BF16), side_rows(inner, quarter // 2)], axis=0)
            got = flip(send, "dp", bit)
            dscaled = dscaled + got[:rows].astype(F32)
            inner = inner + side_values(got[rows:], rows)
            bit *= 2
        dnorm = dscaled * gain_half
        dy_half = halves(dy, core).astype(F32)
        grad_x = (dy_half + scale * (dnorm - normed_half * (inner / width)[:, None])).astype(BF16)
        if not final:
            down = lax.ppermute(grad_x, "section", [(i, i - 4) for i in range(4, sections)])
            other = flip(down, "dp", 1)
            pairs = jnp.where(
                core == 0,
                jnp.stack([down.reshape(rows, n_dp // 2, share), other.reshape(rows, n_dp // 2, share)], axis=2),
                jnp.stack([other.reshape(rows, n_dp // 2, share), down.reshape(rows, n_dp // 2, share)], axis=2),
            )
            incoming = pairs.reshape(rows, quarter)

    grad_out = jnp.dot(hid_full.T, dy, preferred_element_type=F32).astype(BF16)
    grad_in = jnp.dot(scaled.T, dact_full, preferred_element_type=F32).astype(BF16)
    grad_gain = jnp.sum(own(dscaled) * own(normed_half), axis=0)
    return (
        grad_in[None],
        grad_out[None],
        grad_gain[None],
        own(grad_x).reshape(1, micro, tok, share),
    )


SIDE = 16
GELU_IN = 0.7978845608028654
GELU_CUBE = 0.044715


def resident(shape, dtype):
    return pltpu.VMEM(shape, dtype)


def local(body, outs, *args, scratch=(), flops=0):
    spec = pl.BlockSpec(memory_space=pltpu.VMEM)
    moved = sum(a.size * a.dtype.itemsize for a in args)
    return pl.pallas_call(
        body,
        out_shape=tuple(outs),
        in_specs=[spec] * len(args),
        out_specs=tuple(spec for _ in outs),
        scratch_shapes=list(scratch),
        compiler_params=pltpu.CompilerParams(vmem_limit_bytes=16 * 1024 * 1024),
        cost_estimate=pl.CostEstimate(flops=flops, bytes_accessed=moved, transcendentals=0),
    )(*args)


def diagonal(rows, width):
    return lax.broadcasted_iota(jnp.int32, (rows, width), 0) == lax.broadcasted_iota(jnp.int32, (rows, width), 1)


def as_row(column, width):
    rows = column.shape[0]
    return jnp.sum(jnp.where(diagonal(rows, width), column, 0.0), axis=0, keepdims=True)


def as_column(row, rows):
    return jnp.sum(jnp.where(diagonal(rows, row.shape[1]), row, 0.0), axis=1, keepdims=True)


def side_block(row):
    lead = row.astype(BF16).astype(F32)
    at = lax.broadcasted_iota(jnp.int32, (SIDE, row.shape[1]), 0)
    return jnp.where(at == 0, lead, jnp.where(at == 1, row - lead, 0.0)).astype(BF16)


def side_row(block):
    wide = block.astype(F32)
    return wide[0:1] + wide[1:2]


def load_kernel(*refs):
    count = len(refs) // 2
    copies = [pltpu.make_async_copy(refs[i], refs[count + i], refs[-1].at[i]) for i in range(count)]
    for copy in copies:
        copy.start()
    for copy in copies:
        copy.wait()


def load(*arrays):
    return pl.pallas_call(
        load_kernel,
        out_shape=tuple(resident(a.shape, a.dtype) for a in arrays),
        in_specs=[pl.BlockSpec(memory_space=pl.ANY)] * len(arrays),
        out_specs=tuple(pl.BlockSpec(memory_space=pltpu.VMEM) for _ in arrays),
        scratch_shapes=[pltpu.SemaphoreType.DMA((len(arrays),))],
        compiler_params=pltpu.CompilerParams(vmem_limit_bytes=1024 * 1024),
        cost_estimate=pl.CostEstimate(flops=0, bytes_accessed=sum(2 * a.size * a.dtype.itemsize for a in arrays), transcendentals=0),
    )(*(pltpu.with_memory_space_constraint(a, pltpu.HBM) for a in arrays))


def place():
    return lax.axis_index("section") % 4, lax.axis_index("dp")


def dot_nt(left, right):
    return lax.dot_general(left, right, (((1,), (1,)), ((), ())), preferred_element_type=F32)


def dot_tn(left, right):
    return lax.dot_general(left, right, (((0,), (0,)), ((), ())), preferred_element_type=F32)


def slot(index, size):
    return pl.ds(pl.multiple_of(index * size, size), size)


def spread_in_part(part, at, gain, weight, mine, total, begin):
    share = part.shape[1]
    piece = weight.shape[1] // 4
    scaled = (part[...].astype(F32) * gain[:, slot(at, share)]).astype(BF16)
    for d in (3, 2, 1, 0):
        block = jnp.dot(scaled, weight[slot(at, share), slot(mine ^ d, piece)], preferred_element_type=F32)
        columns = slice(d * piece, (d + 1) * piece)
        total[:, columns] = block if begin else total[:, columns] + block


def square_sum(part):
    wide = part[...].astype(F32)
    return jnp.sum(wide * wide, axis=1, keepdims=True)


def spread_in_first_kernel(x0, x1, gain, weight, total):
    mine, lane = place()
    spread_in_part(x0, lane, gain, weight, mine, total, True)
    spread_in_part(x1, lane ^ 1, gain, weight, mine, total, False)


def spread_in_last_kernel(x0, x1, x2, x3, gain, weight, before, own, s1, s2, s3, x_full, total):
    mine, lane = place()
    rows, share = x0.shape
    piece = own.shape[1]
    total[...] = before[...]
    spread_in_part(x2, lane ^ 2, gain, weight, mine, total, False)
    spread_in_part(x3, lane ^ 3, gain, weight, mine, total, False)
    row = as_row(square_sum(x0) + square_sum(x1) + square_sum(x2) + square_sum(x3), piece)
    block = side_block(row)
    for d, out in ((3, s3), (2, s2), (1, s1)):
        out[:rows] = total[:, d * piece:(d + 1) * piece].astype(BF16)
        out[rows:] = block
    own[:rows] = total[:, :piece]
    own[rows:] = jnp.broadcast_to(row, (SIDE, piece))
    for d, part in enumerate((x0, x1, x2, x3)):
        x_full[:, slot(lane ^ d, share)] = part[...]


def spread_dy(dy, weight, mine, own, s1, s2, s3):
    piece = own.shape[1]
    for d, out in ((3, s3), (2, s2), (1, s1)):
        out[...] = dot_nt(dy[...], weight[slot(mine ^ d, piece), :]).astype(BF16)
    own[...] = dot_nt(dy[...], weight[slot(mine, piece), :])


def spread_first_kernel(cot, sent, weight, own, s1, s2, s3, dy):
    mine, lane = place()

    @pl.when(lane == mine)
    def _():
        dy[...] = cot[...]

    @pl.when(lane != mine)
    def _():
        dy[...] = sent[...]

    spread_dy(dy, weight, mine, own, s1, s2, s3)


def spread_next_kernel(layers, ds, begin, end, *refs):
    parts, refs = refs[:len(ds)], refs[len(ds):]
    before, weight = refs[:2]
    refs = refs[2:]
    mine, lane = place()
    rows, share = parts[0].shape
    piece = weight.shape[0] // 4
    last = lax.axis_index("section") // 4 == layers - 1
    if begin:
        (total,) = refs
    elif end:
        earlier, *others, own, s1, s2, s3, dy, total = refs
        total[...] = earlier[...]
    else:
        earlier, total = refs
        total[...] = earlier[...]
    for i, (d, part) in enumerate(zip(ds, parts)):
        at = slot(lane ^ d, share)
        value = jnp.where(last, before[:, at], part[...])
        for j in (3, 2, 1, 0):
            block = dot_nt(value, weight[slot(mine ^ j, piece), at])
            columns = slice(j * piece, (j + 1) * piece)
            total[:, columns] = block if begin and i == 0 else total[:, columns] + block
    if end:
        for j, out in ((3, s3), (2, s2), (1, s1)):
            out[...] = total[:, j * piece:(j + 1) * piece].astype(BF16)
        own[...] = total[:, :piece]
        done = [d for d in range(4) if d not in ds]

        @pl.when(last)
        def _():
            dy[...] = before[...]

        @pl.when(jnp.logical_not(last))
        def _():
            for d, part in zip((*done, *ds), (*others, *parts)):
                dy[:, slot(lane ^ d, share)] = part[...]


def act_kernel(width, own, g1, g2, g3, act, slope, hid, scale):
    rows = act.shape[0]
    row = own[rows:rows + 1] + side_row(g1[rows:]) + side_row(g2[rows:]) + side_row(g3[rows:])
    r = lax.rsqrt(as_column(row, rows) / width + 1e-06)
    scale[...] = r
    a = (own[:rows] + g1[:rows].astype(F32) + g2[:rows].astype(F32) + g3[:rows].astype(F32)) * r
    act[...] = a
    square = a * a
    t = jnp.tanh(GELU_IN * (a + GELU_CUBE * (square * a)))
    half = 0.5 * (1.0 + t)
    hid[...] = (a * half).astype(BF16)
    slope[...] = half + 0.5 * a * (1.0 - t * t) * (GELU_IN * (1.0 + 3.0 * GELU_CUBE * square))


def dact_kernel(own, g1, g2, g3, act, slope, pay):
    rows, piece = own.shape
    dhid = own[...] + g1[...].astype(F32) + g2[...].astype(F32) + g3[...].astype(F32)
    da = (dhid * slope[...]).astype(BF16)
    pay[:rows] = da
    pay[rows:] = side_block(as_row(jnp.sum(da.astype(F32) * act[...], axis=1, keepdims=True), piece))


def back_part(part, j, weight, mine, lane, total, begin):
    rows = total.shape[0]
    piece = part.shape[1]
    share = weight.shape[0] // 4
    for d in (1, 3, 0, 2):
        block = dot_nt(part[:rows], weight[slot(lane ^ d, share), slot(mine ^ j, piece)])
        columns = slice(d * share, (d + 1) * share)
        total[:, columns] = block if begin else total[:, columns] + block


def back_kernel(js, begin, *refs):
    *parts, weight = refs[:len(js) + 1]
    *earlier, total = refs[len(js) + 1:]
    mine, lane = place()
    if not begin:
        total[...] = earlier[0][...]
    for i, (j, part) in enumerate(zip(js, parts)):
        back_part(part, j, weight, mine, lane, total, begin and i == 0)


def back_last_kernel(p0, p1, p2, p3, weight, earlier, keep, send, total):
    mine, lane = place()
    rows = total.shape[0]
    share = weight.shape[0] // 4
    total[...] = earlier[...]
    back_part(p1, 1, weight, mine, lane, total, False)
    row = side_row(p0[rows:]) + side_row(p1[rows:]) + side_row(p2[rows:]) + side_row(p3[rows:])
    for at, d in ((0, 1), (1, 3)):
        send[:rows, at * share:(at + 1) * share] = total[:, d * share:(d + 1) * share].astype(BF16)
    send[rows:] = side_block(row)
    for at, d in ((0, 0), (1, 2)):
        keep[:rows, at * share:(at + 1) * share] = total[:, d * share:(d + 1) * share]
    keep[rows:] = jnp.broadcast_to(row, (SIDE, keep.shape[1]))


def middle_kernel(keep, got, rest, send):
    rows = keep.shape[0] - SIDE
    share = rest.shape[1]
    row = (keep[rows:rows + 1] + side_row(got[rows:]))[:, :share]
    send[:rows] = (keep[:rows, share:] + got[:rows, share:].astype(F32)).astype(BF16)
    send[rows:] = side_block(row)
    rest[:rows] = keep[:rows, :share] + got[:rows, :share].astype(F32)
    rest[rows:] = jnp.broadcast_to(row, (SIDE, share))


def finish_kernel(width, rest, got, x_own, dy, gain, scale, grad_x, *grad_gain):
    _, lane = place()
    rows, share = x_own.shape
    at = slot(lane, share)
    r = scale[...]
    du = rest[:rows] + got[:rows].astype(F32)
    normed = x_own[...].astype(F32) * r
    inner = as_column(rest[rows:rows + 1] + side_row(got[rows:]), rows) / width
    dnorm = du * gain[:, at]
    grad_x[...] = (dy[:, at].astype(F32) + r * (dnorm - normed * inner)).astype(BF16)
    if grad_gain:
        grad_gain[0][...] = jnp.sum(du * normed, axis=0, keepdims=True)


def grad_out_kernel(h0, h1, h2, h3, dy, out, held, sems):
    mine, _ = place()
    piece = h0.shape[1]
    copies = []
    for d, part in enumerate((h0, h1, h2, h3)):
        held[d] = dot_tn(part[...], dy[...]).astype(BF16)
        copies.append(pltpu.make_async_copy(held.at[d], out.at[slot(mine ^ d, piece), :], sems.at[d]))
        copies[-1].start()
    for copy in copies:
        copy.wait()


def grad_in_kernel(p0, p1, p2, p3, x_full, gain, scale, out, scaled, held, sems):
    mine, _ = place()
    rows = x_full.shape[0]
    piece = p0.shape[1]
    scaled[...] = (x_full[...].astype(F32) * scale[...] * gain[...]).astype(BF16)
    copies = []
    for d, part in enumerate((p0, p1, p2, p3)):
        held[d] = dot_tn(scaled[...], part[:rows]).astype(BF16)
        copies.append(pltpu.make_async_copy(held.at[d], out.at[:, slot(mine ^ d, piece)], sems.at[d]))
        copies[-1].start()
    for copy in copies:
        copy.wait()


def gradient(body, shape, block, *args, scratch=(), flops=0):
    return pl.pallas_call(
        body,
        out_shape=jax.ShapeDtypeStruct(shape, BF16),
        in_specs=[pl.BlockSpec(memory_space=pltpu.VMEM)] * len(args),
        out_specs=pl.BlockSpec(memory_space=pl.ANY),
        scratch_shapes=[*scratch, pltpu.VMEM((4,) + block, BF16), pltpu.SemaphoreType.DMA((4,))],
        compiler_params=pltpu.CompilerParams(vmem_limit_bytes=16 * 1024 * 1024),
        cost_estimate=pl.CostEstimate(flops=flops, bytes_accessed=2 * shape[0] * shape[1], transcendentals=0),
    )(*args)


def shards_of_four(checkpoints, gain, w_in, w_out, cotangent):
    sections = lax.axis_size("section")
    here = lax.axis_index("section")
    lane = lax.axis_index("dp")
    layers = sections // 4
    mine = here % 4
    _, micro, tok, share = checkpoints.shape
    rows = micro * tok
    quarter = share * 4
    width = 4 * quarter
    hidden = w_in.shape[2]
    piece = hidden // 4
    work = 2 * rows * quarter * hidden

    x0 = checkpoints[0].reshape(rows, share)
    cot = cotangent.reshape(rows, quarter)
    top = [s * 4 + d for s in range(sections) for d in range(4) if s // 4 == layers - 1]
    x2 = flip(x0, "dp", 2)
    x1 = flip(x0, "dp", 1)
    weight_in, x0, gain = load(w_in[0], x0, gain)
    cot, weight_in = lax.optimization_barrier((cot, weight_in))
    x2, x1, weight_in = lax.optimization_barrier((x2, x1, weight_in))
    sent = lax.ppermute(cot, ("section", "dp"), [((i // 4 ^ near) * 4 + i // 4 % 4, i) for i in top for near in (1, 0, 2) if i // 4 % 4 ^ i % 4 == (2, 1, 3)[near]])
    x3 = flip(x2, "dp", 1)

    wide = (rows + SIDE, piece)
    (begun,) = local(spread_in_first_kernel, [resident((rows, hidden), F32)], x0, x1, gain, weight_in, flops=work)
    own, s1, s2, s3, x_full = local(
        spread_in_last_kernel,
        [resident(wide, F32)] + [resident(wide, BF16)] * 3 + [resident((rows, quarter), BF16)],
        x0, x1, x2, x3, gain, weight_in, begun,
        scratch=[pltpu.VMEM((rows, hidden), F32)], flops=work,
    )
    s1, s2, s3, cot, w_out = lax.optimization_barrier((s1, s2, s3, cot, w_out))
    g3 = flip(s3, "section", 3)
    g2 = flip(s2, "section", 2)
    g1 = flip(s1, "section", 1)
    weight_out, cot = load(w_out[0], cot)
    act, slope, hid, scale = local(
        functools.partial(act_kernel, width),
        [resident((rows, piece), F32), resident((rows, piece), F32), resident((rows, piece), BF16), resident((rows, 1), F32)],
        own, g1, g2, g3,
    )

    spread_outs = [resident((rows, piece), F32)] + [resident((rows, piece), BF16)] * 3 + [resident((rows, quarter), BF16)]

    def gather_hidden(block):
        return [block] + [flip(block, "section", j) for j in (1, 2, 3)]

    if layers == 1:
        hids = gather_hidden(hid)
    for phase in range(layers):
        final = phase == layers - 1
        if phase == 0:
            own, s1, s2, s3, dy = local(spread_first_kernel, spread_outs, cot, sent, weight_out, flops=work)
        else:
            d0, d1, d2, d3 = down
            first, hids = lax.optimization_barrier((d0, hids))
            total = [resident((rows, hidden), F32)]
            step = functools.partial(spread_next_kernel, layers)
            begun = local(functools.partial(step, (0,), True, False), total, first, dy, weight_out, flops=work // 4)
            begun = local(functools.partial(step, (1, 2), False, False), total, d1, d2, dy, weight_out, *begun, flops=work // 2)
            own, s1, s2, s3, dy = local(
                functools.partial(step, (3,), False, True), spread_outs, d3, dy, weight_out, *begun, d0, d1, d2,
                scratch=[pltpu.VMEM((rows, hidden), F32)], flops=work // 4,
            )
        g3 = flip(s3, "section", 3)
        g2 = flip(s2, "section", 2)
        g1 = flip(s1, "section", 1)
        if final:
            grad_out = gradient(grad_out_kernel, (hidden, quarter), (piece, quarter), *hids, dy, flops=work)
            own, grad_out = lax.optimization_barrier((own, grad_out))
        (pay,) = local(dact_kernel, [resident(wide, BF16)], own, g1, g2, g3, act, slope)
        p3 = flip(pay, "section", 3)
        p2 = flip(pay, "section", 2)
        p1 = flip(pay, "section", 1)
        total = [resident((rows, quarter), F32)]
        begun = local(functools.partial(back_kernel, (0,), True), total, pay, weight_in, flops=work // 4)
        begun = local(functools.partial(back_kernel, (3, 2), False), total, p3, p2, weight_in, *begun, flops=work // 2)
        keep, send = local(
            back_last_kernel,
            [resident((rows + SIDE, 2 * share), F32), resident((rows + SIDE, 2 * share), BF16)],
            pay, p1, p2, p3, weight_in, *begun,
            scratch=[pltpu.VMEM((rows, quarter), F32)], flops=work // 4,
        )
        got = flip(send, "dp", 1)
        rest, send = local(
            middle_kernel,
            [resident((rows + SIDE, share), F32), resident((rows + SIDE, share), BF16)],
            keep, got,
        )
        if phase == 0 and not final:
            send, hid = lax.optimization_barrier((send, hid))
            hids = gather_hidden(hid)
        got = flip(send, "dp", 2)
        if final:
            grad_in = gradient(
                grad_in_kernel, (quarter, hidden), (quarter, piece), pay, p1, p2, p3, x_full, gain, scale,
                scratch=[pltpu.VMEM((rows, quarter), BF16)], flops=work,
            )
            got, grad_in = lax.optimization_barrier((got, grad_in))
        outs = [resident((rows, share), BF16)]
        if final:
            outs = [jax.ShapeDtypeStruct((rows, share), BF16), jax.ShapeDtypeStruct((1, share), F32)]
        finished = local(functools.partial(finish_kernel, width), outs, rest, got, x0, dy, gain, scale)
        if not final:
            d0 = lax.ppermute(finished[0], "section", [(i, i - 4) for i in range(4, sections)])
            d2 = flip(d0, "dp", 2)
            d1 = flip(d0, "dp", 1)
            d3 = flip(d2, "dp", 1)
            down = (d0, d1, d2, d3)

    grad_x, grad_gain = finished
    return grad_in[None], grad_out[None], grad_gain, grad_x.reshape(1, micro, tok, share)


def shards(checkpoints, gain, w_in, w_out, cotangent):
    rows = checkpoints.shape[1] * checkpoints.shape[2]
    share = checkpoints.shape[3]
    piece = w_in.shape[2] // 4
    if lax.axis_size("dp") == 4 and rows % 16 == 0 and share % 128 == 0 and piece % 128 == 0 and rows <= min(share, piece):
        return shards_of_four(checkpoints, gain, w_in, w_out, cotangent)
    return shards_of_any(checkpoints, gain, w_in, w_out, cotangent)


def solution(mesh):
    in_specs = (
        P("section", None, None, "dp"),
        P("section", None),
        P("section", None, "dp"),
        P("section", "dp", None),
        P(None, None, "dp"),
    )
    out_specs = (
        P("section", None, "dp"),
        P("section", "dp", None),
        P("section", "dp"),
        P("section", None, None, "dp"),
    )
    return jax.shard_map(shards, mesh=mesh, in_specs=in_specs, out_specs=out_specs, check_vma=False)
```

```python
import functools

import jax
import jax.numpy as jnp
from jax import lax
from jax.experimental import pallas as pl
from jax.experimental.pallas import tpu as pltpu
from jax.sharding import PartitionSpec as P

F32 = jnp.float32
BF16 = jnp.bfloat16


def flip(block, axis, bits):
    count = lax.axis_size(axis)
    return lax.ppermute(block, axis, [(i, i ^ bits) for i in range(count)])


def side_rows(values, width):
    lead = values.astype(BF16)
    trail = (values - lead.astype(F32)).astype(BF16)
    flat = jnp.concatenate([lead, trail])
    return jnp.pad(flat, (0, 16 * width - flat.shape[0])).reshape(16, width)


def side_values(rows, count):
    flat = rows.reshape(-1)
    return flat[:count].astype(F32) + flat[count:2 * count].astype(F32)


def gelu_tanh(value):
    return jax.nn.gelu(value, approximate=True)


def shards_of_any(checkpoints, gain, w_in, w_out, cotangent):
    sections = lax.axis_size("section")
    n_dp = lax.axis_size("dp")
    here = lax.axis_index("section")
    lane = lax.axis_index("dp")
    layers = sections // 4
    mine = here % 4
    last = here // 4 == layers - 1
    _, micro, tok, share = checkpoints.shape
    rows = micro * tok
    quarter = share * n_dp
    width = 4 * quarter
    gain_row = gain[0]
    weight_in = w_in[0]
    weight_out = w_out[0]
    hidden = weight_in.shape[1]
    piece = hidden // 4
    core = lane % 2

    def gather_dp(block):
        bit = n_dp // 2
        parts = {0: block}
        while bit >= 1:
            other = flip(jnp.concatenate([parts[j] for j in parts], axis=1), "dp", bit)
            for at, j in enumerate(list(parts)):
                parts[j ^ bit] = other[:, at * block.shape[1]:(at + 1) * block.shape[1]]
            bit //= 2
        full = jnp.zeros((rows, quarter), block.dtype)
        for j, part in parts.items():
            full = lax.dynamic_update_slice(full, part, (0, (lane ^ j) * block.shape[1]))
        return full

    def cot_quarter(block):
        if n_dp < 4:
            whole = lax.all_gather(block, "dp", axis=1, tiled=True)
            return lax.dynamic_slice_in_dim(whole, mine * quarter, quarter, 1)
        per = n_dp // 4
        top = [s * n_dp + d for s in range(sections) for d in range(n_dp) if s // 4 == layers - 1]
        held = block
        far = lambda i, b: (i % n_dp // per ^ i // n_dp % 4) & b
        got = lax.ppermute(held, ("section", "dp"), [(i, i ^ 2 * per) for i in top if far(i, 3) == 0])
        held = jnp.where((lane // per ^ mine) & 2 == 0, held, got)
        got = lax.ppermute(held, ("section", "dp"), [(i, i ^ per) for i in top if far(i, 1) == 0])
        held = jnp.where((lane // per ^ mine) & 1 == 0, held, got)
        if per == 1:
            return held
        parts = {0: held}
        bit = per // 2
        while bit >= 1:
            for j in list(parts):
                parts[j ^ bit] = flip(parts[j], "dp", bit)
            bit //= 2
        full = jnp.zeros((rows, quarter), block.dtype)
        for j, part in parts.items():
            full = lax.dynamic_update_slice(full, part, (0, (lane % per ^ j) * block.shape[1]))
        return full

    def cut(values, j):
        return lax.dynamic_slice_in_dim(values, (mine ^ j) * piece, piece, 1)

    def fill(parts):
        full = jnp.zeros((rows, hidden), parts[0].dtype)
        for j, part in enumerate(parts):
            full = lax.dynamic_update_slice(full, part, (0, (mine ^ j) * piece))
        return full

    x_full = gather_dp(checkpoints[0].reshape(rows, share))
    cot = cot_quarter(cotangent.reshape(rows, cotangent.shape[2]))
    x_wide = x_full.astype(F32)
    scaled_raw = (x_wide * gain_row).astype(BF16)
    squares = jnp.sum(x_wide * x_wide, axis=1)

    act_raw = jnp.dot(scaled_raw, weight_in, preferred_element_type=F32)
    extra = side_rows(squares, piece)
    act = cut(act_raw, 0)
    for j in (3, 1, 2):
        got = flip(jnp.concatenate([cut(act_raw, j).astype(BF16), extra], axis=0), "section", j)
        act = act + got[:rows].astype(F32)
        squares = squares + side_values(got[rows:], rows)
    scale = lax.rsqrt(squares / width + 1e-06)[:, None]
    act = act * scale
    hid, pull = jax.vjp(gelu_tanh, act)
    hid = hid.astype(BF16)
    hid_full = fill([hid] + [flip(hid, "section", j) for j in (1, 2, 3)])
    normed = x_wide * scale
    scaled = (normed * gain_row).astype(BF16)

    def halves(values, side):
        pairs = values.reshape(rows, n_dp // 2, 2, share)
        return jnp.where(side == 0, pairs[:, :, 0], pairs[:, :, 1]).reshape(rows, quarter // 2)

    def own(values):
        return lax.dynamic_slice_in_dim(values, lane // 2 * share, share, 1)

    incoming = jnp.zeros((rows, quarter), BF16)
    normed_half = halves(normed, core)
    gain_half = halves(jnp.broadcast_to(gain_row, (rows, quarter)), core)
    for phase in range(layers):
        final = phase == layers - 1
        dy = jnp.where(last, cot, incoming) if phase > 0 else cot
        dhid_raw = jnp.dot(dy, weight_out.T, preferred_element_type=F32)
        dhid = cut(dhid_raw, 0)
        for j in (3, 1, 2):
            dhid = dhid + flip(cut(dhid_raw, j).astype(BF16), "section", j).astype(F32)
        dact = pull(dhid)[0].astype(BF16)
        inner = jnp.sum(dact.astype(F32) * act, axis=1)
        payload = jnp.concatenate([dact, side_rows(inner, piece)], axis=0)
        others = [flip(payload, "section", j) for j in (1, 2, 3)]
        for got in others:
            inner = inner + side_values(got[rows:], rows)
        dact_full = fill([dact] + [got[:rows] for got in others])
        part = jnp.dot(dact_full, weight_in.T, preferred_element_type=F32).astype(BF16)

        send = jnp.concatenate([halves(part, 1 - core), side_rows(inner, quarter // 2)], axis=0)
        got = flip(send, "dp", 1)
        dscaled = halves(part, core).astype(F32) + got[:rows].astype(F32)
        inner = inner + side_values(got[rows:], rows)
        bit = 2
        while bit < n_dp:
            send = jnp.concatenate([dscaled.astype(BF16), side_rows(inner, quarter // 2)], axis=0)
            got = flip(send, "dp", bit)
            dscaled = dscaled + got[:rows].astype(F32)
            inner = inner + side_values(got[rows:], rows)
            bit *= 2
        dnorm = dscaled * gain_half
        dy_half = halves(dy, core).astype(F32)
        grad_x = (dy_half + scale * (dnorm - normed_half * (inner / width)[:, None])).astype(BF16)
        if not final:
            down = lax.ppermute(grad_x, "section", [(i, i - 4) for i in range(4, sections)])
            other = flip(down, "dp", 1)
            pairs = jnp.where(
                core == 0,
                jnp.stack([down.reshape(rows, n_dp // 2, share), other.reshape(rows, n_dp // 2, share)], axis=2),
                jnp.stack([other.reshape(rows, n_dp // 2, share), down.reshape(rows, n_dp // 2, share)], axis=2),
            )
            incoming = pairs.reshape(rows, quarter)

    grad_out = jnp.dot(hid_full.T, dy, preferred_element_type=F32).astype(BF16)
    grad_in = jnp.dot(scaled.T, dact_full, preferred_element_type=F32).astype(BF16)
    grad_gain = jnp.sum(own(dscaled) * own(normed_half), axis=0)
    return (
        grad_in[None],
        grad_out[None],
        grad_gain[None],
        own(grad_x).reshape(1, micro, tok, share),
    )


SIDE = 16
GELU_IN = 0.7978845608028654
GELU_CUBE = 0.044715


def resident(shape, dtype):
    return pltpu.VMEM(shape, dtype)


def local(body, outs, *args, scratch=(), flops=0):
    spec = pl.BlockSpec(memory_space=pltpu.VMEM)
    moved = sum(a.size * a.dtype.itemsize for a in args)
    return pl.pallas_call(
        body,
        out_shape=tuple(outs),
        in_specs=[spec] * len(args),
        out_specs=tuple(spec for _ in outs),
        scratch_shapes=list(scratch),
        compiler_params=pltpu.CompilerParams(vmem_limit_bytes=16 * 1024 * 1024),
        cost_estimate=pl.CostEstimate(flops=flops, bytes_accessed=moved, transcendentals=0),
    )(*args)


def diagonal(rows, width):
    return lax.broadcasted_iota(jnp.int32, (rows, width), 0) == lax.broadcasted_iota(jnp.int32, (rows, width), 1)


def as_row(column, width):
    rows = column.shape[0]
    return jnp.sum(jnp.where(diagonal(rows, width), column, 0.0), axis=0, keepdims=True)


def as_column(row, rows):
    return jnp.sum(jnp.where(diagonal(rows, row.shape[1]), row, 0.0), axis=1, keepdims=True)


def side_block(row):
    lead = row.astype(BF16).astype(F32)
    at = lax.broadcasted_iota(jnp.int32, (SIDE, row.shape[1]), 0)
    return jnp.where(at == 0, lead, jnp.where(at == 1, row - lead, 0.0)).astype(BF16)


def side_row(block):
    wide = block.astype(F32)
    return wide[0:1] + wide[1:2]


def load_kernel(*refs):
    count = len(refs) // 2
    copies = [pltpu.make_async_copy(refs[i], refs[count + i], refs[-1].at[i]) for i in range(count)]
    for copy in copies:
        copy.start()
    for copy in copies:
        copy.wait()


def load(*arrays):
    return pl.pallas_call(
        load_kernel,
        out_shape=tuple(resident(a.shape, a.dtype) for a in arrays),
        in_specs=[pl.BlockSpec(memory_space=pl.ANY)] * len(arrays),
        out_specs=tuple(pl.BlockSpec(memory_space=pltpu.VMEM) for _ in arrays),
        scratch_shapes=[pltpu.SemaphoreType.DMA((len(arrays),))],
        compiler_params=pltpu.CompilerParams(vmem_limit_bytes=1024 * 1024),
        cost_estimate=pl.CostEstimate(flops=0, bytes_accessed=sum(2 * a.size * a.dtype.itemsize for a in arrays), transcendentals=0),
    )(*(pltpu.with_memory_space_constraint(a, pltpu.HBM) for a in arrays))


def place():
    return lax.axis_index("section") % 4, lax.axis_index("dp")


def dot_nt(left, right):
    return lax.dot_general(left, right, (((1,), (1,)), ((), ())), preferred_element_type=F32)


def dot_tn(left, right):
    return lax.dot_general(left, right, (((0,), (0,)), ((), ())), preferred_element_type=F32)


def slot(index, size):
    return pl.ds(pl.multiple_of(index * size, size), size)


def spread_in_part(part, at, gain, weight, mine, total, begin):
    share = part.shape[1]
    piece = weight.shape[1] // 4
    scaled = (part[...].astype(F32) * gain[:, slot(at, share)]).astype(BF16)
    for d in (3, 2, 1, 0):
        block = jnp.dot(scaled, weight[slot(at, share), slot(mine ^ d, piece)], preferred_element_type=F32)
        columns = slice(d * piece, (d + 1) * piece)
        total[:, columns] = block if begin else total[:, columns] + block


def square_sum(part):
    wide = part[...].astype(F32)
    return jnp.sum(wide * wide, axis=1, keepdims=True)


def spread_in_first_kernel(x0, x1, gain, weight, total):
    mine, lane = place()
    spread_in_part(x0, lane, gain, weight, mine, total, True)
    spread_in_part(x1, lane ^ 1, gain, weight, mine, total, False)


def spread_in_last_kernel(x0, x1, x2, x3, gain, weight, before, own, s1, s2, k1, k2, x_full, total):
    mine, lane = place()
    rows, share = x0.shape
    piece = own.shape[1]
    half = piece // 2
    total[...] = before[...]
    spread_in_part(x2, lane ^ 2, gain, weight, mine, total, False)
    spread_in_part(x3, lane ^ 3, gain, weight, mine, total, False)
    row = as_row(square_sum(x0) + square_sum(x1) + square_sum(x2) + square_sum(x3), piece)
    block = side_block(row)
    for d, out, left in ((1, s1, 0), (2, s2, half)):
        out[:rows, :half] = total[:, 3 * piece + left:3 * piece + left + half].astype(BF16)
        out[:rows, half:] = total[:, d * piece + left:d * piece + left + half].astype(BF16)
        out[rows:] = block
    k2[:rows] = total[:, 2 * piece:2 * piece + half]
    k2[rows:] = jnp.broadcast_to(row[:, :half], (SIDE, half))
    k1[...] = total[:, piece + half:2 * piece]
    own[:rows] = total[:, :piece]
    own[rows:] = jnp.broadcast_to(row, (SIDE, piece))
    for d, part in enumerate((x0, x1, x2, x3)):
        x_full[:, slot(lane ^ d, share)] = part[...]


def pass_on_kernel(k1, k2, g1, g2, t1, t2):
    rows, half = k1.shape
    t2[:rows] = (k2[:rows] + g1[:rows, :half].astype(F32)).astype(BF16)
    t2[rows:] = side_block(k2[rows:rows + 1] + side_row(g1[rows:, :half]))
    t1[...] = (k1[...] + g2[:rows, :half].astype(F32)).astype(BF16)


def spread_dy(dy, weight, mine, own, s1, s2, s3):
    piece = own.shape[1]
    for d, out in ((3, s3), (2, s2), (1, s1)):
        out[...] = dot_nt(dy[...], weight[slot(mine ^ d, piece), :]).astype(BF16)
    own[...] = dot_nt(dy[...], weight[slot(mine, piece), :])


def spread_first_kernel(cot, sent, weight, own, s1, s2, s3, dy):
    mine, lane = place()

    @pl.when(lane == mine)
    def _():
        dy[...] = cot[...]

    @pl.when(lane != mine)
    def _():
        dy[...] = sent[...]

    spread_dy(dy, weight, mine, own, s1, s2, s3)


def spread_next_kernel(layers, ds, begin, end, *refs):
    parts, refs = refs[:len(ds)], refs[len(ds):]
    before, weight = refs[:2]
    refs = refs[2:]
    mine, lane = place()
    rows, share = parts[0].shape
    piece = weight.shape[0] // 4
    last = lax.axis_index("section") // 4 == layers - 1
    if begin:
        (total,) = refs
    elif end:
        earlier, *others, own, s1, s2, s3, dy, total = refs
        total[...] = earlier[...]
    else:
        earlier, total = refs
        total[...] = earlier[...]
    for i, (d, part) in enumerate(zip(ds, parts)):
        at = slot(lane ^ d, share)
        value = jnp.where(last, before[:, at], part[...])
        for j in (3, 2, 1, 0):
            block = dot_nt(value, weight[slot(mine ^ j, piece), at])
            columns = slice(j * piece, (j + 1) * piece)
            total[:, columns] = block if begin and i == 0 else total[:, columns] + block
    if end:
        for j, out in ((3, s3), (2, s2), (1, s1)):
            out[...] = total[:, j * piece:(j + 1) * piece].astype(BF16)
        own[...] = total[:, :piece]
        done = [d for d in range(4) if d not in ds]

        @pl.when(last)
        def _():
            dy[...] = before[...]

        @pl.when(jnp.logical_not(last))
        def _():
            for d, part in zip((*done, *ds), (*others, *parts)):
                dy[:, slot(lane ^ d, share)] = part[...]


def act_kernel(width, own, g1, g2, q1, q2, act, slope, hid, scale):
    rows, piece = act.shape
    half = piece // 2
    row = own[rows:rows + 1, :half] + side_row(g1[rows:, :half]) + side_row(q2[rows:])
    r = lax.rsqrt(as_column(row, rows) / width + 1e-06)
    scale[...] = r
    for at, near, far in ((slice(0, half), g1, q2), (slice(half, piece), g2, q1)):
        a = (own[:rows, at] + near[:rows, half:].astype(F32) + far[:rows].astype(F32)) * r
        act[:, at] = a
        square = a * a
        t = jnp.tanh(GELU_IN * (a + GELU_CUBE * (square * a)))
        open_part = 0.5 * (1.0 + t)
        hid[:, at] = (a * open_part).astype(BF16)
        slope[:, at] = open_part + 0.5 * a * (1.0 - t * t) * (GELU_IN * (1.0 + 3.0 * GELU_CUBE * square))


def dact_kernel(own, g1, g2, g3, act, slope, pay):
    rows, piece = own.shape
    dhid = own[...] + g1[...].astype(F32) + g2[...].astype(F32) + g3[...].astype(F32)
    da = (dhid * slope[...]).astype(BF16)
    pay[:rows] = da
    pay[rows:] = side_block(as_row(jnp.sum(da.astype(F32) * act[...], axis=1, keepdims=True), piece))


def back_part(part, j, weight, mine, lane, total, begin):
    rows = total.shape[0]
    piece = part.shape[1]
    share = weight.shape[0] // 4
    for d in (1, 3, 0, 2):
        block = dot_nt(part[:rows], weight[slot(lane ^ d, share), slot(mine ^ j, piece)])
        columns = slice(d * share, (d + 1) * share)
        total[:, columns] = block if begin else total[:, columns] + block


def back_kernel(js, begin, *refs):
    *parts, weight = refs[:len(js) + 1]
    *earlier, total = refs[len(js) + 1:]
    mine, lane = place()
    if not begin:
        total[...] = earlier[0][...]
    for i, (j, part) in enumerate(zip(js, parts)):
        back_part(part, j, weight, mine, lane, total, begin and i == 0)


def back_last_kernel(p0, p1, p2, p3, weight, earlier, keep, send, total):
    mine, lane = place()
    rows = total.shape[0]
    share = weight.shape[0] // 4
    total[...] = earlier[...]
    back_part(p1, 1, weight, mine, lane, total, False)
    row = side_row(p0[rows:]) + side_row(p1[rows:]) + side_row(p2[rows:]) + side_row(p3[rows:])
    for at, d in ((0, 1), (1, 3)):
        send[:rows, at * share:(at + 1) * share] = total[:, d * share:(d + 1) * share].astype(BF16)
    send[rows:] = side_block(row)
    for at, d in ((0, 0), (1, 2)):
        keep[:rows, at * share:(at + 1) * share] = total[:, d * share:(d + 1) * share]
    keep[rows:] = jnp.broadcast_to(row, (SIDE, keep.shape[1]))


def middle_kernel(keep, got, rest, send):
    rows = keep.shape[0] - SIDE
    share = rest.shape[1]
    row = (keep[rows:rows + 1] + side_row(got[rows:]))[:, :share]
    send[:rows] = (keep[:rows, share:] + got[:rows, share:].astype(F32)).astype(BF16)
    send[rows:] = side_block(row)
    rest[:rows] = keep[:rows, :share] + got[:rows, :share].astype(F32)
    rest[rows:] = jnp.broadcast_to(row, (SIDE, share))


def finish_kernel(width, rest, got, x_own, dy, gain, scale, grad_x, *grad_gain):
    _, lane = place()
    rows, share = x_own.shape
    at = slot(lane, share)
    r = scale[...]
    du = rest[:rows] + got[:rows].astype(F32)
    normed = x_own[...].astype(F32) * r
    inner = as_column(rest[rows:rows + 1] + side_row(got[rows:]), rows) / width
    dnorm = du * gain[:, at]
    grad_x[...] = (dy[:, at].astype(F32) + r * (dnorm - normed * inner)).astype(BF16)
    if grad_gain:
        grad_gain[0][...] = jnp.sum(du * normed, axis=0, keepdims=True)


def grad_out_kernel(h0, h1, h2, h3, dy, out, held, sems):
    mine, _ = place()
    piece = h0.shape[1]
    copies = []
    for d, part in enumerate((h0, h1, h2, h3)):
        held[d] = dot_tn(part[...], dy[...]).astype(BF16)
        copies.append(pltpu.make_async_copy(held.at[d], out.at[slot(mine ^ d, piece), :], sems.at[d]))
        copies[-1].start()
    for copy in copies:
        copy.wait()


def grad_in_kernel(p0, p1, p2, p3, x_full, gain, scale, out, scaled, held, sems):
    mine, _ = place()
    rows = x_full.shape[0]
    piece = p0.shape[1]
    scaled[...] = (x_full[...].astype(F32) * scale[...] * gain[...]).astype(BF16)
    copies = []
    for d, part in enumerate((p0, p1, p2, p3)):
        held[d] = dot_tn(scaled[...], part[:rows]).astype(BF16)
        copies.append(pltpu.make_async_copy(held.at[d], out.at[:, slot(mine ^ d, piece)], sems.at[d]))
        copies[-1].start()
    for copy in copies:
        copy.wait()


def gradient(body, shape, block, *args, scratch=(), flops=0):
    return pl.pallas_call(
        body,
        out_shape=jax.ShapeDtypeStruct(shape, BF16),
        in_specs=[pl.BlockSpec(memory_space=pltpu.VMEM)] * len(args),
        out_specs=pl.BlockSpec(memory_space=pl.ANY),
        scratch_shapes=[*scratch, pltpu.VMEM((4,) + block, BF16), pltpu.SemaphoreType.DMA((4,))],
        compiler_params=pltpu.CompilerParams(vmem_limit_bytes=16 * 1024 * 1024),
        cost_estimate=pl.CostEstimate(flops=flops, bytes_accessed=2 * shape[0] * shape[1], transcendentals=0),
    )(*args)


def shards_of_four(checkpoints, gain, w_in, w_out, cotangent):
    sections = lax.axis_size("section")
    here = lax.axis_index("section")
    lane = lax.axis_index("dp")
    layers = sections // 4
    mine = here % 4
    _, micro, tok, share = checkpoints.shape
    rows = micro * tok
    quarter = share * 4
    width = 4 * quarter
    hidden = w_in.shape[2]
    piece = hidden // 4
    work = 2 * rows * quarter * hidden

    x0 = checkpoints[0].reshape(rows, share)
    cot = cotangent.reshape(rows, quarter)
    top = [s * 4 + d for s in range(sections) for d in range(4) if s // 4 == layers - 1]
    x2 = flip(x0, "dp", 2)
    x1 = flip(x0, "dp", 1)
    weight_in, x0, gain = load(w_in[0], x0, gain)
    x2, x1, weight_in = lax.optimization_barrier((x2, x1, weight_in))
    sent = lax.ppermute(cot, ("section", "dp"), [((i // 4 ^ near) * 4 + i // 4 % 4, i) for i in top for near in (1, 0, 2) if i // 4 % 4 ^ i % 4 == (2, 1, 3)[near]])
    x3 = flip(x2, "dp", 1)

    wide = (rows + SIDE, piece)
    (begun,) = local(spread_in_first_kernel, [resident((rows, hidden), F32)], x0, x1, gain, weight_in, flops=work)
    half = piece // 2
    own, s1, s2, k1, k2, x_full = local(
        spread_in_last_kernel,
        [resident(wide, F32)] + [resident(wide, BF16)] * 2
        + [resident((rows, half), F32), resident((rows + SIDE, half), F32), resident((rows, quarter), BF16)],
        x0, x1, x2, x3, gain, weight_in, begun,
        scratch=[pltpu.VMEM((rows, hidden), F32)], flops=2 * work,
    )
    s1, s2, cot, w_out = lax.optimization_barrier((s1, s2, cot, w_out))
    g1 = flip(s1, "section", 1)
    g2 = flip(s2, "section", 2)
    t1, t2 = local(pass_on_kernel, [resident((rows, half), BF16), resident((rows + SIDE, half), BF16)], k1, k2, g1, g2)
    q1 = flip(t1, "section", 1)
    q2 = flip(t2, "section", 2)
    weight_out, cot = load(w_out[0], cot)
    act, slope, hid, scale = local(
        functools.partial(act_kernel, width),
        [resident((rows, piece), F32), resident((rows, piece), F32), resident((rows, piece), BF16), resident((rows, 1), F32)],
        own, g1, g2, q1, q2,
    )

    spread_outs = [resident((rows, piece), F32)] + [resident((rows, piece), BF16)] * 3 + [resident((rows, quarter), BF16)]

    def gather_hidden(block):
        return [block] + [flip(block, "section", j) for j in (1, 2, 3)]

    if layers == 1:
        hids = gather_hidden(hid)
    for phase in range(layers):
        final = phase == layers - 1
        if phase == 0:
            own, s1, s2, s3, dy = local(spread_first_kernel, spread_outs, cot, sent, weight_out, flops=work)
        else:
            d0, d1, d2, d3 = down
            first, hids = lax.optimization_barrier((d0, hids))
            total = [resident((rows, hidden), F32)]
            step = functools.partial(spread_next_kernel, layers)
            begun = local(functools.partial(step, (0,), True, False), total, first, dy, weight_out, flops=work // 4)
            begun = local(functools.partial(step, (1, 2), False, False), total, d1, d2, dy, weight_out, *begun, flops=work // 2)
            own, s1, s2, s3, dy = local(
                functools.partial(step, (3,), False, True), spread_outs, d3, dy, weight_out, *begun, d0, d1, d2,
                scratch=[pltpu.VMEM((rows, hidden), F32)], flops=work // 4,
            )
        g3 = flip(s3, "section", 3)
        g2 = flip(s2, "section", 2)
        g1 = flip(s1, "section", 1)
        if final:
            grad_out = gradient(grad_out_kernel, (hidden, quarter), (piece, quarter), *hids, dy, flops=work)
            own, grad_out = lax.optimization_barrier((own, grad_out))
        (pay,) = local(dact_kernel, [resident(wide, BF16)], own, g1, g2, g3, act, slope)
        p3 = flip(pay, "section", 3)
        p2 = flip(pay, "section", 2)
        p1 = flip(pay, "section", 1)
        total = [resident((rows, quarter), F32)]
        begun = local(functools.partial(back_kernel, (0,), True), total, pay, weight_in, flops=work // 4)
        begun = local(functools.partial(back_kernel, (3, 2), False), total, p3, p2, weight_in, *begun, flops=work // 2)
        keep, send = local(
            back_last_kernel,
            [resident((rows + SIDE, 2 * share), F32), resident((rows + SIDE, 2 * share), BF16)],
            pay, p1, p2, p3, weight_in, *begun,
            scratch=[pltpu.VMEM((rows, quarter), F32)], flops=work // 4,
        )
        got = flip(send, "dp", 1)
        rest, send = local(
            middle_kernel,
            [resident((rows + SIDE, share), F32), resident((rows + SIDE, share), BF16)],
            keep, got,
        )
        if phase == 0 and not final:
            send, hid = lax.optimization_barrier((send, hid))
            hids = gather_hidden(hid)
        got = flip(send, "dp", 2)
        if final:
            grad_in = gradient(
                grad_in_kernel, (quarter, hidden), (quarter, piece), pay, p1, p2, p3, x_full, gain, scale,
                scratch=[pltpu.VMEM((rows, quarter), BF16)], flops=work,
            )
            got, grad_in = lax.optimization_barrier((got, grad_in))
        outs = [resident((rows, share), BF16)]
        if final:
            outs = [jax.ShapeDtypeStruct((rows, share), BF16), jax.ShapeDtypeStruct((1, share), F32)]
        finished = local(functools.partial(finish_kernel, width), outs, rest, got, x0, dy, gain, scale)
        if not final:
            d0 = lax.ppermute(finished[0], "section", [(i, i - 4) for i in range(4, sections)])
            d2 = flip(d0, "dp", 2)
            d1 = flip(d0, "dp", 1)
            d3 = flip(d2, "dp", 1)
            down = (d0, d1, d2, d3)

    grad_x, grad_gain = finished
    return grad_in[None], grad_out[None], grad_gain, grad_x.reshape(1, micro, tok, share)


def shards(checkpoints, gain, w_in, w_out, cotangent):
    rows = checkpoints.shape[1] * checkpoints.shape[2]
    share = checkpoints.shape[3]
    piece = w_in.shape[2] // 4
    if lax.axis_size("dp") == 4 and rows % 16 == 0 and share % 128 == 0 and piece % 256 == 0 and rows <= min(share, piece // 2):
        return shards_of_four(checkpoints, gain, w_in, w_out, cotangent)
    return shards_of_any(checkpoints, gain, w_in, w_out, cotangent)


def solution(mesh):
    in_specs = (
        P("section", None, None, "dp"),
        P("section", None),
        P("section", None, "dp"),
        P("section", "dp", None),
        P(None, None, "dp"),
    )
    out_specs = (
        P("section", None, "dp"),
        P("section", "dp", None),
        P("section", "dp"),
        P("section", None, None, "dp"),
    )
    return jax.shard_map(shards, mesh=mesh, in_specs=in_specs, out_specs=out_specs, check_vma=False)
```

```python
import functools

import jax
import jax.numpy as jnp
from jax import lax
from jax.experimental import pallas as pl
from jax.experimental.pallas import tpu as pltpu
from jax.sharding import PartitionSpec as P

F32 = jnp.float32
BF16 = jnp.bfloat16


def flip(block, axis, bits):
    count = lax.axis_size(axis)
    return lax.ppermute(block, axis, [(i, i ^ bits) for i in range(count)])


def side_rows(values, width):
    lead = values.astype(BF16)
    trail = (values - lead.astype(F32)).astype(BF16)
    flat = jnp.concatenate([lead, trail])
    return jnp.pad(flat, (0, 16 * width - flat.shape[0])).reshape(16, width)


def side_values(rows, count):
    flat = rows.reshape(-1)
    return flat[:count].astype(F32) + flat[count:2 * count].astype(F32)


def gelu_tanh(value):
    return jax.nn.gelu(value, approximate=True)


def shards_of_any(checkpoints, gain, w_in, w_out, cotangent):
    sections = lax.axis_size("section")
    n_dp = lax.axis_size("dp")
    here = lax.axis_index("section")
    lane = lax.axis_index("dp")
    layers = sections // 4
    mine = here % 4
    last = here // 4 == layers - 1
    _, micro, tok, share = checkpoints.shape
    rows = micro * tok
    quarter = share * n_dp
    width = 4 * quarter
    gain_row = gain[0]
    weight_in = w_in[0]
    weight_out = w_out[0]
    hidden = weight_in.shape[1]
    piece = hidden // 4
    core = lane % 2

    def gather_dp(block):
        bit = n_dp // 2
        parts = {0: block}
        while bit >= 1:
            other = flip(jnp.concatenate([parts[j] for j in parts], axis=1), "dp", bit)
            for at, j in enumerate(list(parts)):
                parts[j ^ bit] = other[:, at * block.shape[1]:(at + 1) * block.shape[1]]
            bit //= 2
        full = jnp.zeros((rows, quarter), block.dtype)
        for j, part in parts.items():
            full = lax.dynamic_update_slice(full, part, (0, (lane ^ j) * block.shape[1]))
        return full

    def cot_quarter(block):
        if n_dp < 4:
            whole = lax.all_gather(block, "dp", axis=1, tiled=True)
            return lax.dynamic_slice_in_dim(whole, mine * quarter, quarter, 1)
        per = n_dp // 4
        top = [s * n_dp + d for s in range(sections) for d in range(n_dp) if s // 4 == layers - 1]
        held = block
        far = lambda i, b: (i % n_dp // per ^ i // n_dp % 4) & b
        got = lax.ppermute(held, ("section", "dp"), [(i, i ^ 2 * per) for i in top if far(i, 3) == 0])
        held = jnp.where((lane // per ^ mine) & 2 == 0, held, got)
        got = lax.ppermute(held, ("section", "dp"), [(i, i ^ per) for i in top if far(i, 1) == 0])
        held = jnp.where((lane // per ^ mine) & 1 == 0, held, got)
        if per == 1:
            return held
        parts = {0: held}
        bit = per // 2
        while bit >= 1:
            for j in list(parts):
                parts[j ^ bit] = flip(parts[j], "dp", bit)
            bit //= 2
        full = jnp.zeros((rows, quarter), block.dtype)
        for j, part in parts.items():
            full = lax.dynamic_update_slice(full, part, (0, (lane % per ^ j) * block.shape[1]))
        return full

    def cut(values, j):
        return lax.dynamic_slice_in_dim(values, (mine ^ j) * piece, piece, 1)

    def fill(parts):
        full = jnp.zeros((rows, hidden), parts[0].dtype)
        for j, part in enumerate(parts):
            full = lax.dynamic_update_slice(full, part, (0, (mine ^ j) * piece))
        return full

    x_full = gather_dp(checkpoints[0].reshape(rows, share))
    cot = cot_quarter(cotangent.reshape(rows, cotangent.shape[2]))
    x_wide = x_full.astype(F32)
    scaled_raw = (x_wide * gain_row).astype(BF16)
    squares = jnp.sum(x_wide * x_wide, axis=1)

    act_raw = jnp.dot(scaled_raw, weight_in, preferred_element_type=F32)
    extra = side_rows(squares, piece)
    act = cut(act_raw, 0)
    for j in (3, 1, 2):
        got = flip(jnp.concatenate([cut(act_raw, j).astype(BF16), extra], axis=0), "section", j)
        act = act + got[:rows].astype(F32)
        squares = squares + side_values(got[rows:], rows)
    scale = lax.rsqrt(squares / width + 1e-06)[:, None]
    act = act * scale
    hid, pull = jax.vjp(gelu_tanh, act)
    hid = hid.astype(BF16)
    hid_full = fill([hid] + [flip(hid, "section", j) for j in (1, 2, 3)])
    normed = x_wide * scale
    scaled = (normed * gain_row).astype(BF16)

    def halves(values, side):
        pairs = values.reshape(rows, n_dp // 2, 2, share)
        return jnp.where(side == 0, pairs[:, :, 0], pairs[:, :, 1]).reshape(rows, quarter // 2)

    def own(values):
        return lax.dynamic_slice_in_dim(values, lane // 2 * share, share, 1)

    incoming = jnp.zeros((rows, quarter), BF16)
    normed_half = halves(normed, core)
    gain_half = halves(jnp.broadcast_to(gain_row, (rows, quarter)), core)
    for phase in range(layers):
        final = phase == layers - 1
        dy = jnp.where(last, cot, incoming) if phase > 0 else cot
        dhid_raw = jnp.dot(dy, weight_out.T, preferred_element_type=F32)
        dhid = cut(dhid_raw, 0)
        for j in (3, 1, 2):
            dhid = dhid + flip(cut(dhid_raw, j).astype(BF16), "section", j).astype(F32)
        dact = pull(dhid)[0].astype(BF16)
        inner = jnp.sum(dact.astype(F32) * act, axis=1)
        payload = jnp.concatenate([dact, side_rows(inner, piece)], axis=0)
        others = [flip(payload, "section", j) for j in (1, 2, 3)]
        for got in others:
            inner = inner + side_values(got[rows:], rows)
        dact_full = fill([dact] + [got[:rows] for got in others])
        part = jnp.dot(dact_full, weight_in.T, preferred_element_type=F32).astype(BF16)

        send = jnp.concatenate([halves(part, 1 - core), side_rows(inner, quarter // 2)], axis=0)
        got = flip(send, "dp", 1)
        dscaled = halves(part, core).astype(F32) + got[:rows].astype(F32)
        inner = inner + side_values(got[rows:], rows)
        bit = 2
        while bit < n_dp:
            send = jnp.concatenate([dscaled.astype(BF16), side_rows(inner, quarter // 2)], axis=0)
            got = flip(send, "dp", bit)
            dscaled = dscaled + got[:rows].astype(F32)
            inner = inner + side_values(got[rows:], rows)
            bit *= 2
        dnorm = dscaled * gain_half
        dy_half = halves(dy, core).astype(F32)
        grad_x = (dy_half + scale * (dnorm - normed_half * (inner / width)[:, None])).astype(BF16)
        if not final:
            down = lax.ppermute(grad_x, "section", [(i, i - 4) for i in range(4, sections)])
            other = flip(down, "dp", 1)
            pairs = jnp.where(
                core == 0,
                jnp.stack([down.reshape(rows, n_dp // 2, share), other.reshape(rows, n_dp // 2, share)], axis=2),
                jnp.stack([other.reshape(rows, n_dp // 2, share), down.reshape(rows, n_dp // 2, share)], axis=2),
            )
            incoming = pairs.reshape(rows, quarter)

    grad_out = jnp.dot(hid_full.T, dy, preferred_element_type=F32).astype(BF16)
    grad_in = jnp.dot(scaled.T, dact_full, preferred_element_type=F32).astype(BF16)
    grad_gain = jnp.sum(own(dscaled) * own(normed_half), axis=0)
    return (
        grad_in[None],
        grad_out[None],
        grad_gain[None],
        own(grad_x).reshape(1, micro, tok, share),
    )


SIDE = 16
LANES = 128
GELU_IN = 0.7978845608028654
GELU_CUBE = 0.044715


def resident(shape, dtype):
    return pltpu.VMEM(shape, dtype)


def local(body, outs, *args, scratch=(), flops=0):
    spec = pl.BlockSpec(memory_space=pltpu.VMEM)
    moved = sum(a.size * a.dtype.itemsize for a in args)
    return pl.pallas_call(
        body,
        out_shape=tuple(outs),
        in_specs=[spec] * len(args),
        out_specs=tuple(spec for _ in outs),
        scratch_shapes=list(scratch),
        compiler_params=pltpu.CompilerParams(vmem_limit_bytes=16 * 1024 * 1024),
        cost_estimate=pl.CostEstimate(flops=flops, bytes_accessed=moved, transcendentals=0),
    )(*args)


def diagonal(rows, width):
    return lax.broadcasted_iota(jnp.int32, (rows, width), 0) == lax.broadcasted_iota(jnp.int32, (rows, width), 1)


def as_row(column, width):
    rows = column.shape[0]
    return jnp.sum(jnp.where(diagonal(rows, width), column, 0.0), axis=0, keepdims=True)


def as_column(row, rows):
    return jnp.sum(jnp.where(diagonal(rows, row.shape[1]), row, 0.0), axis=1, keepdims=True)


def side_block(row):
    lead = row.astype(BF16).astype(F32)
    at = lax.broadcasted_iota(jnp.int32, (SIDE, row.shape[1]), 0)
    return jnp.where(at == 0, lead, jnp.where(at == 1, row - lead, 0.0)).astype(BF16)


def side_row(block):
    wide = block.astype(F32)
    return wide[0:1] + wide[1:2]


def packed_shape(rows, piece):
    return (piece // LANES * rows + SIDE, LANES)


def pack_block(row):
    lead = row.astype(BF16).astype(F32)
    count = row.shape[1] // LANES
    at = lax.broadcasted_iota(jnp.int32, (SIDE, LANES), 0)
    block = jnp.zeros((SIDE, LANES), F32)
    for i in range(count):
        lanes = slice(i * LANES, (i + 1) * LANES)
        block = jnp.where(at == i, lead[:, lanes], jnp.where(at == count + i, (row - lead)[:, lanes], block))
    return block.astype(BF16)


def pack_row(block, count):
    wide = block.astype(F32)
    return jnp.concatenate([wide[i:i + 1] + wide[count + i:count + i + 1] for i in range(count)], axis=1)


def lane_blocks(rows):
    return -(-rows // LANES)


def unpack(packed, rows):
    blocks = (packed.shape[0] - SIDE) // rows
    return jnp.concatenate([packed[i * rows:(i + 1) * rows] for i in range(blocks)], axis=1)


def load_kernel(*refs):
    count = len(refs) // 2
    copies = [pltpu.make_async_copy(refs[i], refs[count + i], refs[-1].at[i]) for i in range(count)]
    for copy in copies:
        copy.start()
    for copy in copies:
        copy.wait()


def load(*arrays):
    return pl.pallas_call(
        load_kernel,
        out_shape=tuple(resident(a.shape, a.dtype) for a in arrays),
        in_specs=[pl.BlockSpec(memory_space=pl.ANY)] * len(arrays),
        out_specs=tuple(pl.BlockSpec(memory_space=pltpu.VMEM) for _ in arrays),
        scratch_shapes=[pltpu.SemaphoreType.DMA((len(arrays),))],
        compiler_params=pltpu.CompilerParams(vmem_limit_bytes=1024 * 1024),
        cost_estimate=pl.CostEstimate(flops=0, bytes_accessed=sum(2 * a.size * a.dtype.itemsize for a in arrays), transcendentals=0),
    )(*(pltpu.with_memory_space_constraint(a, pltpu.HBM) for a in arrays))


def place():
    return lax.axis_index("section") % 4, lax.axis_index("dp")


def dot_nt(left, right):
    return lax.dot_general(left, right, (((1,), (1,)), ((), ())), preferred_element_type=F32)


def dot_tn(left, right):
    return lax.dot_general(left, right, (((0,), (0,)), ((), ())), preferred_element_type=F32)


def slot(index, size):
    return pl.ds(pl.multiple_of(index * size, size), size)


def spread_in_part(part, at, gain, weight, mine, total, begin):
    share = part.shape[1]
    piece = weight.shape[1] // 4
    scaled = (part[...].astype(F32) * gain[:, slot(at, share)]).astype(BF16)
    for d in (3, 2, 1, 0):
        block = jnp.dot(scaled, weight[slot(at, share), slot(mine ^ d, piece)], preferred_element_type=F32)
        columns = slice(d * piece, (d + 1) * piece)
        total[:, columns] = block if begin else total[:, columns] + block


def square_sum(part):
    wide = part[...].astype(F32)
    return jnp.sum(wide * wide, axis=1, keepdims=True)


def spread_in_first_kernel(x0, x1, gain, weight, total):
    mine, lane = place()
    spread_in_part(x0, lane, gain, weight, mine, total, True)
    spread_in_part(x1, lane ^ 1, gain, weight, mine, total, False)


def spread_in_last_kernel(x0, x1, x2, x3, gain, weight, before, own, s1, s2, s3, x_full, squares, total):
    mine, lane = place()
    rows, share = x0.shape
    piece = own.shape[1]
    total[...] = before[...]
    spread_in_part(x2, lane ^ 2, gain, weight, mine, total, False)
    spread_in_part(x3, lane ^ 3, gain, weight, mine, total, False)
    column = square_sum(x0) + square_sum(x1) + square_sum(x2) + square_sum(x3)
    block = pack_block(as_row(column, lane_blocks(rows) * LANES))
    for d, out in ((3, s3), (2, s2), (1, s1)):
        for i in range(piece // LANES):
            out[i * rows:(i + 1) * rows] = total[:, d * piece + i * LANES:d * piece + (i + 1) * LANES].astype(BF16)
        out[piece // LANES * rows:] = block
    own[...] = total[:, :piece]
    squares[...] = column
    for d, part in enumerate((x0, x1, x2, x3)):
        x_full[:, slot(lane ^ d, share)] = part[...]


def spread_dy(dy, weight, mine, own, s1, s2, s3):
    piece = own.shape[1]
    for d, out in ((3, s3), (2, s2), (1, s1)):
        out[...] = dot_nt(dy[...], weight[slot(mine ^ d, piece), :]).astype(BF16)
    own[...] = dot_nt(dy[...], weight[slot(mine, piece), :])


def spread_first_kernel(cot, sent, weight, own, s1, s2, s3, dy):
    mine, lane = place()

    @pl.when(lane == mine)
    def _():
        dy[...] = cot[...]

    @pl.when(lane != mine)
    def _():
        dy[...] = sent[...]

    spread_dy(dy, weight, mine, own, s1, s2, s3)


def spread_next_kernel(layers, ds, begin, end, *refs):
    parts, refs = refs[:len(ds)], refs[len(ds):]
    before, weight = refs[:2]
    refs = refs[2:]
    mine, lane = place()
    rows, share = parts[0].shape
    piece = weight.shape[0] // 4
    last = lax.axis_index("section") // 4 == layers - 1
    if begin:
        (total,) = refs
    elif end:
        earlier, *others, own, s1, s2, s3, dy, total = refs
        total[...] = earlier[...]
    else:
        earlier, total = refs
        total[...] = earlier[...]
    for i, (d, part) in enumerate(zip(ds, parts)):
        at = slot(lane ^ d, share)
        value = jnp.where(last, before[:, at], part[...])
        for j in (3, 2, 1, 0):
            block = dot_nt(value, weight[slot(mine ^ j, piece), at])
            columns = slice(j * piece, (j + 1) * piece)
            total[:, columns] = block if begin and i == 0 else total[:, columns] + block
    if end:
        for j, out in ((3, s3), (2, s2), (1, s1)):
            out[...] = total[:, j * piece:(j + 1) * piece].astype(BF16)
        own[...] = total[:, :piece]
        done = [d for d in range(4) if d not in ds]

        @pl.when(last)
        def _():
            dy[...] = before[...]

        @pl.when(jnp.logical_not(last))
        def _():
            for d, part in zip((*done, *ds), (*others, *parts)):
                dy[:, slot(lane ^ d, share)] = part[...]


def act_kernel(width, own, squares, g1, g2, g3, act, slope, hid, scale):
    rows, piece = act.shape
    count = lane_blocks(rows)
    sums = piece // LANES * rows
    row = pack_row(g1[sums:], count) + pack_row(g2[sums:], count) + pack_row(g3[sums:], count)
    r = lax.rsqrt((squares[...] + as_column(row, rows)) / width + 1e-06)
    scale[...] = r
    for i in range(piece // LANES):
        at = slice(i * LANES, (i + 1) * LANES)
        got = slice(i * rows, (i + 1) * rows)
        a = (own[:, at] + g1[got].astype(F32) + g2[got].astype(F32) + g3[got].astype(F32)) * r
        act[:, at] = a
        square = a * a
        t = jnp.tanh(GELU_IN * (a + GELU_CUBE * (square * a)))
        half = 0.5 * (1.0 + t)
        hid[:, at] = (a * half).astype(BF16)
        slope[:, at] = half + 0.5 * a * (1.0 - t * t) * (GELU_IN * (1.0 + 3.0 * GELU_CUBE * square))


def dact_kernel(own, g1, g2, g3, act, slope, pay):
    rows, piece = own.shape
    dhid = own[...] + g1[...].astype(F32) + g2[...].astype(F32) + g3[...].astype(F32)
    da = (dhid * slope[...]).astype(BF16)
    blocks = piece // LANES
    for i in range(blocks):
        pay[i * rows:(i + 1) * rows] = da[:, i * LANES:(i + 1) * LANES]
    column = jnp.sum(da.astype(F32) * act[...], axis=1, keepdims=True)
    pay[blocks * rows:] = pack_block(as_row(column, lane_blocks(rows) * LANES))


def back_part(part, j, weight, mine, lane, total, begin):
    value = unpack(part, total.shape[0])
    piece = value.shape[1]
    share = weight.shape[0] // 4
    for d in (1, 3, 0, 2):
        block = dot_nt(value, weight[slot(lane ^ d, share), slot(mine ^ j, piece)])
        columns = slice(d * share, (d + 1) * share)
        total[:, columns] = block if begin else total[:, columns] + block


def back_kernel(js, begin, *refs):
    *parts, weight = refs[:len(js) + 1]
    *earlier, total = refs[len(js) + 1:]
    mine, lane = place()
    if not begin:
        total[...] = earlier[0][...]
    for i, (j, part) in enumerate(zip(js, parts)):
        back_part(part, j, weight, mine, lane, total, begin and i == 0)


def back_last_kernel(p0, p1, p2, p3, weight, earlier, keep, send, total):
    mine, lane = place()
    rows = total.shape[0]
    share = weight.shape[0] // 4
    total[...] = earlier[...]
    back_part(p1, 1, weight, mine, lane, total, False)
    sums = p0.shape[0] - SIDE
    row = sum(pack_row(part[sums:], lane_blocks(rows)) for part in (p0, p1, p2, p3))
    if row.shape[1] < keep.shape[1]:
        row = jnp.concatenate([row, jnp.zeros((1, keep.shape[1] - row.shape[1]), F32)], axis=1)
    for at, d in ((0, 1), (1, 3)):
        send[:rows, at * share:(at + 1) * share] = total[:, d * share:(d + 1) * share].astype(BF16)
    send[rows:] = side_block(row)
    for at, d in ((0, 0), (1, 2)):
        keep[:rows, at * share:(at + 1) * share] = total[:, d * share:(d + 1) * share]
    keep[rows:] = jnp.broadcast_to(row, (SIDE, keep.shape[1]))


def middle_kernel(keep, got, rest, send):
    rows = keep.shape[0] - SIDE
    share = rest.shape[1]
    row = (keep[rows:rows + 1] + side_row(got[rows:]))[:, :share]
    send[:rows] = (keep[:rows, share:] + got[:rows, share:].astype(F32)).astype(BF16)
    send[rows:] = side_block(row)
    rest[:rows] = keep[:rows, :share] + got[:rows, :share].astype(F32)
    rest[rows:] = jnp.broadcast_to(row, (SIDE, share))


def finish_kernel(width, rest, got, x_own, dy, gain, scale, grad_x, *grad_gain):
    _, lane = place()
    rows, share = x_own.shape
    at = slot(lane, share)
    r = scale[...]
    du = rest[:rows] + got[:rows].astype(F32)
    normed = x_own[...].astype(F32) * r
    inner = as_column(rest[rows:rows + 1] + side_row(got[rows:]), rows) / width
    dnorm = du * gain[:, at]
    grad_x[...] = (dy[:, at].astype(F32) + r * (dnorm - normed * inner)).astype(BF16)
    if grad_gain:
        grad_gain[0][...] = jnp.sum(du * normed, axis=0, keepdims=True)


def grad_out_kernel(h0, h1, h2, h3, dy, out, held, sems):
    mine, _ = place()
    piece = h0.shape[1]
    copies = []
    for d, part in enumerate((h0, h1, h2, h3)):
        held[d] = dot_tn(part[...], dy[...]).astype(BF16)
        copies.append(pltpu.make_async_copy(held.at[d], out.at[slot(mine ^ d, piece), :], sems.at[d]))
        copies[-1].start()
    for copy in copies:
        copy.wait()


def grad_in_kernel(p0, p1, p2, p3, x_full, gain, scale, out, scaled, held, sems):
    mine, _ = place()
    rows = x_full.shape[0]
    piece = (p0.shape[0] - SIDE) // rows * LANES
    scaled[...] = (x_full[...].astype(F32) * scale[...] * gain[...]).astype(BF16)
    copies = []
    for d, part in enumerate((p0, p1, p2, p3)):
        held[d] = dot_tn(scaled[...], unpack(part, rows)).astype(BF16)
        copies.append(pltpu.make_async_copy(held.at[d], out.at[:, slot(mine ^ d, piece)], sems.at[d]))
        copies[-1].start()
    for copy in copies:
        copy.wait()


def gradient(body, shape, block, *args, scratch=(), flops=0):
    return pl.pallas_call(
        body,
        out_shape=jax.ShapeDtypeStruct(shape, BF16),
        in_specs=[pl.BlockSpec(memory_space=pltpu.VMEM)] * len(args),
        out_specs=pl.BlockSpec(memory_space=pl.ANY),
        scratch_shapes=[*scratch, pltpu.VMEM((4,) + block, BF16), pltpu.SemaphoreType.DMA((4,))],
        compiler_params=pltpu.CompilerParams(vmem_limit_bytes=16 * 1024 * 1024),
        cost_estimate=pl.CostEstimate(flops=flops, bytes_accessed=2 * shape[0] * shape[1], transcendentals=0),
    )(*args)


def shards_of_four(checkpoints, gain, w_in, w_out, cotangent):
    sections = lax.axis_size("section")
    here = lax.axis_index("section")
    lane = lax.axis_index("dp")
    layers = sections // 4
    mine = here % 4
    _, micro, tok, share = checkpoints.shape
    rows = micro * tok
    quarter = share * 4
    width = 4 * quarter
    hidden = w_in.shape[2]
    piece = hidden // 4
    work = 2 * rows * quarter * hidden

    x0 = checkpoints[0].reshape(rows, share)
    cot = cotangent.reshape(rows, quarter)
    top = [s * 4 + d for s in range(sections) for d in range(4) if s // 4 == layers - 1]
    x2 = flip(x0, "dp", 2)
    x1 = flip(x0, "dp", 1)
    weight_in, x0, gain = load(w_in[0], x0, gain)
    x2, x1, weight_in = lax.optimization_barrier((x2, x1, weight_in))
    sent = lax.ppermute(cot, ("section", "dp"), [((i // 4 ^ near) * 4 + i // 4 % 4, i) for i in top for near in (1, 0, 2) if i // 4 % 4 ^ i % 4 == (2, 1, 3)[near]])
    x3 = flip(x2, "dp", 1)

    packed = packed_shape(rows, piece)
    (begun,) = local(spread_in_first_kernel, [resident((rows, hidden), F32)], x0, x1, gain, weight_in, flops=work)
    own, s1, s2, s3, x_full, squares = local(
        spread_in_last_kernel,
        [resident((rows, piece), F32)] + [resident(packed, BF16)] * 3
        + [resident((rows, quarter), BF16), resident((rows, 1), F32)],
        x0, x1, x2, x3, gain, weight_in, begun,
        scratch=[pltpu.VMEM((rows, hidden), F32)], flops=work,
    )
    s1, s2, s3, cot, w_out = lax.optimization_barrier((s1, s2, s3, cot, w_out))
    g3 = flip(s3, "section", 3)
    g2 = flip(s2, "section", 2)
    g1 = flip(s1, "section", 1)
    weight_out, cot = load(w_out[0], cot)
    act, slope, hid, scale = local(
        functools.partial(act_kernel, width),
        [resident((rows, piece), F32), resident((rows, piece), F32), resident((rows, piece), BF16), resident((rows, 1), F32)],
        own, squares, g1, g2, g3,
    )

    spread_outs = [resident((rows, piece), F32)] + [resident((rows, piece), BF16)] * 3 + [resident((rows, quarter), BF16)]

    def gather_hidden(block):
        return [block] + [flip(block, "section", j) for j in (1, 2, 3)]

    if layers == 1:
        hids = gather_hidden(hid)
    for phase in range(layers):
        final = phase == layers - 1
        if phase == 0:
            own, s1, s2, s3, dy = local(spread_first_kernel, spread_outs, cot, sent, weight_out, flops=work)
        else:
            d0, d1, d2, d3 = down
            first, hids = lax.optimization_barrier((d0, hids))
            total = [resident((rows, hidden), F32)]
            step = functools.partial(spread_next_kernel, layers)
            begun = local(functools.partial(step, (0,), True, False), total, first, dy, weight_out, flops=work // 4)
            begun = local(functools.partial(step, (1, 2), False, False), total, d1, d2, dy, weight_out, *begun, flops=work // 2)
            own, s1, s2, s3, dy = local(
                functools.partial(step, (3,), False, True), spread_outs, d3, dy, weight_out, *begun, d0, d1, d2,
                scratch=[pltpu.VMEM((rows, hidden), F32)], flops=work // 4,
            )
        g3 = flip(s3, "section", 3)
        g2 = flip(s2, "section", 2)
        g1 = flip(s1, "section", 1)
        if final:
            grad_out = gradient(grad_out_kernel, (hidden, quarter), (piece, quarter), *hids, dy, flops=work)
            own, grad_out = lax.optimization_barrier((own, grad_out))
        (pay,) = local(dact_kernel, [resident(packed, BF16)], own, g1, g2, g3, act, slope)
        p3 = flip(pay, "section", 3)
        p2 = flip(pay, "section", 2)
        p1 = flip(pay, "section", 1)
        total = [resident((rows, quarter), F32)]
        begun = local(functools.partial(back_kernel, (0,), True), total, pay, weight_in, flops=work // 4)
        begun = local(functools.partial(back_kernel, (3, 2), False), total, p3, p2, weight_in, *begun, flops=work // 2)
        keep, send = local(
            back_last_kernel,
            [resident((rows + SIDE, 2 * share), F32), resident((rows + SIDE, 2 * share), BF16)],
            pay, p1, p2, p3, weight_in, *begun,
            scratch=[pltpu.VMEM((rows, quarter), F32)], flops=work // 4,
        )
        got = flip(send, "dp", 1)
        rest, send = local(
            middle_kernel,
            [resident((rows + SIDE, share), F32), resident((rows + SIDE, share), BF16)],
            keep, got,
        )
        if phase == 0 and not final:
            send, hid = lax.optimization_barrier((send, hid))
            hids = gather_hidden(hid)
        got = flip(send, "dp", 2)
        if final:
            grad_in = gradient(
                grad_in_kernel, (quarter, hidden), (quarter, piece), pay, p1, p2, p3, x_full, gain, scale,
                scratch=[pltpu.VMEM((rows, quarter), BF16)], flops=work,
            )
            got, grad_in = lax.optimization_barrier((got, grad_in))
        outs = [resident((rows, share), BF16)]
        if final:
            outs = [jax.ShapeDtypeStruct((rows, share), BF16), jax.ShapeDtypeStruct((1, share), F32)]
        finished = local(functools.partial(finish_kernel, width), outs, rest, got, x0, dy, gain, scale)
        if not final:
            d0 = lax.ppermute(finished[0], "section", [(i, i - 4) for i in range(4, sections)])
            d2 = flip(d0, "dp", 2)
            d1 = flip(d0, "dp", 1)
            d3 = flip(d2, "dp", 1)
            down = (d0, d1, d2, d3)

    grad_x, grad_gain = finished
    return grad_in[None], grad_out[None], grad_gain, grad_x.reshape(1, micro, tok, share)


def shards(checkpoints, gain, w_in, w_out, cotangent):
    rows = checkpoints.shape[1] * checkpoints.shape[2]
    share = checkpoints.shape[3]
    piece = w_in.shape[2] // 4
    if lax.axis_size("dp") == 4 and rows % 16 == 0 and share % 128 == 0 and piece % 128 == 0 and rows <= min(share, piece):
        return shards_of_four(checkpoints, gain, w_in, w_out, cotangent)
    return shards_of_any(checkpoints, gain, w_in, w_out, cotangent)


def solution(mesh):
    in_specs = (
        P("section", None, None, "dp"),
        P("section", None),
        P("section", None, "dp"),
        P("section", "dp", None),
        P(None, None, "dp"),
    )
    out_specs = (
        P("section", None, "dp"),
        P("section", "dp", None),
        P("section", "dp"),
        P("section", None, None, "dp"),
    )
    return jax.shard_map(shards, mesh=mesh, in_specs=in_specs, out_specs=out_specs, check_vma=False)
```

```python
import functools

import jax
import jax.numpy as jnp
from jax import lax
from jax.experimental import pallas as pl
from jax.experimental.pallas import tpu as pltpu
from jax.sharding import PartitionSpec as P

F32 = jnp.float32
BF16 = jnp.bfloat16


def flip(block, axis, bits):
    count = lax.axis_size(axis)
    return lax.ppermute(block, axis, [(i, i ^ bits) for i in range(count)])


def side_rows(values, width):
    lead = values.astype(BF16)
    trail = (values - lead.astype(F32)).astype(BF16)
    flat = jnp.concatenate([lead, trail])
    return jnp.pad(flat, (0, 16 * width - flat.shape[0])).reshape(16, width)


def side_values(rows, count):
    flat = rows.reshape(-1)
    return flat[:count].astype(F32) + flat[count:2 * count].astype(F32)


def gelu_tanh(value):
    return jax.nn.gelu(value, approximate=True)


def shards_of_any(checkpoints, gain, w_in, w_out, cotangent):
    sections = lax.axis_size("section")
    n_dp = lax.axis_size("dp")
    here = lax.axis_index("section")
    lane = lax.axis_index("dp")
    layers = sections // 4
    mine = here % 4
    last = here // 4 == layers - 1
    _, micro, tok, share = checkpoints.shape
    rows = micro * tok
    quarter = share * n_dp
    width = 4 * quarter
    gain_row = gain[0]
    weight_in = w_in[0]
    weight_out = w_out[0]
    hidden = weight_in.shape[1]
    piece = hidden // 4
    core = lane % 2

    def gather_dp(block):
        bit = n_dp // 2
        parts = {0: block}
        while bit >= 1:
            other = flip(jnp.concatenate([parts[j] for j in parts], axis=1), "dp", bit)
            for at, j in enumerate(list(parts)):
                parts[j ^ bit] = other[:, at * block.shape[1]:(at + 1) * block.shape[1]]
            bit //= 2
        full = jnp.zeros((rows, quarter), block.dtype)
        for j, part in parts.items():
            full = lax.dynamic_update_slice(full, part, (0, (lane ^ j) * block.shape[1]))
        return full

    def cot_quarter(block):
        if n_dp < 4:
            whole = lax.all_gather(block, "dp", axis=1, tiled=True)
            return lax.dynamic_slice_in_dim(whole, mine * quarter, quarter, 1)
        per = n_dp // 4
        top = [s * n_dp + d for s in range(sections) for d in range(n_dp) if s // 4 == layers - 1]
        held = block
        far = lambda i, b: (i % n_dp // per ^ i // n_dp % 4) & b
        got = lax.ppermute(held, ("section", "dp"), [(i, i ^ 2 * per) for i in top if far(i, 3) == 0])
        held = jnp.where((lane // per ^ mine) & 2 == 0, held, got)
        got = lax.ppermute(held, ("section", "dp"), [(i, i ^ per) for i in top if far(i, 1) == 0])
        held = jnp.where((lane // per ^ mine) & 1 == 0, held, got)
        if per == 1:
            return held
        parts = {0: held}
        bit = per // 2
        while bit >= 1:
            for j in list(parts):
                parts[j ^ bit] = flip(parts[j], "dp", bit)
            bit //= 2
        full = jnp.zeros((rows, quarter), block.dtype)
        for j, part in parts.items():
            full = lax.dynamic_update_slice(full, part, (0, (lane % per ^ j) * block.shape[1]))
        return full

    def cut(values, j):
        return lax.dynamic_slice_in_dim(values, (mine ^ j) * piece, piece, 1)

    def fill(parts):
        full = jnp.zeros((rows, hidden), parts[0].dtype)
        for j, part in enumerate(parts):
            full = lax.dynamic_update_slice(full, part, (0, (mine ^ j) * piece))
        return full

    x_full = gather_dp(checkpoints[0].reshape(rows, share))
    cot = cot_quarter(cotangent.reshape(rows, cotangent.shape[2]))
    x_wide = x_full.astype(F32)
    scaled_raw = (x_wide * gain_row).astype(BF16)
    squares = jnp.sum(x_wide * x_wide, axis=1)

    act_raw = jnp.dot(scaled_raw, weight_in, preferred_element_type=F32)
    extra = side_rows(squares, piece)
    act = cut(act_raw, 0)
    for j in (3, 1, 2):
        got = flip(jnp.concatenate([cut(act_raw, j).astype(BF16), extra], axis=0), "section", j)
        act = act + got[:rows].astype(F32)
        squares = squares + side_values(got[rows:], rows)
    scale = lax.rsqrt(squares / width + 1e-06)[:, None]
    act = act * scale
    hid, pull = jax.vjp(gelu_tanh, act)
    hid = hid.astype(BF16)
    hid_full = fill([hid] + [flip(hid, "section", j) for j in (1, 2, 3)])
    normed = x_wide * scale
    scaled = (normed * gain_row).astype(BF16)

    def halves(values, side):
        pairs = values.reshape(rows, n_dp // 2, 2, share)
        return jnp.where(side == 0, pairs[:, :, 0], pairs[:, :, 1]).reshape(rows, quarter // 2)

    def own(values):
        return lax.dynamic_slice_in_dim(values, lane // 2 * share, share, 1)

    incoming = jnp.zeros((rows, quarter), BF16)
    normed_half = halves(normed, core)
    gain_half = halves(jnp.broadcast_to(gain_row, (rows, quarter)), core)
    for phase in range(layers):
        final = phase == layers - 1
        dy = jnp.where(last, cot, incoming) if phase > 0 else cot
        dhid_raw = jnp.dot(dy, weight_out.T, preferred_element_type=F32)
        dhid = cut(dhid_raw, 0)
        for j in (3, 1, 2):
            dhid = dhid + flip(cut(dhid_raw, j).astype(BF16), "section", j).astype(F32)
        dact = pull(dhid)[0].astype(BF16)
        inner = jnp.sum(dact.astype(F32) * act, axis=1)
        payload = jnp.concatenate([dact, side_rows(inner, piece)], axis=0)
        others = [flip(payload, "section", j) for j in (1, 2, 3)]
        for got in others:
            inner = inner + side_values(got[rows:], rows)
        dact_full = fill([dact] + [got[:rows] for got in others])
        part = jnp.dot(dact_full, weight_in.T, preferred_element_type=F32).astype(BF16)

        send = jnp.concatenate([halves(part, 1 - core), side_rows(inner, quarter // 2)], axis=0)
        got = flip(send, "dp", 1)
        dscaled = halves(part, core).astype(F32) + got[:rows].astype(F32)
        inner = inner + side_values(got[rows:], rows)
        bit = 2
        while bit < n_dp:
            send = jnp.concatenate([dscaled.astype(BF16), side_rows(inner, quarter // 2)], axis=0)
            got = flip(send, "dp", bit)
            dscaled = dscaled + got[:rows].astype(F32)
            inner = inner + side_values(got[rows:], rows)
            bit *= 2
        dnorm = dscaled * gain_half
        dy_half = halves(dy, core).astype(F32)
        grad_x = (dy_half + scale * (dnorm - normed_half * (inner / width)[:, None])).astype(BF16)
        if not final:
            down = lax.ppermute(grad_x, "section", [(i, i - 4) for i in range(4, sections)])
            other = flip(down, "dp", 1)
            pairs = jnp.where(
                core == 0,
                jnp.stack([down.reshape(rows, n_dp // 2, share), other.reshape(rows, n_dp // 2, share)], axis=2),
                jnp.stack([other.reshape(rows, n_dp // 2, share), down.reshape(rows, n_dp // 2, share)], axis=2),
            )
            incoming = pairs.reshape(rows, quarter)

    grad_out = jnp.dot(hid_full.T, dy, preferred_element_type=F32).astype(BF16)
    grad_in = jnp.dot(scaled.T, dact_full, preferred_element_type=F32).astype(BF16)
    grad_gain = jnp.sum(own(dscaled) * own(normed_half), axis=0)
    return (
        grad_in[None],
        grad_out[None],
        grad_gain[None],
        own(grad_x).reshape(1, micro, tok, share),
    )


SIDE = 16
LANES = 128
GELU_IN = 0.7978845608028654
GELU_CUBE = 0.044715


def resident(shape, dtype):
    return pltpu.VMEM(shape, dtype)


def local(body, outs, *args, scratch=(), flops=0):
    spec = pl.BlockSpec(memory_space=pltpu.VMEM)
    moved = sum(a.size * a.dtype.itemsize for a in args)
    return pl.pallas_call(
        body,
        out_shape=tuple(outs),
        in_specs=[spec] * len(args),
        out_specs=tuple(spec for _ in outs),
        scratch_shapes=list(scratch),
        compiler_params=pltpu.CompilerParams(vmem_limit_bytes=16 * 1024 * 1024),
        cost_estimate=pl.CostEstimate(flops=flops, bytes_accessed=moved, transcendentals=0),
    )(*args)


def diagonal(rows, width):
    return lax.broadcasted_iota(jnp.int32, (rows, width), 0) == lax.broadcasted_iota(jnp.int32, (rows, width), 1)


def as_row(column, width):
    rows = column.shape[0]
    return jnp.sum(jnp.where(diagonal(rows, width), column, 0.0), axis=0, keepdims=True)


def as_column(row, rows):
    return jnp.sum(jnp.where(diagonal(rows, row.shape[1]), row, 0.0), axis=1, keepdims=True)


def side_block(row):
    lead = row.astype(BF16).astype(F32)
    at = lax.broadcasted_iota(jnp.int32, (SIDE, row.shape[1]), 0)
    return jnp.where(at == 0, lead, jnp.where(at == 1, row - lead, 0.0)).astype(BF16)


def side_row(block):
    wide = block.astype(F32)
    return wide[0:1] + wide[1:2]


def packed_shape(rows, piece):
    return (piece // LANES * rows + SIDE, LANES)


def pack_block(row):
    lead = row.astype(BF16).astype(F32)
    count = row.shape[1] // LANES
    at = lax.broadcasted_iota(jnp.int32, (SIDE, LANES), 0)
    block = jnp.zeros((SIDE, LANES), F32)
    for i in range(count):
        lanes = slice(i * LANES, (i + 1) * LANES)
        block = jnp.where(at == i, lead[:, lanes], jnp.where(at == count + i, (row - lead)[:, lanes], block))
    return block.astype(BF16)


def pack_row(block, count):
    wide = block.astype(F32)
    return jnp.concatenate([wide[i:i + 1] + wide[count + i:count + i + 1] for i in range(count)], axis=1)


def lane_blocks(rows):
    return -(-rows // LANES)


def unpack(packed, rows):
    blocks = (packed.shape[0] - SIDE) // rows
    return jnp.concatenate([packed[i * rows:(i + 1) * rows] for i in range(blocks)], axis=1)


def load_kernel(*refs):
    count = len(refs) // 2
    copies = [pltpu.make_async_copy(refs[i], refs[count + i], refs[-1].at[i]) for i in range(count)]
    for copy in copies:
        copy.start()
    for copy in copies:
        copy.wait()


def load(*arrays):
    return pl.pallas_call(
        load_kernel,
        out_shape=tuple(resident(a.shape, a.dtype) for a in arrays),
        in_specs=[pl.BlockSpec(memory_space=pl.ANY)] * len(arrays),
        out_specs=tuple(pl.BlockSpec(memory_space=pltpu.VMEM) for _ in arrays),
        scratch_shapes=[pltpu.SemaphoreType.DMA((len(arrays),))],
        compiler_params=pltpu.CompilerParams(vmem_limit_bytes=1024 * 1024),
        cost_estimate=pl.CostEstimate(flops=0, bytes_accessed=sum(2 * a.size * a.dtype.itemsize for a in arrays), transcendentals=0),
    )(*(pltpu.with_memory_space_constraint(a, pltpu.HBM) for a in arrays))


def place():
    return lax.axis_index("section") % 4, lax.axis_index("dp")


def dot_nt(left, right):
    return lax.dot_general(left, right, (((1,), (1,)), ((), ())), preferred_element_type=F32)


def dot_tn(left, right):
    return lax.dot_general(left, right, (((0,), (0,)), ((), ())), preferred_element_type=F32)


def slot(index, size):
    return pl.ds(pl.multiple_of(index * size, size), size)


def spread_in_part(part, at, gain, weight, mine, total, begin):
    share = part.shape[1]
    piece = weight.shape[1] // 4
    scaled = (part[...].astype(F32) * gain[:, slot(at, share)]).astype(BF16)
    for d in (3, 2, 1, 0):
        block = jnp.dot(scaled, weight[slot(at, share), slot(mine ^ d, piece)], preferred_element_type=F32)
        columns = slice(d * piece, (d + 1) * piece)
        total[:, columns] = block if begin else total[:, columns] + block


def square_sum(part):
    wide = part[...].astype(F32)
    return jnp.sum(wide * wide, axis=1, keepdims=True)


def load_spread_kernel(x1, weight, x0, gain, weight_held, x0_held, gain_held, total, sems):
    mine, lane = place()
    share = x1.shape[1]
    small = [pltpu.make_async_copy(source, held, sems.at[i]) for i, (source, held) in enumerate(((x0, x0_held), (gain, gain_held)))]
    slices = [slot(lane ^ d, share) for d in range(4)]
    large = [pltpu.make_async_copy(weight.at[at], weight_held.at[at], sems.at[2 + d]) for d, at in enumerate(slices)]
    for copy in (*small, *large):
        copy.start()
    for copy in (*small, large[0]):
        copy.wait()
    spread_in_part(x0_held, lane, gain_held, weight_held, mine, total, True)
    large[1].wait()
    spread_in_part(x1, lane ^ 1, gain_held, weight_held, mine, total, False)
    large[2].wait()
    large[3].wait()


def load_spread(x1, weight, x0, gain):
    keep = pl.BlockSpec(memory_space=pltpu.VMEM)
    rows, hidden = x0.shape[0], weight.shape[1]
    outs = [(a.shape, a.dtype) for a in (weight, x0, gain)] + [((rows, hidden), F32)]
    far = [pltpu.with_memory_space_constraint(a, pltpu.HBM) for a in (weight, x0, gain)]
    return pl.pallas_call(
        load_spread_kernel,
        out_shape=tuple(resident(*out) for out in outs),
        in_specs=[keep] + [pl.BlockSpec(memory_space=pl.ANY)] * 3,
        out_specs=(keep,) * 4,
        scratch_shapes=[pltpu.SemaphoreType.DMA((6,))],
        compiler_params=pltpu.CompilerParams(vmem_limit_bytes=8 * 1024 * 1024),
        cost_estimate=pl.CostEstimate(flops=rows * weight.size, bytes_accessed=4 * weight.size, transcendentals=0),
    )(x1, *far)


def spread_in_last_kernel(x0, x1, x2, x3, gain, weight, before, own, s1, s2, s3, x_full, squares, total):
    mine, lane = place()
    rows, share = x0.shape
    piece = own.shape[1]
    total[...] = before[...]
    spread_in_part(x2, lane ^ 2, gain, weight, mine, total, False)
    spread_in_part(x3, lane ^ 3, gain, weight, mine, total, False)
    column = square_sum(x0) + square_sum(x1) + square_sum(x2) + square_sum(x3)
    block = pack_block(as_row(column, lane_blocks(rows) * LANES))
    for d, out in ((3, s3), (2, s2), (1, s1)):
        for i in range(piece // LANES):
            out[i * rows:(i + 1) * rows] = total[:, d * piece + i * LANES:d * piece + (i + 1) * LANES].astype(BF16)
        out[piece // LANES * rows:] = block
    own[...] = total[:, :piece]
    squares[...] = column
    for d, part in enumerate((x0, x1, x2, x3)):
        x_full[:, slot(lane ^ d, share)] = part[...]


def spread_dy(dy, weight, mine, own, s1, s2, s3):
    piece = own.shape[1]
    for d, out in ((3, s3), (2, s2), (1, s1)):
        out[...] = dot_nt(dy[...], weight[slot(mine ^ d, piece), :]).astype(BF16)
    own[...] = dot_nt(dy[...], weight[slot(mine, piece), :])


def spread_first_kernel(cot, sent, weight, own, s1, s2, s3, dy):
    mine, lane = place()

    @pl.when(lane == mine)
    def _():
        dy[...] = cot[...]

    @pl.when(lane != mine)
    def _():
        dy[...] = sent[...]

    spread_dy(dy, weight, mine, own, s1, s2, s3)


def spread_next_kernel(layers, ds, begin, end, *refs):
    parts, refs = refs[:len(ds)], refs[len(ds):]
    before, weight = refs[:2]
    refs = refs[2:]
    mine, lane = place()
    rows, share = parts[0].shape
    piece = weight.shape[0] // 4
    last = lax.axis_index("section") // 4 == layers - 1
    if begin:
        (total,) = refs
    elif end:
        earlier, *others, own, s1, s2, s3, dy, total = refs
        total[...] = earlier[...]
    else:
        earlier, total = refs
        total[...] = earlier[...]
    for i, (d, part) in enumerate(zip(ds, parts)):
        at = slot(lane ^ d, share)
        value = jnp.where(last, before[:, at], part[...])
        for j in (3, 2, 1, 0):
            block = dot_nt(value, weight[slot(mine ^ j, piece), at])
            columns = slice(j * piece, (j + 1) * piece)
            total[:, columns] = block if begin and i == 0 else total[:, columns] + block
    if end:
        for j, out in ((3, s3), (2, s2), (1, s1)):
            out[...] = total[:, j * piece:(j + 1) * piece].astype(BF16)
        own[...] = total[:, :piece]
        done = [d for d in range(4) if d not in ds]

        @pl.when(last)
        def _():
            dy[...] = before[...]

        @pl.when(jnp.logical_not(last))
        def _():
            for d, part in zip((*done, *ds), (*others, *parts)):
                dy[:, slot(lane ^ d, share)] = part[...]


def act_kernel(width, own, squares, g1, g2, g3, act, slope, hid, scale):
    rows, piece = act.shape
    count = lane_blocks(rows)
    sums = piece // LANES * rows
    row = pack_row(g1[sums:], count) + pack_row(g2[sums:], count) + pack_row(g3[sums:], count)
    r = lax.rsqrt((squares[...] + as_column(row, rows)) / width + 1e-06)
    scale[...] = r
    for i in range(piece // LANES):
        at = slice(i * LANES, (i + 1) * LANES)
        got = slice(i * rows, (i + 1) * rows)
        a = (own[:, at] + g1[got].astype(F32) + g2[got].astype(F32) + g3[got].astype(F32)) * r
        act[:, at] = a
        square = a * a
        t = jnp.tanh(GELU_IN * (a + GELU_CUBE * (square * a)))
        half = 0.5 * (1.0 + t)
        hid[:, at] = (a * half).astype(BF16)
        slope[:, at] = half + 0.5 * a * (1.0 - t * t) * (GELU_IN * (1.0 + 3.0 * GELU_CUBE * square))


def dact_kernel(own, g1, g2, g3, act, slope, pay):
    rows, piece = own.shape
    dhid = own[...] + g1[...].astype(F32) + g2[...].astype(F32) + g3[...].astype(F32)
    da = (dhid * slope[...]).astype(BF16)
    blocks = piece // LANES
    for i in range(blocks):
        pay[i * rows:(i + 1) * rows] = da[:, i * LANES:(i + 1) * LANES]
    column = jnp.sum(da.astype(F32) * act[...], axis=1, keepdims=True)
    pay[blocks * rows:] = pack_block(as_row(column, lane_blocks(rows) * LANES))


def back_part(part, j, weight, mine, lane, total, begin):
    value = unpack(part, total.shape[0])
    piece = value.shape[1]
    share = weight.shape[0] // 4
    for d in (1, 3, 0, 2):
        block = dot_nt(value, weight[slot(lane ^ d, share), slot(mine ^ j, piece)])
        columns = slice(d * share, (d + 1) * share)
        total[:, columns] = block if begin else total[:, columns] + block


def back_kernel(js, begin, *refs):
    *parts, weight = refs[:len(js) + 1]
    *earlier, total = refs[len(js) + 1:]
    mine, lane = place()
    if not begin:
        total[...] = earlier[0][...]
    for i, (j, part) in enumerate(zip(js, parts)):
        back_part(part, j, weight, mine, lane, total, begin and i == 0)


def back_last_kernel(p0, p1, p2, p3, weight, earlier, keep, send, total):
    mine, lane = place()
    rows = total.shape[0]
    share = weight.shape[0] // 4
    total[...] = earlier[...]
    back_part(p1, 1, weight, mine, lane, total, False)
    sums = p0.shape[0] - SIDE
    row = sum(pack_row(part[sums:], lane_blocks(rows)) for part in (p0, p1, p2, p3))
    if row.shape[1] < keep.shape[1]:
        row = jnp.concatenate([row, jnp.zeros((1, keep.shape[1] - row.shape[1]), F32)], axis=1)
    for at, d in ((0, 1), (1, 3)):
        send[:rows, at * share:(at + 1) * share] = total[:, d * share:(d + 1) * share].astype(BF16)
    send[rows:] = side_block(row)
    for at, d in ((0, 0), (1, 2)):
        keep[:rows, at * share:(at + 1) * share] = total[:, d * share:(d + 1) * share]
    keep[rows:] = jnp.broadcast_to(row, (SIDE, keep.shape[1]))


def middle_kernel(keep, got, rest, send):
    rows = keep.shape[0] - SIDE
    share = rest.shape[1]
    row = (keep[rows:rows + 1] + side_row(got[rows:]))[:, :share]
    send[:rows] = (keep[:rows, share:] + got[:rows, share:].astype(F32)).astype(BF16)
    send[rows:] = side_block(row)
    rest[:rows] = keep[:rows, :share] + got[:rows, :share].astype(F32)
    rest[rows:] = jnp.broadcast_to(row, (SIDE, share))


def finish_kernel(width, rest, got, x_own, dy, gain, scale, grad_x, *grad_gain):
    _, lane = place()
    rows, share = x_own.shape
    at = slot(lane, share)
    r = scale[...]
    du = rest[:rows] + got[:rows].astype(F32)
    normed = x_own[...].astype(F32) * r
    inner = as_column(rest[rows:rows + 1] + side_row(got[rows:]), rows) / width
    dnorm = du * gain[:, at]
    grad_x[...] = (dy[:, at].astype(F32) + r * (dnorm - normed * inner)).astype(BF16)
    if grad_gain:
        grad_gain[0][...] = jnp.sum(du * normed, axis=0, keepdims=True)


def grad_out_kernel(h0, h1, h2, h3, dy, out, held, sems):
    mine, _ = place()
    piece = h0.shape[1]
    copies = []
    for d, part in enumerate((h0, h1, h2, h3)):
        held[d] = dot_tn(part[...], dy[...]).astype(BF16)
        copies.append(pltpu.make_async_copy(held.at[d], out.at[slot(mine ^ d, piece), :], sems.at[d]))
        copies[-1].start()
    for copy in copies:
        copy.wait()


def grad_in_kernel(p0, p1, p2, p3, x_full, gain, scale, out, scaled, held, sems):
    mine, _ = place()
    rows = x_full.shape[0]
    piece = (p0.shape[0] - SIDE) // rows * LANES
    scaled[...] = (x_full[...].astype(F32) * scale[...] * gain[...]).astype(BF16)
    copies = []
    for d, part in enumerate((p0, p1, p2, p3)):
        held[d] = dot_tn(scaled[...], unpack(part, rows)).astype(BF16)
        copies.append(pltpu.make_async_copy(held.at[d], out.at[:, slot(mine ^ d, piece)], sems.at[d]))
        copies[-1].start()
    for copy in copies:
        copy.wait()


def gradient(body, shape, block, *args, scratch=(), flops=0):
    return pl.pallas_call(
        body,
        out_shape=jax.ShapeDtypeStruct(shape, BF16),
        in_specs=[pl.BlockSpec(memory_space=pltpu.VMEM)] * len(args),
        out_specs=pl.BlockSpec(memory_space=pl.ANY),
        scratch_shapes=[*scratch, pltpu.VMEM((4,) + block, BF16), pltpu.SemaphoreType.DMA((4,))],
        compiler_params=pltpu.CompilerParams(vmem_limit_bytes=16 * 1024 * 1024),
        cost_estimate=pl.CostEstimate(flops=flops, bytes_accessed=2 * shape[0] * shape[1], transcendentals=0),
    )(*args)


def shards_of_four(checkpoints, gain, w_in, w_out, cotangent):
    sections = lax.axis_size("section")
    here = lax.axis_index("section")
    lane = lax.axis_index("dp")
    layers = sections // 4
    mine = here % 4
    _, micro, tok, share = checkpoints.shape
    rows = micro * tok
    quarter = share * 4
    width = 4 * quarter
    hidden = w_in.shape[2]
    piece = hidden // 4
    work = 2 * rows * quarter * hidden

    x0 = checkpoints[0].reshape(rows, share)
    cot = cotangent.reshape(rows, quarter)
    top = [s * 4 + d for s in range(sections) for d in range(4) if s // 4 == layers - 1]
    x2 = flip(x0, "dp", 2)
    x1 = flip(x0, "dp", 1)
    weight_in, x0, gain, begun = load_spread(x1, w_in[0], x0, gain)
    x2, weight_in = lax.optimization_barrier((x2, weight_in))
    sent = lax.ppermute(cot, ("section", "dp"), [((i // 4 ^ near) * 4 + i // 4 % 4, i) for i in top for near in (1, 0, 2) if i // 4 % 4 ^ i % 4 == (2, 1, 3)[near]])
    x3 = flip(x2, "dp", 1)

    packed = packed_shape(rows, piece)
    own, s1, s2, s3, x_full, squares = local(
        spread_in_last_kernel,
        [resident((rows, piece), F32)] + [resident(packed, BF16)] * 3
        + [resident((rows, quarter), BF16), resident((rows, 1), F32)],
        x0, x1, x2, x3, gain, weight_in, begun,
        scratch=[pltpu.VMEM((rows, hidden), F32)], flops=work,
    )
    s1, s2, s3, cot, w_out = lax.optimization_barrier((s1, s2, s3, cot, w_out))
    g3 = flip(s3, "section", 3)
    g2 = flip(s2, "section", 2)
    g1 = flip(s1, "section", 1)
    weight_out, cot = load(w_out[0], cot)
    act, slope, hid, scale = local(
        functools.partial(act_kernel, width),
        [resident((rows, piece), F32), resident((rows, piece), F32), resident((rows, piece), BF16), resident((rows, 1), F32)],
        own, squares, g1, g2, g3,
    )

    spread_outs = [resident((rows, piece), F32)] + [resident((rows, piece), BF16)] * 3 + [resident((rows, quarter), BF16)]

    def gather_hidden(block):
        return [block] + [flip(block, "section", j) for j in (1, 2, 3)]

    if layers == 1:
        hids = gather_hidden(hid)
    for phase in range(layers):
        final = phase == layers - 1
        if phase == 0:
            own, s1, s2, s3, dy = local(spread_first_kernel, spread_outs, cot, sent, weight_out, flops=work)
        else:
            d0, d1, d2, d3 = down
            first, hids = lax.optimization_barrier((d0, hids))
            total = [resident((rows, hidden), F32)]
            step = functools.partial(spread_next_kernel, layers)
            begun = local(functools.partial(step, (0,), True, False), total, first, dy, weight_out, flops=work // 4)
            begun = local(functools.partial(step, (1, 2), False, False), total, d1, d2, dy, weight_out, *begun, flops=work // 2)
            own, s1, s2, s3, dy = local(
                functools.partial(step, (3,), False, True), spread_outs, d3, dy, weight_out, *begun, d0, d1, d2,
                scratch=[pltpu.VMEM((rows, hidden), F32)], flops=work // 4,
            )
        g3 = flip(s3, "section", 3)
        g2 = flip(s2, "section", 2)
        g1 = flip(s1, "section", 1)
        if final:
            grad_out = gradient(grad_out_kernel, (hidden, quarter), (piece, quarter), *hids, dy, flops=work)
            own, grad_out = lax.optimization_barrier((own, grad_out))
        (pay,) = local(dact_kernel, [resident(packed, BF16)], own, g1, g2, g3, act, slope)
        p3 = flip(pay, "section", 3)
        p2 = flip(pay, "section", 2)
        p1 = flip(pay, "section", 1)
        total = [resident((rows, quarter), F32)]
        begun = local(functools.partial(back_kernel, (0,), True), total, pay, weight_in, flops=work // 4)
        begun = local(functools.partial(back_kernel, (3, 2), False), total, p3, p2, weight_in, *begun, flops=work // 2)
        keep, send = local(
            back_last_kernel,
            [resident((rows + SIDE, 2 * share), F32), resident((rows + SIDE, 2 * share), BF16)],
            pay, p1, p2, p3, weight_in, *begun,
            scratch=[pltpu.VMEM((rows, quarter), F32)], flops=work // 4,
        )
        got = flip(send, "dp", 1)
        rest, send = local(
            middle_kernel,
            [resident((rows + SIDE, share), F32), resident((rows + SIDE, share), BF16)],
            keep, got,
        )
        if phase == 0 and not final:
            send, hid = lax.optimization_barrier((send, hid))
            hids = gather_hidden(hid)
        got = flip(send, "dp", 2)
        if final:
            grad_in = gradient(
                grad_in_kernel, (quarter, hidden), (quarter, piece), pay, p1, p2, p3, x_full, gain, scale,
                scratch=[pltpu.VMEM((rows, quarter), BF16)], flops=work,
            )
            got, grad_in = lax.optimization_barrier((got, grad_in))
        outs = [resident((rows, share), BF16)]
        if final:
            outs = [jax.ShapeDtypeStruct((rows, share), BF16), jax.ShapeDtypeStruct((1, share), F32)]
        finished = local(functools.partial(finish_kernel, width), outs, rest, got, x0, dy, gain, scale)
        if not final:
            d0 = lax.ppermute(finished[0], "section", [(i, i - 4) for i in range(4, sections)])
            d2 = flip(d0, "dp", 2)
            d1 = flip(d0, "dp", 1)
            d3 = flip(d2, "dp", 1)
            down = (d0, d1, d2, d3)

    grad_x, grad_gain = finished
    return grad_in[None], grad_out[None], grad_gain, grad_x.reshape(1, micro, tok, share)


def shards(checkpoints, gain, w_in, w_out, cotangent):
    rows = checkpoints.shape[1] * checkpoints.shape[2]
    share = checkpoints.shape[3]
    piece = w_in.shape[2] // 4
    if lax.axis_size("dp") == 4 and rows % 16 == 0 and share % 128 == 0 and piece % 128 == 0 and rows <= min(share, piece):
        return shards_of_four(checkpoints, gain, w_in, w_out, cotangent)
    return shards_of_any(checkpoints, gain, w_in, w_out, cotangent)


def solution(mesh):
    in_specs = (
        P("section", None, None, "dp"),
        P("section", None),
        P("section", None, "dp"),
        P("section", "dp", None),
        P(None, None, "dp"),
    )
    out_specs = (
        P("section", None, "dp"),
        P("section", "dp", None),
        P("section", "dp"),
        P("section", None, None, "dp"),
    )
    return jax.shard_map(shards, mesh=mesh, in_specs=in_specs, out_specs=out_specs, check_vma=False)
```

```python
import functools

import jax
import jax.numpy as jnp
from jax import lax
from jax.experimental import pallas as pl
from jax.experimental.pallas import tpu as pltpu
from jax.sharding import PartitionSpec as P

F32 = jnp.float32
BF16 = jnp.bfloat16


def flip(block, axis, bits):
    count = lax.axis_size(axis)
    return lax.ppermute(block, axis, [(i, i ^ bits) for i in range(count)])


def side_rows(values, width):
    lead = values.astype(BF16)
    trail = (values - lead.astype(F32)).astype(BF16)
    flat = jnp.concatenate([lead, trail])
    return jnp.pad(flat, (0, 16 * width - flat.shape[0])).reshape(16, width)


def side_values(rows, count):
    flat = rows.reshape(-1)
    return flat[:count].astype(F32) + flat[count:2 * count].astype(F32)


def gelu_tanh(value):
    return jax.nn.gelu(value, approximate=True)


def shards_of_any(checkpoints, gain, w_in, w_out, cotangent):
    sections = lax.axis_size("section")
    n_dp = lax.axis_size("dp")
    here = lax.axis_index("section")
    lane = lax.axis_index("dp")
    layers = sections // 4
    mine = here % 4
    last = here // 4 == layers - 1
    _, micro, tok, share = checkpoints.shape
    rows = micro * tok
    quarter = share * n_dp
    width = 4 * quarter
    gain_row = gain[0]
    weight_in = w_in[0]
    weight_out = w_out[0]
    hidden = weight_in.shape[1]
    piece = hidden // 4
    core = lane % 2

    def gather_dp(block):
        bit = n_dp // 2
        parts = {0: block}
        while bit >= 1:
            other = flip(jnp.concatenate([parts[j] for j in parts], axis=1), "dp", bit)
            for at, j in enumerate(list(parts)):
                parts[j ^ bit] = other[:, at * block.shape[1]:(at + 1) * block.shape[1]]
            bit //= 2
        full = jnp.zeros((rows, quarter), block.dtype)
        for j, part in parts.items():
            full = lax.dynamic_update_slice(full, part, (0, (lane ^ j) * block.shape[1]))
        return full

    def cot_quarter(block):
        if n_dp < 4:
            whole = lax.all_gather(block, "dp", axis=1, tiled=True)
            return lax.dynamic_slice_in_dim(whole, mine * quarter, quarter, 1)
        per = n_dp // 4
        top = [s * n_dp + d for s in range(sections) for d in range(n_dp) if s // 4 == layers - 1]
        held = block
        far = lambda i, b: (i % n_dp // per ^ i // n_dp % 4) & b
        got = lax.ppermute(held, ("section", "dp"), [(i, i ^ 2 * per) for i in top if far(i, 3) == 0])
        held = jnp.where((lane // per ^ mine) & 2 == 0, held, got)
        got = lax.ppermute(held, ("section", "dp"), [(i, i ^ per) for i in top if far(i, 1) == 0])
        held = jnp.where((lane // per ^ mine) & 1 == 0, held, got)
        if per == 1:
            return held
        parts = {0: held}
        bit = per // 2
        while bit >= 1:
            for j in list(parts):
                parts[j ^ bit] = flip(parts[j], "dp", bit)
            bit //= 2
        full = jnp.zeros((rows, quarter), block.dtype)
        for j, part in parts.items():
            full = lax.dynamic_update_slice(full, part, (0, (lane % per ^ j) * block.shape[1]))
        return full

    def cut(values, j):
        return lax.dynamic_slice_in_dim(values, (mine ^ j) * piece, piece, 1)

    def fill(parts):
        full = jnp.zeros((rows, hidden), parts[0].dtype)
        for j, part in enumerate(parts):
            full = lax.dynamic_update_slice(full, part, (0, (mine ^ j) * piece))
        return full

    x_full = gather_dp(checkpoints[0].reshape(rows, share))
    cot = cot_quarter(cotangent.reshape(rows, cotangent.shape[2]))
    x_wide = x_full.astype(F32)
    scaled_raw = (x_wide * gain_row).astype(BF16)
    squares = jnp.sum(x_wide * x_wide, axis=1)

    act_raw = jnp.dot(scaled_raw, weight_in, preferred_element_type=F32)
    extra = side_rows(squares, piece)
    act = cut(act_raw, 0)
    for j in (3, 1, 2):
        got = flip(jnp.concatenate([cut(act_raw, j).astype(BF16), extra], axis=0), "section", j)
        act = act + got[:rows].astype(F32)
        squares = squares + side_values(got[rows:], rows)
    scale = lax.rsqrt(squares / width + 1e-06)[:, None]
    act = act * scale
    hid, pull = jax.vjp(gelu_tanh, act)
    hid = hid.astype(BF16)
    hid_full = fill([hid] + [flip(hid, "section", j) for j in (1, 2, 3)])
    normed = x_wide * scale
    scaled = (normed * gain_row).astype(BF16)

    def halves(values, side):
        pairs = values.reshape(rows, n_dp // 2, 2, share)
        return jnp.where(side == 0, pairs[:, :, 0], pairs[:, :, 1]).reshape(rows, quarter // 2)

    def own(values):
        return lax.dynamic_slice_in_dim(values, lane // 2 * share, share, 1)

    incoming = jnp.zeros((rows, quarter), BF16)
    normed_half = halves(normed, core)
    gain_half = halves(jnp.broadcast_to(gain_row, (rows, quarter)), core)
    for phase in range(layers):
        final = phase == layers - 1
        dy = jnp.where(last, cot, incoming) if phase > 0 else cot
        dhid_raw = jnp.dot(dy, weight_out.T, preferred_element_type=F32)
        dhid = cut(dhid_raw, 0)
        for j in (3, 1, 2):
            dhid = dhid + flip(cut(dhid_raw, j).astype(BF16), "section", j).astype(F32)
        dact = pull(dhid)[0].astype(BF16)
        inner = jnp.sum(dact.astype(F32) * act, axis=1)
        payload = jnp.concatenate([dact, side_rows(inner, piece)], axis=0)
        others = [flip(payload, "section", j) for j in (1, 2, 3)]
        for got in others:
            inner = inner + side_values(got[rows:], rows)
        dact_full = fill([dact] + [got[:rows] for got in others])
        part = jnp.dot(dact_full, weight_in.T, preferred_element_type=F32).astype(BF16)

        send = jnp.concatenate([halves(part, 1 - core), side_rows(inner, quarter // 2)], axis=0)
        got = flip(send, "dp", 1)
        dscaled = halves(part, core).astype(F32) + got[:rows].astype(F32)
        inner = inner + side_values(got[rows:], rows)
        bit = 2
        while bit < n_dp:
            send = jnp.concatenate([dscaled.astype(BF16), side_rows(inner, quarter // 2)], axis=0)
            got = flip(send, "dp", bit)
            dscaled = dscaled + got[:rows].astype(F32)
            inner = inner + side_values(got[rows:], rows)
            bit *= 2
        dnorm = dscaled * gain_half
        dy_half = halves(dy, core).astype(F32)
        grad_x = (dy_half + scale * (dnorm - normed_half * (inner / width)[:, None])).astype(BF16)
        if not final:
            down = lax.ppermute(grad_x, "section", [(i, i - 4) for i in range(4, sections)])
            other = flip(down, "dp", 1)
            pairs = jnp.where(
                core == 0,
                jnp.stack([down.reshape(rows, n_dp // 2, share), other.reshape(rows, n_dp // 2, share)], axis=2),
                jnp.stack([other.reshape(rows, n_dp // 2, share), down.reshape(rows, n_dp // 2, share)], axis=2),
            )
            incoming = pairs.reshape(rows, quarter)

    grad_out = jnp.dot(hid_full.T, dy, preferred_element_type=F32).astype(BF16)
    grad_in = jnp.dot(scaled.T, dact_full, preferred_element_type=F32).astype(BF16)
    grad_gain = jnp.sum(own(dscaled) * own(normed_half), axis=0)
    return (
        grad_in[None],
        grad_out[None],
        grad_gain[None],
        own(grad_x).reshape(1, micro, tok, share),
    )


SIDE = 16
LANES = 128
GELU_IN = 0.7978845608028654
GELU_CUBE = 0.044715


def resident(shape, dtype):
    return pltpu.VMEM(shape, dtype)


def local(body, outs, *args, scratch=(), flops=0):
    spec = pl.BlockSpec(memory_space=pltpu.VMEM)
    moved = sum(a.size * a.dtype.itemsize for a in args)
    return pl.pallas_call(
        body,
        out_shape=tuple(outs),
        in_specs=[spec] * len(args),
        out_specs=tuple(spec for _ in outs),
        scratch_shapes=list(scratch),
        compiler_params=pltpu.CompilerParams(vmem_limit_bytes=16 * 1024 * 1024),
        cost_estimate=pl.CostEstimate(flops=flops, bytes_accessed=moved, transcendentals=0),
    )(*args)


def diagonal(rows, width):
    return lax.broadcasted_iota(jnp.int32, (rows, width), 0) == lax.broadcasted_iota(jnp.int32, (rows, width), 1)


def as_row(column, width):
    rows = column.shape[0]
    return jnp.sum(jnp.where(diagonal(rows, width), column, 0.0), axis=0, keepdims=True)


def as_column(row, rows):
    return jnp.sum(jnp.where(diagonal(rows, row.shape[1]), row, 0.0), axis=1, keepdims=True)


def side_block(row):
    lead = row.astype(BF16).astype(F32)
    at = lax.broadcasted_iota(jnp.int32, (SIDE, row.shape[1]), 0)
    return jnp.where(at == 0, lead, jnp.where(at == 1, row - lead, 0.0)).astype(BF16)


def side_row(block):
    wide = block.astype(F32)
    return wide[0:1] + wide[1:2]


def packed_shape(rows, piece):
    return (piece // LANES * rows + SIDE, LANES)


def pack_block(row):
    lead = row.astype(BF16).astype(F32)
    count = row.shape[1] // LANES
    at = lax.broadcasted_iota(jnp.int32, (SIDE, LANES), 0)
    block = jnp.zeros((SIDE, LANES), F32)
    for i in range(count):
        lanes = slice(i * LANES, (i + 1) * LANES)
        block = jnp.where(at == i, lead[:, lanes], jnp.where(at == count + i, (row - lead)[:, lanes], block))
    return block.astype(BF16)


def pack_row(block, count):
    wide = block.astype(F32)
    return jnp.concatenate([wide[i:i + 1] + wide[count + i:count + i + 1] for i in range(count)], axis=1)


def lane_blocks(rows):
    return -(-rows // LANES)


def unpack(packed, rows):
    blocks = (packed.shape[0] - SIDE) // rows
    return jnp.concatenate([packed[i * rows:(i + 1) * rows] for i in range(blocks)], axis=1)


def load_kernel(*refs):
    count = len(refs) // 2
    copies = [pltpu.make_async_copy(refs[i], refs[count + i], refs[-1].at[i]) for i in range(count)]
    for copy in copies:
        copy.start()
    for copy in copies:
        copy.wait()


def load(*arrays):
    return pl.pallas_call(
        load_kernel,
        out_shape=tuple(resident(a.shape, a.dtype) for a in arrays),
        in_specs=[pl.BlockSpec(memory_space=pl.ANY)] * len(arrays),
        out_specs=tuple(pl.BlockSpec(memory_space=pltpu.VMEM) for _ in arrays),
        scratch_shapes=[pltpu.SemaphoreType.DMA((len(arrays),))],
        compiler_params=pltpu.CompilerParams(vmem_limit_bytes=1024 * 1024),
        cost_estimate=pl.CostEstimate(flops=0, bytes_accessed=sum(2 * a.size * a.dtype.itemsize for a in arrays), transcendentals=0),
    )(*(pltpu.with_memory_space_constraint(a, pltpu.HBM) for a in arrays))


def place():
    return lax.axis_index("section") % 4, lax.axis_index("dp")


def dot_nt(left, right):
    return lax.dot_general(left, right, (((1,), (1,)), ((), ())), preferred_element_type=F32)


def dot_tn(left, right):
    return lax.dot_general(left, right, (((0,), (0,)), ((), ())), preferred_element_type=F32)


def slot(index, size):
    return pl.ds(pl.multiple_of(index * size, size), size)


def spread_in_part(part, at, gain, weight, mine, total, begin):
    share = part.shape[1]
    piece = weight.shape[1] // 4
    scaled = (part[...].astype(F32) * gain[:, slot(at, share)]).astype(BF16)
    for d in (3, 2, 1, 0):
        block = jnp.dot(scaled, weight[slot(at, share), slot(mine ^ d, piece)], preferred_element_type=F32)
        columns = slice(d * piece, (d + 1) * piece)
        total[:, columns] = block if begin else total[:, columns] + block


def square_sum(part):
    wide = part[...].astype(F32)
    return jnp.sum(wide * wide, axis=1, keepdims=True)


def load_spread_kernel(x1, weight, x0, gain, weight_held, x0_held, gain_held, total, sems):
    mine, lane = place()
    share = x1.shape[1]
    small = [pltpu.make_async_copy(source, held, sems.at[i]) for i, (source, held) in enumerate(((x0, x0_held), (gain, gain_held)))]
    slices = [slot(lane ^ d, share) for d in range(4)]
    large = [pltpu.make_async_copy(weight.at[at], weight_held.at[at], sems.at[2 + d]) for d, at in enumerate(slices)]
    for copy in (*small, *large):
        copy.start()
    for copy in (*small, large[0]):
        copy.wait()
    spread_in_part(x0_held, lane, gain_held, weight_held, mine, total, True)
    large[1].wait()
    spread_in_part(x1, lane ^ 1, gain_held, weight_held, mine, total, False)
    large[2].wait()
    large[3].wait()


def load_spread(x1, weight, x0, gain):
    keep = pl.BlockSpec(memory_space=pltpu.VMEM)
    rows, hidden = x0.shape[0], weight.shape[1]
    outs = [(a.shape, a.dtype) for a in (weight, x0, gain)] + [((rows, hidden), F32)]
    far = [pltpu.with_memory_space_constraint(a, pltpu.HBM) for a in (weight, x0, gain)]
    return pl.pallas_call(
        load_spread_kernel,
        out_shape=tuple(resident(*out) for out in outs),
        in_specs=[keep] + [pl.BlockSpec(memory_space=pl.ANY)] * 3,
        out_specs=(keep,) * 4,
        scratch_shapes=[pltpu.SemaphoreType.DMA((6,))],
        compiler_params=pltpu.CompilerParams(vmem_limit_bytes=8 * 1024 * 1024),
        cost_estimate=pl.CostEstimate(flops=rows * weight.size, bytes_accessed=4 * weight.size, transcendentals=0),
    )(x1, *far)


def spread_in_last_kernel(x0, x1, x2, x3, gain, weight, before, own, s1, s2, s3, x_full, squares, total):
    mine, lane = place()
    rows, share = x0.shape
    piece = own.shape[1]
    total[...] = before[...]
    spread_in_part(x2, lane ^ 2, gain, weight, mine, total, False)
    spread_in_part(x3, lane ^ 3, gain, weight, mine, total, False)
    column = square_sum(x0) + square_sum(x1) + square_sum(x2) + square_sum(x3)
    block = pack_block(as_row(column, lane_blocks(rows) * LANES))
    for d, out in ((3, s3), (2, s2), (1, s1)):
        for i in range(piece // LANES):
            out[i * rows:(i + 1) * rows] = total[:, d * piece + i * LANES:d * piece + (i + 1) * LANES].astype(BF16)
        out[piece // LANES * rows:] = block
    own[...] = total[:, :piece]
    squares[...] = column
    for d, part in enumerate((x0, x1, x2, x3)):
        x_full[:, slot(lane ^ d, share)] = part[...]


def spread_dy(dy, weight, mine, own, s1, s2, s3):
    piece = own.shape[1]
    for d, out in ((3, s3), (2, s2), (1, s1)):
        out[...] = dot_nt(dy[...], weight[slot(mine ^ d, piece), :]).astype(BF16)
    own[...] = dot_nt(dy[...], weight[slot(mine, piece), :])


def spread_first_kernel(cot, sent, weight, own, s1, s2, s3, dy):
    mine, lane = place()

    @pl.when(lane == mine)
    def _():
        dy[...] = cot[...]

    @pl.when(lane != mine)
    def _():
        dy[...] = sent[...]

    spread_dy(dy, weight, mine, own, s1, s2, s3)


def spread_next_kernel(layers, ds, begin, end, *refs):
    parts, refs = refs[:len(ds)], refs[len(ds):]
    before, weight = refs[:2]
    refs = refs[2:]
    mine, lane = place()
    rows, share = parts[0].shape
    piece = weight.shape[0] // 4
    last = lax.axis_index("section") // 4 == layers - 1
    if begin:
        (total,) = refs
    elif end:
        earlier, *others, own, s1, s2, s3, dy, total = refs
        total[...] = earlier[...]
    else:
        earlier, total = refs
        total[...] = earlier[...]
    for i, (d, part) in enumerate(zip(ds, parts)):
        at = slot(lane ^ d, share)
        value = jnp.where(last, before[:, at], part[...])
        for j in (3, 2, 1, 0):
            block = dot_nt(value, weight[slot(mine ^ j, piece), at])
            columns = slice(j * piece, (j + 1) * piece)
            total[:, columns] = block if begin and i == 0 else total[:, columns] + block
    if end:
        for j, out in ((3, s3), (2, s2), (1, s1)):
            out[...] = total[:, j * piece:(j + 1) * piece].astype(BF16)
        own[...] = total[:, :piece]
        done = [d for d in range(4) if d not in ds]

        @pl.when(last)
        def _():
            dy[...] = before[...]

        @pl.when(jnp.logical_not(last))
        def _():
            for d, part in zip((*done, *ds), (*others, *parts)):
                dy[:, slot(lane ^ d, share)] = part[...]


def act_kernel(width, own, squares, g1, g2, g3, act, slope, hid, scale):
    rows, piece = act.shape
    count = lane_blocks(rows)
    sums = piece // LANES * rows
    row = pack_row(g1[sums:], count) + pack_row(g2[sums:], count) + pack_row(g3[sums:], count)
    r = lax.rsqrt((squares[...] + as_column(row, rows)) / width + 1e-06)
    scale[...] = r
    for i in range(piece // LANES):
        at = slice(i * LANES, (i + 1) * LANES)
        got = slice(i * rows, (i + 1) * rows)
        a = (own[:, at] + g1[got].astype(F32) + g2[got].astype(F32) + g3[got].astype(F32)) * r
        act[:, at] = a
        square = a * a
        t = jnp.tanh(GELU_IN * (a + GELU_CUBE * (square * a)))
        half = 0.5 * (1.0 + t)
        hid[:, at] = (a * half).astype(BF16)
        slope[:, at] = half + 0.5 * a * (1.0 - t * t) * (GELU_IN * (1.0 + 3.0 * GELU_CUBE * square))


def dact_kernel(own, g1, g2, g3, act, slope, pay):
    rows, piece = own.shape
    dhid = own[...] + g1[...].astype(F32) + g2[...].astype(F32) + g3[...].astype(F32)
    da = (dhid * slope[...]).astype(BF16)
    blocks = piece // LANES
    for i in range(blocks):
        pay[i * rows:(i + 1) * rows] = da[:, i * LANES:(i + 1) * LANES]
    column = jnp.sum(da.astype(F32) * act[...], axis=1, keepdims=True)
    pay[blocks * rows:] = pack_block(as_row(column, lane_blocks(rows) * LANES))


def back_part(part, j, weight, mine, lane, total, begin):
    value = unpack(part, total.shape[0])
    piece = value.shape[1]
    share = weight.shape[0] // 4
    for d in (1, 3, 0, 2):
        block = dot_nt(value, weight[slot(lane ^ d, share), slot(mine ^ j, piece)])
        columns = slice(d * share, (d + 1) * share)
        total[:, columns] = block if begin else total[:, columns] + block


def back_kernel(js, begin, *refs):
    *parts, weight = refs[:len(js) + 1]
    *earlier, total = refs[len(js) + 1:]
    mine, lane = place()
    if not begin:
        total[...] = earlier[0][...]
    for i, (j, part) in enumerate(zip(js, parts)):
        back_part(part, j, weight, mine, lane, total, begin and i == 0)


def back_last_kernel(p0, p1, p2, p3, weight, earlier, keep, send, total):
    mine, lane = place()
    rows = total.shape[0]
    share = weight.shape[0] // 4
    total[...] = earlier[...]
    back_part(p1, 1, weight, mine, lane, total, False)
    sums = p0.shape[0] - SIDE
    row = sum(pack_row(part[sums:], lane_blocks(rows)) for part in (p0, p1, p2, p3))
    if row.shape[1] < keep.shape[1]:
        row = jnp.concatenate([row, jnp.zeros((1, keep.shape[1] - row.shape[1]), F32)], axis=1)
    for at, d in ((0, 1), (1, 3)):
        send[:rows, at * share:(at + 1) * share] = total[:, d * share:(d + 1) * share].astype(BF16)
    send[rows:] = side_block(row)
    for at, d in ((0, 0), (1, 2)):
        keep[:rows, at * share:(at + 1) * share] = total[:, d * share:(d + 1) * share]
    keep[rows:] = jnp.broadcast_to(row, (SIDE, keep.shape[1]))


def middle_kernel(keep, got, rest, send):
    rows = keep.shape[0] - SIDE
    share = rest.shape[1]
    row = (keep[rows:rows + 1] + side_row(got[rows:]))[:, :share]
    send[:rows] = (keep[:rows, share:] + got[:rows, share:].astype(F32)).astype(BF16)
    send[rows:] = side_block(row)
    rest[:rows] = keep[:rows, :share] + got[:rows, :share].astype(F32)
    rest[rows:] = jnp.broadcast_to(row, (SIDE, share))


def finish_kernel(width, rest, got, x_own, dy, gain, scale, grad_x, *grad_gain):
    _, lane = place()
    rows, share = x_own.shape
    at = slot(lane, share)
    r = scale[...]
    du = rest[:rows] + got[:rows].astype(F32)
    normed = x_own[...].astype(F32) * r
    inner = as_column(rest[rows:rows + 1] + side_row(got[rows:]), rows) / width
    dnorm = du * gain[:, at]
    grad_x[...] = (dy[:, at].astype(F32) + r * (dnorm - normed * inner)).astype(BF16)
    if grad_gain:
        grad_gain[0][...] = jnp.sum(du * normed, axis=0, keepdims=True)


def grad_out_kernel(h0, h1, h2, h3, dy, out, held, sems):
    mine, _ = place()
    piece = h0.shape[1]
    copies = []
    for d, part in enumerate((h0, h1, h2, h3)):
        held[d] = dot_tn(part[...], dy[...]).astype(BF16)
        copies.append(pltpu.make_async_copy(held.at[d], out.at[slot(mine ^ d, piece), :], sems.at[d]))
        copies[-1].start()
    for copy in copies:
        copy.wait()


def grad_in_kernel(p0, p1, p2, p3, x_full, gain, scale, out, scaled, held, sems):
    mine, _ = place()
    rows = x_full.shape[0]
    piece = (p0.shape[0] - SIDE) // rows * LANES
    scaled[...] = (x_full[...].astype(F32) * scale[...] * gain[...]).astype(BF16)
    copies = []
    for d, part in enumerate((p0, p1, p2, p3)):
        held[d] = dot_tn(scaled[...], unpack(part, rows)).astype(BF16)
        copies.append(pltpu.make_async_copy(held.at[d], out.at[:, slot(mine ^ d, piece)], sems.at[d]))
        copies[-1].start()
    for copy in copies:
        copy.wait()


def gradient(body, shape, block, *args, scratch=(), flops=0):
    return pl.pallas_call(
        body,
        out_shape=jax.ShapeDtypeStruct(shape, BF16),
        in_specs=[pl.BlockSpec(memory_space=pltpu.VMEM)] * len(args),
        out_specs=pl.BlockSpec(memory_space=pl.ANY),
        scratch_shapes=[*scratch, pltpu.VMEM((4,) + block, BF16), pltpu.SemaphoreType.DMA((4,))],
        compiler_params=pltpu.CompilerParams(vmem_limit_bytes=16 * 1024 * 1024),
        cost_estimate=pl.CostEstimate(flops=flops, bytes_accessed=2 * shape[0] * shape[1], transcendentals=0),
    )(*args)


def shards_of_four(checkpoints, gain, w_in, w_out, cotangent):
    sections = lax.axis_size("section")
    here = lax.axis_index("section")
    lane = lax.axis_index("dp")
    layers = sections // 4
    mine = here % 4
    _, micro, tok, share = checkpoints.shape
    rows = micro * tok
    quarter = share * 4
    width = 4 * quarter
    hidden = w_in.shape[2]
    piece = hidden // 4
    work = 2 * rows * quarter * hidden

    x0 = checkpoints[0].reshape(rows, share)
    cot = cotangent.reshape(rows, quarter)
    top = [s * 4 + d for s in range(sections) for d in range(4) if s // 4 == layers - 1]
    x_sent = x0
    x2 = flip(x0, "dp", 2)
    x1 = flip(x0, "dp", 1)
    weight_in, x0, gain, begun = load_spread(x1, w_in[0], x0, gain)
    x2, weight_in = lax.optimization_barrier((x2, weight_in))
    sent = lax.ppermute(cot, ("section", "dp"), [((i // 4 ^ near) * 4 + i // 4 % 4, i) for i in top for near in (1, 0, 2) if i // 4 % 4 ^ i % 4 == (2, 1, 3)[near]])
    x3 = flip(x_sent, "dp", 3)

    packed = packed_shape(rows, piece)
    own, s1, s2, s3, x_full, squares = local(
        spread_in_last_kernel,
        [resident((rows, piece), F32)] + [resident(packed, BF16)] * 3
        + [resident((rows, quarter), BF16), resident((rows, 1), F32)],
        x0, x1, x2, x3, gain, weight_in, begun,
        scratch=[pltpu.VMEM((rows, hidden), F32)], flops=3 * work,
    )
    s1, s2, s3, cot, w_out = lax.optimization_barrier((s1, s2, s3, cot, w_out))
    g3 = flip(s3, "section", 3)
    g2 = flip(s2, "section", 2)
    g1 = flip(s1, "section", 1)
    weight_out, cot = load(w_out[0], cot)
    act, slope, hid, scale = local(
        functools.partial(act_kernel, width),
        [resident((rows, piece), F32), resident((rows, piece), F32), resident((rows, piece), BF16), resident((rows, 1), F32)],
        own, squares, g1, g2, g3,
    )

    spread_outs = [resident((rows, piece), F32)] + [resident((rows, piece), BF16)] * 3 + [resident((rows, quarter), BF16)]

    def gather_hidden(block):
        return [block] + [flip(block, "section", j) for j in (1, 2, 3)]

    if layers == 1:
        hids = gather_hidden(hid)
    for phase in range(layers):
        final = phase == layers - 1
        if phase == 0:
            own, s1, s2, s3, dy = local(spread_first_kernel, spread_outs, cot, sent, weight_out, flops=work)
        else:
            d0, d1, d2, d3 = down
            first, hids = lax.optimization_barrier((d0, hids))
            total = [resident((rows, hidden), F32)]
            step = functools.partial(spread_next_kernel, layers)
            begun = local(functools.partial(step, (0,), True, False), total, first, dy, weight_out, flops=work // 4)
            begun = local(functools.partial(step, (1, 2), False, False), total, d1, d2, dy, weight_out, *begun, flops=work // 2)
            own, s1, s2, s3, dy = local(
                functools.partial(step, (3,), False, True), spread_outs, d3, dy, weight_out, *begun, d0, d1, d2,
                scratch=[pltpu.VMEM((rows, hidden), F32)], flops=work // 4,
            )
        g3 = flip(s3, "section", 3)
        g2 = flip(s2, "section", 2)
        g1 = flip(s1, "section", 1)
        if final:
            grad_out = gradient(grad_out_kernel, (hidden, quarter), (piece, quarter), *hids, dy, flops=work)
            own, grad_out = lax.optimization_barrier((own, grad_out))
        (pay,) = local(dact_kernel, [resident(packed, BF16)], own, g1, g2, g3, act, slope)
        p3 = flip(pay, "section", 3)
        p2 = flip(pay, "section", 2)
        p1 = flip(pay, "section", 1)
        total = [resident((rows, quarter), F32)]
        begun = local(functools.partial(back_kernel, (0,), True), total, pay, weight_in, flops=work // 4)
        begun = local(functools.partial(back_kernel, (3, 2), False), total, p3, p2, weight_in, *begun, flops=work // 2)
        keep, send = local(
            back_last_kernel,
            [resident((rows + SIDE, 2 * share), F32), resident((rows + SIDE, 2 * share), BF16)],
            pay, p1, p2, p3, weight_in, *begun,
            scratch=[pltpu.VMEM((rows, quarter), F32)], flops=work // 4,
        )
        got = flip(send, "dp", 1)
        rest, send = local(
            middle_kernel,
            [resident((rows + SIDE, share), F32), resident((rows + SIDE, share), BF16)],
            keep, got,
        )
        if phase == 0 and not final:
            send, hid = lax.optimization_barrier((send, hid))
            hids = gather_hidden(hid)
        got = flip(send, "dp", 2)
        if final:
            grad_in = gradient(
                grad_in_kernel, (quarter, hidden), (quarter, piece), pay, p1, p2, p3, x_full, gain, scale,
                scratch=[pltpu.VMEM((rows, quarter), BF16)], flops=work,
            )
            got, grad_in = lax.optimization_barrier((got, grad_in))
        outs = [resident((rows, share), BF16)]
        if final:
            outs = [jax.ShapeDtypeStruct((rows, share), BF16), jax.ShapeDtypeStruct((1, share), F32)]
        finished = local(functools.partial(finish_kernel, width), outs, rest, got, x0, dy, gain, scale)
        if not final:
            d0 = lax.ppermute(finished[0], "section", [(i, i - 4) for i in range(4, sections)])
            d2 = flip(d0, "dp", 2)
            d1 = flip(d0, "dp", 1)
            d3 = flip(d2, "dp", 1)
            down = (d0, d1, d2, d3)

    grad_x, grad_gain = finished
    return grad_in[None], grad_out[None], grad_gain, grad_x.reshape(1, micro, tok, share)


def shards(checkpoints, gain, w_in, w_out, cotangent):
    rows = checkpoints.shape[1] * checkpoints.shape[2]
    share = checkpoints.shape[3]
    piece = w_in.shape[2] // 4
    if lax.axis_size("dp") == 4 and rows % 16 == 0 and share % 128 == 0 and piece % 128 == 0 and rows <= min(share, piece):
        return shards_of_four(checkpoints, gain, w_in, w_out, cotangent)
    return shards_of_any(checkpoints, gain, w_in, w_out, cotangent)


def solution(mesh):
    in_specs = (
        P("section", None, None, "dp"),
        P("section", None),
        P("section", None, "dp"),
        P("section", "dp", None),
        P(None, None, "dp"),
    )
    out_specs = (
        P("section", None, "dp"),
        P("section", "dp", None),
        P("section", "dp"),
        P("section", None, None, "dp"),
    )
    return jax.shard_map(shards, mesh=mesh, in_specs=in_specs, out_specs=out_specs, check_vma=False)
```

```python
import functools

import jax
import jax.numpy as jnp
from jax import lax
from jax.experimental import pallas as pl
from jax.experimental.pallas import tpu as pltpu
from jax.sharding import PartitionSpec as P

F32 = jnp.float32
BF16 = jnp.bfloat16


def flip(block, axis, bits):
    count = lax.axis_size(axis)
    return lax.ppermute(block, axis, [(i, i ^ bits) for i in range(count)])


def side_rows(values, width):
    lead = values.astype(BF16)
    trail = (values - lead.astype(F32)).astype(BF16)
    flat = jnp.concatenate([lead, trail])
    return jnp.pad(flat, (0, 16 * width - flat.shape[0])).reshape(16, width)


def side_values(rows, count):
    flat = rows.reshape(-1)
    return flat[:count].astype(F32) + flat[count:2 * count].astype(F32)


def gelu_tanh(value):
    return jax.nn.gelu(value, approximate=True)


def shards_of_any(checkpoints, gain, w_in, w_out, cotangent):
    sections = lax.axis_size("section")
    n_dp = lax.axis_size("dp")
    here = lax.axis_index("section")
    lane = lax.axis_index("dp")
    layers = sections // 4
    mine = here % 4
    last = here // 4 == layers - 1
    _, micro, tok, share = checkpoints.shape
    rows = micro * tok
    quarter = share * n_dp
    width = 4 * quarter
    gain_row = gain[0]
    weight_in = w_in[0]
    weight_out = w_out[0]
    hidden = weight_in.shape[1]
    piece = hidden // 4
    core = lane % 2

    def gather_dp(block):
        bit = n_dp // 2
        parts = {0: block}
        while bit >= 1:
            other = flip(jnp.concatenate([parts[j] for j in parts], axis=1), "dp", bit)
            for at, j in enumerate(list(parts)):
                parts[j ^ bit] = other[:, at * block.shape[1]:(at + 1) * block.shape[1]]
            bit //= 2
        full = jnp.zeros((rows, quarter), block.dtype)
        for j, part in parts.items():
            full = lax.dynamic_update_slice(full, part, (0, (lane ^ j) * block.shape[1]))
        return full

    def cot_quarter(block):
        if n_dp < 4:
            whole = lax.all_gather(block, "dp", axis=1, tiled=True)
            return lax.dynamic_slice_in_dim(whole, mine * quarter, quarter, 1)
        per = n_dp // 4
        top = [s * n_dp + d for s in range(sections) for d in range(n_dp) if s // 4 == layers - 1]
        held = block
        far = lambda i, b: (i % n_dp // per ^ i // n_dp % 4) & b
        got = lax.ppermute(held, ("section", "dp"), [(i, i ^ 2 * per) for i in top if far(i, 3) == 0])
        held = jnp.where((lane // per ^ mine) & 2 == 0, held, got)
        got = lax.ppermute(held, ("section", "dp"), [(i, i ^ per) for i in top if far(i, 1) == 0])
        held = jnp.where((lane // per ^ mine) & 1 == 0, held, got)
        if per == 1:
            return held
        parts = {0: held}
        bit = per // 2
        while bit >= 1:
            for j in list(parts):
                parts[j ^ bit] = flip(parts[j], "dp", bit)
            bit //= 2
        full = jnp.zeros((rows, quarter), block.dtype)
        for j, part in parts.items():
            full = lax.dynamic_update_slice(full, part, (0, (lane % per ^ j) * block.shape[1]))
        return full

    def cut(values, j):
        return lax.dynamic_slice_in_dim(values, (mine ^ j) * piece, piece, 1)

    def fill(parts):
        full = jnp.zeros((rows, hidden), parts[0].dtype)
        for j, part in enumerate(parts):
            full = lax.dynamic_update_slice(full, part, (0, (mine ^ j) * piece))
        return full

    x_full = gather_dp(checkpoints[0].reshape(rows, share))
    cot = cot_quarter(cotangent.reshape(rows, cotangent.shape[2]))
    x_wide = x_full.astype(F32)
    scaled_raw = (x_wide * gain_row).astype(BF16)
    squares = jnp.sum(x_wide * x_wide, axis=1)

    act_raw = jnp.dot(scaled_raw, weight_in, preferred_element_type=F32)
    extra = side_rows(squares, piece)
    act = cut(act_raw, 0)
    for j in (3, 1, 2):
        got = flip(jnp.concatenate([cut(act_raw, j).astype(BF16), extra], axis=0), "section", j)
        act = act + got[:rows].astype(F32)
        squares = squares + side_values(got[rows:], rows)
    scale = lax.rsqrt(squares / width + 1e-06)[:, None]
    act = act * scale
    hid, pull = jax.vjp(gelu_tanh, act)
    hid = hid.astype(BF16)
    hid_full = fill([hid] + [flip(hid, "section", j) for j in (1, 2, 3)])
    normed = x_wide * scale
    scaled = (normed * gain_row).astype(BF16)

    def halves(values, side):
        pairs = values.reshape(rows, n_dp // 2, 2, share)
        return jnp.where(side == 0, pairs[:, :, 0], pairs[:, :, 1]).reshape(rows, quarter // 2)

    def own(values):
        return lax.dynamic_slice_in_dim(values, lane // 2 * share, share, 1)

    incoming = jnp.zeros((rows, quarter), BF16)
    normed_half = halves(normed, core)
    gain_half = halves(jnp.broadcast_to(gain_row, (rows, quarter)), core)
    for phase in range(layers):
        final = phase == layers - 1
        dy = jnp.where(last, cot, incoming) if phase > 0 else cot
        dhid_raw = jnp.dot(dy, weight_out.T, preferred_element_type=F32)
        dhid = cut(dhid_raw, 0)
        for j in (3, 1, 2):
            dhid = dhid + flip(cut(dhid_raw, j).astype(BF16), "section", j).astype(F32)
        dact = pull(dhid)[0].astype(BF16)
        inner = jnp.sum(dact.astype(F32) * act, axis=1)
        payload = jnp.concatenate([dact, side_rows(inner, piece)], axis=0)
        others = [flip(payload, "section", j) for j in (1, 2, 3)]
        for got in others:
            inner = inner + side_values(got[rows:], rows)
        dact_full = fill([dact] + [got[:rows] for got in others])
        part = jnp.dot(dact_full, weight_in.T, preferred_element_type=F32).astype(BF16)

        send = jnp.concatenate([halves(part, 1 - core), side_rows(inner, quarter // 2)], axis=0)
        got = flip(send, "dp", 1)
        dscaled = halves(part, core).astype(F32) + got[:rows].astype(F32)
        inner = inner + side_values(got[rows:], rows)
        bit = 2
        while bit < n_dp:
            send = jnp.concatenate([dscaled.astype(BF16), side_rows(inner, quarter // 2)], axis=0)
            got = flip(send, "dp", bit)
            dscaled = dscaled + got[:rows].astype(F32)
            inner = inner + side_values(got[rows:], rows)
            bit *= 2
        dnorm = dscaled * gain_half
        dy_half = halves(dy, core).astype(F32)
        grad_x = (dy_half + scale * (dnorm - normed_half * (inner / width)[:, None])).astype(BF16)
        if not final:
            down = lax.ppermute(grad_x, "section", [(i, i - 4) for i in range(4, sections)])
            other = flip(down, "dp", 1)
            pairs = jnp.where(
                core == 0,
                jnp.stack([down.reshape(rows, n_dp // 2, share), other.reshape(rows, n_dp // 2, share)], axis=2),
                jnp.stack([other.reshape(rows, n_dp // 2, share), down.reshape(rows, n_dp // 2, share)], axis=2),
            )
            incoming = pairs.reshape(rows, quarter)

    grad_out = jnp.dot(hid_full.T, dy, preferred_element_type=F32).astype(BF16)
    grad_in = jnp.dot(scaled.T, dact_full, preferred_element_type=F32).astype(BF16)
    grad_gain = jnp.sum(own(dscaled) * own(normed_half), axis=0)
    return (
        grad_in[None],
        grad_out[None],
        grad_gain[None],
        own(grad_x).reshape(1, micro, tok, share),
    )


SIDE = 16
LANES = 128
GELU_IN = 0.7978845608028654
GELU_CUBE = 0.044715


def resident(shape, dtype):
    return pltpu.VMEM(shape, dtype)


def local(body, outs, *args, scratch=(), flops=0):
    spec = pl.BlockSpec(memory_space=pltpu.VMEM)
    moved = sum(a.size * a.dtype.itemsize for a in args)
    return pl.pallas_call(
        body,
        out_shape=tuple(outs),
        in_specs=[spec] * len(args),
        out_specs=tuple(spec for _ in outs),
        scratch_shapes=list(scratch),
        compiler_params=pltpu.CompilerParams(vmem_limit_bytes=16 * 1024 * 1024),
        cost_estimate=pl.CostEstimate(flops=flops, bytes_accessed=moved, transcendentals=0),
    )(*args)


def diagonal(rows, width):
    return lax.broadcasted_iota(jnp.int32, (rows, width), 0) == lax.broadcasted_iota(jnp.int32, (rows, width), 1)


def as_row(column, width):
    rows = column.shape[0]
    return jnp.sum(jnp.where(diagonal(rows, width), column, 0.0), axis=0, keepdims=True)


def as_column(row, rows):
    return jnp.sum(jnp.where(diagonal(rows, row.shape[1]), row, 0.0), axis=1, keepdims=True)


def side_block(row):
    lead = row.astype(BF16).astype(F32)
    at = lax.broadcasted_iota(jnp.int32, (SIDE, row.shape[1]), 0)
    return jnp.where(at == 0, lead, jnp.where(at == 1, row - lead, 0.0)).astype(BF16)


def side_row(block):
    wide = block.astype(F32)
    return wide[0:1] + wide[1:2]


def packed_shape(rows, piece):
    return (piece // LANES * rows + SIDE, LANES)


def pack_block(row):
    lead = row.astype(BF16).astype(F32)
    count = row.shape[1] // LANES
    at = lax.broadcasted_iota(jnp.int32, (SIDE, LANES), 0)
    block = jnp.zeros((SIDE, LANES), F32)
    for i in range(count):
        lanes = slice(i * LANES, (i + 1) * LANES)
        block = jnp.where(at == i, lead[:, lanes], jnp.where(at == count + i, (row - lead)[:, lanes], block))
    return block.astype(BF16)


def pack_row(block, count):
    wide = block.astype(F32)
    return jnp.concatenate([wide[i:i + 1] + wide[count + i:count + i + 1] for i in range(count)], axis=1)


def lane_blocks(rows):
    return -(-rows // LANES)


def unpack(packed, rows):
    blocks = (packed.shape[0] - SIDE) // rows
    return jnp.concatenate([packed[i * rows:(i + 1) * rows] for i in range(blocks)], axis=1)


def load_kernel(*refs):
    count = len(refs) // 2
    copies = [pltpu.make_async_copy(refs[i], refs[count + i], refs[-1].at[i]) for i in range(count)]
    for copy in copies:
        copy.start()
    for copy in copies:
        copy.wait()


def load(*arrays):
    return pl.pallas_call(
        load_kernel,
        out_shape=tuple(resident(a.shape, a.dtype) for a in arrays),
        in_specs=[pl.BlockSpec(memory_space=pl.ANY)] * len(arrays),
        out_specs=tuple(pl.BlockSpec(memory_space=pltpu.VMEM) for _ in arrays),
        scratch_shapes=[pltpu.SemaphoreType.DMA((len(arrays),))],
        compiler_params=pltpu.CompilerParams(vmem_limit_bytes=1024 * 1024),
        cost_estimate=pl.CostEstimate(flops=0, bytes_accessed=sum(2 * a.size * a.dtype.itemsize for a in arrays), transcendentals=0),
    )(*(pltpu.with_memory_space_constraint(a, pltpu.HBM) for a in arrays))


def place():
    return lax.axis_index("section") % 4, lax.axis_index("dp")


def dot_nt(left, right):
    return lax.dot_general(left, right, (((1,), (1,)), ((), ())), preferred_element_type=F32)


def dot_tn(left, right):
    return lax.dot_general(left, right, (((0,), (0,)), ((), ())), preferred_element_type=F32)


def slot(index, size):
    return pl.ds(pl.multiple_of(index * size, size), size)


def spread_in_part(part, at, gain, weight, mine, total, begin):
    share = part.shape[1]
    piece = weight.shape[1] // 4
    scaled = (part[...].astype(F32) * gain[:, slot(at, share)]).astype(BF16)
    for d in (3, 2, 1, 0):
        block = jnp.dot(scaled, weight[slot(at, share), slot(mine ^ d, piece)], preferred_element_type=F32)
        columns = slice(d * piece, (d + 1) * piece)
        total[:, columns] = block if begin else total[:, columns] + block


def square_sum(part):
    wide = part[...].astype(F32)
    return jnp.sum(wide * wide, axis=1, keepdims=True)


def load_spread_kernel(x1, weight, x0, gain, weight_held, x0_held, gain_held, total, sems):
    mine, lane = place()
    share = x1.shape[1]
    small = [pltpu.make_async_copy(source, held, sems.at[i]) for i, (source, held) in enumerate(((x0, x0_held), (gain, gain_held)))]
    slices = [slot(lane ^ d, share) for d in range(4)]
    large = [pltpu.make_async_copy(weight.at[at], weight_held.at[at], sems.at[2 + d]) for d, at in enumerate(slices)]
    for copy in (*small, *large):
        copy.start()
    for copy in (*small, large[0]):
        copy.wait()
    spread_in_part(x0_held, lane, gain_held, weight_held, mine, total, True)
    large[1].wait()
    spread_in_part(x1, lane ^ 1, gain_held, weight_held, mine, total, False)
    large[2].wait()
    large[3].wait()


def load_spread(x1, weight, x0, gain):
    keep = pl.BlockSpec(memory_space=pltpu.VMEM)
    rows, hidden = x0.shape[0], weight.shape[1]
    outs = [(a.shape, a.dtype) for a in (weight, x0, gain)] + [((rows, hidden), F32)]
    far = [pltpu.with_memory_space_constraint(a, pltpu.HBM) for a in (weight, x0, gain)]
    return pl.pallas_call(
        load_spread_kernel,
        out_shape=tuple(resident(*out) for out in outs),
        in_specs=[keep] + [pl.BlockSpec(memory_space=pl.ANY)] * 3,
        out_specs=(keep,) * 4,
        scratch_shapes=[pltpu.SemaphoreType.DMA((6,))],
        compiler_params=pltpu.CompilerParams(vmem_limit_bytes=8 * 1024 * 1024),
        cost_estimate=pl.CostEstimate(flops=rows * weight.size, bytes_accessed=4 * weight.size, transcendentals=0),
    )(x1, *far)


def spread_in_last_kernel(x0, x1, x2, x3, gain, weight, before, own, s1, s2, s3, x_full, squares):
    mine, lane = place()
    rows, share = x0.shape
    piece = own.shape[1]
    ends = [(slot(lane ^ d, share), part) for d, part in ((2, x2), (3, x3))]
    ends = [(at, (part[...].astype(F32) * gain[:, at]).astype(BF16)) for at, part in ends]
    column = square_sum(x0) + square_sum(x1) + square_sum(x2) + square_sum(x3)
    block = pack_block(as_row(column, lane_blocks(rows) * LANES))
    for d, out in ((1, s1), (2, s2), (3, s3), (0, own)):
        value = before[:, d * piece:(d + 1) * piece]
        for at, scaled in ends:
            value = value + jnp.dot(scaled, weight[at, slot(mine ^ d, piece)], preferred_element_type=F32)
        if d == 0:
            out[...] = value
            continue
        for i in range(piece // LANES):
            out[i * rows:(i + 1) * rows] = value[:, i * LANES:(i + 1) * LANES].astype(BF16)
        out[piece // LANES * rows:] = block
    squares[...] = column
    for d, part in enumerate((x0, x1, x2, x3)):
        x_full[:, slot(lane ^ d, share)] = part[...]


def spread_dy(dy, weight, mine, own, s1, s2, s3):
    piece = own.shape[1]
    for d, out in ((3, s3), (2, s2), (1, s1)):
        out[...] = dot_nt(dy[...], weight[slot(mine ^ d, piece), :]).astype(BF16)
    own[...] = dot_nt(dy[...], weight[slot(mine, piece), :])


def spread_first_kernel(cot, sent, weight, own, s1, s2, s3, dy):
    mine, lane = place()

    @pl.when(lane == mine)
    def _():
        dy[...] = cot[...]

    @pl.when(lane != mine)
    def _():
        dy[...] = sent[...]

    spread_dy(dy, weight, mine, own, s1, s2, s3)


def spread_next_kernel(layers, ds, begin, end, *refs):
    parts, refs = refs[:len(ds)], refs[len(ds):]
    before, weight = refs[:2]
    earlier, refs = (None, refs[2:]) if begin else (refs[2], refs[3:])
    mine, lane = place()
    share = parts[0].shape[1]
    piece = weight.shape[0] // 4
    last = lax.axis_index("section") // 4 == layers - 1
    if end:
        *others, own, s1, s2, s3, dy = refs
        outs = (own, s1, s2, s3)
    else:
        outs = [refs[0].at[:, j * piece:(j + 1) * piece] for j in range(4)]
    slices = [slot(lane ^ d, share) for d in ds]
    values = [jnp.where(last, before[:, at], part[...]) for at, part in zip(slices, parts)]
    for j in (1, 2, 3, 0):
        total = None if begin else earlier[:, j * piece:(j + 1) * piece]
        for at, value in zip(slices, values):
            block = dot_nt(value, weight[slot(mine ^ j, piece), at])
            total = block if total is None else total + block
        outs[j][...] = total.astype(outs[j].dtype)
    if end:
        done = [d for d in range(4) if d not in ds]

        @pl.when(last)
        def _():
            dy[...] = before[...]

        @pl.when(jnp.logical_not(last))
        def _():
            for d, part in zip((*done, *ds), (*others, *parts)):
                dy[:, slot(lane ^ d, share)] = part[...]


def act_kernel(width, own, squares, g1, g2, g3, act, slope, hid, scale):
    rows, piece = act.shape
    count = lane_blocks(rows)
    sums = piece // LANES * rows
    row = pack_row(g1[sums:], count) + pack_row(g2[sums:], count) + pack_row(g3[sums:], count)
    r = lax.rsqrt((squares[...] + as_column(row, rows)) / width + 1e-06)
    scale[...] = r
    for i in range(piece // LANES):
        at = slice(i * LANES, (i + 1) * LANES)
        got = slice(i * rows, (i + 1) * rows)
        a = (own[:, at] + g1[got].astype(F32) + g2[got].astype(F32) + g3[got].astype(F32)) * r
        act[:, at] = a
        square = a * a
        t = jnp.tanh(GELU_IN * (a + GELU_CUBE * (square * a)))
        half = 0.5 * (1.0 + t)
        hid[:, at] = (a * half).astype(BF16)
        slope[:, at] = half + 0.5 * a * (1.0 - t * t) * (GELU_IN * (1.0 + 3.0 * GELU_CUBE * square))


def dact_kernel(own, g1, g2, g3, act, slope, pay):
    rows, piece = own.shape
    dhid = own[...] + g1[...].astype(F32) + g2[...].astype(F32) + g3[...].astype(F32)
    da = (dhid * slope[...]).astype(BF16)
    blocks = piece // LANES
    for i in range(blocks):
        pay[i * rows:(i + 1) * rows] = da[:, i * LANES:(i + 1) * LANES]
    column = jnp.sum(da.astype(F32) * act[...], axis=1, keepdims=True)
    pay[blocks * rows:] = pack_block(as_row(column, lane_blocks(rows) * LANES))


def back_block(d, js, values, earlier, weight, mine, lane):
    share = weight.shape[0] // 4
    total = None if earlier is None else earlier[:, d * share:(d + 1) * share]
    for j, value in zip(js, values):
        block = dot_nt(value, weight[slot(lane ^ d, share), slot(mine ^ j, value.shape[1])])
        total = block if total is None else total + block
    return total


def back_kernel(js, begin, *refs):
    *parts, weight = refs[:len(js) + 1]
    *earlier, total = refs[len(js) + 1:]
    mine, lane = place()
    share = weight.shape[0] // 4
    values = [unpack(part, total.shape[0]) for part in parts]
    for d in range(4):
        total[:, d * share:(d + 1) * share] = back_block(d, js, values, None if begin else earlier[0], weight, mine, lane)


def back_last_kernel(p0, p1, p2, p3, weight, earlier, keep, send):
    mine, lane = place()
    rows = earlier.shape[0]
    share = weight.shape[0] // 4
    sums = p0.shape[0] - SIDE
    values = [unpack(p1, rows)]
    row = sum(pack_row(part[sums:], lane_blocks(rows)) for part in (p0, p1, p2, p3))
    if row.shape[1] < keep.shape[1]:
        row = jnp.concatenate([row, jnp.zeros((1, keep.shape[1] - row.shape[1]), F32)], axis=1)
    for at, d in ((0, 1), (1, 3)):
        send[:rows, at * share:(at + 1) * share] = back_block(d, (1,), values, earlier, weight, mine, lane).astype(BF16)
    send[rows:] = side_block(row)
    for at, d in ((0, 0), (1, 2)):
        keep[:rows, at * share:(at + 1) * share] = back_block(d, (1,), values, earlier, weight, mine, lane)
    keep[rows:] = jnp.broadcast_to(row, (SIDE, keep.shape[1]))


def middle_kernel(keep, got, rest, send):
    rows = keep.shape[0] - SIDE
    share = rest.shape[1]
    row = (keep[rows:rows + 1] + side_row(got[rows:]))[:, :share]
    send[:rows] = (keep[:rows, share:] + got[:rows, share:].astype(F32)).astype(BF16)
    send[rows:] = side_block(row)
    rest[:rows] = keep[:rows, :share] + got[:rows, :share].astype(F32)
    rest[rows:] = jnp.broadcast_to(row, (SIDE, share))


def finish_kernel(width, rest, got, x_own, dy, gain, scale, grad_x, *grad_gain):
    _, lane = place()
    rows, share = x_own.shape
    at = slot(lane, share)
    r = scale[...]
    du = rest[:rows] + got[:rows].astype(F32)
    normed = x_own[...].astype(F32) * r
    inner = as_column(rest[rows:rows + 1] + side_row(got[rows:]), rows) / width
    dnorm = du * gain[:, at]
    grad_x[...] = (dy[:, at].astype(F32) + r * (dnorm - normed * inner)).astype(BF16)
    if grad_gain:
        grad_gain[0][...] = jnp.sum(du * normed, axis=0, keepdims=True)


def grad_out_kernel(h0, h1, h2, h3, dy, out, held, sems):
    mine, _ = place()
    piece = h0.shape[1]
    copies = []
    for d, part in enumerate((h0, h1, h2, h3)):
        held[d] = dot_tn(part[...], dy[...]).astype(BF16)
        copies.append(pltpu.make_async_copy(held.at[d], out.at[slot(mine ^ d, piece), :], sems.at[d]))
        copies[-1].start()
    for copy in copies:
        copy.wait()


def grad_in_kernel(p0, p1, p2, p3, x_full, gain, scale, out, scaled, held, sems):
    mine, _ = place()
    rows = x_full.shape[0]
    piece = (p0.shape[0] - SIDE) // rows * LANES
    scaled[...] = (x_full[...].astype(F32) * scale[...] * gain[...]).astype(BF16)
    copies = []
    for d, part in enumerate((p0, p1, p2, p3)):
        held[d] = dot_tn(scaled[...], unpack(part, rows)).astype(BF16)
        copies.append(pltpu.make_async_copy(held.at[d], out.at[:, slot(mine ^ d, piece)], sems.at[d]))
        copies[-1].start()
    for copy in copies:
        copy.wait()


def gradient(body, shape, block, *args, scratch=(), flops=0):
    return pl.pallas_call(
        body,
        out_shape=jax.ShapeDtypeStruct(shape, BF16),
        in_specs=[pl.BlockSpec(memory_space=pltpu.VMEM)] * len(args),
        out_specs=pl.BlockSpec(memory_space=pl.ANY),
        scratch_shapes=[*scratch, pltpu.VMEM((4,) + block, BF16), pltpu.SemaphoreType.DMA((4,))],
        compiler_params=pltpu.CompilerParams(vmem_limit_bytes=16 * 1024 * 1024),
        cost_estimate=pl.CostEstimate(flops=flops, bytes_accessed=2 * shape[0] * shape[1], transcendentals=0),
    )(*args)


def shards_of_four(checkpoints, gain, w_in, w_out, cotangent):
    sections = lax.axis_size("section")
    here = lax.axis_index("section")
    lane = lax.axis_index("dp")
    layers = sections // 4
    mine = here % 4
    _, micro, tok, share = checkpoints.shape
    rows = micro * tok
    quarter = share * 4
    width = 4 * quarter
    hidden = w_in.shape[2]
    piece = hidden // 4
    work = 2 * rows * quarter * hidden

    x0 = checkpoints[0].reshape(rows, share)
    cot = cotangent.reshape(rows, quarter)
    top = [s * 4 + d for s in range(sections) for d in range(4) if s // 4 == layers - 1]
    x2 = flip(x0, "dp", 2)
    x1 = flip(x0, "dp", 1)
    weight_in, x0, gain, begun = load_spread(x1, w_in[0], x0, gain)
    x2, weight_in = lax.optimization_barrier((x2, weight_in))
    sent = lax.ppermute(cot, ("section", "dp"), [((i // 4 ^ near) * 4 + i // 4 % 4, i) for i in top for near in (1, 0, 2) if i // 4 % 4 ^ i % 4 == (2, 1, 3)[near]])
    x3 = flip(x2, "dp", 1)

    packed = packed_shape(rows, piece)
    own, s1, s2, s3, x_full, squares = local(
        spread_in_last_kernel,
        [resident((rows, piece), F32)] + [resident(packed, BF16)] * 3
        + [resident((rows, quarter), BF16), resident((rows, 1), F32)],
        x0, x1, x2, x3, gain, weight_in, begun,
        flops=work,
    )
    s1, s2, s3, cot, w_out = lax.optimization_barrier((s1, s2, s3, cot, w_out))
    g3 = flip(s3, "section", 3)
    g2 = flip(s2, "section", 2)
    g1 = flip(s1, "section", 1)
    weight_out, cot = load(w_out[0], cot)
    act, slope, hid, scale = local(
        functools.partial(act_kernel, width),
        [resident((rows, piece), F32), resident((rows, piece), F32), resident((rows, piece), BF16), resident((rows, 1), F32)],
        own, squares, g1, g2, g3,
    )

    spread_outs = [resident((rows, piece), F32)] + [resident((rows, piece), BF16)] * 3 + [resident((rows, quarter), BF16)]

    def gather_hidden(block):
        return [block] + [flip(block, "section", j) for j in (1, 2, 3)]

    if layers == 1:
        hids = gather_hidden(hid)
    for phase in range(layers):
        final = phase == layers - 1
        if phase == 0:
            own, s1, s2, s3, dy = local(spread_first_kernel, spread_outs, cot, sent, weight_out, flops=work)
        else:
            d0, d1, d2, d3 = down
            first, hids = lax.optimization_barrier((d0, hids))
            total = [resident((rows, hidden), F32)]
            step = functools.partial(spread_next_kernel, layers)
            begun = local(functools.partial(step, (0,), True, False), total, first, dy, weight_out, flops=work // 4)
            begun = local(functools.partial(step, (1, 2), False, False), total, d1, d2, dy, weight_out, *begun, flops=work // 2)
            own, s1, s2, s3, dy = local(
                functools.partial(step, (3,), False, True), spread_outs, d3, dy, weight_out, *begun, d0, d1, d2,
                flops=work // 4,
            )
        g3 = flip(s3, "section", 3)
        g2 = flip(s2, "section", 2)
        g1 = flip(s1, "section", 1)
        if final:
            grad_out = gradient(grad_out_kernel, (hidden, quarter), (piece, quarter), *hids, dy, flops=work)
            own, grad_out = lax.optimization_barrier((own, grad_out))
        (pay,) = local(dact_kernel, [resident(packed, BF16)], own, g1, g2, g3, act, slope)
        p3 = flip(pay, "section", 3)
        p2 = flip(pay, "section", 2)
        p1 = flip(pay, "section", 1)
        total = [resident((rows, quarter), F32)]
        begun = local(functools.partial(back_kernel, (0,), True), total, pay, weight_in, flops=work // 4)
        begun = local(functools.partial(back_kernel, (3, 2), False), total, p3, p2, weight_in, *begun, flops=work // 2)
        keep, send = local(
            back_last_kernel,
            [resident((rows + SIDE, 2 * share), F32), resident((rows + SIDE, 2 * share), BF16)],
            pay, p1, p2, p3, weight_in, *begun,
            flops=work // 4,
        )
        got = flip(send, "dp", 1)
        rest, send = local(
            middle_kernel,
            [resident((rows + SIDE, share), F32), resident((rows + SIDE, share), BF16)],
            keep, got,
        )
        if phase == 0 and not final:
            send, hid = lax.optimization_barrier((send, hid))
            hids = gather_hidden(hid)
        got = flip(send, "dp", 2)
        if final:
            grad_in = gradient(
                grad_in_kernel, (quarter, hidden), (quarter, piece), pay, p1, p2, p3, x_full, gain, scale,
                scratch=[pltpu.VMEM((rows, quarter), BF16)], flops=work,
            )
            got, grad_in = lax.optimization_barrier((got, grad_in))
        outs = [resident((rows, share), BF16)]
        if final:
            outs = [jax.ShapeDtypeStruct((rows, share), BF16), jax.ShapeDtypeStruct((1, share), F32)]
        finished = local(functools.partial(finish_kernel, width), outs, rest, got, x0, dy, gain, scale)
        if not final:
            d0 = lax.ppermute(finished[0], "section", [(i, i - 4) for i in range(4, sections)])
            d2 = flip(d0, "dp", 2)
            d1 = flip(d0, "dp", 1)
            d3 = flip(d2, "dp", 1)
            down = (d0, d1, d2, d3)

    grad_x, grad_gain = finished
    return grad_in[None], grad_out[None], grad_gain, grad_x.reshape(1, micro, tok, share)


def shards(checkpoints, gain, w_in, w_out, cotangent):
    rows = checkpoints.shape[1] * checkpoints.shape[2]
    share = checkpoints.shape[3]
    piece = w_in.shape[2] // 4
    if lax.axis_size("dp") == 4 and rows % 16 == 0 and share % 128 == 0 and piece % 128 == 0 and rows <= min(share, piece):
        return shards_of_four(checkpoints, gain, w_in, w_out, cotangent)
    return shards_of_any(checkpoints, gain, w_in, w_out, cotangent)


def solution(mesh):
    in_specs = (
        P("section", None, None, "dp"),
        P("section", None),
        P("section", None, "dp"),
        P("section", "dp", None),
        P(None, None, "dp"),
    )
    out_specs = (
        P("section", None, "dp"),
        P("section", "dp", None),
        P("section", "dp"),
        P("section", None, None, "dp"),
    )
    return jax.shard_map(shards, mesh=mesh, in_specs=in_specs, out_specs=out_specs, check_vma=False)
```

```python
import functools

import jax
import jax.numpy as jnp
from jax import lax
from jax.experimental import pallas as pl
from jax.experimental.pallas import tpu as pltpu
from jax.sharding import PartitionSpec as P

F32 = jnp.float32
BF16 = jnp.bfloat16


def flip(block, axis, bits):
    count = lax.axis_size(axis)
    return lax.ppermute(block, axis, [(i, i ^ bits) for i in range(count)])


def side_rows(values, width):
    lead = values.astype(BF16)
    trail = (values - lead.astype(F32)).astype(BF16)
    flat = jnp.concatenate([lead, trail])
    return jnp.pad(flat, (0, 16 * width - flat.shape[0])).reshape(16, width)


def side_values(rows, count):
    flat = rows.reshape(-1)
    return flat[:count].astype(F32) + flat[count:2 * count].astype(F32)


def gelu_tanh(value):
    return jax.nn.gelu(value, approximate=True)


def shards_of_any(checkpoints, gain, w_in, w_out, cotangent):
    sections = lax.axis_size("section")
    n_dp = lax.axis_size("dp")
    here = lax.axis_index("section")
    lane = lax.axis_index("dp")
    layers = sections // 4
    mine = here % 4
    last = here // 4 == layers - 1
    _, micro, tok, share = checkpoints.shape
    rows = micro * tok
    quarter = share * n_dp
    width = 4 * quarter
    gain_row = gain[0]
    weight_in = w_in[0]
    weight_out = w_out[0]
    hidden = weight_in.shape[1]
    piece = hidden // 4
    core = lane % 2

    def gather_dp(block):
        bit = n_dp // 2
        parts = {0: block}
        while bit >= 1:
            other = flip(jnp.concatenate([parts[j] for j in parts], axis=1), "dp", bit)
            for at, j in enumerate(list(parts)):
                parts[j ^ bit] = other[:, at * block.shape[1]:(at + 1) * block.shape[1]]
            bit //= 2
        full = jnp.zeros((rows, quarter), block.dtype)
        for j, part in parts.items():
            full = lax.dynamic_update_slice(full, part, (0, (lane ^ j) * block.shape[1]))
        return full

    def cot_quarter(block):
        if n_dp < 4:
            whole = lax.all_gather(block, "dp", axis=1, tiled=True)
            return lax.dynamic_slice_in_dim(whole, mine * quarter, quarter, 1)
        per = n_dp // 4
        top = [s * n_dp + d for s in range(sections) for d in range(n_dp) if s // 4 == layers - 1]
        held = block
        far = lambda i, b: (i % n_dp // per ^ i // n_dp % 4) & b
        got = lax.ppermute(held, ("section", "dp"), [(i, i ^ 2 * per) for i in top if far(i, 3) == 0])
        held = jnp.where((lane // per ^ mine) & 2 == 0, held, got)
        got = lax.ppermute(held, ("section", "dp"), [(i, i ^ per) for i in top if far(i, 1) == 0])
        held = jnp.where((lane // per ^ mine) & 1 == 0, held, got)
        if per == 1:
            return held
        parts = {0: held}
        bit = per // 2
        while bit >= 1:
            for j in list(parts):
                parts[j ^ bit] = flip(parts[j], "dp", bit)
            bit //= 2
        full = jnp.zeros((rows, quarter), block.dtype)
        for j, part in parts.items():
            full = lax.dynamic_update_slice(full, part, (0, (lane % per ^ j) * block.shape[1]))
        return full

    def cut(values, j):
        return lax.dynamic_slice_in_dim(values, (mine ^ j) * piece, piece, 1)

    def fill(parts):
        full = jnp.zeros((rows, hidden), parts[0].dtype)
        for j, part in enumerate(parts):
            full = lax.dynamic_update_slice(full, part, (0, (mine ^ j) * piece))
        return full

    x_full = gather_dp(checkpoints[0].reshape(rows, share))
    cot = cot_quarter(cotangent.reshape(rows, cotangent.shape[2]))
    x_wide = x_full.astype(F32)
    scaled_raw = (x_wide * gain_row).astype(BF16)
    squares = jnp.sum(x_wide * x_wide, axis=1)

    act_raw = jnp.dot(scaled_raw, weight_in, preferred_element_type=F32)
    extra = side_rows(squares, piece)
    act = cut(act_raw, 0)
    for j in (3, 1, 2):
        got = flip(jnp.concatenate([cut(act_raw, j).astype(BF16), extra], axis=0), "section", j)
        act = act + got[:rows].astype(F32)
        squares = squares + side_values(got[rows:], rows)
    scale = lax.rsqrt(squares / width + 1e-06)[:, None]
    act = act * scale
    hid, pull = jax.vjp(gelu_tanh, act)
    hid = hid.astype(BF16)
    hid_full = fill([hid] + [flip(hid, "section", j) for j in (1, 2, 3)])
    normed = x_wide * scale
    scaled = (normed * gain_row).astype(BF16)

    def halves(values, side):
        pairs = values.reshape(rows, n_dp // 2, 2, share)
        return jnp.where(side == 0, pairs[:, :, 0], pairs[:, :, 1]).reshape(rows, quarter // 2)

    def own(values):
        return lax.dynamic_slice_in_dim(values, lane // 2 * share, share, 1)

    incoming = jnp.zeros((rows, quarter), BF16)
    normed_half = halves(normed, core)
    gain_half = halves(jnp.broadcast_to(gain_row, (rows, quarter)), core)
    for phase in range(layers):
        final = phase == layers - 1
        dy = jnp.where(last, cot, incoming) if phase > 0 else cot
        dhid_raw = jnp.dot(dy, weight_out.T, preferred_element_type=F32)
        dhid = cut(dhid_raw, 0)
        for j in (3, 1, 2):
            dhid = dhid + flip(cut(dhid_raw, j).astype(BF16), "section", j).astype(F32)
        dact = pull(dhid)[0].astype(BF16)
        inner = jnp.sum(dact.astype(F32) * act, axis=1)
        payload = jnp.concatenate([dact, side_rows(inner, piece)], axis=0)
        others = [flip(payload, "section", j) for j in (1, 2, 3)]
        for got in others:
            inner = inner + side_values(got[rows:], rows)
        dact_full = fill([dact] + [got[:rows] for got in others])
        part = jnp.dot(dact_full, weight_in.T, preferred_element_type=F32).astype(BF16)

        send = jnp.concatenate([halves(part, 1 - core), side_rows(inner, quarter // 2)], axis=0)
        got = flip(send, "dp", 1)
        dscaled = halves(part, core).astype(F32) + got[:rows].astype(F32)
        inner = inner + side_values(got[rows:], rows)
        bit = 2
        while bit < n_dp:
            send = jnp.concatenate([dscaled.astype(BF16), side_rows(inner, quarter // 2)], axis=0)
            got = flip(send, "dp", bit)
            dscaled = dscaled + got[:rows].astype(F32)
            inner = inner + side_values(got[rows:], rows)
            bit *= 2
        dnorm = dscaled * gain_half
        dy_half = halves(dy, core).astype(F32)
        grad_x = (dy_half + scale * (dnorm - normed_half * (inner / width)[:, None])).astype(BF16)
        if not final:
            down = lax.ppermute(grad_x, "section", [(i, i - 4) for i in range(4, sections)])
            other = flip(down, "dp", 1)
            pairs = jnp.where(
                core == 0,
                jnp.stack([down.reshape(rows, n_dp // 2, share), other.reshape(rows, n_dp // 2, share)], axis=2),
                jnp.stack([other.reshape(rows, n_dp // 2, share), down.reshape(rows, n_dp // 2, share)], axis=2),
            )
            incoming = pairs.reshape(rows, quarter)

    grad_out = jnp.dot(hid_full.T, dy, preferred_element_type=F32).astype(BF16)
    grad_in = jnp.dot(scaled.T, dact_full, preferred_element_type=F32).astype(BF16)
    grad_gain = jnp.sum(own(dscaled) * own(normed_half), axis=0)
    return (
        grad_in[None],
        grad_out[None],
        grad_gain[None],
        own(grad_x).reshape(1, micro, tok, share),
    )


SIDE = 16
LANES = 128
GELU_IN = 0.7978845608028654
GELU_CUBE = 0.044715


def resident(shape, dtype):
    return pltpu.VMEM(shape, dtype)


def local(body, outs, *args, scratch=(), flops=0):
    spec = pl.BlockSpec(memory_space=pltpu.VMEM)
    moved = sum(a.size * a.dtype.itemsize for a in args)
    return pl.pallas_call(
        body,
        out_shape=tuple(outs),
        in_specs=[spec] * len(args),
        out_specs=tuple(spec for _ in outs),
        scratch_shapes=list(scratch),
        compiler_params=pltpu.CompilerParams(vmem_limit_bytes=16 * 1024 * 1024),
        cost_estimate=pl.CostEstimate(flops=flops, bytes_accessed=moved, transcendentals=0),
    )(*args)


def diagonal(rows, width):
    return lax.broadcasted_iota(jnp.int32, (rows, width), 0) == lax.broadcasted_iota(jnp.int32, (rows, width), 1)


def as_row(column, width):
    rows = column.shape[0]
    return jnp.sum(jnp.where(diagonal(rows, width), column, 0.0), axis=0, keepdims=True)


def as_column(row, rows):
    return jnp.sum(jnp.where(diagonal(rows, row.shape[1]), row, 0.0), axis=1, keepdims=True)


def side_block(row):
    lead = row.astype(BF16).astype(F32)
    at = lax.broadcasted_iota(jnp.int32, (SIDE, row.shape[1]), 0)
    return jnp.where(at == 0, lead, jnp.where(at == 1, row - lead, 0.0)).astype(BF16)


def side_row(block):
    wide = block.astype(F32)
    return wide[0:1] + wide[1:2]


def packed_shape(rows, piece):
    return (piece // LANES * rows + SIDE, LANES)


def pack_block(row):
    lead = row.astype(BF16).astype(F32)
    count = row.shape[1] // LANES
    at = lax.broadcasted_iota(jnp.int32, (SIDE, LANES), 0)
    block = jnp.zeros((SIDE, LANES), F32)
    for i in range(count):
        lanes = slice(i * LANES, (i + 1) * LANES)
        block = jnp.where(at == i, lead[:, lanes], jnp.where(at == count + i, (row - lead)[:, lanes], block))
    return block.astype(BF16)


def pack_row(block, count):
    wide = block.astype(F32)
    return jnp.concatenate([wide[i:i + 1] + wide[count + i:count + i + 1] for i in range(count)], axis=1)


def lane_blocks(rows):
    return -(-rows // LANES)


def unpack(packed, rows):
    blocks = (packed.shape[0] - SIDE) // rows
    return jnp.concatenate([packed[i * rows:(i + 1) * rows] for i in range(blocks)], axis=1)


def load_kernel(*refs):
    count = len(refs) // 2
    copies = [pltpu.make_async_copy(refs[i], refs[count + i], refs[-1].at[i]) for i in range(count)]
    for copy in copies:
        copy.start()
    for copy in copies:
        copy.wait()


def load(*arrays):
    return pl.pallas_call(
        load_kernel,
        out_shape=tuple(resident(a.shape, a.dtype) for a in arrays),
        in_specs=[pl.BlockSpec(memory_space=pl.ANY)] * len(arrays),
        out_specs=tuple(pl.BlockSpec(memory_space=pltpu.VMEM) for _ in arrays),
        scratch_shapes=[pltpu.SemaphoreType.DMA((len(arrays),))],
        compiler_params=pltpu.CompilerParams(vmem_limit_bytes=1024 * 1024),
        cost_estimate=pl.CostEstimate(flops=0, bytes_accessed=sum(2 * a.size * a.dtype.itemsize for a in arrays), transcendentals=0),
    )(*(pltpu.with_memory_space_constraint(a, pltpu.HBM) for a in arrays))


def place():
    return lax.axis_index("section") % 4, lax.axis_index("dp")


def dot_nt(left, right):
    return lax.dot_general(left, right, (((1,), (1,)), ((), ())), preferred_element_type=F32)


def dot_tn(left, right):
    return lax.dot_general(left, right, (((0,), (0,)), ((), ())), preferred_element_type=F32)


def slot(index, size):
    return pl.ds(pl.multiple_of(index * size, size), size)


def spread_in_part(part, at, gain, weight, mine, total, begin):
    share = part.shape[1]
    piece = weight.shape[1] // 4
    scaled = (part[...].astype(F32) * gain[:, slot(at, share)]).astype(BF16)
    for d in (3, 2, 1, 0):
        block = jnp.dot(scaled, weight[slot(at, share), slot(mine ^ d, piece)], preferred_element_type=F32)
        columns = slice(d * piece, (d + 1) * piece)
        total[:, columns] = block if begin else total[:, columns] + block


def square_sum(part):
    wide = part[...].astype(F32)
    return jnp.sum(wide * wide, axis=1, keepdims=True)


def load_spread_kernel(x1, weight, x0, gain, weight_held, x0_held, gain_held, total, sems):
    mine, lane = place()
    share = x1.shape[1]
    small = [pltpu.make_async_copy(source, held, sems.at[i]) for i, (source, held) in enumerate(((x0, x0_held), (gain, gain_held)))]
    slices = [slot(lane ^ d, share) for d in range(4)]
    large = [pltpu.make_async_copy(weight.at[at], weight_held.at[at], sems.at[2 + d]) for d, at in enumerate(slices)]
    for copy in (*small, *large):
        copy.start()
    for copy in (*small, large[0]):
        copy.wait()
    spread_in_part(x0_held, lane, gain_held, weight_held, mine, total, True)
    large[1].wait()
    spread_in_part(x1, lane ^ 1, gain_held, weight_held, mine, total, False)
    large[2].wait()
    large[3].wait()


def load_spread(x1, weight, x0, gain):
    keep = pl.BlockSpec(memory_space=pltpu.VMEM)
    rows, hidden = x0.shape[0], weight.shape[1]
    outs = [(a.shape, a.dtype) for a in (weight, x0, gain)] + [((rows, hidden), F32)]
    far = [pltpu.with_memory_space_constraint(a, pltpu.HBM) for a in (weight, x0, gain)]
    return pl.pallas_call(
        load_spread_kernel,
        out_shape=tuple(resident(*out) for out in outs),
        in_specs=[keep] + [pl.BlockSpec(memory_space=pl.ANY)] * 3,
        out_specs=(keep,) * 4,
        scratch_shapes=[pltpu.SemaphoreType.DMA((6,))],
        compiler_params=pltpu.CompilerParams(vmem_limit_bytes=8 * 1024 * 1024),
        cost_estimate=pl.CostEstimate(flops=rows * weight.size, bytes_accessed=4 * weight.size, transcendentals=0),
    )(x1, *far)


def spread_in_last_kernel(x0, x1, x2, x3, gain, weight, before, own, s1, s2, s3, x_full, squares):
    mine, lane = place()
    rows, share = x0.shape
    piece = own.shape[1]
    ends = [(slot(lane ^ d, share), part) for d, part in ((2, x2), (3, x3))]
    ends = [(at, (part[...].astype(F32) * gain[:, at]).astype(BF16)) for at, part in ends]
    column = square_sum(x0) + square_sum(x1) + square_sum(x2) + square_sum(x3)
    block = pack_block(as_row(column, lane_blocks(rows) * LANES))
    for d, out in ((1, s1), (2, s2), (3, s3), (0, own)):
        value = before[:, d * piece:(d + 1) * piece]
        for at, scaled in ends:
            value = value + jnp.dot(scaled, weight[at, slot(mine ^ d, piece)], preferred_element_type=F32)
        if d == 0:
            out[...] = value
            continue
        for i in range(piece // LANES):
            out[i * rows:(i + 1) * rows] = value[:, i * LANES:(i + 1) * LANES].astype(BF16)
        out[piece // LANES * rows:] = block
    squares[...] = column
    for d, part in enumerate((x0, x1, x2, x3)):
        x_full[:, slot(lane ^ d, share)] = part[...]


def spread_dy(dy, weight, mine, own, s1, s2, s3):
    piece = own.shape[1]
    for d, out in ((3, s3), (2, s2), (1, s1)):
        out[...] = dot_nt(dy[...], weight[slot(mine ^ d, piece), :]).astype(BF16)
    own[...] = dot_nt(dy[...], weight[slot(mine, piece), :])


def spread_first_kernel(cot, sent, weight, own, s1, s2, s3, dy):
    mine, lane = place()

    @pl.when(lane == mine)
    def _():
        dy[...] = cot[...]

    @pl.when(lane != mine)
    def _():
        dy[...] = sent[...]

    spread_dy(dy, weight, mine, own, s1, s2, s3)


def spread_next_kernel(layers, ds, begin, end, *refs):
    parts, refs = refs[:len(ds)], refs[len(ds):]
    before, weight = refs[:2]
    earlier, refs = (None, refs[2:]) if begin else (refs[2], refs[3:])
    mine, lane = place()
    share = parts[0].shape[1]
    piece = weight.shape[0] // 4
    last = lax.axis_index("section") // 4 == layers - 1
    if end:
        *others, own, s1, s2, s3, dy = refs
        outs = (own, s1, s2, s3)
    else:
        outs = [refs[0].at[:, j * piece:(j + 1) * piece] for j in range(4)]
    slices = [slot(lane ^ d, share) for d in ds]
    values = [jnp.where(last, before[:, at], part[...]) for at, part in zip(slices, parts)]
    for j in (1, 2, 3, 0):
        total = None if begin else earlier[:, j * piece:(j + 1) * piece]
        for at, value in zip(slices, values):
            block = dot_nt(value, weight[slot(mine ^ j, piece), at])
            total = block if total is None else total + block
        outs[j][...] = total.astype(outs[j].dtype)
    if end:
        done = [d for d in range(4) if d not in ds]

        @pl.when(last)
        def _():
            dy[...] = before[...]

        @pl.when(jnp.logical_not(last))
        def _():
            for d, part in zip((*done, *ds), (*others, *parts)):
                dy[:, slot(lane ^ d, share)] = part[...]


def act_kernel(width, own, squares, g1, g2, g3, act, slope, hid, scale):
    rows, piece = act.shape
    count = lane_blocks(rows)
    sums = piece // LANES * rows
    row = pack_row(g1[sums:], count) + pack_row(g2[sums:], count) + pack_row(g3[sums:], count)
    r = lax.rsqrt((squares[...] + as_column(row, rows)) / width + 1e-06)
    scale[...] = r
    for i in range(piece // LANES):
        at = slice(i * LANES, (i + 1) * LANES)
        got = slice(i * rows, (i + 1) * rows)
        a = (own[:, at] + g1[got].astype(F32) + g2[got].astype(F32) + g3[got].astype(F32)) * r
        act[:, at] = a
        square = a * a
        t = jnp.tanh(GELU_IN * (a + GELU_CUBE * (square * a)))
        half = 0.5 * (1.0 + t)
        hid[:, at] = (a * half).astype(BF16)
        slope[:, at] = half + 0.5 * a * (1.0 - t * t) * (GELU_IN * (1.0 + 3.0 * GELU_CUBE * square))


def dact_kernel(own, g1, g2, g3, act, slope, pay):
    rows, piece = own.shape
    dhid = own[...] + g1[...].astype(F32) + g2[...].astype(F32) + g3[...].astype(F32)
    da = (dhid * slope[...]).astype(BF16)
    blocks = piece // LANES
    for i in range(blocks):
        pay[i * rows:(i + 1) * rows] = da[:, i * LANES:(i + 1) * LANES]
    column = jnp.sum(da.astype(F32) * act[...], axis=1, keepdims=True)
    pay[blocks * rows:] = pack_block(as_row(column, lane_blocks(rows) * LANES))


def back_block(d, js, values, earlier, weight, mine, lane):
    share = weight.shape[0] // 4
    total = None if earlier is None else earlier[:, d * share:(d + 1) * share]
    for j, value in zip(js, values):
        block = dot_nt(value, weight[slot(lane ^ d, share), slot(mine ^ j, value.shape[1])])
        total = block if total is None else total + block
    return total


def back_kernel(js, begin, *refs):
    *parts, weight = refs[:len(js) + 1]
    *earlier, total = refs[len(js) + 1:]
    mine, lane = place()
    share = weight.shape[0] // 4
    values = [unpack(part, total.shape[0]) for part in parts]
    for d in range(4):
        total[:, d * share:(d + 1) * share] = back_block(d, js, values, None if begin else earlier[0], weight, mine, lane)


def back_last_kernel(p0, p1, p2, p3, weight, earlier, keep, send):
    mine, lane = place()
    rows = earlier.shape[0]
    share = weight.shape[0] // 4
    sums = p0.shape[0] - SIDE
    values = [unpack(p2, rows), unpack(p1, rows)]
    row = sum(pack_row(part[sums:], lane_blocks(rows)) for part in (p0, p1, p2, p3))
    if row.shape[1] < keep.shape[1]:
        row = jnp.concatenate([row, jnp.zeros((1, keep.shape[1] - row.shape[1]), F32)], axis=1)
    for at, d in ((0, 1), (1, 3)):
        send[:rows, at * share:(at + 1) * share] = back_block(d, (2, 1), values, earlier, weight, mine, lane).astype(BF16)
    send[rows:] = side_block(row)
    for at, d in ((0, 0), (1, 2)):
        keep[:rows, at * share:(at + 1) * share] = back_block(d, (2, 1), values, earlier, weight, mine, lane)
    keep[rows:] = jnp.broadcast_to(row, (SIDE, keep.shape[1]))


def middle_kernel(keep, got, rest, send):
    rows = keep.shape[0] - SIDE
    share = rest.shape[1]
    row = (keep[rows:rows + 1] + side_row(got[rows:]))[:, :share]
    send[:rows] = (keep[:rows, share:] + got[:rows, share:].astype(F32)).astype(BF16)
    send[rows:] = side_block(row)
    rest[:rows] = keep[:rows, :share] + got[:rows, :share].astype(F32)
    rest[rows:] = jnp.broadcast_to(row, (SIDE, share))


def finish_kernel(width, rest, got, x_own, dy, gain, scale, grad_x, *grad_gain):
    _, lane = place()
    rows, share = x_own.shape
    at = slot(lane, share)
    r = scale[...]
    du = rest[:rows] + got[:rows].astype(F32)
    normed = x_own[...].astype(F32) * r
    inner = as_column(rest[rows:rows + 1] + side_row(got[rows:]), rows) / width
    dnorm = du * gain[:, at]
    grad_x[...] = (dy[:, at].astype(F32) + r * (dnorm - normed * inner)).astype(BF16)
    if grad_gain:
        grad_gain[0][...] = jnp.sum(du * normed, axis=0, keepdims=True)


def grad_out_kernel(h0, h1, h2, h3, dy, out, held, sems):
    mine, _ = place()
    piece = h0.shape[1]
    copies = []
    for d, part in enumerate((h0, h1, h2, h3)):
        held[d] = dot_tn(part[...], dy[...]).astype(BF16)
        copies.append(pltpu.make_async_copy(held.at[d], out.at[slot(mine ^ d, piece), :], sems.at[d]))
        copies[-1].start()
    for copy in copies:
        copy.wait()


def grad_in_kernel(p0, p1, p2, p3, x_full, gain, scale, out, scaled, held, sems):
    mine, _ = place()
    rows = x_full.shape[0]
    piece = (p0.shape[0] - SIDE) // rows * LANES
    scaled[...] = (x_full[...].astype(F32) * scale[...] * gain[...]).astype(BF16)
    copies = []
    for d, part in enumerate((p0, p1, p2, p3)):
        held[d] = dot_tn(scaled[...], unpack(part, rows)).astype(BF16)
        copies.append(pltpu.make_async_copy(held.at[d], out.at[:, slot(mine ^ d, piece)], sems.at[d]))
        copies[-1].start()
    for copy in copies:
        copy.wait()


def gradient(body, shape, block, *args, scratch=(), flops=0):
    return pl.pallas_call(
        body,
        out_shape=jax.ShapeDtypeStruct(shape, BF16),
        in_specs=[pl.BlockSpec(memory_space=pltpu.VMEM)] * len(args),
        out_specs=pl.BlockSpec(memory_space=pl.ANY),
        scratch_shapes=[*scratch, pltpu.VMEM((4,) + block, BF16), pltpu.SemaphoreType.DMA((4,))],
        compiler_params=pltpu.CompilerParams(vmem_limit_bytes=16 * 1024 * 1024),
        cost_estimate=pl.CostEstimate(flops=flops, bytes_accessed=2 * shape[0] * shape[1], transcendentals=0),
    )(*args)


def shards_of_four(checkpoints, gain, w_in, w_out, cotangent):
    sections = lax.axis_size("section")
    here = lax.axis_index("section")
    lane = lax.axis_index("dp")
    layers = sections // 4
    mine = here % 4
    _, micro, tok, share = checkpoints.shape
    rows = micro * tok
    quarter = share * 4
    width = 4 * quarter
    hidden = w_in.shape[2]
    piece = hidden // 4
    work = 2 * rows * quarter * hidden

    x0 = checkpoints[0].reshape(rows, share)
    cot = cotangent.reshape(rows, quarter)
    top = [s * 4 + d for s in range(sections) for d in range(4) if s // 4 == layers - 1]
    x2 = flip(x0, "dp", 2)
    x1 = flip(x0, "dp", 1)
    weight_in, x0, gain, begun = load_spread(x1, w_in[0], x0, gain)
    x2, weight_in = lax.optimization_barrier((x2, weight_in))
    sent = lax.ppermute(cot, ("section", "dp"), [((i // 4 ^ near) * 4 + i // 4 % 4, i) for i in top for near in (1, 0, 2) if i // 4 % 4 ^ i % 4 == (2, 1, 3)[near]])
    x3 = flip(x2, "dp", 1)

    packed = packed_shape(rows, piece)
    own, s1, s2, s3, x_full, squares = local(
        spread_in_last_kernel,
        [resident((rows, piece), F32)] + [resident(packed, BF16)] * 3
        + [resident((rows, quarter), BF16), resident((rows, 1), F32)],
        x0, x1, x2, x3, gain, weight_in, begun,
        flops=work,
    )
    s1, s2, s3, cot, w_out = lax.optimization_barrier((s1, s2, s3, cot, w_out))
    g3 = flip(s3, "section", 3)
    g2 = flip(s2, "section", 2)
    g1 = flip(s1, "section", 1)
    weight_out, cot = load(w_out[0], cot)
    act, slope, hid, scale = local(
        functools.partial(act_kernel, width),
        [resident((rows, piece), F32), resident((rows, piece), F32), resident((rows, piece), BF16), resident((rows, 1), F32)],
        own, squares, g1, g2, g3,
    )

    spread_outs = [resident((rows, piece), F32)] + [resident((rows, piece), BF16)] * 3 + [resident((rows, quarter), BF16)]

    def gather_hidden(block):
        return [block] + [flip(block, "section", j) for j in (1, 2, 3)]

    if layers == 1:
        hids = gather_hidden(hid)
    for phase in range(layers):
        final = phase == layers - 1
        if phase == 0:
            own, s1, s2, s3, dy = local(spread_first_kernel, spread_outs, cot, sent, weight_out, flops=work)
        else:
            d0, d1, d2, d3 = down
            first, hids = lax.optimization_barrier((d0, hids))
            total = [resident((rows, hidden), F32)]
            step = functools.partial(spread_next_kernel, layers)
            begun = local(functools.partial(step, (0,), True, False), total, first, dy, weight_out, flops=work // 4)
            begun = local(functools.partial(step, (1, 2), False, False), total, d1, d2, dy, weight_out, *begun, flops=work // 2)
            own, s1, s2, s3, dy = local(
                functools.partial(step, (3,), False, True), spread_outs, d3, dy, weight_out, *begun, d0, d1, d2,
                flops=work // 4,
            )
        g3 = flip(s3, "section", 3)
        g2 = flip(s2, "section", 2)
        g1 = flip(s1, "section", 1)
        if final:
            grad_out = gradient(grad_out_kernel, (hidden, quarter), (piece, quarter), *hids, dy, flops=work)
            own, grad_out = lax.optimization_barrier((own, grad_out))
        (pay,) = local(dact_kernel, [resident(packed, BF16)], own, g1, g2, g3, act, slope)
        p3 = flip(pay, "section", 3)
        p2 = flip(pay, "section", 2)
        p1 = flip(pay, "section", 1)
        total = [resident((rows, quarter), F32)]
        begun = local(functools.partial(back_kernel, (0,), True), total, pay, weight_in, flops=work // 4)
        begun = local(functools.partial(back_kernel, (3,), False), total, p3, weight_in, *begun, flops=work // 4)
        keep, send = local(
            back_last_kernel,
            [resident((rows + SIDE, 2 * share), F32), resident((rows + SIDE, 2 * share), BF16)],
            pay, p1, p2, p3, weight_in, *begun,
            flops=work // 2,
        )
        got = flip(send, "dp", 1)
        rest, send = local(
            middle_kernel,
            [resident((rows + SIDE, share), F32), resident((rows + SIDE, share), BF16)],
            keep, got,
        )
        if phase == 0 and not final:
            send, hid = lax.optimization_barrier((send, hid))
            hids = gather_hidden(hid)
        got = flip(send, "dp", 2)
        if final:
            grad_in = gradient(
                grad_in_kernel, (quarter, hidden), (quarter, piece), pay, p1, p2, p3, x_full, gain, scale,
                scratch=[pltpu.VMEM((rows, quarter), BF16)], flops=work,
            )
            got, grad_in = lax.optimization_barrier((got, grad_in))
        outs = [resident((rows, share), BF16)]
        if final:
            outs = [jax.ShapeDtypeStruct((rows, share), BF16), jax.ShapeDtypeStruct((1, share), F32)]
        finished = local(functools.partial(finish_kernel, width), outs, rest, got, x0, dy, gain, scale)
        if not final:
            d0 = lax.ppermute(finished[0], "section", [(i, i - 4) for i in range(4, sections)])
            d2 = flip(d0, "dp", 2)
            d1 = flip(d0, "dp", 1)
            d3 = flip(d2, "dp", 1)
            down = (d0, d1, d2, d3)

    grad_x, grad_gain = finished
    return grad_in[None], grad_out[None], grad_gain, grad_x.reshape(1, micro, tok, share)


def shards(checkpoints, gain, w_in, w_out, cotangent):
    rows = checkpoints.shape[1] * checkpoints.shape[2]
    share = checkpoints.shape[3]
    piece = w_in.shape[2] // 4
    if lax.axis_size("dp") == 4 and rows % 16 == 0 and share % 128 == 0 and piece % 128 == 0 and rows <= min(share, piece):
        return shards_of_four(checkpoints, gain, w_in, w_out, cotangent)
    return shards_of_any(checkpoints, gain, w_in, w_out, cotangent)


def solution(mesh):
    in_specs = (
        P("section", None, None, "dp"),
        P("section", None),
        P("section", None, "dp"),
        P("section", "dp", None),
        P(None, None, "dp"),
    )
    out_specs = (
        P("section", None, "dp"),
        P("section", "dp", None),
        P("section", "dp"),
        P("section", None, None, "dp"),
    )
    return jax.shard_map(shards, mesh=mesh, in_specs=in_specs, out_specs=out_specs, check_vma=False)
```

```python
import functools

import jax
import jax.numpy as jnp
from jax import lax
from jax.experimental import pallas as pl
from jax.experimental.pallas import tpu as pltpu
from jax.sharding import PartitionSpec as P

F32 = jnp.float32
BF16 = jnp.bfloat16


def flip(block, axis, bits):
    count = lax.axis_size(axis)
    return lax.ppermute(block, axis, [(i, i ^ bits) for i in range(count)])


def side_rows(values, width):
    lead = values.astype(BF16)
    trail = (values - lead.astype(F32)).astype(BF16)
    flat = jnp.concatenate([lead, trail])
    return jnp.pad(flat, (0, 16 * width - flat.shape[0])).reshape(16, width)


def side_values(rows, count):
    flat = rows.reshape(-1)
    return flat[:count].astype(F32) + flat[count:2 * count].astype(F32)


def gelu_tanh(value):
    return jax.nn.gelu(value, approximate=True)


def shards_of_any(checkpoints, gain, w_in, w_out, cotangent):
    sections = lax.axis_size("section")
    n_dp = lax.axis_size("dp")
    here = lax.axis_index("section")
    lane = lax.axis_index("dp")
    layers = sections // 4
    mine = here % 4
    last = here // 4 == layers - 1
    _, micro, tok, share = checkpoints.shape
    rows = micro * tok
    quarter = share * n_dp
    width = 4 * quarter
    gain_row = gain[0]
    weight_in = w_in[0]
    weight_out = w_out[0]
    hidden = weight_in.shape[1]
    piece = hidden // 4
    core = lane % 2

    def gather_dp(block):
        bit = n_dp // 2
        parts = {0: block}
        while bit >= 1:
            other = flip(jnp.concatenate([parts[j] for j in parts], axis=1), "dp", bit)
            for at, j in enumerate(list(parts)):
                parts[j ^ bit] = other[:, at * block.shape[1]:(at + 1) * block.shape[1]]
            bit //= 2
        full = jnp.zeros((rows, quarter), block.dtype)
        for j, part in parts.items():
            full = lax.dynamic_update_slice(full, part, (0, (lane ^ j) * block.shape[1]))
        return full

    def cot_quarter(block):
        if n_dp < 4:
            whole = lax.all_gather(block, "dp", axis=1, tiled=True)
            return lax.dynamic_slice_in_dim(whole, mine * quarter, quarter, 1)
        per = n_dp // 4
        top = [s * n_dp + d for s in range(sections) for d in range(n_dp) if s // 4 == layers - 1]
        held = block
        far = lambda i, b: (i % n_dp // per ^ i // n_dp % 4) & b
        got = lax.ppermute(held, ("section", "dp"), [(i, i ^ 2 * per) for i in top if far(i, 3) == 0])
        held = jnp.where((lane // per ^ mine) & 2 == 0, held, got)
        got = lax.ppermute(held, ("section", "dp"), [(i, i ^ per) for i in top if far(i, 1) == 0])
        held = jnp.where((lane // per ^ mine) & 1 == 0, held, got)
        if per == 1:
            return held
        parts = {0: held}
        bit = per // 2
        while bit >= 1:
            for j in list(parts):
                parts[j ^ bit] = flip(parts[j], "dp", bit)
            bit //= 2
        full = jnp.zeros((rows, quarter), block.dtype)
        for j, part in parts.items():
            full = lax.dynamic_update_slice(full, part, (0, (lane % per ^ j) * block.shape[1]))
        return full

    def cut(values, j):
        return lax.dynamic_slice_in_dim(values, (mine ^ j) * piece, piece, 1)

    def fill(parts):
        full = jnp.zeros((rows, hidden), parts[0].dtype)
        for j, part in enumerate(parts):
            full = lax.dynamic_update_slice(full, part, (0, (mine ^ j) * piece))
        return full

    x_full = gather_dp(checkpoints[0].reshape(rows, share))
    cot = cot_quarter(cotangent.reshape(rows, cotangent.shape[2]))
    x_wide = x_full.astype(F32)
    scaled_raw = (x_wide * gain_row).astype(BF16)
    squares = jnp.sum(x_wide * x_wide, axis=1)

    act_raw = jnp.dot(scaled_raw, weight_in, preferred_element_type=F32)
    extra = side_rows(squares, piece)
    act = cut(act_raw, 0)
    for j in (3, 1, 2):
        got = flip(jnp.concatenate([cut(act_raw, j).astype(BF16), extra], axis=0), "section", j)
        act = act + got[:rows].astype(F32)
        squares = squares + side_values(got[rows:], rows)
    scale = lax.rsqrt(squares / width + 1e-06)[:, None]
    act = act * scale
    hid, pull = jax.vjp(gelu_tanh, act)
    hid = hid.astype(BF16)
    hid_full = fill([hid] + [flip(hid, "section", j) for j in (1, 2, 3)])
    normed = x_wide * scale
    scaled = (normed * gain_row).astype(BF16)

    def halves(values, side):
        pairs = values.reshape(rows, n_dp // 2, 2, share)
        return jnp.where(side == 0, pairs[:, :, 0], pairs[:, :, 1]).reshape(rows, quarter // 2)

    def own(values):
        return lax.dynamic_slice_in_dim(values, lane // 2 * share, share, 1)

    incoming = jnp.zeros((rows, quarter), BF16)
    normed_half = halves(normed, core)
    gain_half = halves(jnp.broadcast_to(gain_row, (rows, quarter)), core)
    for phase in range(layers):
        final = phase == layers - 1
        dy = jnp.where(last, cot, incoming) if phase > 0 else cot
        dhid_raw = jnp.dot(dy, weight_out.T, preferred_element_type=F32)
        dhid = cut(dhid_raw, 0)
        for j in (3, 1, 2):
            dhid = dhid + flip(cut(dhid_raw, j).astype(BF16), "section", j).astype(F32)
        dact = pull(dhid)[0].astype(BF16)
        inner = jnp.sum(dact.astype(F32) * act, axis=1)
        payload = jnp.concatenate([dact, side_rows(inner, piece)], axis=0)
        others = [flip(payload, "section", j) for j in (1, 2, 3)]
        for got in others:
            inner = inner + side_values(got[rows:], rows)
        dact_full = fill([dact] + [got[:rows] for got in others])
        part = jnp.dot(dact_full, weight_in.T, preferred_element_type=F32).astype(BF16)

        send = jnp.concatenate([halves(part, 1 - core), side_rows(inner, quarter // 2)], axis=0)
        got = flip(send, "dp", 1)
        dscaled = halves(part, core).astype(F32) + got[:rows].astype(F32)
        inner = inner + side_values(got[rows:], rows)
        bit = 2
        while bit < n_dp:
            send = jnp.concatenate([dscaled.astype(BF16), side_rows(inner, quarter // 2)], axis=0)
            got = flip(send, "dp", bit)
            dscaled = dscaled + got[:rows].astype(F32)
            inner = inner + side_values(got[rows:], rows)
            bit *= 2
        dnorm = dscaled * gain_half
        dy_half = halves(dy, core).astype(F32)
        grad_x = (dy_half + scale * (dnorm - normed_half * (inner / width)[:, None])).astype(BF16)
        if not final:
            down = lax.ppermute(grad_x, "section", [(i, i - 4) for i in range(4, sections)])
            other = flip(down, "dp", 1)
            pairs = jnp.where(
                core == 0,
                jnp.stack([down.reshape(rows, n_dp // 2, share), other.reshape(rows, n_dp // 2, share)], axis=2),
                jnp.stack([other.reshape(rows, n_dp // 2, share), down.reshape(rows, n_dp // 2, share)], axis=2),
            )
            incoming = pairs.reshape(rows, quarter)

    grad_out = jnp.dot(hid_full.T, dy, preferred_element_type=F32).astype(BF16)
    grad_in = jnp.dot(scaled.T, dact_full, preferred_element_type=F32).astype(BF16)
    grad_gain = jnp.sum(own(dscaled) * own(normed_half), axis=0)
    return (
        grad_in[None],
        grad_out[None],
        grad_gain[None],
        own(grad_x).reshape(1, micro, tok, share),
    )


SIDE = 16
LANES = 128
GELU_IN = 0.7978845608028654
GELU_CUBE = 0.044715


def resident(shape, dtype):
    return pltpu.VMEM(shape, dtype)


def local(body, outs, *args, scratch=(), flops=0):
    spec = pl.BlockSpec(memory_space=pltpu.VMEM)
    moved = sum(a.size * a.dtype.itemsize for a in args)
    return pl.pallas_call(
        body,
        out_shape=tuple(outs),
        in_specs=[spec] * len(args),
        out_specs=tuple(spec for _ in outs),
        scratch_shapes=list(scratch),
        compiler_params=pltpu.CompilerParams(vmem_limit_bytes=16 * 1024 * 1024),
        cost_estimate=pl.CostEstimate(flops=flops, bytes_accessed=moved, transcendentals=0),
    )(*args)


def diagonal(rows, width):
    return lax.broadcasted_iota(jnp.int32, (rows, width), 0) == lax.broadcasted_iota(jnp.int32, (rows, width), 1)


def as_row(column, width):
    rows = column.shape[0]
    return jnp.sum(jnp.where(diagonal(rows, width), column, 0.0), axis=0, keepdims=True)


def as_column(row, rows):
    return jnp.sum(jnp.where(diagonal(rows, row.shape[1]), row, 0.0), axis=1, keepdims=True)


def side_block(row):
    lead = row.astype(BF16).astype(F32)
    at = lax.broadcasted_iota(jnp.int32, (SIDE, row.shape[1]), 0)
    return jnp.where(at == 0, lead, jnp.where(at == 1, row - lead, 0.0)).astype(BF16)


def side_row(block):
    wide = block.astype(F32)
    return wide[0:1] + wide[1:2]


def packed_shape(rows, piece):
    return (piece // LANES * rows + SIDE, LANES)


def pack_block(row):
    lead = row.astype(BF16).astype(F32)
    count = row.shape[1] // LANES
    at = lax.broadcasted_iota(jnp.int32, (SIDE, LANES), 0)
    block = jnp.zeros((SIDE, LANES), F32)
    for i in range(count):
        lanes = slice(i * LANES, (i + 1) * LANES)
        block = jnp.where(at == i, lead[:, lanes], jnp.where(at == count + i, (row - lead)[:, lanes], block))
    return block.astype(BF16)


def pack_row(block, count):
    wide = block.astype(F32)
    return jnp.concatenate([wide[i:i + 1] + wide[count + i:count + i + 1] for i in range(count)], axis=1)


def lane_blocks(rows):
    return -(-rows // LANES)


def unpack(packed, rows):
    blocks = (packed.shape[0] - SIDE) // rows
    return jnp.concatenate([packed[i * rows:(i + 1) * rows] for i in range(blocks)], axis=1)


def load_kernel(*refs):
    count = len(refs) // 2
    copies = [pltpu.make_async_copy(refs[i], refs[count + i], refs[-1].at[i]) for i in range(count)]
    for copy in copies:
        copy.start()
    for copy in copies:
        copy.wait()


def load(*arrays):
    return pl.pallas_call(
        load_kernel,
        out_shape=tuple(resident(a.shape, a.dtype) for a in arrays),
        in_specs=[pl.BlockSpec(memory_space=pl.ANY)] * len(arrays),
        out_specs=tuple(pl.BlockSpec(memory_space=pltpu.VMEM) for _ in arrays),
        scratch_shapes=[pltpu.SemaphoreType.DMA((len(arrays),))],
        compiler_params=pltpu.CompilerParams(vmem_limit_bytes=1024 * 1024),
        cost_estimate=pl.CostEstimate(flops=0, bytes_accessed=sum(2 * a.size * a.dtype.itemsize for a in arrays), transcendentals=0),
    )(*(pltpu.with_memory_space_constraint(a, pltpu.HBM) for a in arrays))


def place():
    return lax.axis_index("section") % 4, lax.axis_index("dp")


def dot_nt(left, right):
    return lax.dot_general(left, right, (((1,), (1,)), ((), ())), preferred_element_type=F32)


def dot_tn(left, right):
    return lax.dot_general(left, right, (((0,), (0,)), ((), ())), preferred_element_type=F32)


def slot(index, size):
    return pl.ds(pl.multiple_of(index * size, size), size)


def spread_in_part(part, at, gain, weight, mine, total, begin):
    share = part.shape[1]
    piece = weight.shape[1] // 4
    scaled = (part[...].astype(F32) * gain[:, slot(at, share)]).astype(BF16)
    for d in (3, 2, 1, 0):
        block = jnp.dot(scaled, weight[slot(at, share), slot(mine ^ d, piece)], preferred_element_type=F32)
        columns = slice(d * piece, (d + 1) * piece)
        total[:, columns] = block if begin else total[:, columns] + block


def square_sum(part):
    wide = part[...].astype(F32)
    return jnp.sum(wide * wide, axis=1, keepdims=True)


def load_spread_kernel(x1, weight, x0, gain, weight_held, x0_held, gain_held, total, sems):
    mine, lane = place()
    share = x1.shape[1]
    small = [pltpu.make_async_copy(source, held, sems.at[i]) for i, (source, held) in enumerate(((x0, x0_held), (gain, gain_held)))]
    slices = [slot(lane ^ d, share) for d in range(4)]
    large = [pltpu.make_async_copy(weight.at[at], weight_held.at[at], sems.at[2 + d]) for d, at in enumerate(slices)]
    for copy in (*small, *large):
        copy.start()
    for copy in (*small, large[0]):
        copy.wait()
    spread_in_part(x0_held, lane, gain_held, weight_held, mine, total, True)
    large[1].wait()
    spread_in_part(x1, lane ^ 1, gain_held, weight_held, mine, total, False)
    large[2].wait()
    large[3].wait()


def load_spread(x1, weight, x0, gain):
    keep = pl.BlockSpec(memory_space=pltpu.VMEM)
    rows, hidden = x0.shape[0], weight.shape[1]
    outs = [(a.shape, a.dtype) for a in (weight, x0, gain)] + [((rows, hidden), F32)]
    far = [pltpu.with_memory_space_constraint(a, pltpu.HBM) for a in (weight, x0, gain)]
    return pl.pallas_call(
        load_spread_kernel,
        out_shape=tuple(resident(*out) for out in outs),
        in_specs=[keep] + [pl.BlockSpec(memory_space=pl.ANY)] * 3,
        out_specs=(keep,) * 4,
        scratch_shapes=[pltpu.SemaphoreType.DMA((6,))],
        compiler_params=pltpu.CompilerParams(vmem_limit_bytes=8 * 1024 * 1024),
        cost_estimate=pl.CostEstimate(flops=rows * weight.size, bytes_accessed=4 * weight.size, transcendentals=0),
    )(x1, *far)


def spread_in_last_kernel(x0, x1, x2, x3, gain, weight, before, own, s1, s2, s3, x_full, squares):
    mine, lane = place()
    rows, share = x0.shape
    piece = own.shape[1]
    ends = [(slot(lane ^ d, share), part) for d, part in ((2, x2), (3, x3))]
    ends = [(at, (part[...].astype(F32) * gain[:, at]).astype(BF16)) for at, part in ends]
    column = square_sum(x0) + square_sum(x1) + square_sum(x2) + square_sum(x3)
    block = pack_block(as_row(column, lane_blocks(rows) * LANES))
    for d, out in ((1, s1), (2, s2), (3, s3), (0, own)):
        value = before[:, d * piece:(d + 1) * piece]
        for at, scaled in ends:
            value = value + jnp.dot(scaled, weight[at, slot(mine ^ d, piece)], preferred_element_type=F32)
        if d == 0:
            out[...] = value
            continue
        for i in range(piece // LANES):
            out[i * rows:(i + 1) * rows] = value[:, i * LANES:(i + 1) * LANES].astype(BF16)
        out[piece // LANES * rows:] = block
    squares[...] = column
    for d, part in enumerate((x0, x1, x2, x3)):
        x_full[:, slot(lane ^ d, share)] = part[...]


def spread_dy(dy, weight, mine, own, s1, s2, s3):
    piece = own.shape[1]
    for d, out in ((3, s3), (2, s2), (1, s1)):
        out[...] = dot_nt(dy[...], weight[slot(mine ^ d, piece), :]).astype(BF16)
    own[...] = dot_nt(dy[...], weight[slot(mine, piece), :])


def spread_first_kernel(cot, sent, weight, own, s1, s2, s3, dy):
    mine, lane = place()

    @pl.when(lane == mine)
    def _():
        dy[...] = cot[...]

    @pl.when(lane != mine)
    def _():
        dy[...] = sent[...]

    spread_dy(dy, weight, mine, own, s1, s2, s3)


def spread_next_kernel(layers, ds, begin, end, *refs):
    parts, refs = refs[:len(ds)], refs[len(ds):]
    before, weight = refs[:2]
    earlier, refs = (None, refs[2:]) if begin else (refs[2], refs[3:])
    mine, lane = place()
    share = parts[0].shape[1]
    piece = weight.shape[0] // 4
    last = lax.axis_index("section") // 4 == layers - 1
    if end:
        *others, own, s1, s2, s3, dy = refs
        outs = (own, s1, s2, s3)
    else:
        outs = [refs[0].at[:, j * piece:(j + 1) * piece] for j in range(4)]
    slices = [slot(lane ^ d, share) for d in ds]
    values = [jnp.where(last, before[:, at], part[...]) for at, part in zip(slices, parts)]
    for j in (1, 2, 3, 0):
        total = None if begin else earlier[:, j * piece:(j + 1) * piece]
        for at, value in zip(slices, values):
            block = dot_nt(value, weight[slot(mine ^ j, piece), at])
            total = block if total is None else total + block
        outs[j][...] = total.astype(outs[j].dtype)
    if end:
        done = [d for d in range(4) if d not in ds]

        @pl.when(last)
        def _():
            dy[...] = before[...]

        @pl.when(jnp.logical_not(last))
        def _():
            for d, part in zip((*done, *ds), (*others, *parts)):
                dy[:, slot(lane ^ d, share)] = part[...]


def act_kernel(width, own, squares, g1, g2, g3, act, slope, hid, scale):
    rows, piece = act.shape
    count = lane_blocks(rows)
    sums = piece // LANES * rows
    row = pack_row(g1[sums:], count) + pack_row(g2[sums:], count) + pack_row(g3[sums:], count)
    r = lax.rsqrt((squares[...] + as_column(row, rows)) / width + 1e-06)
    scale[...] = r
    for i in range(piece // LANES):
        at = slice(i * LANES, (i + 1) * LANES)
        got = slice(i * rows, (i + 1) * rows)
        a = (own[:, at] + g1[got].astype(F32) + g2[got].astype(F32) + g3[got].astype(F32)) * r
        act[:, at] = a
        square = a * a
        t = jnp.tanh(GELU_IN * (a + GELU_CUBE * (square * a)))
        half = 0.5 * (1.0 + t)
        hid[:, at] = (a * half).astype(BF16)
        slope[:, at] = half + 0.5 * a * (1.0 - t * t) * (GELU_IN * (1.0 + 3.0 * GELU_CUBE * square))


def dact_kernel(own, g1, g2, g3, act, slope, pay):
    rows, piece = own.shape
    dhid = own[...] + g1[...].astype(F32) + g2[...].astype(F32) + g3[...].astype(F32)
    da = (dhid * slope[...]).astype(BF16)
    blocks = piece // LANES
    for i in range(blocks):
        pay[i * rows:(i + 1) * rows] = da[:, i * LANES:(i + 1) * LANES]
    column = jnp.sum(da.astype(F32) * act[...], axis=1, keepdims=True)
    pay[blocks * rows:] = pack_block(as_row(column, lane_blocks(rows) * LANES))


def back_block(d, js, values, earlier, weight, mine, lane):
    share = weight.shape[0] // 4
    total = None if earlier is None else earlier[:, d * share:(d + 1) * share]
    for j, value in zip(js, values):
        block = dot_nt(value, weight[slot(lane ^ d, share), slot(mine ^ j, value.shape[1])])
        total = block if total is None else total + block
    return total


def back_kernel(js, begin, *refs):
    *parts, weight = refs[:len(js) + 1]
    *earlier, total = refs[len(js) + 1:]
    mine, lane = place()
    share = weight.shape[0] // 4
    values = [unpack(part, total.shape[0]) for part in parts]
    for d in range(4):
        total[:, d * share:(d + 1) * share] = back_block(d, js, values, None if begin else earlier[0], weight, mine, lane)


def back_last_kernel(p0, p1, p2, p3, weight, earlier, keep, send):
    mine, lane = place()
    rows = earlier.shape[0]
    share = weight.shape[0] // 4
    sums = p0.shape[0] - SIDE
    values = [unpack(p2, rows), unpack(p1, rows)]
    row = sum(pack_row(part[sums:], lane_blocks(rows)) for part in (p0, p1, p2, p3))
    if row.shape[1] < keep.shape[1]:
        row = jnp.concatenate([row, jnp.zeros((1, keep.shape[1] - row.shape[1]), F32)], axis=1)
    for at, d in ((0, 1), (1, 3)):
        send[:rows, at * share:(at + 1) * share] = back_block(d, (2, 1), values, earlier, weight, mine, lane).astype(BF16)
    send[rows:] = side_block(row)
    for at, d in ((0, 0), (1, 2)):
        keep[:rows, at * share:(at + 1) * share] = back_block(d, (2, 1), values, earlier, weight, mine, lane)
    keep[rows:] = jnp.broadcast_to(row, (SIDE, keep.shape[1]))


def middle_kernel(keep, got, rest, send):
    rows = keep.shape[0] - SIDE
    share = rest.shape[1]
    row = (keep[rows:rows + 1] + side_row(got[rows:]))[:, :share]
    send[:rows] = (keep[:rows, share:] + got[:rows, share:].astype(F32)).astype(BF16)
    send[rows:] = side_block(row)
    rest[:rows] = keep[:rows, :share] + got[:rows, :share].astype(F32)
    rest[rows:] = jnp.broadcast_to(row, (SIDE, share))


def finish_kernel(width, rest, got, x_own, dy, gain, scale, grad_x, *grad_gain):
    _, lane = place()
    rows, share = x_own.shape
    at = slot(lane, share)
    r = scale[...]
    du = rest[:rows] + got[:rows].astype(F32)
    normed = x_own[...].astype(F32) * r
    inner = as_column(rest[rows:rows + 1] + side_row(got[rows:]), rows) / width
    dnorm = du * gain[:, at]
    grad_x[...] = (dy[:, at].astype(F32) + r * (dnorm - normed * inner)).astype(BF16)
    if grad_gain:
        grad_gain[0][...] = jnp.sum(du * normed, axis=0, keepdims=True)


def grad_out_kernel(h0, h1, h2, h3, dy, out, held, sems):
    mine, _ = place()
    piece = h0.shape[1]
    copies = []
    for d, part in enumerate((h0, h1, h2, h3)):
        held[d] = dot_tn(part[...], dy[...]).astype(BF16)
        copies.append(pltpu.make_async_copy(held.at[d], out.at[slot(mine ^ d, piece), :], sems.at[d]))
        copies[-1].start()
    for copy in copies:
        copy.wait()


def grad_in_kernel(p0, p1, p2, p3, x_full, gain, scale, out, scaled, held, sems):
    mine, _ = place()
    rows = x_full.shape[0]
    piece = (p0.shape[0] - SIDE) // rows * LANES
    scaled[...] = (x_full[...].astype(F32) * scale[...] * gain[...]).astype(BF16)
    copies = []
    for d, part in enumerate((p0, p1, p2, p3)):
        held[d] = dot_tn(scaled[...], unpack(part, rows)).astype(BF16)
        copies.append(pltpu.make_async_copy(held.at[d], out.at[:, slot(mine ^ d, piece)], sems.at[d]))
        copies[-1].start()
    for copy in copies:
        copy.wait()


def gradient(body, shape, block, *args, scratch=(), flops=0):
    return pl.pallas_call(
        body,
        out_shape=jax.ShapeDtypeStruct(shape, BF16),
        in_specs=[pl.BlockSpec(memory_space=pltpu.VMEM)] * len(args),
        out_specs=pl.BlockSpec(memory_space=pl.ANY),
        scratch_shapes=[*scratch, pltpu.VMEM((4,) + block, BF16), pltpu.SemaphoreType.DMA((4,))],
        compiler_params=pltpu.CompilerParams(vmem_limit_bytes=16 * 1024 * 1024),
        cost_estimate=pl.CostEstimate(flops=flops, bytes_accessed=2 * shape[0] * shape[1], transcendentals=0),
    )(*args)


def shards_of_four(checkpoints, gain, w_in, w_out, cotangent):
    sections = lax.axis_size("section")
    here = lax.axis_index("section")
    lane = lax.axis_index("dp")
    layers = sections // 4
    mine = here % 4
    _, micro, tok, share = checkpoints.shape
    rows = micro * tok
    quarter = share * 4
    width = 4 * quarter
    hidden = w_in.shape[2]
    piece = hidden // 4
    work = 2 * rows * quarter * hidden

    x0 = checkpoints[0].reshape(rows, share)
    cot = cotangent.reshape(rows, quarter)
    top = [s * 4 + d for s in range(sections) for d in range(4) if s // 4 == layers - 1]
    x2 = flip(x0, "dp", 2)
    x1 = flip(x0, "dp", 1)
    weight_in, x0, gain, begun = load_spread(x1, w_in[0], x0, gain)
    x2, weight_in = lax.optimization_barrier((x2, weight_in))
    sent = lax.ppermute(cot, ("section", "dp"), [((i // 4 ^ near) * 4 + i // 4 % 4, i) for i in top for near in (1, 0, 2) if i // 4 % 4 ^ i % 4 == (2, 1, 3)[near]])
    x3 = flip(x2, "dp", 1)

    packed = packed_shape(rows, piece)
    own, s1, s2, s3, x_full, squares = local(
        spread_in_last_kernel,
        [resident((rows, piece), F32)] + [resident(packed, BF16)] * 3
        + [resident((rows, quarter), BF16), resident((rows, 1), F32)],
        x0, x1, x2, x3, gain, weight_in, begun,
        flops=work,
    )
    s1, s2, s3, cot, w_out = lax.optimization_barrier((s1, s2, s3, cot, w_out))
    g3 = flip(s3, "section", 3)
    g2 = flip(s2, "section", 2)
    g1 = flip(s1, "section", 1)
    weight_out, cot = load(w_out[0], cot)
    act, slope, hid, scale = local(
        functools.partial(act_kernel, width),
        [resident((rows, piece), F32), resident((rows, piece), F32), resident((rows, piece), BF16), resident((rows, 1), F32)],
        own, squares, g1, g2, g3,
    )

    spread_outs = [resident((rows, piece), F32)] + [resident((rows, piece), BF16)] * 3 + [resident((rows, quarter), BF16)]

    def gather_hidden(block):
        return [block] + [flip(block, "section", j) for j in (1, 2, 3)]

    if layers == 1:
        hids = gather_hidden(hid)
    for phase in range(layers):
        final = phase == layers - 1
        if phase == 0:
            own, s1, s2, s3, dy = local(spread_first_kernel, spread_outs, cot, sent, weight_out, flops=work)
        else:
            d0, d1, d2 = down
            first, hids = lax.optimization_barrier((d0, hids))
            total = [resident((rows, hidden), F32)]
            step = functools.partial(spread_next_kernel, layers)
            begun = local(functools.partial(step, (0,), True, False), total, first, dy, weight_out, flops=work // 4)
            d2, begun = lax.optimization_barrier((d2, begun))
            d3 = flip(d2, "dp", 1)
            begun = local(functools.partial(step, (1, 2), False, False), total, d1, d2, dy, weight_out, *begun, flops=work // 2)
            own, s1, s2, s3, dy = local(
                functools.partial(step, (3,), False, True), spread_outs, d3, dy, weight_out, *begun, d0, d1, d2,
                flops=work // 4,
            )
        g3 = flip(s3, "section", 3)
        g2 = flip(s2, "section", 2)
        g1 = flip(s1, "section", 1)
        if final:
            grad_out = gradient(grad_out_kernel, (hidden, quarter), (piece, quarter), *hids, dy, flops=work)
            own, grad_out = lax.optimization_barrier((own, grad_out))
        (pay,) = local(dact_kernel, [resident(packed, BF16)], own, g1, g2, g3, act, slope)
        p3 = flip(pay, "section", 3)
        p2 = flip(pay, "section", 2)
        p1 = flip(pay, "section", 1)
        total = [resident((rows, quarter), F32)]
        begun = local(functools.partial(back_kernel, (0,), True), total, pay, weight_in, flops=work // 4)
        begun = local(functools.partial(back_kernel, (3,), False), total, p3, weight_in, *begun, flops=work // 4)
        keep, send = local(
            back_last_kernel,
            [resident((rows + SIDE, 2 * share), F32), resident((rows + SIDE, 2 * share), BF16)],
            pay, p1, p2, p3, weight_in, *begun,
            flops=work // 2,
        )
        got = flip(send, "dp", 1)
        rest, send = local(
            middle_kernel,
            [resident((rows + SIDE, share), F32), resident((rows + SIDE, share), BF16)],
            keep, got,
        )
        if phase == 0 and not final:
            send, hid = lax.optimization_barrier((send, hid))
            hids = gather_hidden(hid)
        got = flip(send, "dp", 2)
        if final:
            grad_in = gradient(
                grad_in_kernel, (quarter, hidden), (quarter, piece), pay, p1, p2, p3, x_full, gain, scale,
                scratch=[pltpu.VMEM((rows, quarter), BF16)], flops=work,
            )
            got, grad_in = lax.optimization_barrier((got, grad_in))
        outs = [resident((rows, share), BF16)]
        if final:
            outs = [jax.ShapeDtypeStruct((rows, share), BF16), jax.ShapeDtypeStruct((1, share), F32)]
        finished = local(functools.partial(finish_kernel, width), outs, rest, got, x0, dy, gain, scale)
        if not final:
            d0 = lax.ppermute(finished[0], "section", [(i, i - 4) for i in range(4, sections)])
            d2 = flip(d0, "dp", 2)
            d1 = flip(d0, "dp", 1)
            down = (d0, d1, d2)

    grad_x, grad_gain = finished
    return grad_in[None], grad_out[None], grad_gain, grad_x.reshape(1, micro, tok, share)


def shards(checkpoints, gain, w_in, w_out, cotangent):
    rows = checkpoints.shape[1] * checkpoints.shape[2]
    share = checkpoints.shape[3]
    piece = w_in.shape[2] // 4
    if lax.axis_size("dp") == 4 and rows % 16 == 0 and share % 128 == 0 and piece % 128 == 0 and rows <= min(share, piece):
        return shards_of_four(checkpoints, gain, w_in, w_out, cotangent)
    return shards_of_any(checkpoints, gain, w_in, w_out, cotangent)


def solution(mesh):
    in_specs = (
        P("section", None, None, "dp"),
        P("section", None),
        P("section", None, "dp"),
        P("section", "dp", None),
        P(None, None, "dp"),
    )
    out_specs = (
        P("section", None, "dp"),
        P("section", "dp", None),
        P("section", "dp"),
        P("section", None, None, "dp"),
    )
    return jax.shard_map(shards, mesh=mesh, in_specs=in_specs, out_specs=out_specs, check_vma=False)
```

```python
import functools

import jax
import jax.numpy as jnp
from jax import lax
from jax.experimental import pallas as pl
from jax.experimental.pallas import tpu as pltpu
from jax.sharding import PartitionSpec as P

F32 = jnp.float32
BF16 = jnp.bfloat16


def flip(block, axis, bits):
    count = lax.axis_size(axis)
    return lax.ppermute(block, axis, [(i, i ^ bits) for i in range(count)])


def side_rows(values, width):
    lead = values.astype(BF16)
    trail = (values - lead.astype(F32)).astype(BF16)
    flat = jnp.concatenate([lead, trail])
    return jnp.pad(flat, (0, 16 * width - flat.shape[0])).reshape(16, width)


def side_values(rows, count):
    flat = rows.reshape(-1)
    return flat[:count].astype(F32) + flat[count:2 * count].astype(F32)


def gelu_tanh(value):
    return jax.nn.gelu(value, approximate=True)


def shards_of_any(checkpoints, gain, w_in, w_out, cotangent):
    sections = lax.axis_size("section")
    n_dp = lax.axis_size("dp")
    here = lax.axis_index("section")
    lane = lax.axis_index("dp")
    layers = sections // 4
    mine = here % 4
    last = here // 4 == layers - 1
    _, micro, tok, share = checkpoints.shape
    rows = micro * tok
    quarter = share * n_dp
    width = 4 * quarter
    gain_row = gain[0]
    weight_in = w_in[0]
    weight_out = w_out[0]
    hidden = weight_in.shape[1]
    piece = hidden // 4
    core = lane % 2

    def gather_dp(block):
        bit = n_dp // 2
        parts = {0: block}
        while bit >= 1:
            other = flip(jnp.concatenate([parts[j] for j in parts], axis=1), "dp", bit)
            for at, j in enumerate(list(parts)):
                parts[j ^ bit] = other[:, at * block.shape[1]:(at + 1) * block.shape[1]]
            bit //= 2
        full = jnp.zeros((rows, quarter), block.dtype)
        for j, part in parts.items():
            full = lax.dynamic_update_slice(full, part, (0, (lane ^ j) * block.shape[1]))
        return full

    def cot_quarter(block):
        if n_dp < 4:
            whole = lax.all_gather(block, "dp", axis=1, tiled=True)
            return lax.dynamic_slice_in_dim(whole, mine * quarter, quarter, 1)
        per = n_dp // 4
        top = [s * n_dp + d for s in range(sections) for d in range(n_dp) if s // 4 == layers - 1]
        held = block
        far = lambda i, b: (i % n_dp // per ^ i // n_dp % 4) & b
        got = lax.ppermute(held, ("section", "dp"), [(i, i ^ 2 * per) for i in top if far(i, 3) == 0])
        held = jnp.where((lane // per ^ mine) & 2 == 0, held, got)
        got = lax.ppermute(held, ("section", "dp"), [(i, i ^ per) for i in top if far(i, 1) == 0])
        held = jnp.where((lane // per ^ mine) & 1 == 0, held, got)
        if per == 1:
            return held
        parts = {0: held}
        bit = per // 2
        while bit >= 1:
            for j in list(parts):
                parts[j ^ bit] = flip(parts[j], "dp", bit)
            bit //= 2
        full = jnp.zeros((rows, quarter), block.dtype)
        for j, part in parts.items():
            full = lax.dynamic_update_slice(full, part, (0, (lane % per ^ j) * block.shape[1]))
        return full

    def cut(values, j):
        return lax.dynamic_slice_in_dim(values, (mine ^ j) * piece, piece, 1)

    def fill(parts):
        full = jnp.zeros((rows, hidden), parts[0].dtype)
        for j, part in enumerate(parts):
            full = lax.dynamic_update_slice(full, part, (0, (mine ^ j) * piece))
        return full

    x_full = gather_dp(checkpoints[0].reshape(rows, share))
    cot = cot_quarter(cotangent.reshape(rows, cotangent.shape[2]))
    x_wide = x_full.astype(F32)
    scaled_raw = (x_wide * gain_row).astype(BF16)
    squares = jnp.sum(x_wide * x_wide, axis=1)

    act_raw = jnp.dot(scaled_raw, weight_in, preferred_element_type=F32)
    extra = side_rows(squares, piece)
    act = cut(act_raw, 0)
    for j in (3, 1, 2):
        got = flip(jnp.concatenate([cut(act_raw, j).astype(BF16), extra], axis=0), "section", j)
        act = act + got[:rows].astype(F32)
        squares = squares + side_values(got[rows:], rows)
    scale = lax.rsqrt(squares / width + 1e-06)[:, None]
    act = act * scale
    hid, pull = jax.vjp(gelu_tanh, act)
    hid = hid.astype(BF16)
    hid_full = fill([hid] + [flip(hid, "section", j) for j in (1, 2, 3)])
    normed = x_wide * scale
    scaled = (normed * gain_row).astype(BF16)

    def halves(values, side):
        pairs = values.reshape(rows, n_dp // 2, 2, share)
        return jnp.where(side == 0, pairs[:, :, 0], pairs[:, :, 1]).reshape(rows, quarter // 2)

    def own(values):
        return lax.dynamic_slice_in_dim(values, lane // 2 * share, share, 1)

    incoming = jnp.zeros((rows, quarter), BF16)
    normed_half = halves(normed, core)
    gain_half = halves(jnp.broadcast_to(gain_row, (rows, quarter)), core)
    for phase in range(layers):
        final = phase == layers - 1
        dy = jnp.where(last, cot, incoming) if phase > 0 else cot
        dhid_raw = jnp.dot(dy, weight_out.T, preferred_element_type=F32)
        dhid = cut(dhid_raw, 0)
        for j in (3, 1, 2):
            dhid = dhid + flip(cut(dhid_raw, j).astype(BF16), "section", j).astype(F32)
        dact = pull(dhid)[0].astype(BF16)
        inner = jnp.sum(dact.astype(F32) * act, axis=1)
        payload = jnp.concatenate([dact, side_rows(inner, piece)], axis=0)
        others = [flip(payload, "section", j) for j in (1, 2, 3)]
        for got in others:
            inner = inner + side_values(got[rows:], rows)
        dact_full = fill([dact] + [got[:rows] for got in others])
        part = jnp.dot(dact_full, weight_in.T, preferred_element_type=F32).astype(BF16)

        send = jnp.concatenate([halves(part, 1 - core), side_rows(inner, quarter // 2)], axis=0)
        got = flip(send, "dp", 1)
        dscaled = halves(part, core).astype(F32) + got[:rows].astype(F32)
        inner = inner + side_values(got[rows:], rows)
        bit = 2
        while bit < n_dp:
            send = jnp.concatenate([dscaled.astype(BF16), side_rows(inner, quarter // 2)], axis=0)
            got = flip(send, "dp", bit)
            dscaled = dscaled + got[:rows].astype(F32)
            inner = inner + side_values(got[rows:], rows)
            bit *= 2
        dnorm = dscaled * gain_half
        dy_half = halves(dy, core).astype(F32)
        grad_x = (dy_half + scale * (dnorm - normed_half * (inner / width)[:, None])).astype(BF16)
        if not final:
            down = lax.ppermute(grad_x, "section", [(i, i - 4) for i in range(4, sections)])
            other = flip(down, "dp", 1)
            pairs = jnp.where(
                core == 0,
                jnp.stack([down.reshape(rows, n_dp // 2, share), other.reshape(rows, n_dp // 2, share)], axis=2),
                jnp.stack([other.reshape(rows, n_dp // 2, share), down.reshape(rows, n_dp // 2, share)], axis=2),
            )
            incoming = pairs.reshape(rows, quarter)

    grad_out = jnp.dot(hid_full.T, dy, preferred_element_type=F32).astype(BF16)
    grad_in = jnp.dot(scaled.T, dact_full, preferred_element_type=F32).astype(BF16)
    grad_gain = jnp.sum(own(dscaled) * own(normed_half), axis=0)
    return (
        grad_in[None],
        grad_out[None],
        grad_gain[None],
        own(grad_x).reshape(1, micro, tok, share),
    )


SIDE = 16
LANES = 128
GELU_IN = 0.7978845608028654
GELU_CUBE = 0.044715


def resident(shape, dtype):
    return pltpu.VMEM(shape, dtype)


def local(body, outs, *args, scratch=(), flops=0):
    spec = pl.BlockSpec(memory_space=pltpu.VMEM)
    moved = sum(a.size * a.dtype.itemsize for a in args)
    return pl.pallas_call(
        body,
        out_shape=tuple(outs),
        in_specs=[spec] * len(args),
        out_specs=tuple(spec for _ in outs),
        scratch_shapes=list(scratch),
        compiler_params=pltpu.CompilerParams(vmem_limit_bytes=16 * 1024 * 1024),
        cost_estimate=pl.CostEstimate(flops=flops, bytes_accessed=moved, transcendentals=0),
    )(*args)


def diagonal(rows, width):
    return lax.broadcasted_iota(jnp.int32, (rows, width), 0) == lax.broadcasted_iota(jnp.int32, (rows, width), 1)


def as_row(column, width):
    rows = column.shape[0]
    return jnp.sum(jnp.where(diagonal(rows, width), column, 0.0), axis=0, keepdims=True)


def as_column(row, rows):
    return jnp.sum(jnp.where(diagonal(rows, row.shape[1]), row, 0.0), axis=1, keepdims=True)


def side_block(row):
    lead = row.astype(BF16).astype(F32)
    at = lax.broadcasted_iota(jnp.int32, (SIDE, row.shape[1]), 0)
    return jnp.where(at == 0, lead, jnp.where(at == 1, row - lead, 0.0)).astype(BF16)


def side_row(block):
    wide = block.astype(F32)
    return wide[0:1] + wide[1:2]


def packed_shape(rows, piece):
    return (piece // LANES * rows + SIDE, LANES)


def pack_block(row):
    lead = row.astype(BF16).astype(F32)
    count = row.shape[1] // LANES
    at = lax.broadcasted_iota(jnp.int32, (SIDE, LANES), 0)
    block = jnp.zeros((SIDE, LANES), F32)
    for i in range(count):
        lanes = slice(i * LANES, (i + 1) * LANES)
        block = jnp.where(at == i, lead[:, lanes], jnp.where(at == count + i, (row - lead)[:, lanes], block))
    return block.astype(BF16)


def pack_row(block, count):
    wide = block.astype(F32)
    return jnp.concatenate([wide[i:i + 1] + wide[count + i:count + i + 1] for i in range(count)], axis=1)


def lane_blocks(rows):
    return -(-rows // LANES)


def unpack(packed, rows):
    blocks = (packed.shape[0] - SIDE) // rows
    return jnp.concatenate([packed[i * rows:(i + 1) * rows] for i in range(blocks)], axis=1)


def place():
    return lax.axis_index("section") % 4, lax.axis_index("dp")


def dot_nt(left, right):
    return lax.dot_general(left, right, (((1,), (1,)), ((), ())), preferred_element_type=F32)


def dot_tn(left, right):
    return lax.dot_general(left, right, (((0,), (0,)), ((), ())), preferred_element_type=F32)


def slot(index, size):
    return pl.ds(pl.multiple_of(index * size, size), size)


def spread_in_part(part, at, gain, weight, mine, total, begin):
    share = part.shape[1]
    piece = weight.shape[1] // 4
    scaled = (part[...].astype(F32) * gain[:, slot(at, share)]).astype(BF16)
    for d in (3, 2, 1, 0):
        block = jnp.dot(scaled, weight[slot(at, share), slot(mine ^ d, piece)], preferred_element_type=F32)
        columns = slice(d * piece, (d + 1) * piece)
        total[:, columns] = block if begin else total[:, columns] + block


def square_sum(part):
    wide = part[...].astype(F32)
    return jnp.sum(wide * wide, axis=1, keepdims=True)


def load_spread_kernel(x1, weight, x0, gain, weight_held, x0_held, gain_held, total, sems):
    mine, lane = place()
    share = x1.shape[1]
    small = [pltpu.make_async_copy(source, held, sems.at[i]) for i, (source, held) in enumerate(((x0, x0_held), (gain, gain_held)))]
    slices = [slot(lane ^ d, share) for d in range(4)]
    large = [pltpu.make_async_copy(weight.at[at], weight_held.at[at], sems.at[2 + d]) for d, at in enumerate(slices)]
    for copy in (*small, *large):
        copy.start()
    for copy in (*small, large[0]):
        copy.wait()
    spread_in_part(x0_held, lane, gain_held, weight_held, mine, total, True)
    large[1].wait()
    spread_in_part(x1, lane ^ 1, gain_held, weight_held, mine, total, False)
    large[2].wait()
    large[3].wait()


def load_spread(x1, weight, x0, gain):
    keep = pl.BlockSpec(memory_space=pltpu.VMEM)
    rows, hidden = x0.shape[0], weight.shape[1]
    outs = [(a.shape, a.dtype) for a in (weight, x0, gain)] + [((rows, hidden), F32)]
    far = [pltpu.with_memory_space_constraint(a, pltpu.HBM) for a in (weight, x0, gain)]
    return pl.pallas_call(
        load_spread_kernel,
        out_shape=tuple(resident(*out) for out in outs),
        in_specs=[keep] + [pl.BlockSpec(memory_space=pl.ANY)] * 3,
        out_specs=(keep,) * 4,
        scratch_shapes=[pltpu.SemaphoreType.DMA((6,))],
        compiler_params=pltpu.CompilerParams(vmem_limit_bytes=8 * 1024 * 1024),
        cost_estimate=pl.CostEstimate(flops=rows * weight.size, bytes_accessed=4 * weight.size, transcendentals=0),
    )(x1, *far)


def spread_in_last_kernel(x0, x1, x2, x3, gain, weight, before, own, s1, s2, s3, x_full, squares):
    mine, lane = place()
    rows, share = x0.shape
    piece = own.shape[1]
    ends = [(slot(lane ^ d, share), part) for d, part in ((2, x2), (3, x3))]
    ends = [(at, (part[...].astype(F32) * gain[:, at]).astype(BF16)) for at, part in ends]
    column = square_sum(x0) + square_sum(x1) + square_sum(x2) + square_sum(x3)
    block = pack_block(as_row(column, lane_blocks(rows) * LANES))
    for d, out in ((1, s1), (2, s2), (3, s3), (0, own)):
        value = before[:, d * piece:(d + 1) * piece]
        for at, scaled in ends:
            value = value + jnp.dot(scaled, weight[at, slot(mine ^ d, piece)], preferred_element_type=F32)
        if d == 0:
            out[...] = value
            continue
        for i in range(piece // LANES):
            out[i * rows:(i + 1) * rows] = value[:, i * LANES:(i + 1) * LANES].astype(BF16)
        out[piece // LANES * rows:] = block
    squares[...] = column
    for d, part in enumerate((x0, x1, x2, x3)):
        x_full[:, slot(lane ^ d, share)] = part[...]


def load_first_kernel(sent, cot, weight, held, own, s1, s2, s3, dy, sems):
    mine, lane = place()
    piece = own.shape[1]
    slices = [slot(mine ^ d, piece) for d in (1, 2, 3, 0)]
    copies = [pltpu.make_async_copy(cot, dy, sems.at[4])]
    copies += [pltpu.make_async_copy(weight.at[at], held.at[at], sems.at[i]) for i, at in enumerate(slices)]
    for copy in copies:
        copy.start()
    copies[0].wait()

    @pl.when(lane != mine)
    def _():
        dy[...] = sent[...]

    for copy, at, out in zip(copies[1:], slices, (s1, s2, s3, own)):
        copy.wait()
        out[...] = dot_nt(dy[...], held[at, :]).astype(out.dtype)


def load_first(outs, sent, cot, weight):
    keep = pl.BlockSpec(memory_space=pltpu.VMEM)
    outs = [resident(weight.shape, weight.dtype), *outs]
    far = [pltpu.with_memory_space_constraint(a, pltpu.HBM) for a in (cot, weight)]
    return pl.pallas_call(
        load_first_kernel,
        out_shape=tuple(outs),
        in_specs=[keep] + [pl.BlockSpec(memory_space=pl.ANY)] * 2,
        out_specs=(keep,) * len(outs),
        scratch_shapes=[pltpu.SemaphoreType.DMA((5,))],
        compiler_params=pltpu.CompilerParams(vmem_limit_bytes=8 * 1024 * 1024),
        cost_estimate=pl.CostEstimate(flops=2 * cot.shape[0] * weight.size, bytes_accessed=4 * weight.size, transcendentals=0),
    )(sent, *far)


def spread_next_kernel(layers, ds, begin, end, *refs):
    parts, refs = refs[:len(ds)], refs[len(ds):]
    before, weight = refs[:2]
    earlier, refs = (None, refs[2:]) if begin else (refs[2], refs[3:])
    mine, lane = place()
    share = parts[0].shape[1]
    piece = weight.shape[0] // 4
    last = lax.axis_index("section") // 4 == layers - 1
    if end:
        *others, own, s1, s2, s3, dy = refs
        outs = (own, s1, s2, s3)
    else:
        outs = [refs[0].at[:, j * piece:(j + 1) * piece] for j in range(4)]
    slices = [slot(lane ^ d, share) for d in ds]
    values = [jnp.where(last, before[:, at], part[...]) for at, part in zip(slices, parts)]
    for j in (1, 2, 3, 0):
        total = None if begin else earlier[:, j * piece:(j + 1) * piece]
        for at, value in zip(slices, values):
            block = dot_nt(value, weight[slot(mine ^ j, piece), at])
            total = block if total is None else total + block
        outs[j][...] = total.astype(outs[j].dtype)
    if end:
        done = [d for d in range(4) if d not in ds]

        @pl.when(last)
        def _():
            dy[...] = before[...]

        @pl.when(jnp.logical_not(last))
        def _():
            for d, part in zip((*done, *ds), (*others, *parts)):
                dy[:, slot(lane ^ d, share)] = part[...]


def act_kernel(width, own, squares, g1, g2, g3, act, slope, hid, scale):
    rows, piece = act.shape
    count = lane_blocks(rows)
    sums = piece // LANES * rows
    row = pack_row(g1[sums:], count) + pack_row(g2[sums:], count) + pack_row(g3[sums:], count)
    r = lax.rsqrt((squares[...] + as_column(row, rows)) / width + 1e-06)
    scale[...] = r
    for i in range(piece // LANES):
        at = slice(i * LANES, (i + 1) * LANES)
        got = slice(i * rows, (i + 1) * rows)
        a = (own[:, at] + g1[got].astype(F32) + g2[got].astype(F32) + g3[got].astype(F32)) * r
        act[:, at] = a
        square = a * a
        t = jnp.tanh(GELU_IN * (a + GELU_CUBE * (square * a)))
        half = 0.5 * (1.0 + t)
        hid[:, at] = (a * half).astype(BF16)
        slope[:, at] = half + 0.5 * a * (1.0 - t * t) * (GELU_IN * (1.0 + 3.0 * GELU_CUBE * square))


def dact_kernel(own, g1, g2, g3, act, slope, pay):
    rows, piece = own.shape
    dhid = own[...] + g1[...].astype(F32) + g2[...].astype(F32) + g3[...].astype(F32)
    da = (dhid * slope[...]).astype(BF16)
    blocks = piece // LANES
    for i in range(blocks):
        pay[i * rows:(i + 1) * rows] = da[:, i * LANES:(i + 1) * LANES]
    column = jnp.sum(da.astype(F32) * act[...], axis=1, keepdims=True)
    pay[blocks * rows:] = pack_block(as_row(column, lane_blocks(rows) * LANES))


def back_block(d, js, values, earlier, weight, mine, lane):
    share = weight.shape[0] // 4
    total = None if earlier is None else earlier[:, d * share:(d + 1) * share]
    for j, value in zip(js, values):
        block = dot_nt(value, weight[slot(lane ^ d, share), slot(mine ^ j, value.shape[1])])
        total = block if total is None else total + block
    return total


def back_kernel(js, begin, *refs):
    *parts, weight = refs[:len(js) + 1]
    *earlier, total = refs[len(js) + 1:]
    mine, lane = place()
    share = weight.shape[0] // 4
    values = [unpack(part, total.shape[0]) for part in parts]
    for d in range(4):
        total[:, d * share:(d + 1) * share] = back_block(d, js, values, None if begin else earlier[0], weight, mine, lane)


def back_last_kernel(p0, p1, p2, p3, weight, earlier, keep, send):
    mine, lane = place()
    rows = earlier.shape[0]
    share = weight.shape[0] // 4
    sums = p0.shape[0] - SIDE
    values = [unpack(p2, rows), unpack(p1, rows)]
    row = sum(pack_row(part[sums:], lane_blocks(rows)) for part in (p0, p1, p2, p3))
    if row.shape[1] < keep.shape[1]:
        row = jnp.concatenate([row, jnp.zeros((1, keep.shape[1] - row.shape[1]), F32)], axis=1)
    for at, d in ((0, 1), (1, 3)):
        send[:rows, at * share:(at + 1) * share] = back_block(d, (2, 1), values, earlier, weight, mine, lane).astype(BF16)
    send[rows:] = side_block(row)
    for at, d in ((0, 0), (1, 2)):
        keep[:rows, at * share:(at + 1) * share] = back_block(d, (2, 1), values, earlier, weight, mine, lane)
    keep[rows:] = jnp.broadcast_to(row, (SIDE, keep.shape[1]))


def middle_kernel(keep, got, rest, send):
    rows = keep.shape[0] - SIDE
    share = rest.shape[1]
    row = (keep[rows:rows + 1] + side_row(got[rows:]))[:, :share]
    send[:rows] = (keep[:rows, share:] + got[:rows, share:].astype(F32)).astype(BF16)
    send[rows:] = side_block(row)
    rest[:rows] = keep[:rows, :share] + got[:rows, :share].astype(F32)
    rest[rows:] = jnp.broadcast_to(row, (SIDE, share))


def finish_kernel(width, rest, got, x_own, dy, gain, scale, grad_x, *grad_gain):
    _, lane = place()
    rows, share = x_own.shape
    at = slot(lane, share)
    r = scale[...]
    du = rest[:rows] + got[:rows].astype(F32)
    normed = x_own[...].astype(F32) * r
    inner = as_column(rest[rows:rows + 1] + side_row(got[rows:]), rows) / width
    dnorm = du * gain[:, at]
    grad_x[...] = (dy[:, at].astype(F32) + r * (dnorm - normed * inner)).astype(BF16)
    if grad_gain:
        grad_gain[0][...] = jnp.sum(du * normed, axis=0, keepdims=True)


def grad_out_kernel(h0, h1, h2, h3, dy, out, held, sems):
    mine, _ = place()
    piece = h0.shape[1]
    copies = []
    for d, part in enumerate((h0, h1, h2, h3)):
        held[d] = dot_tn(part[...], dy[...]).astype(BF16)
        copies.append(pltpu.make_async_copy(held.at[d], out.at[slot(mine ^ d, piece), :], sems.at[d]))
        copies[-1].start()
    for copy in copies:
        copy.wait()


def grad_in_kernel(p0, p1, p2, p3, x_full, gain, scale, out, scaled, held, sems):
    mine, _ = place()
    rows = x_full.shape[0]
    piece = (p0.shape[0] - SIDE) // rows * LANES
    scaled[...] = (x_full[...].astype(F32) * scale[...] * gain[...]).astype(BF16)
    copies = []
    for d, part in enumerate((p0, p1, p2, p3)):
        held[d] = dot_tn(scaled[...], unpack(part, rows)).astype(BF16)
        copies.append(pltpu.make_async_copy(held.at[d], out.at[:, slot(mine ^ d, piece)], sems.at[d]))
        copies[-1].start()
    for copy in copies:
        copy.wait()


def gradient(body, shape, block, *args, scratch=(), flops=0):
    return pl.pallas_call(
        body,
        out_shape=jax.ShapeDtypeStruct(shape, BF16),
        in_specs=[pl.BlockSpec(memory_space=pltpu.VMEM)] * len(args),
        out_specs=pl.BlockSpec(memory_space=pl.ANY),
        scratch_shapes=[*scratch, pltpu.VMEM((4,) + block, BF16), pltpu.SemaphoreType.DMA((4,))],
        compiler_params=pltpu.CompilerParams(vmem_limit_bytes=16 * 1024 * 1024),
        cost_estimate=pl.CostEstimate(flops=flops, bytes_accessed=2 * shape[0] * shape[1], transcendentals=0),
    )(*args)


def shards_of_four(checkpoints, gain, w_in, w_out, cotangent):
    sections = lax.axis_size("section")
    here = lax.axis_index("section")
    lane = lax.axis_index("dp")
    layers = sections // 4
    mine = here % 4
    _, micro, tok, share = checkpoints.shape
    rows = micro * tok
    quarter = share * 4
    width = 4 * quarter
    hidden = w_in.shape[2]
    piece = hidden // 4
    work = 2 * rows * quarter * hidden

    x0 = checkpoints[0].reshape(rows, share)
    cot = cotangent.reshape(rows, quarter)
    top = [s * 4 + d for s in range(sections) for d in range(4) if s // 4 == layers - 1]
    x2 = flip(x0, "dp", 2)
    x1 = flip(x0, "dp", 1)
    weight_in, x0, gain, begun = load_spread(x1, w_in[0], x0, gain)
    x2, weight_in = lax.optimization_barrier((x2, weight_in))
    sent = lax.ppermute(cot, ("section", "dp"), [((i // 4 ^ near) * 4 + i // 4 % 4, i) for i in top for near in (1, 0, 2) if i // 4 % 4 ^ i % 4 == (2, 1, 3)[near]])
    x3 = flip(x2, "dp", 1)

    packed = packed_shape(rows, piece)
    own, s1, s2, s3, x_full, squares = local(
        spread_in_last_kernel,
        [resident((rows, piece), F32)] + [resident(packed, BF16)] * 3
        + [resident((rows, quarter), BF16), resident((rows, 1), F32)],
        x0, x1, x2, x3, gain, weight_in, begun,
        flops=work,
    )
    s1, s2, s3, cot, w_out = lax.optimization_barrier((s1, s2, s3, cot, w_out))
    g3 = flip(s3, "section", 3)
    g2 = flip(s2, "section", 2)
    g1 = flip(s1, "section", 1)
    act, slope, hid, scale = local(
        functools.partial(act_kernel, width),
        [resident((rows, piece), F32), resident((rows, piece), F32), resident((rows, piece), BF16), resident((rows, 1), F32)],
        own, squares, g1, g2, g3,
    )

    spread_outs = [resident((rows, piece), F32)] + [resident((rows, piece), BF16)] * 3 + [resident((rows, quarter), BF16)]

    def gather_hidden(block):
        return [block] + [flip(block, "section", j) for j in (1, 2, 3)]

    if layers == 1:
        hids = gather_hidden(hid)
    for phase in range(layers):
        final = phase == layers - 1
        if phase == 0:
            weight_out, own, s1, s2, s3, dy = load_first(spread_outs, sent, cot, w_out[0])
        else:
            d0, d1, d2, d3 = down
            first, hids = lax.optimization_barrier((d0, hids))
            total = [resident((rows, hidden), F32)]
            step = functools.partial(spread_next_kernel, layers)
            begun = local(functools.partial(step, (0,), True, False), total, first, dy, weight_out, flops=work // 4)
            begun = local(functools.partial(step, (1, 2), False, False), total, d1, d2, dy, weight_out, *begun, flops=work // 2)
            own, s1, s2, s3, dy = local(
                functools.partial(step, (3,), False, True), spread_outs, d3, dy, weight_out, *begun, d0, d1, d2,
                flops=work // 4,
            )
        g3 = flip(s3, "section", 3)
        g2 = flip(s2, "section", 2)
        g1 = flip(s1, "section", 1)
        if final:
            grad_out = gradient(grad_out_kernel, (hidden, quarter), (piece, quarter), *hids, dy, flops=work)
            own, grad_out = lax.optimization_barrier((own, grad_out))
        (pay,) = local(dact_kernel, [resident(packed, BF16)], own, g1, g2, g3, act, slope)
        p3 = flip(pay, "section", 3)
        p2 = flip(pay, "section", 2)
        p1 = flip(pay, "section", 1)
        total = [resident((rows, quarter), F32)]
        begun = local(functools.partial(back_kernel, (0,), True), total, pay, weight_in, flops=work // 4)
        begun = local(functools.partial(back_kernel, (3,), False), total, p3, weight_in, *begun, flops=work // 4)
        keep, send = local(
            back_last_kernel,
            [resident((rows + SIDE, 2 * share), F32), resident((rows + SIDE, 2 * share), BF16)],
            pay, p1, p2, p3, weight_in, *begun,
            flops=work // 2,
        )
        got = flip(send, "dp", 1)
        rest, send = local(
            middle_kernel,
            [resident((rows + SIDE, share), F32), resident((rows + SIDE, share), BF16)],
            keep, got,
        )
        if phase == 0 and not final:
            send, hid = lax.optimization_barrier((send, hid))
            hids = gather_hidden(hid)
        got = flip(send, "dp", 2)
        if final:
            grad_in = gradient(
                grad_in_kernel, (quarter, hidden), (quarter, piece), pay, p1, p2, p3, x_full, gain, scale,
                scratch=[pltpu.VMEM((rows, quarter), BF16)], flops=work,
            )
            got, grad_in = lax.optimization_barrier((got, grad_in))
        outs = [resident((rows, share), BF16)]
        if final:
            outs = [jax.ShapeDtypeStruct((rows, share), BF16), jax.ShapeDtypeStruct((1, share), F32)]
        finished = local(functools.partial(finish_kernel, width), outs, rest, got, x0, dy, gain, scale)
        if not final:
            d0 = lax.ppermute(finished[0], "section", [(i, i - 4) for i in range(4, sections)])
            d2 = flip(d0, "dp", 2)
            d1 = flip(d0, "dp", 1)
            d3 = flip(d2, "dp", 1)
            down = (d0, d1, d2, d3)

    grad_x, grad_gain = finished
    return grad_in[None], grad_out[None], grad_gain, grad_x.reshape(1, micro, tok, share)


def shards(checkpoints, gain, w_in, w_out, cotangent):
    rows = checkpoints.shape[1] * checkpoints.shape[2]
    share = checkpoints.shape[3]
    piece = w_in.shape[2] // 4
    if lax.axis_size("dp") == 4 and rows % 16 == 0 and share % 128 == 0 and piece % 128 == 0 and rows <= min(share, piece):
        return shards_of_four(checkpoints, gain, w_in, w_out, cotangent)
    return shards_of_any(checkpoints, gain, w_in, w_out, cotangent)


def solution(mesh):
    in_specs = (
        P("section", None, None, "dp"),
        P("section", None),
        P("section", None, "dp"),
        P("section", "dp", None),
        P(None, None, "dp"),
    )
    out_specs = (
        P("section", None, "dp"),
        P("section", "dp", None),
        P("section", "dp"),
        P("section", None, None, "dp"),
    )
    return jax.shard_map(shards, mesh=mesh, in_specs=in_specs, out_specs=out_specs, check_vma=False)
```
